32 devices in a mesh: batch: 2 (over y), freq: 8 (over z, x), elem: 2 (over core).
Axes of the slice: x: 2, y: 2, z: 4, core: 2. Of those that a mesh axis runs over, the one named last changes fastest.
Arguments:
- flaw_cells: int32 [512], P('batch'), parts along dimension 0, may hold values from 0 to 255, each once
- flaw_blocks: int32 [16], P('batch'), parts along dimension 0, may hold values from 0 to 7, each once
- element_channel: int32 [256], P('elem'), may hold values from 0 to 255, each once
- focal_delay: float32 [256, 256], replicated, may hold values from 0 to 64
- beam_field: bfloat16 [128, 2, 256, 256], P('freq', None, 'elem'), may hold values from -0.125 to 0.125
- flaw_size: float32 [4, 128], P('batch'), parts along dimension 0, may hold values from 0.5 to 4
- flaw_slope: float32 [4, 128], P('batch'), parts along dimension 0, may hold values from 0.2 to 1
- noise_level: float32 [4, 128], P(('batch', 'elem'), 'freq'), parts along dimension 0, may hold values from 0.5 to 5
Outputs:
- flaw_peak: float32 [4, 128], P(('batch', 'elem'), 'freq'), parts along dimension 0
- detection: float32 [4, 128], P(('batch', 'elem'), 'freq'), parts along dimension 0
The draws below stay inside these ranges and needn't reach their ends.
There are 2 independent parts, one for each index of `batch`. The reference program is written for one: setup_inputs(seed, part) draws one part's arguments, and reference() takes and returns one part's arrays. A program takes and returns all parts, laid end to end along the dimension named above; an argument that names none is the same for every part. Nothing has to cross between parts.
Inputs may be any that keep to these rules, and one draw needn't show every extreme that they name: `flaw_cells`: every site holds exactly one flaw. `flaw_blocks`: every scan block belongs to exactly one flaw group. `element_channel`: every channel drives exactly one element.
All inputs are finite; a program needn't handle non-finite values.
Results may differ from the reference program's by a relative error of at most 0.0011.
Values may be sent and summed in bfloat16 or wider, within the bound.
No kernel may reach another device: no remote copies, remote signals or barrier semaphores. Data moves between devices by JAX's collectives and lax.ppermute only.
A program may use at most 64 MiB of HBM per device.

```python
import math
import jax
import jax.numpy as jnp
from jax import lax

W_DEV = 16
NW = 128
E = 256
E_GRP = 128
FG = 128
NG = 2
NB = 4
SB = 32
NSB = 8
S = 256
CELLS = 256
NT = 256
N_ELEM = 2


def levels(stream_key, dims, pieces, least, top_value):
    factor_of, own = 1.0, jax.random.fold_in(stream_key, 6)
    for position, blocks in pieces:
        draws = jnp.exp(jax.random.uniform(jax.random.fold_in(own, position), (blocks,), jnp.float32, least / len(pieces), top_value / len(pieces)))
        factor_of = factor_of * jnp.repeat(draws, dims[position] // blocks).reshape([-1 if axis == position else 1 for axis in range(len(dims))])
    return factor_of


def gaussian(own_key, shape, spread, most, shards=(), kind=jnp.bfloat16):
    entries = jax.random.normal(own_key, shape, jnp.float32) * spread
    if len(shards) > 0:
        entries = levels(own_key, shape, shards, -0.22, 0.18) * entries
    return jnp.clip(entries, min=-most, max=most).astype(kind)


def setup_inputs(seed: int = 0, part: int = 0) -> dict:
    key_of = jax.random.split(jax.random.key(seed), 9)
    own_keys = jax.random.split(jax.random.fold_in(key_of[8], part), 9)
    return {
        "flaw_cells": jax.random.permutation(own_keys[0], CELLS).astype(jnp.int32),
        "flaw_blocks": jax.random.permutation(own_keys[1], NSB).astype(jnp.int32),
        "element_channel": jax.random.permutation(key_of[2], E).astype(jnp.int32),
        "focal_delay": jnp.clip(jax.random.uniform(key_of[3], (E, S), jnp.float32, 0.0, 64.0), 0.0, 64.0),
        "beam_field": gaussian(key_of[4], (NW, 2, E, CELLS), (8 * E) ** -0.5, 0.125, ((0, 8), (2, 2))),
        "flaw_size": jnp.clip(jnp.exp(jax.random.uniform(own_keys[5], (NG, FG), jnp.float32, math.log(0.5), math.log(4.0))), 0.5, 4.0),
        "flaw_slope": jnp.clip(jax.random.uniform(own_keys[6], (NG, FG), jnp.float32, 0.2, 1.0), 0.2, 1.0),
        "noise_level": jnp.clip(jnp.exp(math.log(5.0) - 2.3025851 * jax.random.uniform(own_keys[7], (NG, FG), jnp.float32) ** levels(own_keys[7], (NG, FG), ((0, 2), (1, 8)), -0.2, 0.2)), 0.5, 5.0),
    }


EDGE = 0.6
STEEP = 3.0
EPS = 1e-05

def kirchhoff(angular, flaw_size, flaw_slope):
    angles = angular[None, :, None] * (2.0 * flaw_size * flaw_slope)[:, None, :]
    real_part = flaw_size[:, None, :] * (1.0 + EDGE) * jnp.cos(angles)
    imag_part = flaw_size[:, None, :] * (EDGE - 1.0) * jnp.sin(angles)
    return (real_part, imag_part)

def focal_law(angular, delays):
    phases = angular[:, None, None, None] * delays[None]
    return jnp.concatenate([jnp.cos(phases), -jnp.sin(phases)], axis=-1).astype(jnp.bfloat16)

def field_matrix(fields):
    real_part = fields[:, 0]
    imag_part = fields[:, 1]
    upper_rows = jnp.concatenate([real_part, imag_part], axis=-1)
    lower_rows = jnp.concatenate([-imag_part, real_part], axis=-1)
    return jnp.concatenate([upper_rows, lower_rows], axis=1)

def combine(product, k_real, k_imag):
    columns = k_real.shape[-1]
    real_part = product[..., :columns]
    imag_part = product[..., columns:]
    scale_real = k_real[:, :, None, :]
    scale_imag = k_imag[:, :, None, :]
    return jnp.stack([scale_real * real_part - scale_imag * imag_part, scale_real * imag_part + scale_imag * real_part], axis=2)

def reference(flaw_cells, flaw_blocks, element_channel, focal_delay, beam_field, flaw_size, flaw_slope, noise_level):
    row_total = NB * SB
    scan_rows = (flaw_blocks.reshape(NG, NB)[:, :, None] * SB + jnp.arange(SB, dtype=jnp.int32)[None, None, :]).reshape(NG, row_total)
    delays = jnp.moveaxis(jnp.take(jnp.take(focal_delay, element_channel, axis=0), scan_rows, axis=1), 0, 2)

    def one_block(starts):
        freq_index = starts + jnp.arange(W_DEV, dtype=jnp.int32)
        angular = freq_index.astype(jnp.float32) * (math.pi / NW)
        k_real, k_imag = kirchhoff(angular, flaw_size, flaw_slope)
        beam_block = lax.dynamic_slice_in_dim(beam_field, starts, W_DEV, 0)
        fields = jnp.take(beam_block, flaw_cells, axis=3).reshape(W_DEV, 2, E, NG, FG)
        summed = jnp.zeros((NG, W_DEV, 2, row_total, FG), jnp.float32)
        for member in range(N_ELEM):
            offset = member * E_GRP
            focal_terms = focal_law(angular, delays[:, :, offset:offset + E_GRP])
            field_terms = field_matrix(fields[:, :, offset:offset + E_GRP])
            product = jnp.einsum('wgre,wegf->gwrf', focal_terms.astype(jnp.float32), field_terms.astype(jnp.float32))
            partial_value = combine(product, k_real, k_imag).astype(jnp.bfloat16)
            summed = summed + partial_value.astype(jnp.float32)
        return summed.astype(jnp.bfloat16)
    block_starts = jnp.arange(NW // W_DEV, dtype=jnp.int32) * W_DEV
    spectra = lax.map(one_block, block_starts)

    def envelope(group_spectra):
        values = group_spectra.reshape(NW, 2, row_total, FG).astype(jnp.float32)
        signal = lax.complex(values[:, 0], values[:, 1])
        padded = jnp.concatenate([signal, jnp.zeros_like(signal)], axis=0)
        in_time = jnp.fft.ifft(padded, axis=0)[:NT] * (2.0 * NW / math.sqrt(NW))
        return lax.optimization_barrier(jnp.max(jnp.abs(in_time), axis=(0, 1)))
    flaw_peak = lax.map(envelope, jnp.moveaxis(spectra, 1, 0))
    detection = jax.nn.sigmoid(STEEP * (jnp.log(flaw_peak + EPS) - jnp.log(noise_level)))
    return (flaw_peak, detection)
```

```python
import functools
import math

import jax
import jax.numpy as jnp
from jax import lax
from jax.experimental import pallas as pl
from jax.experimental.pallas import tpu as pltpu
from jax.sharding import PartitionSpec as P

W_DEV = 16
FG = 128
NB = 4
SB = 32
T_CAP = 1024

EDGE = 0.6
STEEP = 3.0
EPS = 1e-05

ROWS = NB * SB
W_STEP = 8
VMEM_BYTES = 48 * 1024 * 1024


def sin_half_turn(turns):
    angle = turns * math.pi
    square = angle * angle
    sine = 1.0 / 6227020800.0
    for factorial in (-39916800.0, 362880.0, -5040.0, 120.0, -6.0, 1.0):
        sine = sine * square + 1.0 / factorial
    cosine = 1.0 / 479001600.0
    for factorial in (-3628800.0, 40320.0, -720.0, 24.0, -2.0, 1.0):
        cosine = cosine * square + 1.0 / factorial
    return sine * angle, cosine


def sincos_turns(turns):
    rest = turns - jnp.floor(turns + 0.5)
    sine, cosine = sin_half_turn(rest)
    return 2.0 * sine * cosine, 1.0 - 2.0 * sine * sine


def dot(left, right, contract):
    return lax.dot_general(
        left, right, (contract, ((), ())), preferred_element_type=jnp.float32
    )


def front_kernel(
    freq_total,
    cells_ref,
    blocks_ref,
    own_channel_ref,
    other_channel_ref,
    delay_ref,
    own_ref,
    other_ref,
    size_ref,
    slope_ref,
    out_ref,
    cos_ref,
    sin_ref,
    step_cos_ref,
    step_sin_ref,
    pick_ref,
    size_col_ref,
    turn_col_ref,
    rows_ref,
):
    step = pl.program_id(0)
    group = lax.axis_index("elem")
    first_freq = lax.axis_index("freq") * W_DEV
    sites = delay_ref.shape[0]

    @pl.when(step == 0)
    def _():
        lane = lax.broadcasted_iota(jnp.int32, (1, ROWS), 1)
        position = lane & (SB - 1)
        for j in range(NB):
            position = position + jnp.where(
                (lane >> 5) == j, blocks_ref[group * NB + j] * SB, 0
            )
        scan_sel = (
            lax.broadcasted_iota(jnp.int32, (delay_ref.shape[1], ROWS), 0) == position
        ).astype(jnp.bfloat16)
        channel_iota = lax.broadcasted_iota(jnp.int32, (delay_ref.shape[0], FG), 0)
        channel_sel = jnp.concatenate(
            [
                (channel_iota == own_channel_ref[...]).astype(jnp.float32),
                (channel_iota == other_channel_ref[...]).astype(jnp.float32),
            ],
            axis=1,
        ).T.astype(jnp.bfloat16)
        rest = delay_ref[...]
        delays = None
        for _piece in range(3):
            piece = rest.astype(jnp.bfloat16)
            rest = rest - piece.astype(jnp.float32)
            moved = dot(piece, scan_sel, ((1,), (0,))).astype(jnp.bfloat16)
            moved = dot(channel_sel, moved, ((1,), (0,)))
            delays = moved if delays is None else delays + moved
        turns = delays * (0.5 / freq_total)
        sine, cosine = sincos_turns(turns)
        step_cos_ref[...] = cosine
        step_sin_ref[...] = sine
        sine, cosine = sincos_turns(turns * first_freq.astype(jnp.float32))
        cos_ref[...] = cosine
        sin_ref[...] = sine
        cells = jnp.where(group == 0, cells_ref[:, :FG], cells_ref[:, FG:])
        cell_sel = lax.broadcasted_iota(jnp.int32, (sites, FG), 0) == cells
        pick_ref[...] = cell_sel.astype(jnp.float32).T.astype(jnp.bfloat16)
        diagonal = lax.broadcasted_iota(
            jnp.int32, (FG, FG), 0
        ) == lax.broadcasted_iota(jnp.int32, (FG, FG), 1)
        size = size_ref[pl.ds(group, 1), :]
        slope = slope_ref[pl.ds(group, 1), :]
        turn = size * slope * (1.0 / freq_total)
        size_col = jnp.sum(jnp.where(diagonal, size, 0.0), axis=1, keepdims=True)
        turn_col = jnp.sum(jnp.where(diagonal, turn, 0.0), axis=1, keepdims=True)
        size_col_ref[...] = jnp.broadcast_to(size_col, (FG, FG))
        turn_col_ref[...] = jnp.broadcast_to(turn_col, (FG, FG))

    freq = first_freq + step * W_STEP + lax.broadcasted_iota(jnp.int32, (FG, FG), 1)
    sine, cosine = sincos_turns(turn_col_ref[...] * freq.astype(jnp.float32))
    k_real = size_col_ref[...] * (1.0 + EDGE) * cosine
    k_imag = size_col_ref[...] * (EDGE - 1.0) * sine
    pick = pick_ref[...]
    cosine = cos_ref[...]
    sine = sin_ref[...]
    step_cos = step_cos_ref[...]
    step_sin = step_sin_ref[...]
    for w in range(W_STEP):
        fields = jnp.concatenate(
            [
                dot(pick, ref[w].reshape(2 * FG, sites), ((1,), (1,))).astype(jnp.bfloat16)
                for ref in (own_ref, other_ref)
            ],
            axis=1,
        )
        c = cosine.astype(jnp.bfloat16)
        s = sine.astype(jnp.bfloat16)
        both = jnp.concatenate([c, -s], axis=1)
        turned = jnp.concatenate([s, c], axis=1)
        law = jnp.concatenate([both[:FG], turned[:FG], both[FG:], turned[FG:]], axis=0)
        product = dot(fields, law, ((1,), (0,)))
        real_part = product[:, :ROWS]
        imag_part = product[:, ROWS:]
        kr = k_real[:, w : w + 1]
        ki = k_imag[:, w : w + 1]
        rows_ref[pl.ds(2 * w, FG, stride=2 * W_STEP), :] = kr * real_part - ki * imag_part
        rows_ref[pl.ds(2 * w + 1, FG, stride=2 * W_STEP), :] = (
            kr * imag_part + ki * real_part
        )
        cosine, sine = (
            cosine * step_cos - sine * step_sin,
            sine * step_cos + cosine * step_sin,
        )
    cos_ref[...] = cosine
    sin_ref[...] = sine
    out_ref[...] = rows_ref[...].reshape(FG, 2 * W_STEP, ROWS).astype(jnp.bfloat16)


def front(
    flaw_cells,
    flaw_blocks,
    own_channel,
    other_channel,
    focal_delay,
    own_field,
    other_field,
    flaw_size,
    flaw_slope,
    freq_total,
):
    def whole(array):
        return pl.BlockSpec(array.shape, lambda i: (0,) * array.ndim)

    small = [
        flaw_cells.reshape(1, -1),
        flaw_blocks,
        own_channel.reshape(1, -1),
        other_channel.reshape(1, -1),
        focal_delay,
    ]
    field_spec = pl.BlockSpec((W_STEP, *own_field.shape[1:]), lambda i: (i, 0, 0, 0))
    elements = 2 * own_channel.shape[0]
    in_specs = [whole(a) for a in small]
    in_specs[1] = pl.BlockSpec(memory_space=pltpu.SMEM)
    in_specs += [field_spec, field_spec, whole(flaw_size), whole(flaw_slope)]
    return pl.pallas_call(
        functools.partial(front_kernel, freq_total),
        grid=(W_DEV // W_STEP,),
        in_specs=in_specs,
        out_specs=pl.BlockSpec((FG, 2 * W_STEP, ROWS), lambda i: (0, i, 0)),
        out_shape=jax.ShapeDtypeStruct((FG, 2 * W_DEV, ROWS), jnp.bfloat16),
        scratch_shapes=[pltpu.VMEM((elements, ROWS), jnp.float32)] * 4
        + [
            pltpu.VMEM((FG, focal_delay.shape[0]), jnp.bfloat16),
            pltpu.VMEM((FG, FG), jnp.float32),
            pltpu.VMEM((FG, FG), jnp.float32),
            pltpu.VMEM((FG * 2 * W_STEP, ROWS), jnp.float32),
        ],
        compiler_params=pltpu.CompilerParams(vmem_limit_bytes=VMEM_BYTES),
        name="front",
    )(*small, own_field, other_field, flaw_size, flaw_slope)


def table_kernel(freq_total, high_ref, low_ref):
    _, height, depth = high_ref.shape
    time_block = height // 2
    row = lax.broadcasted_iota(jnp.int32, (height, depth), 0)
    column = lax.broadcasted_iota(jnp.int32, (height, depth), 1)
    out_imag = (row >= time_block).astype(jnp.int32)
    time = pl.program_id(0) * time_block + row - out_imag * time_block
    steps = (column >> 1) * time + ((column & 1) - out_imag) * (freq_total // 2)
    steps = (steps + 2 * freq_total) & (2 * freq_total - 1)
    _, value = sincos_turns(steps.astype(jnp.float32) * (0.5 / freq_total))
    high = value.astype(jnp.bfloat16)
    high_ref[0] = high
    low_ref[0] = (value - high.astype(jnp.float32)).astype(jnp.bfloat16)


def table(freq_total, sample_count, time_block):
    blocks = sample_count // time_block
    shape = (blocks, 2 * time_block, 2 * freq_total)
    spec = pl.BlockSpec((1, *shape[1:]), lambda i: (i, 0, 0))
    return pl.pallas_call(
        functools.partial(table_kernel, freq_total),
        grid=(blocks,),
        out_specs=[spec, spec],
        out_shape=[jax.ShapeDtypeStruct(shape, jnp.bfloat16)] * 2,
        compiler_params=pltpu.CompilerParams(vmem_limit_bytes=VMEM_BYTES),
        name="table",
    )()


def peak_kernel(freq_total, spectra_ref, high_ref, low_ref, noise_ref, peak_ref, found_ref, best_ref):
    step = pl.program_id(0)
    sources, columns, planes, rows = spectra_ref.shape
    time_block = high_ref.shape[1] // 2

    @pl.when(step == 0)
    def _():
        best_ref[...] = jnp.zeros_like(best_ref)

    high = high_ref[0]
    low = low_ref[0]
    width = min(2, columns)
    for first in range(0, columns, width):
        spectra = jnp.concatenate(
            [
                spectra_ref[:, first + k].reshape(sources * planes, rows)
                for k in range(width)
            ],
            axis=1,
        )
        signal = dot(high, spectra, ((1,), (0,))) + dot(low, spectra, ((1,), (0,)))
        real_part = signal[:time_block]
        imag_part = signal[time_block:]
        power = jnp.max(real_part * real_part + imag_part * imag_part, axis=0, keepdims=True)
        for k in range(width):
            row = pl.ds(first + k, 1)
            best_ref[row, :] = jnp.maximum(
                best_ref[row, :], power[:, k * rows : (k + 1) * rows]
            )

    @pl.when(step == pl.num_programs(0) - 1)
    def _():
        largest = jnp.max(best_ref[...], axis=1, keepdims=True)
        shape = best_ref.shape
        diagonal = lax.broadcasted_iota(jnp.int32, shape, 0) == lax.broadcasted_iota(
            jnp.int32, shape, 1
        )
        largest = jnp.max(jnp.where(diagonal, largest, 0.0), axis=0, keepdims=True)
        peak = jnp.sqrt(largest[:, :columns]) * (1.0 / math.sqrt(freq_total))
        score = STEEP * (jnp.log(peak + EPS) - jnp.log(noise_ref[...]))
        peak_ref[...] = peak
        found_ref[...] = 1.0 / (1.0 + jnp.exp(-score))


def peaks(spectra, high, low, noise_level, freq_total):
    columns = spectra.shape[1]
    blocks = high.shape[0]
    table_spec = pl.BlockSpec((1, *high.shape[1:]), lambda i: (i, 0, 0))
    out_spec = pl.BlockSpec((1, columns), lambda i: (0, 0))
    return pl.pallas_call(
        functools.partial(peak_kernel, freq_total),
        grid=(blocks,),
        in_specs=[
            pl.BlockSpec(spectra.shape, lambda i: (0, 0, 0, 0)),
            table_spec,
            table_spec,
            out_spec,
        ],
        out_specs=[out_spec, out_spec],
        out_shape=[jax.ShapeDtypeStruct((1, columns), jnp.float32)] * 2,
        scratch_shapes=[pltpu.VMEM((max(8, columns), ROWS), jnp.float32)],
        compiler_params=pltpu.CompilerParams(vmem_limit_bytes=VMEM_BYTES),
        name="peaks",
    )(spectra, high, low, noise_level)


def body(
    flaw_cells,
    flaw_blocks,
    element_channel,
    focal_delay,
    beam_field,
    flaw_size,
    flaw_slope,
    noise_level,
):
    freq_count = lax.axis_size("freq")
    freq_total = W_DEV * freq_count
    sample_count = min(T_CAP, 2 * freq_total)
    swap = [(0, 1), (1, 0)]
    other_channel = lax.ppermute(element_channel, "elem", swap)
    other_field = lax.ppermute(beam_field, "elem", swap)
    spectra = front(
        flaw_cells,
        flaw_blocks,
        element_channel,
        other_channel,
        focal_delay,
        beam_field,
        other_field,
        flaw_size,
        flaw_slope,
        freq_total,
    )
    high, low = table(freq_total, sample_count, 256 if freq_total <= 128 else 128)
    moved = lax.all_to_all(spectra, "freq", split_axis=0, concat_axis=0, tiled=True)
    moved = moved.reshape(freq_count, FG // freq_count, 2 * W_DEV, ROWS)
    return tuple(peaks(moved, high, low, noise_level, freq_total))


def solution(mesh):
    in_specs = (
        P("batch"),
        P("batch"),
        P("elem"),
        P(),
        P("freq", None, "elem", None),
        P("batch", None),
        P("batch", None),
        P(("batch", "elem"), "freq"),
    )
    out_specs = (P(("batch", "elem"), "freq"), P(("batch", "elem"), "freq"))
    return jax.shard_map(body, mesh=mesh, in_specs=in_specs, out_specs=out_specs, check_vma=False)
```

```python
import functools
import math

import jax
import jax.numpy as jnp
from jax import lax
from jax.experimental import pallas as pl
from jax.experimental.pallas import tpu as pltpu
from jax.sharding import PartitionSpec as P

W_DEV = 16
FG = 128
NB = 4
SB = 32
T_CAP = 1024

EDGE = 0.6
STEEP = 3.0
EPS = 1e-05

ROWS = NB * SB
W_STEP = 8
MOST_SLOTS = 8
VMEM_BYTES = 48 * 1024 * 1024


def sin_half_turn(turns):
    angle = turns * math.pi
    square = angle * angle
    sine = 1.0 / 6227020800.0
    for factorial in (-39916800.0, 362880.0, -5040.0, 120.0, -6.0, 1.0):
        sine = sine * square + 1.0 / factorial
    cosine = 1.0 / 479001600.0
    for factorial in (-3628800.0, 40320.0, -720.0, 24.0, -2.0, 1.0):
        cosine = cosine * square + 1.0 / factorial
    return sine * angle, cosine


def sincos_turns(turns):
    rest = turns - jnp.floor(turns + 0.5)
    sine, cosine = sin_half_turn(rest)
    return 2.0 * sine * cosine, 1.0 - 2.0 * sine * sine


def dot(left, right, contract):
    return lax.dot_general(
        left, right, (contract, ((), ())), preferred_element_type=jnp.float32
    )


def slot_order(size, slots):
    row = lax.broadcasted_iota(jnp.int32, (FG, FG), 0)
    column = lax.broadcasted_iota(jnp.int32, (FG, FG), 1)
    if slots > 1:
        row = row ^ (lax.axis_index("freq") * size)
    return row == column


def partial_kernel(freq_total, slots, first_step, *refs):
    if first_step == 0:
        (
            cells_ref,
            size_ref,
            slope_ref,
            field_hbm,
            blocks_ref,
            channel_ref,
            delay_hbm,
            other_ref,
            own_ref,
            next_cos_ref,
            next_sin_ref,
            step_cos_ref,
            step_sin_ref,
            field_ref,
            field_sem,
            delay_ref,
            delay_sem,
            picked_ref,
            law_ref,
            rows_ref,
        ) = refs
    else:
        (
            cells_ref,
            size_ref,
            slope_ref,
            field_hbm,
            cos_ref,
            sin_ref,
            step_cos_ref,
            step_sin_ref,
            other_ref,
            own_ref,
            field_ref,
            field_sem,
            picked_ref,
            law_ref,
            rows_ref,
        ) = refs
    field_copy = pltpu.make_async_copy(
        field_hbm.at[pl.ds(first_step * W_STEP, W_STEP)], field_ref, field_sem
    )
    field_copy.start()
    if first_step == 0:
        delay_copy = pltpu.make_async_copy(delay_hbm, delay_ref, delay_sem)
        delay_copy.start()
    group = lax.axis_index("elem")
    other = 1 - group
    first_freq = lax.axis_index("freq") * W_DEV
    elements, sites = field_ref.shape[2:]

    order = slot_order(FG // slots, slots)
    order_sel = order.astype(jnp.bfloat16)
    picks, sizes, turns = [], [], []
    for which in (other, group):
        cells = jnp.where(which == 0, cells_ref[:, :FG], cells_ref[:, FG:])
        cell_sel = lax.broadcasted_iota(jnp.int32, (sites, FG), 0) == cells
        picks.append(dot(order_sel, cell_sel.astype(jnp.bfloat16), ((1,), (1,))))
        size = size_ref[pl.ds(which, 1), :]
        turn = size * slope_ref[pl.ds(which, 1), :] * (1.0 / freq_total)
        sizes.append(jnp.sum(jnp.where(order, size, 0.0), axis=1, keepdims=True))
        turns.append(jnp.sum(jnp.where(order, turn, 0.0), axis=1, keepdims=True))
    pick = jnp.concatenate(picks, axis=0).astype(jnp.bfloat16)
    size = jnp.concatenate(sizes, axis=0)
    turn = jnp.concatenate(turns, axis=0)
    freq = (
        first_freq
        + first_step * W_STEP
        + lax.broadcasted_iota(jnp.int32, (2 * FG, FG), 1)
    )
    sine, cosine = sincos_turns(turn * freq.astype(jnp.float32))
    k_real = size * (1.0 + EDGE) * cosine
    k_imag = size * (EDGE - 1.0) * sine

    if first_step == 0:
        lane = lax.broadcasted_iota(jnp.int32, (1, 2 * ROWS), 1)
        position = lane & (SB - 1)
        for j in range(2 * NB):
            block = blocks_ref[(other if j < NB else group) * NB + j % NB]
            position = position + jnp.where((lane >> 5) == j, block * SB, 0)
        scan_sel = (
            lax.broadcasted_iota(jnp.int32, (delay_ref.shape[1], 2 * ROWS), 0) == position
        ).astype(jnp.bfloat16)
        channel_sel = (
            (
                lax.broadcasted_iota(jnp.int32, (delay_ref.shape[0], elements), 0)
                == channel_ref[...]
            )
            .astype(jnp.float32)
            .T.astype(jnp.bfloat16)
        )
        delay_copy.wait()
        rest = delay_ref[...]
        delays = None
        for _piece in range(3):
            piece = rest.astype(jnp.bfloat16)
            rest = rest - piece.astype(jnp.float32)
            moved = dot(channel_sel, piece, ((1,), (0,))).astype(jnp.bfloat16)
            moved = dot(moved, scan_sel, ((1,), (0,)))
            delays = moved if delays is None else delays + moved
        phase = delays * (0.5 / freq_total)
        step_sin, step_cos = sincos_turns(phase)
        step_cos_ref[...] = step_cos
        step_sin_ref[...] = step_sin
        sine, cosine = sincos_turns(phase * first_freq.astype(jnp.float32))
    else:
        cosine = cos_ref[...]
        sine = sin_ref[...]
        step_cos = step_cos_ref[...]
        step_sin = step_sin_ref[...]

    for w in range(W_STEP):
        c = cosine.astype(jnp.bfloat16)
        s = sine.astype(jnp.bfloat16)
        for k in range(2):
            columns = slice(k * ROWS, (k + 1) * ROWS)
            law_ref[w, k, :elements, :ROWS] = c[:, columns]
            law_ref[w, k, :elements, ROWS:] = -s[:, columns]
            law_ref[w, k, elements:, :ROWS] = s[:, columns]
            law_ref[w, k, elements:, ROWS:] = c[:, columns]
        if w < W_STEP - 1 or first_step == 0:
            cosine, sine = (
                cosine * step_cos - sine * step_sin,
                sine * step_cos + cosine * step_sin,
            )
    if first_step == 0:
        next_cos_ref[...] = cosine
        next_sin_ref[...] = sine

    field_copy.wait()
    for w in range(W_STEP):
        picked_ref[w] = dot(
            pick, field_ref[w].reshape(2 * elements, sites), ((1,), (1,))
        ).astype(jnp.bfloat16)
    for k, out_ref in enumerate((other_ref, own_ref)):
        rows = slice(k * FG, (k + 1) * FG)
        for w in range(W_STEP):
            product = dot(picked_ref[w, rows, :], law_ref[w, k], ((1,), (0,)))
            real_part = product[:, :ROWS]
            imag_part = product[:, ROWS:]
            kr = k_real[rows, w : w + 1]
            ki = k_imag[rows, w : w + 1]
            rows_ref[k, pl.ds(2 * w, FG, stride=2 * W_STEP), :] = (
                kr * real_part - ki * imag_part
            )
            rows_ref[k, pl.ds(2 * w + 1, FG, stride=2 * W_STEP), :] = (
                kr * imag_part + ki * real_part
            )
        out_ref[...] = (
            rows_ref[k].reshape(FG, 2 * W_STEP, ROWS).astype(jnp.bfloat16)
        )


def partials(small, field, extra, freq_total, slots, first_step):
    elements, sites = field.shape[2:]
    vmem = pl.BlockSpec(memory_space=pltpu.VMEM)
    hbm = pl.BlockSpec(memory_space=pltpu.HBM)
    smem = pl.BlockSpec(memory_space=pltpu.SMEM)
    out_shape = [jax.ShapeDtypeStruct((FG, 2 * W_STEP, ROWS), jnp.bfloat16)] * 2
    scratch = [
        pltpu.VMEM((W_STEP, 2, elements, sites), jnp.bfloat16),
        pltpu.SemaphoreType.DMA,
    ]
    if first_step == 0:
        extra_specs = [smem, vmem, hbm]
        out_shape += [jax.ShapeDtypeStruct((elements, 2 * ROWS), jnp.float32)] * 4
        scratch += [pltpu.VMEM(extra[2].shape, jnp.float32), pltpu.SemaphoreType.DMA]
    else:
        extra_specs = [vmem] * 4
    scratch += [
        pltpu.VMEM((W_STEP, 2 * FG, 2 * elements), jnp.bfloat16),
        pltpu.VMEM((W_STEP, 2, 2 * elements, 2 * ROWS), jnp.bfloat16),
        pltpu.VMEM((2, FG * 2 * W_STEP, ROWS), jnp.float32),
    ]
    return pl.pallas_call(
        functools.partial(partial_kernel, freq_total, slots, first_step),
        in_specs=[vmem] * 3 + [hbm] + extra_specs,
        out_specs=[vmem] * len(out_shape),
        out_shape=out_shape,
        scratch_shapes=scratch,
        compiler_params=pltpu.CompilerParams(vmem_limit_bytes=VMEM_BYTES),
        cost_estimate=pl.CostEstimate(
            flops=2 * W_STEP * 2 * 256**3, bytes_accessed=3 << 20, transcendentals=0
        ),
        name=f"partials_{first_step}",
    )(*small, field, *extra)


def add_kernel(own_ref, moved_ref, *out_refs):
    size = out_refs[0].shape[0]
    for slot, out_ref in enumerate(out_refs):
        rows = pl.ds(slot * size, size)
        out_ref[...] = (
            own_ref[rows].astype(jnp.float32) + moved_ref[rows].astype(jnp.float32)
        ).astype(jnp.bfloat16)


def add(own, moved, slots):
    vmem = pl.BlockSpec(memory_space=pltpu.VMEM)
    shape = jax.ShapeDtypeStruct((FG // slots, *own.shape[1:]), jnp.bfloat16)
    return pl.pallas_call(
        add_kernel,
        in_specs=[vmem, vmem],
        out_specs=[vmem] * slots,
        out_shape=[shape] * slots,
        compiler_params=pltpu.CompilerParams(vmem_limit_bytes=VMEM_BYTES),
        cost_estimate=pl.CostEstimate(flops=0, bytes_accessed=3 << 19, transcendentals=0),
        name="add_groups",
    )(own, moved)


def table_kernel(freq_total, slots, high_ref, low_ref):
    _, height, depth = high_ref.shape
    time_block = height // 2
    row = lax.broadcasted_iota(jnp.int32, (height, depth), 0)
    column = lax.broadcasted_iota(jnp.int32, (height, depth), 1)
    out_imag = (row >= time_block).astype(jnp.int32)
    time = pl.program_id(0) * time_block + row - out_imag * time_block
    freq = column >> 1
    if slots > 1:
        freq = freq ^ (lax.axis_index("freq") * W_DEV)
    steps = freq * time + ((column & 1) - out_imag) * (freq_total // 2)
    steps = (steps + 2 * freq_total) & (2 * freq_total - 1)
    _, value = sincos_turns(steps.astype(jnp.float32) * (0.5 / freq_total))
    high = value.astype(jnp.bfloat16)
    high_ref[0] = high
    low_ref[0] = (value - high.astype(jnp.float32)).astype(jnp.bfloat16)


def table(freq_total, slots, sample_count, time_block):
    blocks = sample_count // time_block
    shape = (blocks, 2 * time_block, 2 * freq_total)
    spec = pl.BlockSpec((1, *shape[1:]), lambda i: (i, 0, 0))
    return pl.pallas_call(
        functools.partial(table_kernel, freq_total, slots),
        grid=(blocks,),
        out_specs=[spec, spec],
        out_shape=[jax.ShapeDtypeStruct(shape, jnp.bfloat16)] * 2,
        compiler_params=pltpu.CompilerParams(vmem_limit_bytes=VMEM_BYTES),
        name="table",
    )()


def peak_kernel(freq_total, count, *refs):
    spectra_refs = refs[:count]
    high_ref, low_ref, noise_ref, peak_ref, found_ref, best_ref = refs[count:]
    step = pl.program_id(0)
    columns = peak_ref.shape[1]
    rows = ROWS
    time_block = high_ref.shape[1] // 2

    @pl.when(step == 0)
    def _():
        best_ref[...] = jnp.zeros_like(best_ref)

    high = high_ref[0]
    low = low_ref[0]
    width = min(2, columns)
    for first in range(0, columns, width):
        spectra = jnp.concatenate(
            [
                jnp.concatenate(
                    [ref[:, first + k].reshape(-1, rows) for ref in spectra_refs], axis=0
                )
                for k in range(width)
            ],
            axis=1,
        )
        signal = dot(high, spectra, ((1,), (0,))) + dot(low, spectra, ((1,), (0,)))
        real_part = signal[:time_block]
        imag_part = signal[time_block:]
        power = jnp.max(real_part * real_part + imag_part * imag_part, axis=0, keepdims=True)
        for k in range(width):
            row = pl.ds(first + k, 1)
            best_ref[row, :] = jnp.maximum(
                best_ref[row, :], power[:, k * rows : (k + 1) * rows]
            )

    @pl.when(step == pl.num_programs(0) - 1)
    def _():
        largest = jnp.max(best_ref[...], axis=1, keepdims=True)
        shape = best_ref.shape
        diagonal = lax.broadcasted_iota(jnp.int32, shape, 0) == lax.broadcasted_iota(
            jnp.int32, shape, 1
        )
        largest = jnp.max(jnp.where(diagonal, largest, 0.0), axis=0, keepdims=True)
        peak = jnp.sqrt(largest[:, :columns]) * (1.0 / math.sqrt(freq_total))
        score = STEEP * (jnp.log(peak + EPS) - jnp.log(noise_ref[...]))
        peak_ref[...] = peak
        found_ref[...] = 1.0 / (1.0 + jnp.exp(-score))


def peaks(spectra, high, low, noise_level, freq_total):
    columns = noise_level.shape[1]
    blocks = high.shape[0]
    table_spec = pl.BlockSpec((1, *high.shape[1:]), lambda i: (i, 0, 0))
    out_spec = pl.BlockSpec((1, columns), lambda i: (0, 0))
    return pl.pallas_call(
        functools.partial(peak_kernel, freq_total, len(spectra)),
        grid=(blocks,),
        in_specs=[pl.BlockSpec(a.shape, lambda i: (0, 0, 0, 0)) for a in spectra]
        + [table_spec, table_spec, out_spec],
        out_specs=[out_spec, out_spec],
        out_shape=[jax.ShapeDtypeStruct((1, columns), jnp.float32)] * 2,
        scratch_shapes=[pltpu.VMEM((max(8, columns), ROWS), jnp.float32)],
        compiler_params=pltpu.CompilerParams(vmem_limit_bytes=VMEM_BYTES),
        name="peaks",
    )(*spectra, high, low, noise_level)


def body(
    flaw_cells,
    flaw_blocks,
    element_channel,
    focal_delay,
    beam_field,
    flaw_size,
    flaw_slope,
    noise_level,
):
    freq_count = lax.axis_size("freq")
    freq_total = W_DEV * freq_count
    sample_count = min(T_CAP, 2 * freq_total)
    swap = [(0, 1), (1, 0)]
    slots = freq_count if freq_count <= MOST_SLOTS else 1
    small = (flaw_cells.reshape(1, -1), flaw_size, flaw_slope)
    extra = (flaw_blocks, element_channel.reshape(1, -1), focal_delay)
    chunks = []
    for first_step in range(W_DEV // W_STEP):
        other, own, *state = partials(small, beam_field, extra, freq_total, slots, first_step)
        extra = state if state else extra
        chunks.append(add(own, lax.ppermute(other, "elem", swap), slots))
    high, low = table(freq_total, slots, sample_count, 256 if freq_total <= 128 else 128)
    if slots > 1:
        spectra = []
        for slot in range(slots):
            pairs = [(a, a ^ slot) for a in range(slots)]
            for chunk in chunks:
                moved = lax.ppermute(chunk[slot], "freq", pairs) if slot else chunk[slot]
                spectra.append(moved[None])
    else:
        moved = lax.all_to_all(
            jnp.concatenate([chunk[0] for chunk in chunks], axis=1),
            "freq",
            split_axis=0,
            concat_axis=0,
            tiled=True,
        )
        spectra = [moved.reshape(freq_count, FG // freq_count, 2 * W_DEV, ROWS)]
    return tuple(peaks(spectra, high, low, noise_level, freq_total))


def solution(mesh):
    in_specs = (
        P("batch"),
        P("batch"),
        P("elem"),
        P(),
        P("freq", None, "elem", None),
        P("batch", None),
        P("batch", None),
        P(("batch", "elem"), "freq"),
    )
    out_specs = (P(("batch", "elem"), "freq"), P(("batch", "elem"), "freq"))
    return jax.shard_map(body, mesh=mesh, in_specs=in_specs, out_specs=out_specs, check_vma=False)
```

```python
import functools
import math

import jax
import jax.numpy as jnp
from jax import lax
from jax.experimental import pallas as pl
from jax.experimental.pallas import tpu as pltpu
from jax.sharding import PartitionSpec as P

W_DEV = 16
FG = 128
NB = 4
SB = 32
T_CAP = 1024

EDGE = 0.6
STEEP = 3.0
EPS = 1e-05

ROWS = NB * SB
W_STEP = 8
MOST_SLOTS = 8
VMEM_BYTES = 48 * 1024 * 1024


def sin_half_turn(turns):
    angle = turns * math.pi
    square = angle * angle
    sine = 1.0 / 6227020800.0
    for factorial in (-39916800.0, 362880.0, -5040.0, 120.0, -6.0, 1.0):
        sine = sine * square + 1.0 / factorial
    cosine = 1.0 / 479001600.0
    for factorial in (-3628800.0, 40320.0, -720.0, 24.0, -2.0, 1.0):
        cosine = cosine * square + 1.0 / factorial
    return sine * angle, cosine


def sincos_turns(turns):
    rest = turns - jnp.floor(turns + 0.5)
    sine, cosine = sin_half_turn(rest)
    return 2.0 * sine * cosine, 1.0 - 2.0 * sine * sine


def dot(left, right, contract):
    return lax.dot_general(
        left, right, (contract, ((), ())), preferred_element_type=jnp.float32
    )


def slot_order(size, slots):
    row = lax.broadcasted_iota(jnp.int32, (FG, FG), 0)
    column = lax.broadcasted_iota(jnp.int32, (FG, FG), 1)
    if slots > 1:
        row = row ^ (lax.axis_index("freq") * size)
    return row == column


def partial_kernel(freq_total, slots, first_step, *refs):
    if first_step == 0:
        hbm, outs, scratch = refs[:7], refs[7:16], refs[16:]
        field_hbm, *small_hbm = hbm
        other_ref, own_ref, next_cos_ref, next_sin_ref, *kept = outs
        step_cos_ref, step_sin_ref, pick_ref, k_real_ref, k_imag_ref = kept
        field_ref, picked_ref, law_ref, rows_ref, field_sem, small_sem, *small = scratch
        cells_ref, size_ref, slope_ref, channel_ref, delay_ref, blocks_ref = small
    else:
        field_hbm, cos_ref, sin_ref, *kept = refs[:8]
        step_cos_ref, step_sin_ref, pick_ref, k_real_ref, k_imag_ref = kept
        other_ref, own_ref = refs[8:10]
        field_ref, picked_ref, law_ref, rows_ref, field_sem = refs[10:]
    field_copy = pltpu.make_async_copy(
        field_hbm.at[pl.ds(first_step * W_STEP, W_STEP)], field_ref, field_sem
    )
    elements, sites = field_ref.shape[2:]
    if first_step == 0:
        copies = [
            pltpu.make_async_copy(source, target, small_sem.at[i])
            for i, (source, target) in enumerate(zip(small_hbm, small))
        ]
        for copy in copies:
            copy.start()
        field_copy.start()
        group = lax.axis_index("elem")
        other = 1 - group
        first_freq = lax.axis_index("freq") * W_DEV
        order = slot_order(FG // slots, slots)
        order_sel = order.astype(jnp.bfloat16)
        for copy in copies:
            copy.wait()
        sizes, turns = [], []
        for k, which in enumerate((other, group)):
            cells = jnp.where(which == 0, cells_ref[:, :FG], cells_ref[:, FG:])
            cell_sel = lax.broadcasted_iota(jnp.int32, (sites, FG), 0) == cells
            pick_ref[k * FG : (k + 1) * FG, :] = dot(
                order_sel, cell_sel.astype(jnp.bfloat16), ((1,), (1,))
            ).astype(jnp.bfloat16)
            size = size_ref[pl.ds(which, 1), :]
            turn = size * slope_ref[pl.ds(which, 1), :] * (1.0 / freq_total)
            sizes.append(jnp.sum(jnp.where(order, size, 0.0), axis=1, keepdims=True))
            turns.append(jnp.sum(jnp.where(order, turn, 0.0), axis=1, keepdims=True))
        size = jnp.concatenate(sizes, axis=0)
        turn = jnp.concatenate(turns, axis=0)
        freq = first_freq + lax.broadcasted_iota(jnp.int32, (2 * FG, FG), 1)
        sine, cosine = sincos_turns(turn * freq.astype(jnp.float32))
        k_real_ref[...] = size * (1.0 + EDGE) * cosine
        k_imag_ref[...] = size * (EDGE - 1.0) * sine
        lane = lax.broadcasted_iota(jnp.int32, (1, 2 * ROWS), 1)
        position = lane & (SB - 1)
        for j in range(2 * NB):
            block = blocks_ref[(other if j < NB else group) * NB + j % NB]
            position = position + jnp.where((lane >> 5) == j, block * SB, 0)
        scan_sel = (
            lax.broadcasted_iota(jnp.int32, (delay_ref.shape[1], 2 * ROWS), 0) == position
        ).astype(jnp.bfloat16)
        channel_sel = (
            (
                lax.broadcasted_iota(jnp.int32, (delay_ref.shape[0], elements), 0)
                == channel_ref[...]
            )
            .astype(jnp.float32)
            .T.astype(jnp.bfloat16)
        )
        rest = delay_ref[...]
        delays = None
        for _piece in range(3):
            piece = rest.astype(jnp.bfloat16)
            rest = rest - piece.astype(jnp.float32)
            moved = dot(channel_sel, piece, ((1,), (0,))).astype(jnp.bfloat16)
            moved = dot(moved, scan_sel, ((1,), (0,)))
            delays = moved if delays is None else delays + moved
        phase = delays * (0.5 / freq_total)
        step_sin, step_cos = sincos_turns(phase)
        step_cos_ref[...] = step_cos
        step_sin_ref[...] = step_sin
        sine, cosine = sincos_turns(phase * first_freq.astype(jnp.float32))
    else:
        field_copy.start()
        cosine = cos_ref[...]
        sine = sin_ref[...]
        step_cos = step_cos_ref[...]
        step_sin = step_sin_ref[...]

    for w in range(W_STEP):
        c = cosine.astype(jnp.bfloat16)
        s = sine.astype(jnp.bfloat16)
        for k in range(2):
            columns = slice(k * ROWS, (k + 1) * ROWS)
            law_ref[w, k, :elements, :ROWS] = c[:, columns]
            law_ref[w, k, :elements, ROWS:] = -s[:, columns]
            law_ref[w, k, elements:, :ROWS] = s[:, columns]
            law_ref[w, k, elements:, ROWS:] = c[:, columns]
        if w < W_STEP - 1 or first_step == 0:
            cosine, sine = (
                cosine * step_cos - sine * step_sin,
                sine * step_cos + cosine * step_sin,
            )
    if first_step == 0:
        next_cos_ref[...] = cosine
        next_sin_ref[...] = sine

    field_copy.wait()
    for w in range(W_STEP):
        picked_ref[w] = dot(
            pick_ref[...], field_ref[w].reshape(2 * elements, sites), ((1,), (1,))
        ).astype(jnp.bfloat16)
    for k, out_ref in enumerate((other_ref, own_ref)):
        rows = slice(k * FG, (k + 1) * FG)
        for w in range(W_STEP):
            product = dot(picked_ref[w, rows, :], law_ref[w, k], ((1,), (0,)))
            real_part = product[:, :ROWS]
            imag_part = product[:, ROWS:]
            freq = first_step * W_STEP + w
            kr = k_real_ref[rows, freq : freq + 1]
            ki = k_imag_ref[rows, freq : freq + 1]
            rows_ref[k, pl.ds(2 * w, FG, stride=2 * W_STEP), :] = (
                kr * real_part - ki * imag_part
            )
            rows_ref[k, pl.ds(2 * w + 1, FG, stride=2 * W_STEP), :] = (
                kr * imag_part + ki * real_part
            )
        out_ref[...] = (
            rows_ref[k].reshape(FG, 2 * W_STEP, ROWS).astype(jnp.bfloat16)
        )


def partials(field, others, freq_total, slots, first_step):
    elements, sites = field.shape[2:]
    vmem = pl.BlockSpec(memory_space=pltpu.VMEM)
    hbm = pl.BlockSpec(memory_space=pltpu.HBM)
    out_shape = [jax.ShapeDtypeStruct((FG, 2 * W_STEP, ROWS), jnp.bfloat16)] * 2
    scratch = [
        pltpu.VMEM((W_STEP, 2, elements, sites), jnp.bfloat16),
        pltpu.VMEM((W_STEP, 2 * FG, 2 * elements), jnp.bfloat16),
        pltpu.VMEM((W_STEP, 2, 2 * elements, 2 * ROWS), jnp.bfloat16),
        pltpu.VMEM((2, FG * 2 * W_STEP, ROWS), jnp.float32),
        pltpu.SemaphoreType.DMA,
    ]
    if first_step == 0:
        out_shape += [jax.ShapeDtypeStruct((elements, 2 * ROWS), jnp.float32)] * 4
        out_shape += [jax.ShapeDtypeStruct((2 * FG, sites), jnp.bfloat16)]
        out_shape += [jax.ShapeDtypeStruct((2 * FG, FG), jnp.float32)] * 2
        scratch += [pltpu.SemaphoreType.DMA((len(others),))]
        scratch += [pltpu.VMEM(a.shape, a.dtype) for a in others[:-1]]
        scratch += [pltpu.SMEM(others[-1].shape, others[-1].dtype)]
        others = [pltpu.with_memory_space_constraint(a, pltpu.HBM) for a in others]
        specs = [hbm] * len(others)
    else:
        specs = [vmem] * len(others)
    return pl.pallas_call(
        functools.partial(partial_kernel, freq_total, slots, first_step),
        in_specs=[hbm] + specs,
        out_specs=[vmem] * len(out_shape),
        out_shape=out_shape,
        scratch_shapes=scratch,
        compiler_params=pltpu.CompilerParams(vmem_limit_bytes=VMEM_BYTES),
        cost_estimate=pl.CostEstimate(
            flops=2 * W_STEP * 2 * 256**3, bytes_accessed=3 << 20, transcendentals=0
        ),
        name=f"partials_{first_step}",
    )(pltpu.with_memory_space_constraint(field, pltpu.HBM), *others)


def add_kernel(own_ref, moved_ref, *out_refs):
    size = out_refs[0].shape[0]
    for slot, out_ref in enumerate(out_refs):
        rows = pl.ds(slot * size, size)
        out_ref[...] = (
            own_ref[rows].astype(jnp.float32) + moved_ref[rows].astype(jnp.float32)
        ).astype(jnp.bfloat16)


def add(own, moved, slots):
    vmem = pl.BlockSpec(memory_space=pltpu.VMEM)
    shape = jax.ShapeDtypeStruct((FG // slots, *own.shape[1:]), jnp.bfloat16)
    return pl.pallas_call(
        add_kernel,
        in_specs=[vmem, vmem],
        out_specs=[vmem] * slots,
        out_shape=[shape] * slots,
        compiler_params=pltpu.CompilerParams(vmem_limit_bytes=VMEM_BYTES),
        cost_estimate=pl.CostEstimate(flops=0, bytes_accessed=3 << 19, transcendentals=0),
        name="add_groups",
    )(own, moved)


def table_kernel(freq_total, slots, high_ref, low_ref):
    _, height, depth = high_ref.shape
    time_block = height // 2
    row = lax.broadcasted_iota(jnp.int32, (height, depth), 0)
    column = lax.broadcasted_iota(jnp.int32, (height, depth), 1)
    out_imag = (row >= time_block).astype(jnp.int32)
    time = pl.program_id(0) * time_block + row - out_imag * time_block
    freq = column >> 1
    if slots > 1:
        freq = freq ^ (lax.axis_index("freq") * W_DEV)
    steps = freq * time + ((column & 1) - out_imag) * (freq_total // 2)
    steps = (steps + 2 * freq_total) & (2 * freq_total - 1)
    _, value = sincos_turns(steps.astype(jnp.float32) * (0.5 / freq_total))
    high = value.astype(jnp.bfloat16)
    high_ref[0] = high
    low_ref[0] = (value - high.astype(jnp.float32)).astype(jnp.bfloat16)


def table(freq_total, slots, sample_count, time_block):
    blocks = sample_count // time_block
    shape = (blocks, 2 * time_block, 2 * freq_total)
    spec = pl.BlockSpec((1, *shape[1:]), lambda i: (i, 0, 0))
    return pl.pallas_call(
        functools.partial(table_kernel, freq_total, slots),
        grid=(blocks,),
        out_specs=[spec, spec],
        out_shape=[jax.ShapeDtypeStruct(shape, jnp.bfloat16)] * 2,
        compiler_params=pltpu.CompilerParams(vmem_limit_bytes=VMEM_BYTES),
        name="table",
    )()


def peak_kernel(freq_total, count, *refs):
    spectra_refs = refs[:count]
    high_ref, low_ref, noise_ref, peak_ref, found_ref, best_ref = refs[count:]
    step = pl.program_id(0)
    columns = peak_ref.shape[1]
    rows = ROWS
    time_block = high_ref.shape[1] // 2

    @pl.when(step == 0)
    def _():
        best_ref[...] = jnp.zeros_like(best_ref)

    high = high_ref[0]
    low = low_ref[0]
    width = min(2, columns)
    for first in range(0, columns, width):
        spectra = jnp.concatenate(
            [
                jnp.concatenate(
                    [ref[:, first + k].reshape(-1, rows) for ref in spectra_refs], axis=0
                )
                for k in range(width)
            ],
            axis=1,
        )
        signal = dot(high, spectra, ((1,), (0,))) + dot(low, spectra, ((1,), (0,)))
        real_part = signal[:time_block]
        imag_part = signal[time_block:]
        power = jnp.max(real_part * real_part + imag_part * imag_part, axis=0, keepdims=True)
        for k in range(width):
            row = pl.ds(first + k, 1)
            best_ref[row, :] = jnp.maximum(
                best_ref[row, :], power[:, k * rows : (k + 1) * rows]
            )

    @pl.when(step == pl.num_programs(0) - 1)
    def _():
        largest = jnp.max(best_ref[...], axis=1, keepdims=True)
        shape = best_ref.shape
        diagonal = lax.broadcasted_iota(jnp.int32, shape, 0) == lax.broadcasted_iota(
            jnp.int32, shape, 1
        )
        largest = jnp.max(jnp.where(diagonal, largest, 0.0), axis=0, keepdims=True)
        peak = jnp.sqrt(largest[:, :columns]) * (1.0 / math.sqrt(freq_total))
        score = STEEP * (jnp.log(peak + EPS) - jnp.log(noise_ref[...]))
        peak_ref[...] = peak
        found_ref[...] = 1.0 / (1.0 + jnp.exp(-score))


def peaks(spectra, high, low, noise_level, freq_total):
    columns = noise_level.shape[1]
    blocks = high.shape[0]
    table_spec = pl.BlockSpec((1, *high.shape[1:]), lambda i: (i, 0, 0))
    out_spec = pl.BlockSpec((1, columns), lambda i: (0, 0))
    return pl.pallas_call(
        functools.partial(peak_kernel, freq_total, len(spectra)),
        grid=(blocks,),
        in_specs=[pl.BlockSpec(a.shape, lambda i: (0, 0, 0, 0)) for a in spectra]
        + [table_spec, table_spec, out_spec],
        out_specs=[out_spec, out_spec],
        out_shape=[jax.ShapeDtypeStruct((1, columns), jnp.float32)] * 2,
        scratch_shapes=[pltpu.VMEM((max(8, columns), ROWS), jnp.float32)],
        compiler_params=pltpu.CompilerParams(vmem_limit_bytes=VMEM_BYTES),
        name="peaks",
    )(*spectra, high, low, noise_level)


def body(
    flaw_cells,
    flaw_blocks,
    element_channel,
    focal_delay,
    beam_field,
    flaw_size,
    flaw_slope,
    noise_level,
):
    freq_count = lax.axis_size("freq")
    freq_total = W_DEV * freq_count
    sample_count = min(T_CAP, 2 * freq_total)
    swap = [(0, 1), (1, 0)]
    slots = freq_count if freq_count <= MOST_SLOTS else 1
    others = (
        flaw_cells.reshape(1, -1),
        flaw_size,
        flaw_slope,
        element_channel.reshape(1, -1),
        focal_delay,
        flaw_blocks,
    )
    chunks = []
    for first_step in range(W_DEV // W_STEP):
        other, own, *others = partials(beam_field, others, freq_total, slots, first_step)
        chunks.append(add(own, lax.ppermute(other, "elem", swap), slots))
    high, low = table(freq_total, slots, sample_count, 256 if freq_total <= 128 else 128)
    if slots > 1:
        spectra = {}
        half = slots // 2
        for chunk, arrays in enumerate(chunks):
            for slot in [*range(half, slots), *range(1, half)]:
                pairs = [(a, a ^ slot) for a in range(slots)]
                spectra[slot, chunk] = lax.ppermute(arrays[slot], "freq", pairs)
            spectra[0, chunk] = arrays[0]
        spectra = [spectra[key][None] for key in sorted(spectra)]
    else:
        moved = lax.all_to_all(
            jnp.concatenate([chunk[0] for chunk in chunks], axis=1),
            "freq",
            split_axis=0,
            concat_axis=0,
            tiled=True,
        )
        spectra = [moved.reshape(freq_count, FG // freq_count, 2 * W_DEV, ROWS)]
    return tuple(peaks(spectra, high, low, noise_level, freq_total))


def solution(mesh):
    in_specs = (
        P("batch"),
        P("batch"),
        P("elem"),
        P(),
        P("freq", None, "elem", None),
        P("batch", None),
        P("batch", None),
        P(("batch", "elem"), "freq"),
    )
    out_specs = (P(("batch", "elem"), "freq"), P(("batch", "elem"), "freq"))
    return jax.shard_map(body, mesh=mesh, in_specs=in_specs, out_specs=out_specs, check_vma=False)
```

```python
import functools
import math

import jax
import jax.numpy as jnp
from jax import lax
from jax.experimental import pallas as pl
from jax.experimental.pallas import tpu as pltpu
from jax.sharding import PartitionSpec as P

W_DEV = 16
FG = 128
NB = 4
SB = 32
T_CAP = 1024

EDGE = 0.6
STEEP = 3.0
EPS = 1e-05

ROWS = NB * SB
W_STEP = 8
MOST_SLOTS = 8
VMEM_BYTES = 48 * 1024 * 1024


def sin_half_turn(turns):
    angle = turns * math.pi
    square = angle * angle
    sine = 1.0 / 6227020800.0
    for factorial in (-39916800.0, 362880.0, -5040.0, 120.0, -6.0, 1.0):
        sine = sine * square + 1.0 / factorial
    cosine = 1.0 / 479001600.0
    for factorial in (-3628800.0, 40320.0, -720.0, 24.0, -2.0, 1.0):
        cosine = cosine * square + 1.0 / factorial
    return sine * angle, cosine


def sincos_turns(turns):
    rest = turns - jnp.floor(turns + 0.5)
    sine, cosine = sin_half_turn(rest)
    return 2.0 * sine * cosine, 1.0 - 2.0 * sine * sine


def dot(left, right, contract):
    return lax.dot_general(
        left, right, (contract, ((), ())), preferred_element_type=jnp.float32
    )


def slot_order(size, slots):
    row = lax.broadcasted_iota(jnp.int32, (FG, FG), 0)
    column = lax.broadcasted_iota(jnp.int32, (FG, FG), 1)
    if slots > 1:
        row = row ^ (lax.axis_index("freq") * size)
    return row == column


def prepare(freq_total, slots, small, state, field_shape):
    cells_ref, size_ref, slope_ref, channel_ref, delay_ref, blocks_ref = small
    cos_ref, sin_ref, step_cos_ref, step_sin_ref, pick_ref, k_real_ref, k_imag_ref = state
    elements, sites = field_shape[2:]
    group = lax.axis_index("elem")
    other = 1 - group
    first_freq = lax.axis_index("freq") * W_DEV
    order = slot_order(FG // slots, slots)
    order_sel = order.astype(jnp.bfloat16)
    for k, which in enumerate((other, group)):
        cells = jnp.where(which == 0, cells_ref[:, :FG], cells_ref[:, FG:])
        cell_sel = lax.broadcasted_iota(jnp.int32, (sites, FG), 0) == cells
        pick_ref[k] = dot(
            order_sel, cell_sel.astype(jnp.bfloat16), ((1,), (1,))
        ).astype(jnp.bfloat16)
        size = size_ref[pl.ds(which, 1), :]
        turn = size * slope_ref[pl.ds(which, 1), :] * (1.0 / freq_total)
        size = jnp.sum(jnp.where(order, size, 0.0), axis=1, keepdims=True)
        turn = jnp.sum(jnp.where(order, turn, 0.0), axis=1, keepdims=True)
        freq = first_freq + lax.broadcasted_iota(jnp.int32, (FG, FG), 1)
        sine, cosine = sincos_turns(turn * freq.astype(jnp.float32))
        k_real_ref[k] = size * (1.0 + EDGE) * cosine
        k_imag_ref[k] = size * (EDGE - 1.0) * sine
    lane = lax.broadcasted_iota(jnp.int32, (1, 2 * ROWS), 1)
    position = lane & (SB - 1)
    for j in range(2 * NB):
        block = blocks_ref[(other if j < NB else group) * NB + j % NB]
        position = position + jnp.where((lane >> 5) == j, block * SB, 0)
    scan_sel = (
        lax.broadcasted_iota(jnp.int32, (delay_ref.shape[1], 2 * ROWS), 0) == position
    ).astype(jnp.bfloat16)
    channel_sel = (
        (
            lax.broadcasted_iota(jnp.int32, (delay_ref.shape[0], elements), 0)
            == channel_ref[...]
        )
        .astype(jnp.float32)
        .T.astype(jnp.bfloat16)
    )
    rest = delay_ref[...]
    delays = None
    for _piece in range(3):
        piece = rest.astype(jnp.bfloat16)
        rest = rest - piece.astype(jnp.float32)
        moved = dot(channel_sel, piece, ((1,), (0,))).astype(jnp.bfloat16)
        moved = dot(moved, scan_sel, ((1,), (0,)))
        delays = moved if delays is None else delays + moved
    phase = delays * (0.5 / freq_total)
    step_sin, step_cos = sincos_turns(phase)
    sin, cos = sincos_turns(phase * first_freq.astype(jnp.float32))
    for k in range(2):
        columns = slice(k * ROWS, (k + 1) * ROWS)
        for ref, value in zip(
            (cos_ref, sin_ref, step_cos_ref, step_sin_ref), (cos, sin, step_cos, step_sin)
        ):
            ref[k] = value[:, columns]


def partial_step(group, first_step, state, after, field_ref, wait, out_ref, scratch):
    cos_ref, sin_ref, step_cos_ref, step_sin_ref, pick_ref, k_real_ref, k_imag_ref = state
    picked_ref, law_ref, rows_ref = scratch
    elements, sites = field_ref.shape[2:]
    cosine, sine = cos_ref[group], sin_ref[group]
    step_cos, step_sin = step_cos_ref[group], step_sin_ref[group]
    for w in range(W_STEP):
        c = cosine.astype(jnp.bfloat16)
        s = sine.astype(jnp.bfloat16)
        law_ref[w, :elements, :ROWS] = c
        law_ref[w, :elements, ROWS:] = -s
        law_ref[w, elements:, :ROWS] = s
        law_ref[w, elements:, ROWS:] = c
        if w < W_STEP - 1 or after:
            cosine, sine = (
                cosine * step_cos - sine * step_sin,
                sine * step_cos + cosine * step_sin,
            )
    if after:
        after[0][...] = cosine
        after[1][...] = sine
    wait()
    pick = pick_ref[group]
    for w in range(W_STEP):
        picked_ref[w] = dot(
            pick, field_ref[w].reshape(2 * elements, sites), ((1,), (1,))
        ).astype(jnp.bfloat16)
    for w in range(W_STEP):
        product = dot(picked_ref[w], law_ref[w], ((1,), (0,)))
        real_part = product[:, :ROWS]
        imag_part = product[:, ROWS:]
        freq = first_step * W_STEP + w
        kr = k_real_ref[group, :, freq : freq + 1]
        ki = k_imag_ref[group, :, freq : freq + 1]
        rows_ref[pl.ds(2 * w, FG, stride=2 * W_STEP), :] = kr * real_part - ki * imag_part
        rows_ref[pl.ds(2 * w + 1, FG, stride=2 * W_STEP), :] = (
            kr * imag_part + ki * real_part
        )
    out_ref[...] = rows_ref[...].reshape(FG, 2 * W_STEP, ROWS).astype(jnp.bfloat16)


def first_kernel(freq_total, slots, field_hbm, *refs):
    small_hbm, refs = refs[:6], refs[6:]
    out_ref, field_ref, next_cos_ref, next_sin_ref, *refs = refs
    state, refs = refs[:7], refs[7:]
    small, refs = refs[:6], refs[6:]
    field_sem, small_sem, *scratch = refs
    copies = [
        pltpu.make_async_copy(source, target, small_sem.at[i])
        for i, (source, target) in enumerate(zip(small_hbm, small))
    ]
    for copy in copies:
        copy.start()
    field_copy = pltpu.make_async_copy(
        field_hbm.at[pl.ds(0, W_STEP)], field_ref, field_sem
    )
    field_copy.start()
    for copy in copies:
        copy.wait()
    prepare(freq_total, slots, small, state, field_ref.shape)
    after = (next_cos_ref, next_sin_ref)
    partial_step(0, 0, state, after, field_ref, field_copy.wait, out_ref, scratch)


def second_kernel(field_hbm, field_ref, *refs):
    state, refs = refs[:7], refs[7:]
    out_ref, next_field_ref, next_cos_ref, next_sin_ref, field_sem, *scratch = refs
    field_copy = pltpu.make_async_copy(
        field_hbm.at[pl.ds(W_STEP, W_STEP)], next_field_ref, field_sem
    )
    field_copy.start()
    after = (next_cos_ref, next_sin_ref)
    partial_step(1, 0, state, after, field_ref, lambda: None, out_ref, scratch)
    field_copy.wait()


def later_kernel(group, field_ref, cos_ref, sin_ref, *refs):
    rest, refs = refs[:5], refs[5:]
    _, out_ref, *scratch = refs
    state = ({group: cos_ref[...]}, {group: sin_ref[...]}, *rest)
    partial_step(group, 1, state, (), field_ref, lambda: None, out_ref, scratch)


def call(kernel, name, in_specs, out_shape, scratch):
    vmem = pl.BlockSpec(memory_space=pltpu.VMEM)
    return pl.pallas_call(
        kernel,
        in_specs=in_specs,
        out_specs=[vmem] * len(out_shape),
        out_shape=out_shape,
        scratch_shapes=scratch,
        compiler_params=pltpu.CompilerParams(vmem_limit_bytes=VMEM_BYTES),
        cost_estimate=pl.CostEstimate(
            flops=2 * W_STEP * 256**3, bytes_accessed=2 << 20, transcendentals=0
        ),
        name=name,
    )


def partials(field, small, swap, freq_total, slots):
    elements, sites = field.shape[2:]
    vmem = pl.BlockSpec(memory_space=pltpu.VMEM)
    hbm = pl.BlockSpec(memory_space=pltpu.HBM)
    out = jax.ShapeDtypeStruct((FG, 2 * W_STEP, ROWS), jnp.bfloat16)
    block = jax.ShapeDtypeStruct((W_STEP, *field.shape[1:]), field.dtype)
    law = jax.ShapeDtypeStruct((elements, ROWS), jnp.float32)
    laws = jax.ShapeDtypeStruct((2, elements, ROWS), jnp.float32)
    factor = jax.ShapeDtypeStruct((2, FG, FG), jnp.float32)
    pick = jax.ShapeDtypeStruct((2, FG, sites), jnp.bfloat16)
    work = [
        pltpu.VMEM((W_STEP, FG, 2 * elements), jnp.bfloat16),
        pltpu.VMEM((W_STEP, 2 * elements, 2 * ROWS), jnp.bfloat16),
        pltpu.VMEM((FG * 2 * W_STEP, ROWS), jnp.float32),
    ]
    field = pltpu.with_memory_space_constraint(field, pltpu.HBM)
    small = [pltpu.with_memory_space_constraint(a, pltpu.HBM) for a in small]
    other, first, *refs = call(
        functools.partial(first_kernel, freq_total, slots),
        "other_first",
        [hbm] * (1 + len(small)),
        [out, block, law, law, laws, laws, laws, laws, pick, factor, factor],
        [pltpu.VMEM(a.shape, a.dtype) for a in small[:-1]]
        + [pltpu.SMEM(small[-1].shape, small[-1].dtype)]
        + [pltpu.SemaphoreType.DMA, pltpu.SemaphoreType.DMA((len(small),))]
        + work,
    )(field, *small)
    (other_law, state) = (refs[:2], refs[2:])
    moved = lax.ppermute(other, "elem", swap)
    own, second, *own_law = call(
        second_kernel,
        "own_first",
        [hbm] + [vmem] * 8,
        [out, block, law, law],
        [pltpu.SemaphoreType.DMA] + work,
    )(field, first, *state)
    start, held = add_first(own, moved, slots)
    specs = [vmem] * 8 + [pl.BlockSpec(memory_space=pl.ANY)]
    (other,) = call(
        functools.partial(later_kernel, 0), "other_second", specs, [out], work
    )(second, *other_law, *state[2:], held)
    moved = lax.ppermute(other, "elem", swap)
    (own,) = call(functools.partial(later_kernel, 1), "own_second", specs, [out], work)(
        second, *own_law, *state[2:], held
    )
    return start, add_second(own, moved, held, slots)


def total(own_ref, moved_ref, rows):
    both = own_ref[rows].astype(jnp.float32) + moved_ref[rows].astype(jnp.float32)
    return both.astype(jnp.bfloat16)


def add_first_kernel(size, own_ref, moved_ref, *refs):
    *far_refs, near_ref = refs
    near = near_ref.shape[0]
    near_ref[...] = total(own_ref, moved_ref, pl.ds(0, near))
    for i, ref in enumerate(far_refs):
        ref[...] = total(own_ref, moved_ref, pl.ds(near + i * size, size))


def add_second_kernel(size, own_ref, moved_ref, held_ref, *refs):
    near = held_ref.shape[0]
    planes = held_ref.shape[1]
    for i in range(near // size):
        rows = pl.ds(i * size, size)
        refs[i][:, :planes] = held_ref[rows]
        refs[i][:, planes:] = total(own_ref, moved_ref, rows)
    for i, ref in enumerate(refs[near // size :]):
        ref[...] = total(own_ref, moved_ref, pl.ds(near + i * size, size))


def add_first(own, moved, slots):
    vmem = pl.BlockSpec(memory_space=pltpu.VMEM)
    size, far = FG // slots, slots // 2
    shape = jax.ShapeDtypeStruct((size, *own.shape[1:]), own.dtype)
    held = jax.ShapeDtypeStruct((FG - far * size, *own.shape[1:]), own.dtype)
    *start, held = call(
        functools.partial(add_first_kernel, size),
        "add_first",
        [vmem] * 2,
        [shape] * far + [held],
        [],
    )(own, moved)
    return start, held


def add_second(own, moved, held, slots):
    vmem = pl.BlockSpec(memory_space=pltpu.VMEM)
    size, far = FG // slots, slots // 2
    shape = jax.ShapeDtypeStruct((size, *own.shape[1:]), own.dtype)
    wide = jax.ShapeDtypeStruct((size, 2 * own.shape[1], own.shape[2]), own.dtype)
    return call(
        functools.partial(add_second_kernel, size),
        "add_second",
        [vmem] * 3,
        [wide] * (slots - far) + [shape] * far,
        [],
    )(own, moved, held)


def table_kernel(freq_total, slots, high_ref, low_ref):
    _, height, depth = high_ref.shape
    time_block = height // 2
    row = lax.broadcasted_iota(jnp.int32, (height, depth), 0)
    column = lax.broadcasted_iota(jnp.int32, (height, depth), 1)
    out_imag = (row >= time_block).astype(jnp.int32)
    time = pl.program_id(0) * time_block + row - out_imag * time_block
    freq = column >> 1
    if slots > 1:
        freq = freq ^ (lax.axis_index("freq") * W_DEV)
    steps = freq * time + ((column & 1) - out_imag) * (freq_total // 2)
    steps = (steps + 2 * freq_total) & (2 * freq_total - 1)
    _, value = sincos_turns(steps.astype(jnp.float32) * (0.5 / freq_total))
    high = value.astype(jnp.bfloat16)
    high_ref[0] = high
    low_ref[0] = (value - high.astype(jnp.float32)).astype(jnp.bfloat16)


def table(freq_total, slots, sample_count, time_block):
    blocks = sample_count // time_block
    shape = (blocks, 2 * time_block, 2 * freq_total)
    spec = pl.BlockSpec((1, *shape[1:]), lambda i: (i, 0, 0))
    return pl.pallas_call(
        functools.partial(table_kernel, freq_total, slots),
        grid=(blocks,),
        out_specs=[spec, spec],
        out_shape=[jax.ShapeDtypeStruct(shape, jnp.bfloat16)] * 2,
        compiler_params=pltpu.CompilerParams(vmem_limit_bytes=VMEM_BYTES),
        name="table",
    )()


def peak_kernel(freq_total, order, *refs):
    count = len(order)
    spectra_refs = [refs[i] for i in order]
    high_ref, low_ref, noise_ref, peak_ref, found_ref, best_ref = refs[count:]
    step = pl.program_id(0)
    columns = peak_ref.shape[1]
    rows = ROWS
    time_block = high_ref.shape[1] // 2

    @pl.when(step == 0)
    def _():
        best_ref[...] = jnp.zeros_like(best_ref)

    high = high_ref[0]
    low = low_ref[0]
    width = min(2, columns)
    for first in range(0, columns, width):
        spectra = jnp.concatenate(
            [
                jnp.concatenate(
                    [ref[:, first + k].reshape(-1, rows) for ref in spectra_refs], axis=0
                )
                for k in range(width)
            ],
            axis=1,
        )
        signal = dot(high, spectra, ((1,), (0,))) + dot(low, spectra, ((1,), (0,)))
        real_part = signal[:time_block]
        imag_part = signal[time_block:]
        power = jnp.max(real_part * real_part + imag_part * imag_part, axis=0, keepdims=True)
        for k in range(width):
            row = pl.ds(first + k, 1)
            best_ref[row, :] = jnp.maximum(
                best_ref[row, :], power[:, k * rows : (k + 1) * rows]
            )

    @pl.when(step == pl.num_programs(0) - 1)
    def _():
        largest = jnp.max(best_ref[...], axis=1, keepdims=True)
        shape = best_ref.shape
        diagonal = lax.broadcasted_iota(jnp.int32, shape, 0) == lax.broadcasted_iota(
            jnp.int32, shape, 1
        )
        largest = jnp.max(jnp.where(diagonal, largest, 0.0), axis=0, keepdims=True)
        peak = jnp.sqrt(largest[:, :columns]) * (1.0 / math.sqrt(freq_total))
        score = STEEP * (jnp.log(peak + EPS) - jnp.log(noise_ref[...]))
        peak_ref[...] = peak
        found_ref[...] = 1.0 / (1.0 + jnp.exp(-score))


def peaks(spectra, order, high, low, noise_level, freq_total):
    columns = noise_level.shape[1]
    blocks = high.shape[0]
    table_spec = pl.BlockSpec((1, *high.shape[1:]), lambda i: (i, 0, 0))
    out_spec = pl.BlockSpec((1, columns), lambda i: (0, 0))
    return pl.pallas_call(
        functools.partial(peak_kernel, freq_total, order),
        grid=(blocks,),
        in_specs=[pl.BlockSpec(a.shape, lambda i: (0, 0, 0, 0)) for a in spectra]
        + [table_spec, table_spec, out_spec],
        out_specs=[out_spec, out_spec],
        out_shape=[jax.ShapeDtypeStruct((1, columns), jnp.float32)] * 2,
        scratch_shapes=[pltpu.VMEM((max(8, columns), ROWS), jnp.float32)],
        compiler_params=pltpu.CompilerParams(vmem_limit_bytes=VMEM_BYTES),
        name="peaks",
    )(*spectra, high, low, noise_level)


def body(
    flaw_cells,
    flaw_blocks,
    element_channel,
    focal_delay,
    beam_field,
    flaw_size,
    flaw_slope,
    noise_level,
):
    freq_count = lax.axis_size("freq")
    freq_total = W_DEV * freq_count
    sample_count = min(T_CAP, 2 * freq_total)
    swap = [(0, 1), (1, 0)]
    slots = freq_count if freq_count <= MOST_SLOTS else 1
    small = (
        flaw_cells.reshape(1, -1),
        flaw_size,
        flaw_slope,
        element_channel.reshape(1, -1),
        focal_delay,
        flaw_blocks,
    )
    start, rest = partials(beam_field, small, swap, freq_total, slots)
    high, low = table(freq_total, slots, sample_count, 256 if freq_total <= 128 else 128)
    if slots > 1:
        half = slots // 2
        near, far = rest[:half], rest[half:]
        sends = [(half + i, 0, array) for i, array in enumerate(start)]
        sends += [(half + i, 1, array) for i, array in enumerate(far)]
        sends += [(i, 0, near[i]) for i in (*range(2, half), 1, 0)]
        spectra = []
        for slot, _, array in sends:
            pairs = [(a, a ^ slot) for a in range(slots)]
            spectra.append((lax.ppermute(array, "freq", pairs) if slot else array)[None])
        order = sorted(range(len(sends)), key=lambda i: sends[i][:2])
    else:
        moved = lax.all_to_all(rest[0], "freq", split_axis=0, concat_axis=0, tiled=True)
        spectra = [moved.reshape(freq_count, FG // freq_count, 2 * W_DEV, ROWS)]
        order = [0]
    return tuple(peaks(spectra, order, high, low, noise_level, freq_total))


def solution(mesh):
    in_specs = (
        P("batch"),
        P("batch"),
        P("elem"),
        P(),
        P("freq", None, "elem", None),
        P("batch", None),
        P("batch", None),
        P(("batch", "elem"), "freq"),
    )
    out_specs = (P(("batch", "elem"), "freq"), P(("batch", "elem"), "freq"))
    return jax.shard_map(body, mesh=mesh, in_specs=in_specs, out_specs=out_specs, check_vma=False)
```

```python
import functools
import math

import jax
import jax.numpy as jnp
from jax import lax
from jax.experimental import pallas as pl
from jax.experimental.pallas import tpu as pltpu
from jax.sharding import PartitionSpec as P

W_DEV = 16
FG = 128
NB = 4
SB = 32
T_CAP = 1024

EDGE = 0.6
STEEP = 3.0
EPS = 1e-05

ROWS = NB * SB
W_STEP = 8
MOST_SLOTS = 8
VMEM_BYTES = 48 * 1024 * 1024


def sin_half_turn(turns):
    angle = turns * math.pi
    square = angle * angle
    sine = 1.0 / 6227020800.0
    for factorial in (-39916800.0, 362880.0, -5040.0, 120.0, -6.0, 1.0):
        sine = sine * square + 1.0 / factorial
    cosine = 1.0 / 479001600.0
    for factorial in (-3628800.0, 40320.0, -720.0, 24.0, -2.0, 1.0):
        cosine = cosine * square + 1.0 / factorial
    return sine * angle, cosine


def sincos_turns(turns):
    rest = turns - jnp.floor(turns + 0.5)
    sine, cosine = sin_half_turn(rest)
    return 2.0 * sine * cosine, 1.0 - 2.0 * sine * sine


def dot(left, right, contract):
    return lax.dot_general(
        left, right, (contract, ((), ())), preferred_element_type=jnp.float32
    )


def slot_order(size, slots):
    row = lax.broadcasted_iota(jnp.int32, (FG, FG), 0)
    column = lax.broadcasted_iota(jnp.int32, (FG, FG), 1)
    if slots > 1:
        row = row ^ (lax.axis_index("freq") * size)
    return row == column


def delay_pieces(channel_ref, delay_ref, elements):
    channel_sel = (
        (
            lax.broadcasted_iota(jnp.int32, (delay_ref.shape[0], elements), 0)
            == channel_ref[...]
        )
        .astype(jnp.float32)
        .T.astype(jnp.bfloat16)
    )
    rest = delay_ref[...]
    pieces = []
    for _ in range(3):
        piece = rest.astype(jnp.bfloat16)
        rest = rest - piece.astype(jnp.float32)
        pieces.append(dot(channel_sel, piece, ((1,), (0,))).astype(jnp.bfloat16))
    return pieces


def prepare(freq_total, slots, which, pieces, cells_ref, size_ref, slope_ref, blocks_ref):
    sites = cells_ref.shape[1]
    first_freq = lax.axis_index("freq") * W_DEV
    order = slot_order(FG // slots, slots)
    cells = jnp.where(which == 0, cells_ref[:, :FG], cells_ref[:, FG:])
    cell_sel = lax.broadcasted_iota(jnp.int32, (sites, FG), 0) == cells
    pick = dot(
        order.astype(jnp.bfloat16), cell_sel.astype(jnp.bfloat16), ((1,), (1,))
    ).astype(jnp.bfloat16)
    size = size_ref[pl.ds(which, 1), :]
    turn = size * slope_ref[pl.ds(which, 1), :] * (1.0 / freq_total)
    size = jnp.sum(jnp.where(order, size, 0.0), axis=1, keepdims=True)
    turn = jnp.sum(jnp.where(order, turn, 0.0), axis=1, keepdims=True)
    freq = first_freq + lax.broadcasted_iota(jnp.int32, (FG, FG), 1)
    sine, cosine = sincos_turns(turn * freq.astype(jnp.float32))
    k_real = size * (1.0 + EDGE) * cosine
    k_imag = size * (EDGE - 1.0) * sine
    lane = lax.broadcasted_iota(jnp.int32, (1, ROWS), 1)
    position = lane & (SB - 1)
    for j in range(NB):
        block = blocks_ref[which * NB + j]
        position = position + jnp.where((lane >> 5) == j, block * SB, 0)
    scan_sel = (
        lax.broadcasted_iota(jnp.int32, (pieces[0].shape[1], ROWS), 0) == position
    ).astype(jnp.bfloat16)
    delays = None
    for piece in pieces:
        moved = dot(piece, scan_sel, ((1,), (0,)))
        delays = moved if delays is None else delays + moved
    phase = delays * (0.5 / freq_total)
    step_sin, step_cos = sincos_turns(phase)
    sin, cos = sincos_turns(phase * first_freq.astype(jnp.float32))
    return cos, sin, step_cos, step_sin, pick, k_real, k_imag


def spectra_of(first, state, field_ref, wait, out_ref, scratch):
    cosine, sine, step_cos, step_sin, pick, k_real, k_imag = state
    picked_ref, law_ref, rows_ref = scratch
    elements, sites = field_ref.shape[2:]
    count = law_ref.shape[0]
    for w in range(count):
        c = cosine.astype(jnp.bfloat16)
        s = sine.astype(jnp.bfloat16)
        law_ref[w, :elements, :ROWS] = c
        law_ref[w, :elements, ROWS:] = -s
        law_ref[w, elements:, :ROWS] = s
        law_ref[w, elements:, ROWS:] = c
        cosine, sine = (
            cosine * step_cos - sine * step_sin,
            sine * step_cos + cosine * step_sin,
        )
    wait()
    for w in range(count):
        picked_ref[w] = dot(
            pick, field_ref[first + w].reshape(2 * elements, sites), ((1,), (1,))
        ).astype(jnp.bfloat16)
    for w in range(count):
        product = dot(picked_ref[w], law_ref[w], ((1,), (0,)))
        real_part = product[:, :ROWS]
        imag_part = product[:, ROWS:]
        kr = k_real[:, first + w : first + w + 1]
        ki = k_imag[:, first + w : first + w + 1]
        rows_ref[pl.ds(2 * w, FG, stride=2 * count), :] = kr * real_part - ki * imag_part
        rows_ref[pl.ds(2 * w + 1, FG, stride=2 * count), :] = (
            kr * imag_part + ki * real_part
        )
    out_ref[...] = rows_ref[...].reshape(FG, 2 * count, ROWS).astype(jnp.bfloat16)
    return cosine, sine


def other_first_kernel(freq_total, slots, *refs):
    field_hbm, *small_hbm = refs[:7]
    out_ref, field_ref, cells_ref, size_ref, slope_ref, pieces_ref, *state = refs[7:20]
    channel_ref, delay_ref, blocks_ref, field_sem, small_sem, *scratch = refs[20:]
    small = (cells_ref, size_ref, slope_ref, channel_ref, delay_ref, blocks_ref)
    copies = [
        pltpu.make_async_copy(source, target, small_sem.at[i])
        for i, (source, target) in enumerate(zip(small_hbm, small))
    ]
    for copy in copies:
        copy.start()
    parts = field_sem.shape[0]
    size = W_DEV // parts
    field_copies = [
        pltpu.make_async_copy(
            field_hbm.at[pl.ds(i * size, size)],
            field_ref.at[pl.ds(i * size, size)],
            field_sem.at[i],
        )
        for i in range(parts)
    ]
    for copy in field_copies:
        copy.start()
    for copy in copies:
        copy.wait()
    pieces = delay_pieces(channel_ref, delay_ref, field_ref.shape[2])
    for i, piece in enumerate(pieces):
        pieces_ref[i] = piece
    other = 1 - lax.axis_index("elem")
    values = prepare(
        freq_total, slots, other, pieces, cells_ref, size_ref, slope_ref, blocks_ref
    )

    def wait():
        for copy in field_copies[: parts // 2]:
            copy.wait()

    following = spectra_of(0, values, field_ref, wait, out_ref, scratch)
    for ref, value in zip(state, (*following, *values[2:])):
        ref[...] = value
    for copy in field_copies[parts // 2 :]:
        copy.wait()


def other_second_kernel(field_ref, *refs):
    state = [ref[...] for ref in refs[:5]]
    k_refs, (out_ref, *scratch) = refs[5:7], refs[7:]
    spectra_of(W_STEP, (*state, *k_refs), field_ref, lambda: None, out_ref, scratch)


def own_kernel(freq_total, slots, field_ref, cells_ref, size_ref, slope_ref, *refs):
    pieces_ref, blocks_ref, out_ref, *scratch = refs
    pieces = [pieces_ref[i] for i in range(pieces_ref.shape[0])]
    group = lax.axis_index("elem")
    values = prepare(
        freq_total, slots, group, pieces, cells_ref, size_ref, slope_ref, blocks_ref
    )
    spectra_of(0, values, field_ref, lambda: None, out_ref, scratch)


def call(kernel, name, in_specs, out_shape, scratch):
    vmem = pl.BlockSpec(memory_space=pltpu.VMEM)
    return pl.pallas_call(
        kernel,
        in_specs=in_specs,
        out_specs=[vmem] * len(out_shape),
        out_shape=out_shape,
        scratch_shapes=scratch,
        compiler_params=pltpu.CompilerParams(vmem_limit_bytes=VMEM_BYTES),
        cost_estimate=pl.CostEstimate(
            flops=2 * W_STEP * 256**3, bytes_accessed=2 << 20, transcendentals=0
        ),
        name=name,
    )


def partials(field, small, swap, freq_total, slots):
    elements, sites = field.shape[2:]
    vmem = pl.BlockSpec(memory_space=pltpu.VMEM)
    hbm = pl.BlockSpec(memory_space=pltpu.HBM)
    smem = pl.BlockSpec(memory_space=pltpu.SMEM)

    def out(count):
        return jax.ShapeDtypeStruct((FG, 2 * count, ROWS), jnp.bfloat16)

    def work(count):
        return [
            pltpu.VMEM((count, FG, 2 * elements), jnp.bfloat16),
            pltpu.VMEM((count, 2 * elements, 2 * ROWS), jnp.bfloat16),
            pltpu.VMEM((FG * 2 * count, ROWS), jnp.float32),
        ]

    def like(array):
        return jax.ShapeDtypeStruct(array.shape, array.dtype)

    cells, size, slope, channel, delay, blocks = small
    pinned = [pltpu.with_memory_space_constraint(a, pltpu.HBM) for a in (field, *small)]
    law = jax.ShapeDtypeStruct((elements, ROWS), jnp.float32)
    factor = jax.ShapeDtypeStruct((FG, FG), jnp.float32)
    pieces = jax.ShapeDtypeStruct((3, elements, delay.shape[1]), jnp.bfloat16)
    pick = jax.ShapeDtypeStruct((FG, sites), jnp.bfloat16)
    first, field, cells, size, slope, pieces, *state = call(
        functools.partial(other_first_kernel, freq_total, slots),
        "other_first",
        [hbm] * len(pinned),
        [out(W_STEP), like(field), like(cells), like(size), like(slope), pieces]
        + [law] * 4
        + [pick, factor, factor],
        [
            pltpu.VMEM(channel.shape, channel.dtype),
            pltpu.VMEM(delay.shape, delay.dtype),
            pltpu.SMEM(blocks.shape, blocks.dtype),
            pltpu.SemaphoreType.DMA((4,)),
            pltpu.SemaphoreType.DMA((len(small),)),
        ]
        + work(W_STEP),
    )(*pinned)
    first = lax.ppermute(first, "elem", swap)
    (second,) = call(
        other_second_kernel, "other_second", [vmem] * 8, [out(W_STEP)], work(W_STEP)
    )(field, *state)
    second = lax.ppermute(second, "elem", swap)
    (own,) = call(
        functools.partial(own_kernel, freq_total, slots),
        "own",
        [vmem] * 5 + [smem],
        [out(W_DEV)],
        work(W_DEV),
    )(field, cells, size, slope, pieces, blocks)
    return own, first, second


def add_kernel(own_ref, first_ref, second_ref, *refs):
    half = first_ref.shape[1]
    size = refs[0].shape[0]
    for slot, ref in enumerate(refs):
        rows = pl.ds(slot * size, size)
        for k, moved_ref in enumerate((first_ref, second_ref)):
            planes = slice(k * half, (k + 1) * half)
            ref[:, planes] = (
                own_ref[rows, planes].astype(jnp.float32)
                + moved_ref[rows].astype(jnp.float32)
            ).astype(jnp.bfloat16)


def add(own, first, second, slots):
    vmem = pl.BlockSpec(memory_space=pltpu.VMEM)
    shape = jax.ShapeDtypeStruct((FG // slots, *own.shape[1:]), own.dtype)
    return call(add_kernel, "add", [vmem] * 3, [shape] * slots, [])(own, first, second)


def table_kernel(freq_total, slots, high_ref, low_ref):
    _, height, depth = high_ref.shape
    time_block = height // 2
    row = lax.broadcasted_iota(jnp.int32, (height, depth), 0)
    column = lax.broadcasted_iota(jnp.int32, (height, depth), 1)
    out_imag = (row >= time_block).astype(jnp.int32)
    time = pl.program_id(0) * time_block + row - out_imag * time_block
    freq = column >> 1
    if slots > 1:
        freq = freq ^ (lax.axis_index("freq") * W_DEV)
    steps = freq * time + ((column & 1) - out_imag) * (freq_total // 2)
    steps = (steps + 2 * freq_total) & (2 * freq_total - 1)
    _, value = sincos_turns(steps.astype(jnp.float32) * (0.5 / freq_total))
    high = value.astype(jnp.bfloat16)
    high_ref[0] = high
    low_ref[0] = (value - high.astype(jnp.float32)).astype(jnp.bfloat16)


def table(freq_total, slots, sample_count, time_block):
    blocks = sample_count // time_block
    shape = (blocks, 2 * time_block, 2 * freq_total)
    spec = pl.BlockSpec((1, *shape[1:]), lambda i: (i, 0, 0))
    return pl.pallas_call(
        functools.partial(table_kernel, freq_total, slots),
        grid=(blocks,),
        out_specs=[spec, spec],
        out_shape=[jax.ShapeDtypeStruct(shape, jnp.bfloat16)] * 2,
        compiler_params=pltpu.CompilerParams(vmem_limit_bytes=VMEM_BYTES),
        name="table",
    )()


def peak_kernel(freq_total, order, *refs):
    count = len(order)
    spectra_refs = [refs[i] for i in order]
    high_ref, low_ref, noise_ref, peak_ref, found_ref, best_ref = refs[count:]
    step = pl.program_id(0)
    columns = peak_ref.shape[1]
    rows = ROWS
    time_block = high_ref.shape[1] // 2

    @pl.when(step == 0)
    def _():
        best_ref[...] = jnp.zeros_like(best_ref)

    high = high_ref[0]
    low = low_ref[0]
    width = min(2, columns)
    for first in range(0, columns, width):
        spectra = jnp.concatenate(
            [
                jnp.concatenate(
                    [ref[:, first + k].reshape(-1, rows) for ref in spectra_refs], axis=0
                )
                for k in range(width)
            ],
            axis=1,
        )
        signal = dot(high, spectra, ((1,), (0,))) + dot(low, spectra, ((1,), (0,)))
        real_part = signal[:time_block]
        imag_part = signal[time_block:]
        power = jnp.max(real_part * real_part + imag_part * imag_part, axis=0, keepdims=True)
        for k in range(width):
            row = pl.ds(first + k, 1)
            best_ref[row, :] = jnp.maximum(
                best_ref[row, :], power[:, k * rows : (k + 1) * rows]
            )

    @pl.when(step == pl.num_programs(0) - 1)
    def _():
        largest = jnp.max(best_ref[...], axis=1, keepdims=True)
        shape = best_ref.shape
        diagonal = lax.broadcasted_iota(jnp.int32, shape, 0) == lax.broadcasted_iota(
            jnp.int32, shape, 1
        )
        largest = jnp.max(jnp.where(diagonal, largest, 0.0), axis=0, keepdims=True)
        peak = jnp.sqrt(largest[:, :columns]) * (1.0 / math.sqrt(freq_total))
        score = STEEP * (jnp.log(peak + EPS) - jnp.log(noise_ref[...]))
        peak_ref[...] = peak
        found_ref[...] = 1.0 / (1.0 + jnp.exp(-score))


def peaks(spectra, order, high, low, noise_level, freq_total):
    columns = noise_level.shape[1]
    blocks = high.shape[0]
    table_spec = pl.BlockSpec((1, *high.shape[1:]), lambda i: (i, 0, 0))
    out_spec = pl.BlockSpec((1, columns), lambda i: (0, 0))
    return pl.pallas_call(
        functools.partial(peak_kernel, freq_total, order),
        grid=(blocks,),
        in_specs=[pl.BlockSpec(a.shape, lambda i: (0, 0, 0, 0)) for a in spectra]
        + [table_spec, table_spec, out_spec],
        out_specs=[out_spec, out_spec],
        out_shape=[jax.ShapeDtypeStruct((1, columns), jnp.float32)] * 2,
        scratch_shapes=[pltpu.VMEM((max(8, columns), ROWS), jnp.float32)],
        compiler_params=pltpu.CompilerParams(vmem_limit_bytes=VMEM_BYTES),
        name="peaks",
    )(*spectra, high, low, noise_level)


def body(
    flaw_cells,
    flaw_blocks,
    element_channel,
    focal_delay,
    beam_field,
    flaw_size,
    flaw_slope,
    noise_level,
):
    freq_count = lax.axis_size("freq")
    freq_total = W_DEV * freq_count
    sample_count = min(T_CAP, 2 * freq_total)
    swap = [(0, 1), (1, 0)]
    slots = freq_count if freq_count <= MOST_SLOTS else 1
    small = (
        flaw_cells.reshape(1, -1),
        flaw_size,
        flaw_slope,
        element_channel.reshape(1, -1),
        focal_delay,
        flaw_blocks,
    )
    parts = add(*partials(beam_field, small, swap, freq_total, slots), slots)
    high, low = table(freq_total, slots, sample_count, 256 if freq_total <= 128 else 128)
    if slots > 1:
        half = slots // 2
        sends = [half, *(slot for pair in zip(range(2, half), range(half + 1, slots)) for slot in pair)]
        sends += [slot for slot in (*range(half, slots - 1), 1, slots - 1, 0) if slot not in sends]
        spectra = []
        for slot in sends:
            pairs = [(a, a ^ slot) for a in range(slots)]
            array = parts[slot]
            spectra.append((lax.ppermute(array, "freq", pairs) if slot else array)[None])
        order = [sends.index(slot) for slot in range(slots)]
    else:
        moved = lax.all_to_all(parts[0], "freq", split_axis=0, concat_axis=0, tiled=True)
        spectra = [moved.reshape(freq_count, FG // freq_count, 2 * W_DEV, ROWS)]
        order = [0]
    return tuple(peaks(spectra, order, high, low, noise_level, freq_total))


def solution(mesh):
    in_specs = (
        P("batch"),
        P("batch"),
        P("elem"),
        P(),
        P("freq", None, "elem", None),
        P("batch", None),
        P("batch", None),
        P(("batch", "elem"), "freq"),
    )
    out_specs = (P(("batch", "elem"), "freq"), P(("batch", "elem"), "freq"))
    return jax.shard_map(body, mesh=mesh, in_specs=in_specs, out_specs=out_specs, check_vma=False)
```

```python
import functools
import math

import jax
import jax.numpy as jnp
from jax import lax
from jax.experimental import pallas as pl
from jax.experimental.pallas import tpu as pltpu
from jax.sharding import PartitionSpec as P

W_DEV = 16
FG = 128
NB = 4
SB = 32
T_CAP = 1024

EDGE = 0.6
STEEP = 3.0
EPS = 1e-05

ROWS = NB * SB
W_STEP = 8
MOST_SLOTS = 8
VMEM_BYTES = 48 * 1024 * 1024


def sin_half_turn(turns):
    angle = turns * math.pi
    square = angle * angle
    sine = 1.0 / 6227020800.0
    for factorial in (-39916800.0, 362880.0, -5040.0, 120.0, -6.0, 1.0):
        sine = sine * square + 1.0 / factorial
    cosine = 1.0 / 479001600.0
    for factorial in (-3628800.0, 40320.0, -720.0, 24.0, -2.0, 1.0):
        cosine = cosine * square + 1.0 / factorial
    return sine * angle, cosine


def sincos_turns(turns):
    rest = turns - jnp.floor(turns + 0.5)
    sine, cosine = sin_half_turn(rest)
    return 2.0 * sine * cosine, 1.0 - 2.0 * sine * sine


def dot(left, right, contract):
    return lax.dot_general(
        left, right, (contract, ((), ())), preferred_element_type=jnp.float32
    )


def slot_masks(slots):
    half = slots // 2
    near, far = [*range(2, half), 1][: half - 1], [*range(half, slots)]
    first = [mask for pair in zip(far, near) for mask in pair] + far[len(near) :]
    second = [mask for pair in zip(near, far) for mask in pair] + far[len(near) :]
    return [0, *first], [0, *second]


def partner(slots, group, slot):
    index = lax.axis_index("freq")
    first, second = slot_masks(slots)
    mask = jnp.zeros_like(slot)
    for s in range(1, slots):
        mask = jnp.where(slot == s, jnp.where(group == 0, first[s], second[s]), mask)
    return mask ^ index


def slot_order(slots, group):
    size = FG // slots
    row = lax.broadcasted_iota(jnp.int32, (FG, 1), 0)
    column = lax.broadcasted_iota(jnp.int32, (FG, FG), 1)
    if slots > 1:
        row = partner(slots, group, row // size) * size + row % size
    return row == column


def delay_pieces(channel_ref, delay_ref, elements):
    channel_sel = (
        (
            lax.broadcasted_iota(jnp.int32, (delay_ref.shape[0], elements), 0)
            == channel_ref[...]
        )
        .astype(jnp.float32)
        .T.astype(jnp.bfloat16)
    )
    rest = delay_ref[...]
    pieces = []
    for _ in range(3):
        piece = rest.astype(jnp.bfloat16)
        rest = rest - piece.astype(jnp.float32)
        pieces.append(dot(channel_sel, piece, ((1,), (0,))).astype(jnp.bfloat16))
    return pieces


def prepare(freq_total, slots, which, pieces, cells_ref, size_ref, slope_ref, blocks_ref):
    sites = cells_ref.shape[1]
    first_freq = lax.axis_index("freq") * W_DEV
    order = slot_order(slots, which)
    cells = jnp.where(which == 0, cells_ref[:, :FG], cells_ref[:, FG:])
    cell_sel = lax.broadcasted_iota(jnp.int32, (sites, FG), 0) == cells
    pick = dot(
        order.astype(jnp.bfloat16), cell_sel.astype(jnp.bfloat16), ((1,), (1,))
    ).astype(jnp.bfloat16)
    size = size_ref[pl.ds(which, 1), :]
    turn = size * slope_ref[pl.ds(which, 1), :] * (1.0 / freq_total)
    size = jnp.sum(jnp.where(order, size, 0.0), axis=1, keepdims=True)
    turn = jnp.sum(jnp.where(order, turn, 0.0), axis=1, keepdims=True)
    freq = first_freq + lax.broadcasted_iota(jnp.int32, (FG, FG), 1)
    sine, cosine = sincos_turns(turn * freq.astype(jnp.float32))
    k_real = size * (1.0 + EDGE) * cosine
    k_imag = size * (EDGE - 1.0) * sine
    lane = lax.broadcasted_iota(jnp.int32, (1, ROWS), 1)
    position = lane & (SB - 1)
    for j in range(NB):
        block = blocks_ref[which * NB + j]
        position = position + jnp.where((lane >> 5) == j, block * SB, 0)
    scan_sel = (
        lax.broadcasted_iota(jnp.int32, (pieces[0].shape[1], ROWS), 0) == position
    ).astype(jnp.bfloat16)
    delays = None
    for piece in pieces:
        moved = dot(piece, scan_sel, ((1,), (0,)))
        delays = moved if delays is None else delays + moved
    phase = delays * (0.5 / freq_total)
    step_sin, step_cos = sincos_turns(phase)
    sin, cos = sincos_turns(phase * first_freq.astype(jnp.float32))
    return cos, sin, step_cos, step_sin, pick, k_real, k_imag


def spectra_of(first, state, field_ref, wait, out_ref, scratch):
    cosine, sine, step_cos, step_sin, pick, k_real, k_imag = state
    picked_ref, law_ref, rows_ref = scratch
    elements, sites = field_ref.shape[2:]
    count = law_ref.shape[0]
    for w in range(count):
        c = cosine.astype(jnp.bfloat16)
        s = sine.astype(jnp.bfloat16)
        law_ref[w, :elements, :ROWS] = c
        law_ref[w, :elements, ROWS:] = -s
        law_ref[w, elements:, :ROWS] = s
        law_ref[w, elements:, ROWS:] = c
        cosine, sine = (
            cosine * step_cos - sine * step_sin,
            sine * step_cos + cosine * step_sin,
        )
    wait()
    for w in range(count):
        picked_ref[w] = dot(
            pick, field_ref[first + w].reshape(2 * elements, sites), ((1,), (1,))
        ).astype(jnp.bfloat16)
    for w in range(count):
        product = dot(picked_ref[w], law_ref[w], ((1,), (0,)))
        real_part = product[:, :ROWS]
        imag_part = product[:, ROWS:]
        kr = k_real[:, first + w : first + w + 1]
        ki = k_imag[:, first + w : first + w + 1]
        rows_ref[pl.ds(2 * w, FG, stride=2 * count), :] = kr * real_part - ki * imag_part
        rows_ref[pl.ds(2 * w + 1, FG, stride=2 * count), :] = (
            kr * imag_part + ki * real_part
        )
    out_ref[...] = rows_ref[...].reshape(FG, 2 * count, ROWS).astype(jnp.bfloat16)
    return cosine, sine


def other_first_kernel(freq_total, slots, *refs):
    field_hbm, *small_hbm = refs[:7]
    out_ref, field_ref, cells_ref, size_ref, slope_ref, pieces_ref, *state = refs[7:20]
    channel_ref, delay_ref, blocks_ref, field_sem, small_sem, *scratch = refs[20:]
    small = (cells_ref, size_ref, slope_ref, channel_ref, delay_ref, blocks_ref)
    copies = [
        pltpu.make_async_copy(source, target, small_sem.at[i])
        for i, (source, target) in enumerate(zip(small_hbm, small))
    ]
    for copy in copies:
        copy.start()
    parts = field_sem.shape[0]
    size = W_DEV // parts
    field_copies = [
        pltpu.make_async_copy(
            field_hbm.at[pl.ds(i * size, size)],
            field_ref.at[pl.ds(i * size, size)],
            field_sem.at[i],
        )
        for i in range(parts)
    ]
    for copy in field_copies:
        copy.start()
    for copy in copies:
        copy.wait()
    pieces = delay_pieces(channel_ref, delay_ref, field_ref.shape[2])
    for i, piece in enumerate(pieces):
        pieces_ref[i] = piece
    other = 1 - lax.axis_index("elem")
    values = prepare(
        freq_total, slots, other, pieces, cells_ref, size_ref, slope_ref, blocks_ref
    )

    def wait():
        for copy in field_copies[: parts // 2]:
            copy.wait()

    following = spectra_of(0, values, field_ref, wait, out_ref, scratch)
    for ref, value in zip(state, (*following, *values[2:])):
        ref[...] = value
    for copy in field_copies[parts // 2 :]:
        copy.wait()


def second_kernel(field_ref, *refs):
    state = [ref[...] for ref in refs[:5]]
    k_refs, (_, out_ref, *scratch) = refs[5:7], refs[7:]
    spectra_of(W_STEP, (*state, *k_refs), field_ref, lambda: None, out_ref, scratch)


def own_first_kernel(freq_total, slots, field_ref, cells_ref, size_ref, slope_ref, *refs):
    pieces_ref, blocks_ref, out_ref, *refs = refs
    state, scratch = refs[:7], refs[7:]
    pieces = [pieces_ref[i] for i in range(pieces_ref.shape[0])]
    group = lax.axis_index("elem")
    values = prepare(
        freq_total, slots, group, pieces, cells_ref, size_ref, slope_ref, blocks_ref
    )
    following = spectra_of(0, values, field_ref, lambda: None, out_ref, scratch)
    for ref, value in zip(state, (*following, *values[2:])):
        ref[...] = value


def call(kernel, name, in_specs, out_shape, scratch):
    vmem = pl.BlockSpec(memory_space=pltpu.VMEM)
    return pl.pallas_call(
        kernel,
        in_specs=in_specs,
        out_specs=[vmem] * len(out_shape),
        out_shape=out_shape,
        scratch_shapes=scratch,
        compiler_params=pltpu.CompilerParams(vmem_limit_bytes=VMEM_BYTES),
        cost_estimate=pl.CostEstimate(
            flops=2 * W_STEP * 256**3, bytes_accessed=2 << 20, transcendentals=0
        ),
        name=name,
    )


def partials(field, small, swap, freq_total, slots):
    elements, sites = field.shape[2:]
    vmem = pl.BlockSpec(memory_space=pltpu.VMEM)
    hbm = pl.BlockSpec(memory_space=pltpu.HBM)
    smem = pl.BlockSpec(memory_space=pltpu.SMEM)

    def out(count):
        return jax.ShapeDtypeStruct((FG, 2 * count, ROWS), jnp.bfloat16)

    def work(count):
        return [
            pltpu.VMEM((count, FG, 2 * elements), jnp.bfloat16),
            pltpu.VMEM((count, 2 * elements, 2 * ROWS), jnp.bfloat16),
            pltpu.VMEM((FG * 2 * count, ROWS), jnp.float32),
        ]

    def like(array):
        return jax.ShapeDtypeStruct(array.shape, array.dtype)

    cells, size, slope, channel, delay, blocks = small
    pinned = [pltpu.with_memory_space_constraint(a, pltpu.HBM) for a in (field, *small)]
    law = jax.ShapeDtypeStruct((elements, ROWS), jnp.float32)
    factor = jax.ShapeDtypeStruct((FG, FG), jnp.float32)
    pieces = jax.ShapeDtypeStruct((3, elements, delay.shape[1]), jnp.bfloat16)
    pick = jax.ShapeDtypeStruct((FG, sites), jnp.bfloat16)
    first, field, cells, size, slope, pieces, *state = call(
        functools.partial(other_first_kernel, freq_total, slots),
        "other_first",
        [hbm] * len(pinned),
        [out(W_STEP), like(field), like(cells), like(size), like(slope), pieces]
        + [law] * 4
        + [pick, factor, factor],
        [
            pltpu.VMEM(channel.shape, channel.dtype),
            pltpu.VMEM(delay.shape, delay.dtype),
            pltpu.SMEM(blocks.shape, blocks.dtype),
            pltpu.SemaphoreType.DMA((4,)),
            pltpu.SemaphoreType.DMA((len(small),)),
        ]
        + work(W_STEP),
    )(*pinned)
    moved = lax.ppermute(first, "elem", swap)
    own, *own_state = call(
        functools.partial(own_first_kernel, freq_total, slots),
        "own_first",
        [vmem] * 5 + [smem],
        [out(W_STEP)] + [law] * 4 + [pick, factor, factor],
        work(W_STEP),
    )(field, cells, size, slope, pieces, blocks)
    chunks = [add(own, moved, slots)]
    specs = [vmem] * 8 + [pl.BlockSpec(memory_space=pl.ANY)]
    seconds = [
        call(second_kernel, name, specs, [out(W_STEP)], work(W_STEP))(
            field, *s, chunks[0][0]
        )[0]
        for name, s in (("other_second", state), ("own_second", own_state))
    ]
    chunks.append(add(seconds[1], lax.ppermute(seconds[0], "elem", swap), slots))
    return chunks


def add_kernel(own_ref, moved_ref, *refs):
    size = refs[0].shape[0]
    for slot, ref in enumerate(refs):
        rows = pl.ds(slot * size, size)
        ref[...] = (
            own_ref[rows].astype(jnp.float32) + moved_ref[rows].astype(jnp.float32)
        ).astype(jnp.bfloat16)


def add(own, moved, slots):
    vmem = pl.BlockSpec(memory_space=pltpu.VMEM)
    shape = jax.ShapeDtypeStruct((FG // slots, *own.shape[1:]), own.dtype)
    return call(add_kernel, "add", [vmem] * 2, [shape] * slots, [])(own, moved)


def table_kernel(freq_total, slots, high_ref, low_ref):
    _, height, depth = high_ref.shape
    time_block = height // 2
    row = lax.broadcasted_iota(jnp.int32, (height, depth), 0)
    column = lax.broadcasted_iota(jnp.int32, (height, depth), 1)
    out_imag = (row >= time_block).astype(jnp.int32)
    time = pl.program_id(0) * time_block + row - out_imag * time_block
    freq = column >> 1
    if slots > 1:
        lane = lax.broadcasted_iota(jnp.int32, (1, depth), 1) >> 1
        source = partner(slots, lax.axis_index("elem"), lane // W_DEV)
        freq = source * W_DEV + lane % W_DEV
    steps = freq * time + ((column & 1) - out_imag) * (freq_total // 2)
    steps = (steps + 2 * freq_total) & (2 * freq_total - 1)
    _, value = sincos_turns(steps.astype(jnp.float32) * (0.5 / freq_total))
    high = value.astype(jnp.bfloat16)
    high_ref[0] = high
    low_ref[0] = (value - high.astype(jnp.float32)).astype(jnp.bfloat16)


def table(freq_total, slots, sample_count, time_block):
    blocks = sample_count // time_block
    shape = (blocks, 2 * time_block, 2 * freq_total)
    spec = pl.BlockSpec((1, *shape[1:]), lambda i: (i, 0, 0))
    return pl.pallas_call(
        functools.partial(table_kernel, freq_total, slots),
        grid=(blocks,),
        out_specs=[spec, spec],
        out_shape=[jax.ShapeDtypeStruct(shape, jnp.bfloat16)] * 2,
        compiler_params=pltpu.CompilerParams(vmem_limit_bytes=VMEM_BYTES),
        name="table",
    )()


def peak_kernel(freq_total, order, *refs):
    count = len(order)
    spectra_refs = [refs[i] for i in order]
    high_ref, low_ref, noise_ref, peak_ref, found_ref, best_ref = refs[count:]
    step = pl.program_id(0)
    columns = peak_ref.shape[1]
    rows = ROWS
    time_block = high_ref.shape[1] // 2

    @pl.when(step == 0)
    def _():
        best_ref[...] = jnp.zeros_like(best_ref)

    high = high_ref[0]
    low = low_ref[0]
    width = min(2, columns)
    for first in range(0, columns, width):
        spectra = jnp.concatenate(
            [
                jnp.concatenate(
                    [ref[:, first + k].reshape(-1, rows) for ref in spectra_refs], axis=0
                )
                for k in range(width)
            ],
            axis=1,
        )
        signal = dot(high, spectra, ((1,), (0,))) + dot(low, spectra, ((1,), (0,)))
        real_part = signal[:time_block]
        imag_part = signal[time_block:]
        power = jnp.max(real_part * real_part + imag_part * imag_part, axis=0, keepdims=True)
        for k in range(width):
            row = pl.ds(first + k, 1)
            best_ref[row, :] = jnp.maximum(
                best_ref[row, :], power[:, k * rows : (k + 1) * rows]
            )

    @pl.when(step == pl.num_programs(0) - 1)
    def _():
        largest = jnp.max(best_ref[...], axis=1, keepdims=True)
        shape = best_ref.shape
        diagonal = lax.broadcasted_iota(jnp.int32, shape, 0) == lax.broadcasted_iota(
            jnp.int32, shape, 1
        )
        largest = jnp.max(jnp.where(diagonal, largest, 0.0), axis=0, keepdims=True)
        peak = jnp.sqrt(largest[:, :columns]) * (1.0 / math.sqrt(freq_total))
        score = STEEP * (jnp.log(peak + EPS) - jnp.log(noise_ref[...]))
        peak_ref[...] = peak
        found_ref[...] = 1.0 / (1.0 + jnp.exp(-score))


def peaks(spectra, order, high, low, noise_level, freq_total):
    columns = noise_level.shape[1]
    blocks = high.shape[0]
    table_spec = pl.BlockSpec((1, *high.shape[1:]), lambda i: (i, 0, 0))
    out_spec = pl.BlockSpec((1, columns), lambda i: (0, 0))
    return pl.pallas_call(
        functools.partial(peak_kernel, freq_total, order),
        grid=(blocks,),
        in_specs=[pl.BlockSpec(a.shape, lambda i: (0, 0, 0, 0)) for a in spectra]
        + [table_spec, table_spec, out_spec],
        out_specs=[out_spec, out_spec],
        out_shape=[jax.ShapeDtypeStruct((1, columns), jnp.float32)] * 2,
        scratch_shapes=[pltpu.VMEM((max(8, columns), ROWS), jnp.float32)],
        compiler_params=pltpu.CompilerParams(vmem_limit_bytes=VMEM_BYTES),
        name="peaks",
    )(*spectra, high, low, noise_level)


def body(
    flaw_cells,
    flaw_blocks,
    element_channel,
    focal_delay,
    beam_field,
    flaw_size,
    flaw_slope,
    noise_level,
):
    freq_count = lax.axis_size("freq")
    freq_total = W_DEV * freq_count
    sample_count = min(T_CAP, 2 * freq_total)
    swap = [(0, 1), (1, 0)]
    slots = freq_count if freq_count <= MOST_SLOTS else 1
    small = (
        flaw_cells.reshape(1, -1),
        flaw_size,
        flaw_slope,
        element_channel.reshape(1, -1),
        focal_delay,
        flaw_blocks,
    )
    chunks = partials(beam_field, small, swap, freq_total, slots)
    high, low = table(freq_total, slots, sample_count, 256 if freq_total <= 128 else 128)
    if slots > 1:
        masks = slot_masks(slots)
        spectra = []
        for chunk in chunks:
            for slot in range(1, slots):
                pairs = [
                    (2 * a + core, 2 * (a ^ masks[core][slot]) + core)
                    for a in range(slots)
                    for core in range(2)
                ]
                spectra.append(lax.ppermute(chunk[slot], ("freq", "elem"), pairs)[None])
        spectra += [chunk[0][None] for chunk in chunks]
        sent = slots - 1
        order = [i for s in range(sent) for i in (s, sent + s)]
        order = [2 * sent, 2 * sent + 1, *order]
    else:
        moved = jnp.concatenate([chunk[0] for chunk in chunks], axis=1)
        moved = lax.all_to_all(moved, "freq", split_axis=0, concat_axis=0, tiled=True)
        spectra = [moved.reshape(freq_count, FG // freq_count, 2 * W_DEV, ROWS)]
        order = [0]
    return tuple(peaks(spectra, order, high, low, noise_level, freq_total))


def solution(mesh):
    in_specs = (
        P("batch"),
        P("batch"),
        P("elem"),
        P(),
        P("freq", None, "elem", None),
        P("batch", None),
        P("batch", None),
        P(("batch", "elem"), "freq"),
    )
    out_specs = (P(("batch", "elem"), "freq"), P(("batch", "elem"), "freq"))
    return jax.shard_map(body, mesh=mesh, in_specs=in_specs, out_specs=out_specs, check_vma=False)
```

```python
import functools
import math

import jax
import jax.numpy as jnp
from jax import lax
from jax.experimental import pallas as pl
from jax.experimental.pallas import tpu as pltpu
from jax.sharding import PartitionSpec as P

W_DEV = 16
FG = 128
NB = 4
SB = 32
T_CAP = 1024

EDGE = 0.6
STEEP = 3.0
EPS = 1e-05

ROWS = NB * SB
VMEM_BYTES = 48 * 1024 * 1024


def sin_half_turn(turns):
    angle = turns * math.pi
    square = angle * angle
    sine = 1.0 / 6227020800.0
    for factorial in (-39916800.0, 362880.0, -5040.0, 120.0, -6.0, 1.0):
        sine = sine * square + 1.0 / factorial
    cosine = 1.0 / 479001600.0
    for factorial in (-3628800.0, 40320.0, -720.0, 24.0, -2.0, 1.0):
        cosine = cosine * square + 1.0 / factorial
    return sine * angle, cosine


def sincos_turns(turns):
    rest = turns - jnp.floor(turns + 0.5)
    sine, cosine = sin_half_turn(rest)
    return 2.0 * sine * cosine, 1.0 - 2.0 * sine * sine


def dot(left, right, contract):
    return lax.dot_general(
        left, right, (contract, ((), ())), preferred_element_type=jnp.float32
    )


def slot_order(slots):
    row = lax.broadcasted_iota(jnp.int32, (FG, FG), 0)
    column = lax.broadcasted_iota(jnp.int32, (FG, FG), 1)
    if slots > 1:
        row = row ^ (lax.axis_index("freq") * (FG // slots))
    return row == column


def delay_pieces(channel_ref, delay_ref, elements):
    channel_sel = (
        (
            lax.broadcasted_iota(jnp.int32, (delay_ref.shape[0], elements), 0)
            == channel_ref[...]
        )
        .astype(jnp.float32)
        .T.astype(jnp.bfloat16)
    )
    rest = delay_ref[...]
    pieces = []
    for _ in range(3):
        piece = rest.astype(jnp.bfloat16)
        rest = rest - piece.astype(jnp.float32)
        pieces.append(dot(channel_sel, piece, ((1,), (0,))).astype(jnp.bfloat16))
    return pieces


def prepare(freq_total, slots, which, pieces, cells_ref, size_ref, slope_ref, blocks_ref):
    sites = cells_ref.shape[1]
    first_freq = lax.axis_index("freq") * W_DEV
    order = slot_order(slots)
    cells = jnp.where(which == 0, cells_ref[:, :FG], cells_ref[:, FG:])
    cell_sel = lax.broadcasted_iota(jnp.int32, (sites, FG), 0) == cells
    pick = dot(
        order.astype(jnp.bfloat16), cell_sel.astype(jnp.bfloat16), ((1,), (1,))
    ).astype(jnp.bfloat16)
    size = size_ref[pl.ds(which, 1), :]
    turn = size * slope_ref[pl.ds(which, 1), :] * (1.0 / freq_total)
    size = jnp.sum(jnp.where(order, size, 0.0), axis=1, keepdims=True)
    turn = jnp.sum(jnp.where(order, turn, 0.0), axis=1, keepdims=True)
    freq = first_freq + lax.broadcasted_iota(jnp.int32, (FG, FG), 1)
    sine, cosine = sincos_turns(turn * freq.astype(jnp.float32))
    k_real = size * (1.0 + EDGE) * cosine
    k_imag = size * (EDGE - 1.0) * sine
    lane = lax.broadcasted_iota(jnp.int32, (1, ROWS), 1)
    position = lane & (SB - 1)
    for j in range(NB):
        block = blocks_ref[which * NB + j]
        position = position + jnp.where((lane >> 5) == j, block * SB, 0)
    scan_sel = (
        lax.broadcasted_iota(jnp.int32, (pieces[0].shape[1], ROWS), 0) == position
    ).astype(jnp.bfloat16)
    delays = None
    for piece in pieces:
        moved = dot(piece, scan_sel, ((1,), (0,)))
        delays = moved if delays is None else delays + moved
    phase = delays * (0.5 / freq_total)
    step_sin, step_cos = sincos_turns(phase)
    sin, cos = sincos_turns(phase * first_freq.astype(jnp.float32))
    return cos, sin, step_cos, step_sin, pick, k_real, k_imag


def plane(w, k):
    return (w % 2) * W_DEV + (w // 2) * 2 + k


def store_spectra(picked, law_ref, k_real, k_imag, out_ref, rows_ref):
    flaws, planes, _ = out_ref.shape
    for w in range(W_DEV):
        product = dot(picked(w), law_ref[w], ((1,), (0,)))
        real_part = product[:, :ROWS]
        imag_part = product[:, ROWS:]
        kr = k_real[:, w : w + 1]
        ki = k_imag[:, w : w + 1]
        rows_ref[pl.ds(plane(w, 0), flaws, stride=planes), :] = (
            kr * real_part - ki * imag_part
        )
        rows_ref[pl.ds(plane(w, 1), flaws, stride=planes), :] = (
            kr * imag_part + ki * real_part
        )
    out_ref[...] = rows_ref[...].reshape(flaws, planes, ROWS).astype(jnp.bfloat16)


def far_spectra(values, field_ref, wait, out_ref, kept, rows_ref):
    cosine, sine, step_cos, step_sin, pick, k_real, k_imag = values
    law_ref, picked_ref, k_real_ref, k_imag_ref = kept
    elements, sites = field_ref.shape[2:]
    for w in range(W_DEV):
        c = cosine.astype(jnp.bfloat16)
        s = sine.astype(jnp.bfloat16)
        law_ref[w, :elements, :ROWS] = c
        law_ref[w, :elements, ROWS:] = -s
        law_ref[w, elements:, :ROWS] = s
        law_ref[w, elements:, ROWS:] = c
        if w < W_DEV - 1:
            cosine, sine = (
                cosine * step_cos - sine * step_sin,
                sine * step_cos + cosine * step_sin,
            )
    k_real_ref[...] = k_real
    k_imag_ref[...] = k_imag
    for w in range(W_DEV):
        wait(w)
        picked_ref[w] = dot(
            pick, field_ref[w].reshape(2 * elements, sites), ((1,), (1,))
        ).astype(jnp.bfloat16)
    near = FG - out_ref.shape[0]
    store_spectra(
        lambda w: picked_ref[w, near:, :],
        law_ref,
        k_real[near:],
        k_imag[near:],
        out_ref,
        rows_ref,
    )


def other_far_kernel(freq_total, slots, *refs):
    field_hbm, *small_hbm = refs[:7]
    out_ref, field_ref, cells_ref, size_ref, slope_ref, pieces_ref, *kept = refs[7:17]
    channel_ref, delay_ref, blocks_ref, field_sem, small_sem, rows_ref = refs[17:]
    small = (cells_ref, size_ref, slope_ref, channel_ref, delay_ref, blocks_ref)
    copies = [
        pltpu.make_async_copy(source, target, small_sem.at[i])
        for i, (source, target) in enumerate(zip(small_hbm, small))
    ]
    for copy in copies:
        copy.start()
    parts = field_sem.shape[0]
    size = W_DEV // parts
    field_copies = [
        pltpu.make_async_copy(
            field_hbm.at[pl.ds(i * size, size)],
            field_ref.at[pl.ds(i * size, size)],
            field_sem.at[i],
        )
        for i in range(parts)
    ]
    for copy in field_copies:
        copy.start()
    for copy in copies:
        copy.wait()
    pieces = delay_pieces(channel_ref, delay_ref, field_ref.shape[2])
    for i, piece in enumerate(pieces):
        pieces_ref[i] = piece
    other = 1 - lax.axis_index("elem")
    values = prepare(
        freq_total, slots, other, pieces, cells_ref, size_ref, slope_ref, blocks_ref
    )

    def wait(w):
        if w % size == 0:
            field_copies[w // size].wait()

    far_spectra(values, field_ref, wait, out_ref, kept, rows_ref)


def own_far_kernel(freq_total, slots, field_ref, cells_ref, size_ref, slope_ref, *refs):
    pieces_ref, blocks_ref, out_ref, *kept, rows_ref = refs
    pieces = [pieces_ref[i] for i in range(pieces_ref.shape[0])]
    group = lax.axis_index("elem")
    values = prepare(
        freq_total, slots, group, pieces, cells_ref, size_ref, slope_ref, blocks_ref
    )
    far_spectra(values, field_ref, lambda w: None, out_ref, kept, rows_ref)


def near_kernel(law_ref, picked_ref, k_real_ref, k_imag_ref, _, out_ref, rows_ref):
    near = out_ref.shape[0]
    store_spectra(
        lambda w: picked_ref[w, :near, :],
        law_ref,
        k_real_ref[:near],
        k_imag_ref[:near],
        out_ref,
        rows_ref,
    )


def call(kernel, name, in_specs, out_shape, scratch):
    vmem = pl.BlockSpec(memory_space=pltpu.VMEM)
    return pl.pallas_call(
        kernel,
        in_specs=in_specs,
        out_specs=[vmem] * len(out_shape),
        out_shape=out_shape,
        scratch_shapes=scratch,
        compiler_params=pltpu.CompilerParams(vmem_limit_bytes=VMEM_BYTES),
        cost_estimate=pl.CostEstimate(flops=1000, bytes_accessed=1000, transcendentals=0),
        name=name,
    )


def spectra_of(field, small, swap, freq_total, slots):
    elements, sites = field.shape[2:]
    vmem = pl.BlockSpec(memory_space=pltpu.VMEM)
    hbm = pl.BlockSpec(memory_space=pltpu.HBM)
    smem = pl.BlockSpec(memory_space=pltpu.SMEM)
    size = FG // slots
    far = FG // 2
    out = jax.ShapeDtypeStruct((far, 2 * W_DEV, ROWS), jnp.bfloat16)
    rows = pltpu.VMEM((far * 2 * W_DEV, ROWS), jnp.float32)

    def like(array):
        return jax.ShapeDtypeStruct(array.shape, array.dtype)

    cells, length, slope, channel, delay, blocks = small
    pinned = [pltpu.with_memory_space_constraint(a, pltpu.HBM) for a in (field, *small)]
    pieces = jax.ShapeDtypeStruct((3, elements, delay.shape[1]), jnp.bfloat16)
    kept = [
        jax.ShapeDtypeStruct((W_DEV, 2 * elements, 2 * ROWS), jnp.bfloat16),
        jax.ShapeDtypeStruct((W_DEV, FG, 2 * elements), jnp.bfloat16),
        jax.ShapeDtypeStruct((FG, FG), jnp.float32),
        jax.ShapeDtypeStruct((FG, FG), jnp.float32),
    ]
    other, field, cells, length, slope, pieces, *other_kept = call(
        functools.partial(other_far_kernel, freq_total, slots),
        "other_far",
        [hbm] * len(pinned),
        [out, like(field), like(cells), like(length), like(slope), pieces, *kept],
        [
            pltpu.VMEM(channel.shape, channel.dtype),
            pltpu.VMEM(delay.shape, delay.dtype),
            pltpu.SMEM(blocks.shape, blocks.dtype),
            pltpu.SemaphoreType.DMA((4,)),
            pltpu.SemaphoreType.DMA((len(small),)),
            rows,
        ],
    )(*pinned)
    moved = lax.ppermute(other, "elem", swap)
    own, *own_kept = call(
        functools.partial(own_far_kernel, freq_total, slots),
        "own_far",
        [vmem] * 5 + [smem],
        [out, *kept],
        [rows],
    )(field, cells, length, slope, pieces, blocks)
    far_sums = add(own, moved, [far - size, size] if slots > 1 else [far])
    specs = [vmem] * 4 + [pl.BlockSpec(memory_space=pl.ANY)]
    near = [
        call(near_kernel, name, specs, [out], [rows])(*kept, far_sums[-1])[0]
        for name, kept in (("other_near", other_kept), ("own_near", own_kept))
    ]
    moved = lax.ppermute(near[0], "elem", swap)
    return far_sums, add(near[1], moved, [size] * (slots // 2) if slots > 1 else [far])


def add_kernel(own_ref, moved_ref, *refs):
    first = 0
    for ref in refs:
        rows = pl.ds(first, ref.shape[0])
        first += ref.shape[0]
        ref[...] = (
            own_ref[rows].astype(jnp.float32) + moved_ref[rows].astype(jnp.float32)
        ).astype(jnp.bfloat16)


def add(own, moved, sizes):
    vmem = pl.BlockSpec(memory_space=pltpu.VMEM)
    shapes = [jax.ShapeDtypeStruct((size, *own.shape[1:]), own.dtype) for size in sizes]
    return call(add_kernel, "add", [vmem] * 2, shapes, [])(own, moved)


def split_kernel(after, source_ref, *refs):
    for i, ref in enumerate(refs[after:]):
        ref[...] = source_ref[pl.ds((i + 1) * ref.shape[0], ref.shape[0])]


def split(array, size, after):
    vmem = pl.BlockSpec(memory_space=pltpu.VMEM)
    shape = jax.ShapeDtypeStruct((size, *array.shape[1:]), array.dtype)
    count = array.shape[0] // size - 1
    return call(
        functools.partial(split_kernel, len(after)),
        "split",
        [vmem] + [pl.BlockSpec(memory_space=pl.ANY)] * len(after),
        [shape] * count,
        [],
    )(array, *after)


def table_kernel(freq_total, slots, table_ref):
    height, depth = table_ref.shape[2:]
    time_block = height // 2
    row = lax.broadcasted_iota(jnp.int32, (height, depth // 2), 0)
    column = lax.broadcasted_iota(jnp.int32, (height, depth // 2), 1)
    out_imag = (row >= time_block).astype(jnp.int32)
    time = pl.program_id(0) * time_block + row - out_imag * time_block
    for parity in range(2):
        freq = (column >> 1) * 2 + parity
        if slots > 1:
            freq = freq ^ (lax.axis_index("freq") * W_DEV)
        steps = freq * time + ((column & 1) - out_imag) * (freq_total // 2)
        steps = (steps + 2 * freq_total) & (2 * freq_total - 1)
        _, value = sincos_turns(steps.astype(jnp.float32) * (0.5 / freq_total))
        high = value.astype(jnp.bfloat16)
        table_ref[0, parity, :, : depth // 2] = high
        table_ref[0, parity, :, depth // 2 :] = (
            value - high.astype(jnp.float32)
        ).astype(jnp.bfloat16)


def table(freq_total, slots, times, time_block):
    blocks = times // time_block
    shape = (blocks, 2, 2 * time_block, 2 * freq_total)
    return pl.pallas_call(
        functools.partial(table_kernel, freq_total, slots),
        grid=(blocks,),
        out_specs=pl.BlockSpec((1, *shape[1:]), lambda i: (i, 0, 0, 0)),
        out_shape=jax.ShapeDtypeStruct(shape, jnp.bfloat16),
        compiler_params=pltpu.CompilerParams(vmem_limit_bytes=VMEM_BYTES),
        name="table",
    )()


def peak_kernel(freq_total, folded, sources, *refs):
    count = len(refs) - 5
    table_ref, noise_ref, peak_ref, found_ref, best_ref = refs[count:]
    step = pl.program_id(0)
    columns = peak_ref.shape[1]
    time_block = table_ref.shape[2] // 2

    @pl.when(step == 0)
    def _():
        best_ref[...] = jnp.zeros_like(best_ref)

    width = min(2, columns)
    for first in range(0, columns, width):
        parts = []
        for parity in range(2):
            planes = slice(parity * W_DEV, (parity + 1) * W_DEV)
            spectra = jnp.concatenate(
                [
                    jnp.concatenate(
                        [refs[i][row + first + k, planes, :] for i, row in sources] * 2,
                        axis=0,
                    )
                    for k in range(width)
                ],
                axis=1,
            )
            parts.append(dot(table_ref[0, parity], spectra, ((1,), (0,))))
        powers = []
        for signal in [parts[0] + parts[1]] + [parts[0] - parts[1]] * folded:
            real_part = signal[:time_block]
            imag_part = signal[time_block:]
            powers.append(real_part * real_part + imag_part * imag_part)
        power = jnp.maximum(powers[0], powers[-1]) if folded else powers[0]
        power = jnp.max(power, axis=0, keepdims=True)
        for k in range(width):
            row = pl.ds(first + k, 1)
            best_ref[row, :] = jnp.maximum(
                best_ref[row, :], power[:, k * ROWS : (k + 1) * ROWS]
            )

    @pl.when(step == pl.num_programs(0) - 1)
    def _():
        largest = jnp.max(best_ref[...], axis=1, keepdims=True)
        shape = best_ref.shape
        diagonal = lax.broadcasted_iota(jnp.int32, shape, 0) == lax.broadcasted_iota(
            jnp.int32, shape, 1
        )
        largest = jnp.max(jnp.where(diagonal, largest, 0.0), axis=0, keepdims=True)
        peak = jnp.sqrt(largest[:, :columns]) * (1.0 / math.sqrt(freq_total))
        score = STEEP * (jnp.log(peak + EPS) - jnp.log(noise_ref[...]))
        peak_ref[...] = peak
        found_ref[...] = 1.0 / (1.0 + jnp.exp(-score))


def peaks(spectra, sources, twiddles, noise_level, freq_total, folded):
    columns = noise_level.shape[1]
    out_spec = pl.BlockSpec((1, columns), lambda i: (0, 0))
    return pl.pallas_call(
        functools.partial(peak_kernel, freq_total, folded, sources),
        grid=(twiddles.shape[0],),
        in_specs=[pl.BlockSpec(a.shape, lambda i: (0, 0, 0)) for a in spectra]
        + [pl.BlockSpec((1, *twiddles.shape[1:]), lambda i: (i, 0, 0, 0)), out_spec],
        out_specs=[out_spec, out_spec],
        out_shape=[jax.ShapeDtypeStruct((1, columns), jnp.float32)] * 2,
        scratch_shapes=[pltpu.VMEM((max(8, columns), ROWS), jnp.float32)],
        compiler_params=pltpu.CompilerParams(vmem_limit_bytes=VMEM_BYTES),
        name="peaks",
    )(*spectra, twiddles, noise_level)


def body(
    flaw_cells,
    flaw_blocks,
    element_channel,
    focal_delay,
    beam_field,
    flaw_size,
    flaw_slope,
    noise_level,
):
    freq_count = lax.axis_size("freq")
    freq_total = W_DEV * freq_count
    sample_count = min(T_CAP, 2 * freq_total)
    swap = [(0, 1), (1, 0)]
    slots = freq_count if freq_count in (4, 8) else 1
    small = (
        flaw_cells.reshape(1, -1),
        flaw_size,
        flaw_slope,
        element_channel.reshape(1, -1),
        focal_delay,
        flaw_blocks,
    )
    far, near = spectra_of(beam_field, small, swap, freq_total, slots)
    folded = sample_count == 2 * freq_total
    times = sample_count // 2 if folded else sample_count
    twiddles = table(freq_total, slots, times, min(128, times))
    if slots > 1:

        def send(array, mask):
            pairs = [(a, a ^ mask) for a in range(slots)]
            return lax.ppermute(array, "freq", pairs)

        half = slots // 2
        size = FG // slots
        across = send(far[0], half)
        spectra = [across, *(send(near[s], s) for s in (*range(2, half), 1))]
        spectra.append(send(far[1], slots - 1))
        passed = split(across, size, spectra[1:half])
        spectra += [send(array, 1 + i) for i, array in enumerate(passed)]
        spectra.append(near[0])
        operands = [len(spectra) - 1, half - 1, *range(1, half - 1)]
        operands += [0, *range(half + 1, len(spectra) - 1), half]
        sources = [(i, 0) for i in operands]
    else:
        moved = jnp.concatenate([near[0], far[0]], axis=0)
        moved = lax.all_to_all(moved, "freq", split_axis=0, concat_axis=0, tiled=True)
        spectra = [moved]
        sources = [(0, s * (FG // freq_count)) for s in range(freq_count)]
    return tuple(peaks(spectra, sources, twiddles, noise_level, freq_total, folded))


def solution(mesh):
    in_specs = (
        P("batch"),
        P("batch"),
        P("elem"),
        P(),
        P("freq", None, "elem", None),
        P("batch", None),
        P("batch", None),
        P(("batch", "elem"), "freq"),
    )
    out_specs = (P(("batch", "elem"), "freq"), P(("batch", "elem"), "freq"))
    return jax.shard_map(body, mesh=mesh, in_specs=in_specs, out_specs=out_specs, check_vma=False)
```

```python
import functools
import math

import jax
import jax.numpy as jnp
from jax import lax
from jax.experimental import pallas as pl
from jax.experimental.pallas import tpu as pltpu
from jax.sharding import PartitionSpec as P

W_DEV = 16
W_HALF = W_DEV // 2
FG = 128
NB = 4
SB = 32
T_CAP = 1024

EDGE = 0.6
STEEP = 3.0
EPS = 1e-05

ROWS = NB * SB
VMEM_BYTES = 48 * 1024 * 1024


def sin_half_turn(turns):
    angle = turns * math.pi
    square = angle * angle
    sine = 1.0 / 6227020800.0
    for factorial in (-39916800.0, 362880.0, -5040.0, 120.0, -6.0, 1.0):
        sine = sine * square + 1.0 / factorial
    cosine = 1.0 / 479001600.0
    for factorial in (-3628800.0, 40320.0, -720.0, 24.0, -2.0, 1.0):
        cosine = cosine * square + 1.0 / factorial
    return sine * angle, cosine


def sincos_turns(turns):
    rest = turns - jnp.floor(turns + 0.5)
    sine, cosine = sin_half_turn(rest)
    return 2.0 * sine * cosine, 1.0 - 2.0 * sine * sine


def dot(left, right, contract):
    return lax.dot_general(
        left, right, (contract, ((), ())), preferred_element_type=jnp.float32
    )


def partner(slots, slot):
    index = lax.axis_index("freq")
    half = slots // 2
    near = (index & half) | slot
    return jnp.where(slot < half, near, index ^ slot)


def slot_order(slots):
    size = FG // slots
    row = lax.broadcasted_iota(jnp.int32, (FG, 1), 0)
    column = lax.broadcasted_iota(jnp.int32, (FG, FG), 1)
    if slots > 1:
        row = partner(slots, row // size) * size + row % size
    return row == column


def delay_pieces(channel_ref, delay_ref, elements):
    channel_sel = (
        (
            lax.broadcasted_iota(jnp.int32, (delay_ref.shape[0], elements), 0)
            == channel_ref[...]
        )
        .astype(jnp.float32)
        .T.astype(jnp.bfloat16)
    )
    rest = delay_ref[...]
    pieces = []
    for _ in range(3):
        piece = rest.astype(jnp.bfloat16)
        rest = rest - piece.astype(jnp.float32)
        pieces.append(dot(channel_sel, piece, ((1,), (0,))).astype(jnp.bfloat16))
    return pieces


def turned(law, step):
    return law[0] * step[0] - law[1] * step[1], law[1] * step[0] + law[0] * step[1]


def prepare(freq_total, slots, which, pieces, cells_ref, size_ref, slope_ref, blocks_ref):
    sites = cells_ref.shape[1]
    first_freq = lax.axis_index("freq") * W_DEV
    order = slot_order(slots)
    cells = jnp.where(which == 0, cells_ref[:, :FG], cells_ref[:, FG:])
    cell_sel = lax.broadcasted_iota(jnp.int32, (sites, FG), 0) == cells
    pick = dot(
        order.astype(jnp.bfloat16), cell_sel.astype(jnp.bfloat16), ((1,), (1,))
    ).astype(jnp.bfloat16)
    size = size_ref[pl.ds(which, 1), :]
    turn = size * slope_ref[pl.ds(which, 1), :] * (1.0 / freq_total)
    size = jnp.sum(jnp.where(order, size, 0.0), axis=1, keepdims=True)
    turn = jnp.sum(jnp.where(order, turn, 0.0), axis=1, keepdims=True)
    freq = first_freq + lax.broadcasted_iota(jnp.int32, (FG, FG), 1)
    sine, cosine = sincos_turns(turn * freq.astype(jnp.float32))
    k_real = size * (1.0 + EDGE) * cosine
    k_imag = size * (EDGE - 1.0) * sine
    lane = lax.broadcasted_iota(jnp.int32, (1, ROWS), 1)
    position = lane & (SB - 1)
    for j in range(NB):
        block = blocks_ref[which * NB + j]
        position = position + jnp.where((lane >> 5) == j, block * SB, 0)
    scan_sel = (
        lax.broadcasted_iota(jnp.int32, (pieces[0].shape[1], ROWS), 0) == position
    ).astype(jnp.bfloat16)
    delays = None
    for piece in pieces:
        moved = dot(piece, scan_sel, ((1,), (0,)))
        delays = moved if delays is None else delays + moved
    phase = delays * (0.5 / freq_total)
    unit = sincos_turns(phase)[::-1]
    base = sincos_turns(phase * first_freq.astype(jnp.float32))[::-1]
    return *base, *turned(unit, unit), *turned(base, unit), pick, k_real, k_imag


def partial_spectra(parity, law, step, pick, k_real, k_imag, field_ref, wait, out_ref, scratch):
    picked_ref, law_ref, rows_ref = scratch
    elements, sites = field_ref.shape[3:]
    for w in range(W_HALF):
        c = law[0].astype(jnp.bfloat16)
        s = law[1].astype(jnp.bfloat16)
        law_ref[w, :elements, :ROWS] = c
        law_ref[w, :elements, ROWS:] = -s
        law_ref[w, elements:, :ROWS] = s
        law_ref[w, elements:, ROWS:] = c
        if w < W_HALF - 1:
            law = turned(law, step)
    for w in range(W_HALF):
        wait(w)
        picked_ref[w] = dot(
            pick, field_ref[w, parity].reshape(2 * elements, sites), ((1,), (1,))
        ).astype(jnp.bfloat16)
    for w in range(W_HALF):
        product = dot(picked_ref[w], law_ref[w], ((1,), (0,)))
        real_part = product[:, :ROWS]
        imag_part = product[:, ROWS:]
        kr = k_real[:, 2 * w + parity : 2 * w + parity + 1]
        ki = k_imag[:, 2 * w + parity : 2 * w + parity + 1]
        rows_ref[pl.ds(2 * w, FG, stride=W_DEV), :] = kr * real_part - ki * imag_part
        rows_ref[pl.ds(2 * w + 1, FG, stride=W_DEV), :] = kr * imag_part + ki * real_part
    out_ref[...] = rows_ref[...].reshape(FG, W_DEV, ROWS).astype(jnp.bfloat16)


def even_spectra(values, field_ref, wait, out_ref, kept, scratch):
    for ref, value in zip(kept, values[2:]):
        ref[...] = value
    partial_spectra(
        0, values[:2], values[2:4], *values[6:], field_ref, wait, out_ref, scratch
    )


def other_even_kernel(freq_total, slots, *refs):
    field_hbm, *small_hbm = refs[:7]
    out_ref, field_ref, cells_ref, size_ref, slope_ref, pieces_ref, *kept = refs[7:20]
    channel_ref, delay_ref, blocks_ref, field_sem, small_sem, *scratch = refs[20:]
    small = (cells_ref, size_ref, slope_ref, channel_ref, delay_ref, blocks_ref)
    copies = [
        pltpu.make_async_copy(source, target, small_sem.at[i])
        for i, (source, target) in enumerate(zip(small_hbm, small))
    ]
    for copy in copies:
        copy.start()
    part = W_HALF // 2
    field_copies = [
        pltpu.make_async_copy(
            field_hbm.at[pl.ds(i * part, part), parity],
            field_ref.at[pl.ds(i * part, part), parity],
            field_sem.at[parity, i],
        )
        for parity in range(2)
        for i in range(2)
    ]
    for copy in field_copies:
        copy.start()
    for copy in copies:
        copy.wait()
    pieces = delay_pieces(channel_ref, delay_ref, field_ref.shape[3])
    for i, piece in enumerate(pieces):
        pieces_ref[i] = piece
    other = 1 - lax.axis_index("elem")
    values = prepare(
        freq_total, slots, other, pieces, cells_ref, size_ref, slope_ref, blocks_ref
    )

    def wait(w):
        if w % part == 0:
            field_copies[w // part].wait()

    even_spectra(values, field_ref, wait, out_ref, kept, scratch)
    for copy in field_copies[2:]:
        copy.wait()


def own_even_kernel(freq_total, slots, field_ref, cells_ref, size_ref, slope_ref, *refs):
    pieces_ref, blocks_ref, out_ref, *refs = refs
    kept, scratch = refs[:7], refs[7:]
    pieces = [pieces_ref[i] for i in range(pieces_ref.shape[0])]
    group = lax.axis_index("elem")
    values = prepare(
        freq_total, slots, group, pieces, cells_ref, size_ref, slope_ref, blocks_ref
    )
    even_spectra(values, field_ref, lambda w: None, out_ref, kept, scratch)


def odd_kernel(after, field_ref, *refs):
    step, law, pick = refs[0:2], refs[2:4], refs[4]
    k_refs, (out_ref, *scratch) = refs[5:7], refs[7 + after :]
    partial_spectra(
        1,
        [ref[...] for ref in law],
        [ref[...] for ref in step],
        pick[...],
        *k_refs,
        field_ref,
        lambda w: None,
        out_ref,
        scratch,
    )


def call(kernel, name, in_specs, out_shape, scratch):
    vmem = pl.BlockSpec(memory_space=pltpu.VMEM)
    return pl.pallas_call(
        kernel,
        in_specs=in_specs,
        out_specs=[vmem] * len(out_shape),
        out_shape=out_shape,
        scratch_shapes=scratch,
        compiler_params=pltpu.CompilerParams(vmem_limit_bytes=VMEM_BYTES),
        cost_estimate=pl.CostEstimate(flops=1000, bytes_accessed=1000, transcendentals=0),
        name=name,
    )


def even_partials(field, small, swap, freq_total, slots):
    elements, sites = field.shape[3:]
    vmem = pl.BlockSpec(memory_space=pltpu.VMEM)
    hbm = pl.BlockSpec(memory_space=pltpu.HBM)
    smem = pl.BlockSpec(memory_space=pltpu.SMEM)
    cells, length, slope, channel, delay, blocks = small
    pinned = [pltpu.with_memory_space_constraint(a, pltpu.HBM) for a in (field, *small)]
    work = [
        pltpu.VMEM((W_HALF, FG, 2 * elements), jnp.bfloat16),
        pltpu.VMEM((W_HALF, 2 * elements, 2 * ROWS), jnp.bfloat16),
        pltpu.VMEM((FG * W_DEV, ROWS), jnp.float32),
    ]
    out = jax.ShapeDtypeStruct((FG, W_DEV, ROWS), jnp.bfloat16)
    pieces = jax.ShapeDtypeStruct((3, elements, delay.shape[1]), jnp.bfloat16)
    kept = [jax.ShapeDtypeStruct((elements, ROWS), jnp.float32)] * 4
    kept += [jax.ShapeDtypeStruct((FG, sites), jnp.bfloat16)]
    kept += [jax.ShapeDtypeStruct((FG, FG), jnp.float32)] * 2
    copied = [jax.ShapeDtypeStruct(a.shape, a.dtype) for a in (field, cells, length, slope)]
    other, field, cells, length, slope, pieces, *other_kept = call(
        functools.partial(other_even_kernel, freq_total, slots),
        "other_even",
        [hbm] * len(pinned),
        [out, *copied, pieces, *kept],
        [
            pltpu.VMEM(channel.shape, channel.dtype),
            pltpu.VMEM(delay.shape, delay.dtype),
            pltpu.SMEM(blocks.shape, blocks.dtype),
            pltpu.SemaphoreType.DMA((2, 2)),
            pltpu.SemaphoreType.DMA((len(small),)),
            *work,
        ],
    )(*pinned)
    moved = lax.ppermute(other, "elem", swap)
    own, *own_kept = call(
        functools.partial(own_even_kernel, freq_total, slots),
        "own_even",
        [vmem] * 5 + [smem],
        [out, *kept],
        work,
    )(field, cells, length, slope, pieces, blocks)

    def odd_partials(*after):
        other, own = (
            call(
                functools.partial(odd_kernel, len(first)),
                name,
                [vmem] * 8 + [pl.BlockSpec(memory_space=pl.ANY)] * len(first),
                [out],
                work,
            )(field, *kept, *first)[0]
            for name, kept, first in (
                ("other_odd", other_kept, ()),
                ("own_odd", own_kept, after),
            )
        )
        return own, lax.ppermute(other, "elem", swap)

    return own, moved, odd_partials


def total(own_ref, moved_ref, rows):
    both = own_ref[rows].astype(jnp.float32) + moved_ref[rows].astype(jnp.float32)
    return both.astype(jnp.bfloat16)


def add_even_kernel(size, early, own_ref, moved_ref, held_ref, *refs):
    slots = range(own_ref.shape[0] // size)
    for slot, ref in zip(early, refs):
        ref[...] = total(own_ref, moved_ref, pl.ds(slot * size, size))
    for i, slot in enumerate([s for s in slots if s not in early]):
        held_ref[pl.ds(i * size, size)] = total(own_ref, moved_ref, pl.ds(slot * size, size))


def add_even(own, moved, size, early):
    vmem = pl.BlockSpec(memory_space=pltpu.VMEM)
    flaws, planes, rows = own.shape
    shapes = [jax.ShapeDtypeStruct((flaws - size * len(early), planes, rows), own.dtype)]
    shapes += [jax.ShapeDtypeStruct((size, planes, rows), own.dtype)] * len(early)
    return call(
        functools.partial(add_even_kernel, size, early), "add_even", [vmem] * 2, shapes, []
    )(own, moved)


def add_odd_kernel(size, early, buffers, after, own_ref, moved_ref, held_ref, *refs):
    refs = refs[after:]
    planes = own_ref.shape[1]
    slots = range(own_ref.shape[0] // size)
    late = [s for s in slots if s not in early]
    alone = len(refs) - len(buffers)
    for slot, ref in zip(early, refs[:alone]):
        ref[...] = total(own_ref, moved_ref, pl.ds(slot * size, size))
    for members, ref in zip(buffers, refs[alone:]):
        for i, slot in enumerate(members):
            rows = pl.ds(i * size, size)
            ref[rows, :planes] = held_ref[pl.ds(late.index(slot) * size, size)]
            ref[rows, planes:] = total(own_ref, moved_ref, pl.ds(slot * size, size))


def add_odd(name, own, moved, held, size, early, alone, buffers, after):
    vmem = pl.BlockSpec(memory_space=pltpu.VMEM)
    _, planes, rows = own.shape
    shapes = [jax.ShapeDtypeStruct((size, planes, rows), own.dtype)] * len(early) * alone
    shapes += [
        jax.ShapeDtypeStruct((size * len(members), 2 * planes, rows), own.dtype)
        for members in buffers
    ]
    return call(
        functools.partial(add_odd_kernel, size, early, buffers, len(after)),
        name,
        [vmem] * 3 + [pl.BlockSpec(memory_space=pl.ANY)] * len(after),
        shapes,
        [],
    )(own, moved, held, *after)


def table_kernel(freq_total, slots, table_ref):
    height, depth = table_ref.shape[2:]
    time_block = height // 2
    row = lax.broadcasted_iota(jnp.int32, (height, depth // 2), 0)
    column = lax.broadcasted_iota(jnp.int32, (height, depth // 2), 1)
    out_imag = (row >= time_block).astype(jnp.int32)
    time = pl.program_id(0) * time_block + row - out_imag * time_block
    for parity in range(2):
        freq = (column >> 1) * 2 + parity
        if slots > 1:
            freq = partner(slots, freq // W_DEV) * W_DEV + freq % W_DEV
        steps = freq * time + ((column & 1) - out_imag) * (freq_total // 2)
        steps = (steps + 2 * freq_total) & (2 * freq_total - 1)
        _, value = sincos_turns(steps.astype(jnp.float32) * (0.5 / freq_total))
        high = value.astype(jnp.bfloat16)
        table_ref[0, parity, :, : depth // 2] = high
        table_ref[0, parity, :, depth // 2 :] = (
            value - high.astype(jnp.float32)
        ).astype(jnp.bfloat16)


def table(freq_total, slots, times, time_block):
    blocks = times // time_block
    shape = (blocks, 2, 2 * time_block, 2 * freq_total)
    return pl.pallas_call(
        functools.partial(table_kernel, freq_total, slots),
        grid=(blocks,),
        out_specs=pl.BlockSpec((1, *shape[1:]), lambda i: (i, 0, 0, 0)),
        out_shape=jax.ShapeDtypeStruct(shape, jnp.bfloat16),
        compiler_params=pltpu.CompilerParams(vmem_limit_bytes=VMEM_BYTES),
        name="table",
    )()


def peak_kernel(freq_total, folded, sources, *refs):
    count = len(refs) - 5
    table_ref, noise_ref, peak_ref, found_ref, best_ref = refs[count:]
    step = pl.program_id(0)
    columns = peak_ref.shape[1]
    time_block = table_ref.shape[2] // 2

    @pl.when(step == 0)
    def _():
        best_ref[...] = jnp.zeros_like(best_ref)

    width = min(2, columns)
    for first in range(0, columns, width):
        parts = []
        for parity in range(2):
            spectra = jnp.concatenate(
                [
                    jnp.concatenate(
                        [
                            refs[i][row + first + k, plane : plane + W_DEV, :]
                            for i, row, plane in sources[parity]
                        ]
                        * 2,
                        axis=0,
                    )
                    for k in range(width)
                ],
                axis=1,
            )
            parts.append(dot(table_ref[0, parity], spectra, ((1,), (0,))))
        powers = []
        for signal in [parts[0] + parts[1]] + [parts[0] - parts[1]] * folded:
            real_part = signal[:time_block]
            imag_part = signal[time_block:]
            powers.append(real_part * real_part + imag_part * imag_part)
        power = jnp.maximum(powers[0], powers[-1]) if folded else powers[0]
        power = jnp.max(power, axis=0, keepdims=True)
        for k in range(width):
            row = pl.ds(first + k, 1)
            best_ref[row, :] = jnp.maximum(
                best_ref[row, :], power[:, k * ROWS : (k + 1) * ROWS]
            )

    @pl.when(step == pl.num_programs(0) - 1)
    def _():
        largest = jnp.max(best_ref[...], axis=1, keepdims=True)
        shape = best_ref.shape
        diagonal = lax.broadcasted_iota(jnp.int32, shape, 0) == lax.broadcasted_iota(
            jnp.int32, shape, 1
        )
        largest = jnp.max(jnp.where(diagonal, largest, 0.0), axis=0, keepdims=True)
        peak = jnp.sqrt(largest[:, :columns]) * (1.0 / math.sqrt(freq_total))
        score = STEEP * (jnp.log(peak + EPS) - jnp.log(noise_ref[...]))
        peak_ref[...] = peak
        found_ref[...] = 1.0 / (1.0 + jnp.exp(-score))


def peaks(spectra, sources, twiddles, noise_level, freq_total, folded):
    columns = noise_level.shape[1]
    out_spec = pl.BlockSpec((1, columns), lambda i: (0, 0))
    return pl.pallas_call(
        functools.partial(peak_kernel, freq_total, folded, sources),
        grid=(twiddles.shape[0],),
        in_specs=[pl.BlockSpec(a.shape, lambda i: (0, 0, 0)) for a in spectra]
        + [pl.BlockSpec((1, *twiddles.shape[1:]), lambda i: (i, 0, 0, 0)), out_spec],
        out_specs=[out_spec, out_spec],
        out_shape=[jax.ShapeDtypeStruct((1, columns), jnp.float32)] * 2,
        scratch_shapes=[pltpu.VMEM((max(8, columns), ROWS), jnp.float32)],
        compiler_params=pltpu.CompilerParams(vmem_limit_bytes=VMEM_BYTES),
        name="peaks",
    )(*spectra, twiddles, noise_level)


def body(
    flaw_cells,
    flaw_blocks,
    element_channel,
    focal_delay,
    beam_field,
    flaw_size,
    flaw_slope,
    noise_level,
):
    freq_count = lax.axis_size("freq")
    freq_total = W_DEV * freq_count
    sample_count = min(T_CAP, 2 * freq_total)
    swap = [(0, 1), (1, 0)]
    direct = freq_count == 8
    slots = freq_count if direct else 1
    small = (
        flaw_cells.reshape(1, -1),
        flaw_size,
        flaw_slope,
        element_channel.reshape(1, -1),
        focal_delay,
        flaw_blocks,
    )
    folded = sample_count == 2 * freq_total
    times = sample_count // 2 if folded else sample_count
    twiddles = table(freq_total, slots, times, min(128, times))
    field = beam_field.reshape(W_HALF, 2, *beam_field.shape[1:])
    own, moved, odd_partials = even_partials(field, small, swap, freq_total, slots)
    size = FG // slots
    if direct:

        def send(array, mask):
            pairs = [(a, a ^ mask) for a in range(slots)]
            return lax.ppermute(array, "freq", pairs)

        half = slots // 2
        early = tuple(range(half, slots - 1))
        held, *sent = add_even(own, moved, size, early)
        even = [send(array, slot) for slot, array in zip(early, sent)]
        own, moved = odd_partials(even[0])
        *sent, last = add_odd(
            "add_far", own, moved, held, size, early, 1, ((slots - 1,),), even[1:2]
        )
        (near,) = add_odd(
            "add_near", own, moved, held, size, early, 0, (tuple(range(half)),), even[2:]
        )
        last = send(last, slots - 1)
        odd = [send(array, slot) for slot, array in zip(early, sent)]
        groups = [[*range(half)], [*range(half, slots)]]
        near = lax.all_to_all(
            near, "freq", split_axis=0, concat_axis=0, axis_index_groups=groups, tiled=True
        )
        spectra = [*even, last, *odd, near]
        count = len(early)
        sources = [
            [(2 * count + 1, s * size, plane) for s in range(half)]
            + [(first + i, 0, 0) for i in range(count)]
            + [(count, 0, plane)]
            for first, plane in ((0, 0), (count + 1, W_DEV))
        ]
    else:
        (held,) = add_even(own, moved, size, ())
        own, moved = odd_partials()
        (whole,) = add_odd("add_odd", own, moved, held, size, (), 0, ((0,),), ())
        spectra = [
            lax.all_to_all(whole, "freq", split_axis=0, concat_axis=0, tiled=True)
        ]
        columns = FG // freq_count
        sources = [
            [(0, s * columns, plane) for s in range(freq_count)] for plane in (0, W_DEV)
        ]
    return tuple(peaks(spectra, sources, twiddles, noise_level, freq_total, folded))


def solution(mesh):
    in_specs = (
        P("batch"),
        P("batch"),
        P("elem"),
        P(),
        P("freq", None, "elem", None),
        P("batch", None),
        P("batch", None),
        P(("batch", "elem"), "freq"),
    )
    out_specs = (P(("batch", "elem"), "freq"), P(("batch", "elem"), "freq"))
    return jax.shard_map(body, mesh=mesh, in_specs=in_specs, out_specs=out_specs, check_vma=False)
```

```python
import functools
import math

import jax
import jax.numpy as jnp
from jax import lax
from jax.experimental import pallas as pl
from jax.experimental.pallas import tpu as pltpu
from jax.sharding import PartitionSpec as P

W_DEV = 16
W_HALF = W_DEV // 2
FG = 128
NB = 4
SB = 32
T_CAP = 1024

EDGE = 0.6
STEEP = 3.0
EPS = 1e-05

ROWS = NB * SB
VMEM_BYTES = 48 * 1024 * 1024


def sin_half_turn(turns):
    angle = turns * math.pi
    square = angle * angle
    sine = 1.0 / 6227020800.0
    for factorial in (-39916800.0, 362880.0, -5040.0, 120.0, -6.0, 1.0):
        sine = sine * square + 1.0 / factorial
    cosine = 1.0 / 479001600.0
    for factorial in (-3628800.0, 40320.0, -720.0, 24.0, -2.0, 1.0):
        cosine = cosine * square + 1.0 / factorial
    return sine * angle, cosine


def sincos_turns(turns):
    rest = turns - jnp.floor(turns + 0.5)
    sine, cosine = sin_half_turn(rest)
    return 2.0 * sine * cosine, 1.0 - 2.0 * sine * sine


def dot(left, right, contract):
    return lax.dot_general(
        left, right, (contract, ((), ())), preferred_element_type=jnp.float32
    )


def slot_order(slots):
    row = lax.broadcasted_iota(jnp.int32, (FG, FG), 0)
    column = lax.broadcasted_iota(jnp.int32, (FG, FG), 1)
    if slots > 1:
        row = row ^ (lax.axis_index("freq") * (FG // slots))
    return row == column


def delay_pieces(channel_ref, delay_ref, elements):
    channel_sel = (
        (
            lax.broadcasted_iota(jnp.int32, (delay_ref.shape[0], elements), 0)
            == channel_ref[...]
        )
        .astype(jnp.float32)
        .T.astype(jnp.bfloat16)
    )
    rest = delay_ref[...]
    pieces = []
    for _ in range(3):
        piece = rest.astype(jnp.bfloat16)
        rest = rest - piece.astype(jnp.float32)
        pieces.append(dot(channel_sel, piece, ((1,), (0,))).astype(jnp.bfloat16))
    return pieces


def turned(law, step):
    return law[0] * step[0] - law[1] * step[1], law[1] * step[0] + law[0] * step[1]


def prepare(freq_total, slots, which, pieces, cells_ref, size_ref, slope_ref, blocks_ref):
    sites = cells_ref.shape[1]
    first_freq = lax.axis_index("freq") * W_DEV
    order = slot_order(slots)
    cells = jnp.where(which == 0, cells_ref[:, :FG], cells_ref[:, FG:])
    cell_sel = lax.broadcasted_iota(jnp.int32, (sites, FG), 0) == cells
    pick = dot(
        order.astype(jnp.bfloat16), cell_sel.astype(jnp.bfloat16), ((1,), (1,))
    ).astype(jnp.bfloat16)
    size = size_ref[pl.ds(which, 1), :]
    turn = size * slope_ref[pl.ds(which, 1), :] * (1.0 / freq_total)
    size = jnp.sum(jnp.where(order, size, 0.0), axis=1, keepdims=True)
    turn = jnp.sum(jnp.where(order, turn, 0.0), axis=1, keepdims=True)
    freq = first_freq + lax.broadcasted_iota(jnp.int32, (FG, FG), 1)
    sine, cosine = sincos_turns(turn * freq.astype(jnp.float32))
    k_real = size * (1.0 + EDGE) * cosine
    k_imag = size * (EDGE - 1.0) * sine
    lane = lax.broadcasted_iota(jnp.int32, (1, ROWS), 1)
    position = lane & (SB - 1)
    for j in range(NB):
        block = blocks_ref[which * NB + j]
        position = position + jnp.where((lane >> 5) == j, block * SB, 0)
    scan_sel = (
        lax.broadcasted_iota(jnp.int32, (pieces[0].shape[1], ROWS), 0) == position
    ).astype(jnp.bfloat16)
    delays = None
    for piece in pieces:
        moved = dot(piece, scan_sel, ((1,), (0,)))
        delays = moved if delays is None else delays + moved
    phase = delays * (0.5 / freq_total)
    unit = sincos_turns(phase)[::-1]
    base = sincos_turns(phase * first_freq.astype(jnp.float32))[::-1]
    return *base, *turned(unit, unit), *turned(base, unit), pick, k_real, k_imag


def partial_spectra(parity, law, step, pick, k_real, k_imag, field_ref, wait, out_ref, scratch):
    picked_ref, law_ref, rows_ref = scratch
    elements, sites = field_ref.shape[3:]
    for w in range(W_HALF):
        c = law[0].astype(jnp.bfloat16)
        s = law[1].astype(jnp.bfloat16)
        law_ref[w, :elements, :ROWS] = c
        law_ref[w, :elements, ROWS:] = -s
        law_ref[w, elements:, :ROWS] = s
        law_ref[w, elements:, ROWS:] = c
        if w < W_HALF - 1:
            law = turned(law, step)
    for w in range(W_HALF):
        wait(w)
        picked_ref[w] = dot(
            pick, field_ref[w, parity].reshape(2 * elements, sites), ((1,), (1,))
        ).astype(jnp.bfloat16)
    for w in range(W_HALF):
        product = dot(picked_ref[w], law_ref[w], ((1,), (0,)))
        real_part = product[:, :ROWS]
        imag_part = product[:, ROWS:]
        kr = k_real[:, 2 * w + parity : 2 * w + parity + 1]
        ki = k_imag[:, 2 * w + parity : 2 * w + parity + 1]
        rows_ref[pl.ds(2 * w, FG, stride=W_DEV), :] = kr * real_part - ki * imag_part
        rows_ref[pl.ds(2 * w + 1, FG, stride=W_DEV), :] = kr * imag_part + ki * real_part
    out_ref[...] = rows_ref[...].reshape(FG, W_DEV, ROWS).astype(jnp.bfloat16)


def even_spectra(values, field_ref, wait, out_ref, kept, scratch):
    for ref, value in zip(kept, values[2:]):
        ref[...] = value
    partial_spectra(
        0, values[:2], values[2:4], *values[6:], field_ref, wait, out_ref, scratch
    )


def other_even_kernel(freq_total, slots, *refs):
    field_hbm, *small_hbm = refs[:7]
    out_ref, field_ref, cells_ref, size_ref, slope_ref, pieces_ref, *kept = refs[7:20]
    channel_ref, delay_ref, blocks_ref, field_sem, small_sem, *scratch = refs[20:]
    small = (cells_ref, size_ref, slope_ref, channel_ref, delay_ref, blocks_ref)
    copies = [
        pltpu.make_async_copy(source, target, small_sem.at[i])
        for i, (source, target) in enumerate(zip(small_hbm, small))
    ]
    for copy in copies:
        copy.start()
    part = W_HALF // 2
    field_copies = [
        pltpu.make_async_copy(
            field_hbm.at[pl.ds(i * part, part), parity],
            field_ref.at[pl.ds(i * part, part), parity],
            field_sem.at[parity, i],
        )
        for parity in range(2)
        for i in range(2)
    ]
    for copy in field_copies:
        copy.start()
    for copy in copies:
        copy.wait()
    pieces = delay_pieces(channel_ref, delay_ref, field_ref.shape[3])
    for i, piece in enumerate(pieces):
        pieces_ref[i] = piece
    other = 1 - lax.axis_index("elem")
    values = prepare(
        freq_total, slots, other, pieces, cells_ref, size_ref, slope_ref, blocks_ref
    )

    def wait(w):
        if w % part == 0:
            field_copies[w // part].wait()

    even_spectra(values, field_ref, wait, out_ref, kept, scratch)
    for copy in field_copies[2:]:
        copy.wait()


def own_even_kernel(freq_total, slots, field_ref, cells_ref, size_ref, slope_ref, *refs):
    pieces_ref, blocks_ref, out_ref, *refs = refs
    kept, scratch = refs[:7], refs[7:]
    pieces = [pieces_ref[i] for i in range(pieces_ref.shape[0])]
    group = lax.axis_index("elem")
    values = prepare(
        freq_total, slots, group, pieces, cells_ref, size_ref, slope_ref, blocks_ref
    )
    even_spectra(values, field_ref, lambda w: None, out_ref, kept, scratch)


def odd_kernel(after, field_ref, *refs):
    step, law, pick = refs[0:2], refs[2:4], refs[4]
    k_refs, (out_ref, *scratch) = refs[5:7], refs[7 + after :]
    partial_spectra(
        1,
        [ref[...] for ref in law],
        [ref[...] for ref in step],
        pick[...],
        *k_refs,
        field_ref,
        lambda w: None,
        out_ref,
        scratch,
    )


def call(kernel, name, in_specs, out_shape, scratch):
    vmem = pl.BlockSpec(memory_space=pltpu.VMEM)
    return pl.pallas_call(
        kernel,
        in_specs=in_specs,
        out_specs=[vmem] * len(out_shape),
        out_shape=out_shape,
        scratch_shapes=scratch,
        compiler_params=pltpu.CompilerParams(vmem_limit_bytes=VMEM_BYTES),
        cost_estimate=pl.CostEstimate(flops=1000, bytes_accessed=1000, transcendentals=0),
        name=name,
    )


def even_partials(field, small, swap, freq_total, slots):
    elements, sites = field.shape[3:]
    vmem = pl.BlockSpec(memory_space=pltpu.VMEM)
    hbm = pl.BlockSpec(memory_space=pltpu.HBM)
    smem = pl.BlockSpec(memory_space=pltpu.SMEM)
    cells, length, slope, channel, delay, blocks = small
    pinned = [pltpu.with_memory_space_constraint(a, pltpu.HBM) for a in (field, *small)]
    work = [
        pltpu.VMEM((W_HALF, FG, 2 * elements), jnp.bfloat16),
        pltpu.VMEM((W_HALF, 2 * elements, 2 * ROWS), jnp.bfloat16),
        pltpu.VMEM((FG * W_DEV, ROWS), jnp.float32),
    ]
    out = jax.ShapeDtypeStruct((FG, W_DEV, ROWS), jnp.bfloat16)
    pieces = jax.ShapeDtypeStruct((3, elements, delay.shape[1]), jnp.bfloat16)
    kept = [jax.ShapeDtypeStruct((elements, ROWS), jnp.float32)] * 4
    kept += [jax.ShapeDtypeStruct((FG, sites), jnp.bfloat16)]
    kept += [jax.ShapeDtypeStruct((FG, FG), jnp.float32)] * 2
    copied = [jax.ShapeDtypeStruct(a.shape, a.dtype) for a in (field, cells, length, slope)]
    other, field, cells, length, slope, pieces, *other_kept = call(
        functools.partial(other_even_kernel, freq_total, slots),
        "other_even",
        [hbm] * len(pinned),
        [out, *copied, pieces, *kept],
        [
            pltpu.VMEM(channel.shape, channel.dtype),
            pltpu.VMEM(delay.shape, delay.dtype),
            pltpu.SMEM(blocks.shape, blocks.dtype),
            pltpu.SemaphoreType.DMA((2, 2)),
            pltpu.SemaphoreType.DMA((len(small),)),
            *work,
        ],
    )(*pinned)
    moved = lax.ppermute(other, "elem", swap)
    own, *own_kept = call(
        functools.partial(own_even_kernel, freq_total, slots),
        "own_even",
        [vmem] * 5 + [smem],
        [out, *kept],
        work,
    )(field, cells, length, slope, pieces, blocks)

    def odd_partials(*after):
        other, own = (
            call(
                functools.partial(odd_kernel, len(first)),
                name,
                [vmem] * 8 + [pl.BlockSpec(memory_space=pl.ANY)] * len(first),
                [out],
                work,
            )(field, *kept, *first)[0]
            for name, kept, first in (
                ("other_odd", other_kept, ()),
                ("own_odd", own_kept, after),
            )
        )
        return own, lax.ppermute(other, "elem", swap)

    return own, moved, odd_partials


def total(own_ref, moved_ref, rows):
    both = own_ref[rows].astype(jnp.float32) + moved_ref[rows].astype(jnp.float32)
    return both.astype(jnp.bfloat16)


def add_even_kernel(size, early, own_ref, moved_ref, held_ref, *refs):
    slots = range(own_ref.shape[0] // size)
    for slot, ref in zip(early, refs):
        ref[...] = total(own_ref, moved_ref, pl.ds(slot * size, size))
    for i, slot in enumerate([s for s in slots if s not in early]):
        held_ref[pl.ds(i * size, size)] = total(own_ref, moved_ref, pl.ds(slot * size, size))


def add_even(own, moved, size, early):
    vmem = pl.BlockSpec(memory_space=pltpu.VMEM)
    flaws, planes, rows = own.shape
    shapes = [jax.ShapeDtypeStruct((flaws - size * len(early), planes, rows), own.dtype)]
    shapes += [jax.ShapeDtypeStruct((size, planes, rows), own.dtype)] * len(early)
    return call(
        functools.partial(add_even_kernel, size, early), "add_even", [vmem] * 2, shapes, []
    )(own, moved)


def add_odd_kernel(size, early, late, own_ref, moved_ref, held_ref, *refs):
    planes = own_ref.shape[1]
    held = sorted(late)
    for slot, ref in zip((*early, *late), refs):
        value = total(own_ref, moved_ref, pl.ds(slot * size, size))
        if slot in early:
            ref[...] = value
        else:
            ref[:, :planes] = held_ref[pl.ds(held.index(slot) * size, size)]
            ref[:, planes:] = value


def add_odd(own, moved, held, size, early, late):
    vmem = pl.BlockSpec(memory_space=pltpu.VMEM)
    _, planes, rows = own.shape
    shapes = [
        jax.ShapeDtypeStruct((size, planes * (1 if slot in early else 2), rows), own.dtype)
        for slot in (*early, *late)
    ]
    return call(
        functools.partial(add_odd_kernel, size, early, late), "add_odd", [vmem] * 3, shapes, []
    )(own, moved, held)


def table_kernel(freq_total, slots, table_ref):
    height, depth = table_ref.shape[2:]
    time_block = height // 2
    row = lax.broadcasted_iota(jnp.int32, (height, depth // 2), 0)
    column = lax.broadcasted_iota(jnp.int32, (height, depth // 2), 1)
    out_imag = (row >= time_block).astype(jnp.int32)
    time = pl.program_id(0) * time_block + row - out_imag * time_block
    for parity in range(2):
        freq = (column >> 1) * 2 + parity
        if slots > 1:
            freq = freq ^ (lax.axis_index("freq") * W_DEV)
        steps = freq * time + ((column & 1) - out_imag) * (freq_total // 2)
        steps = (steps + 2 * freq_total) & (2 * freq_total - 1)
        _, value = sincos_turns(steps.astype(jnp.float32) * (0.5 / freq_total))
        high = value.astype(jnp.bfloat16)
        table_ref[0, parity, :, : depth // 2] = high
        table_ref[0, parity, :, depth // 2 :] = (
            value - high.astype(jnp.float32)
        ).astype(jnp.bfloat16)


def table(freq_total, slots, times, time_block):
    blocks = times // time_block
    shape = (blocks, 2, 2 * time_block, 2 * freq_total)
    return pl.pallas_call(
        functools.partial(table_kernel, freq_total, slots),
        grid=(blocks,),
        out_specs=pl.BlockSpec((1, *shape[1:]), lambda i: (i, 0, 0, 0)),
        out_shape=jax.ShapeDtypeStruct(shape, jnp.bfloat16),
        compiler_params=pltpu.CompilerParams(vmem_limit_bytes=VMEM_BYTES),
        name="table",
    )()


def peak_kernel(freq_total, folded, sources, *refs):
    count = len(refs) - 5
    table_ref, noise_ref, peak_ref, found_ref, best_ref = refs[count:]
    step = pl.program_id(0)
    columns = peak_ref.shape[1]
    time_block = table_ref.shape[2] // 2

    @pl.when(step == 0)
    def _():
        best_ref[...] = jnp.zeros_like(best_ref)

    width = min(2, columns)
    for first in range(0, columns, width):
        parts = []
        for parity in range(2):
            spectra = jnp.concatenate(
                [
                    jnp.concatenate(
                        [
                            refs[i][row + first + k, plane : plane + W_DEV, :]
                            for i, row, plane in sources[parity]
                        ]
                        * 2,
                        axis=0,
                    )
                    for k in range(width)
                ],
                axis=1,
            )
            parts.append(dot(table_ref[0, parity], spectra, ((1,), (0,))))
        powers = []
        for signal in [parts[0] + parts[1]] + [parts[0] - parts[1]] * folded:
            real_part = signal[:time_block]
            imag_part = signal[time_block:]
            powers.append(real_part * real_part + imag_part * imag_part)
        power = jnp.maximum(powers[0], powers[-1]) if folded else powers[0]
        power = jnp.max(power, axis=0, keepdims=True)
        for k in range(width):
            row = pl.ds(first + k, 1)
            best_ref[row, :] = jnp.maximum(
                best_ref[row, :], power[:, k * ROWS : (k + 1) * ROWS]
            )

    @pl.when(step == pl.num_programs(0) - 1)
    def _():
        largest = jnp.max(best_ref[...], axis=1, keepdims=True)
        shape = best_ref.shape
        diagonal = lax.broadcasted_iota(jnp.int32, shape, 0) == lax.broadcasted_iota(
            jnp.int32, shape, 1
        )
        largest = jnp.max(jnp.where(diagonal, largest, 0.0), axis=0, keepdims=True)
        peak = jnp.sqrt(largest[:, :columns]) * (1.0 / math.sqrt(freq_total))
        score = STEEP * (jnp.log(peak + EPS) - jnp.log(noise_ref[...]))
        peak_ref[...] = peak
        found_ref[...] = 1.0 / (1.0 + jnp.exp(-score))


def peaks(spectra, sources, twiddles, noise_level, freq_total, folded):
    columns = noise_level.shape[1]
    out_spec = pl.BlockSpec((1, columns), lambda i: (0, 0))
    return pl.pallas_call(
        functools.partial(peak_kernel, freq_total, folded, sources),
        grid=(twiddles.shape[0],),
        in_specs=[pl.BlockSpec(a.shape, lambda i: (0, 0, 0)) for a in spectra]
        + [pl.BlockSpec((1, *twiddles.shape[1:]), lambda i: (i, 0, 0, 0)), out_spec],
        out_specs=[out_spec, out_spec],
        out_shape=[jax.ShapeDtypeStruct((1, columns), jnp.float32)] * 2,
        scratch_shapes=[pltpu.VMEM((max(8, columns), ROWS), jnp.float32)],
        compiler_params=pltpu.CompilerParams(vmem_limit_bytes=VMEM_BYTES),
        name="peaks",
    )(*spectra, twiddles, noise_level)


def body(
    flaw_cells,
    flaw_blocks,
    element_channel,
    focal_delay,
    beam_field,
    flaw_size,
    flaw_slope,
    noise_level,
):
    freq_count = lax.axis_size("freq")
    freq_total = W_DEV * freq_count
    sample_count = min(T_CAP, 2 * freq_total)
    swap = [(0, 1), (1, 0)]
    direct = freq_count == 8
    slots = freq_count if direct else 1
    small = (
        flaw_cells.reshape(1, -1),
        flaw_size,
        flaw_slope,
        element_channel.reshape(1, -1),
        focal_delay,
        flaw_blocks,
    )
    folded = sample_count == 2 * freq_total
    times = sample_count // 2 if folded else sample_count
    twiddles = table(freq_total, slots, times, min(128, times))
    field = beam_field.reshape(W_HALF, 2, *beam_field.shape[1:])
    own, moved, odd_partials = even_partials(field, small, swap, freq_total, slots)
    size = FG // slots
    if direct:

        def send(array, mask):
            pairs = [(a, a ^ mask) for a in range(slots)]
            return lax.ppermute(array, "freq", pairs)

        half = slots // 2
        early = tuple(range(half, half + 2))
        late = (*range(half + 2, slots), *range(2, half), 1, 0)
        held, *sent = add_even(own, moved, size, early)
        even = [send(array, slot) for slot, array in zip(early, sent)]
        own, moved = odd_partials(held)
        sent = add_odd(own, moved, held, size, early, late)
        odd = [send(array, slot) for slot, array in zip(early, sent)]
        sent = dict(zip(late, sent[len(early) :]))
        wide = {slot: send(array, slot) if slot else array for slot, array in sent.items()}
        spectra = [*even, *(wide[s] for s in late if s >= half), *odd]
        spectra += [wide[s] for s in late if s < half]
        place = {id(array): i for i, array in enumerate(spectra)}
        sources = [
            [
                (place[id(some[slot - half])], 0, 0) if slot in early else (place[id(wide[slot])], 0, plane)
                for slot in range(slots)
            ]
            for some, plane in ((even, 0), (odd, W_DEV))
        ]
    else:
        (held,) = add_even(own, moved, size, ())
        own, moved = odd_partials()
        (whole,) = add_odd(own, moved, held, size, (), (0,))
        spectra = [
            lax.all_to_all(whole, "freq", split_axis=0, concat_axis=0, tiled=True)
        ]
        columns = FG // freq_count
        sources = [
            [(0, s * columns, plane) for s in range(freq_count)] for plane in (0, W_DEV)
        ]
    return tuple(peaks(spectra, sources, twiddles, noise_level, freq_total, folded))


def solution(mesh):
    in_specs = (
        P("batch"),
        P("batch"),
        P("elem"),
        P(),
        P("freq", None, "elem", None),
        P("batch", None),
        P("batch", None),
        P(("batch", "elem"), "freq"),
    )
    out_specs = (P(("batch", "elem"), "freq"), P(("batch", "elem"), "freq"))
    return jax.shard_map(body, mesh=mesh, in_specs=in_specs, out_specs=out_specs, check_vma=False)
```

```python
import functools
import math

import jax
import jax.numpy as jnp
from jax import lax
from jax.experimental import pallas as pl
from jax.experimental.pallas import tpu as pltpu
from jax.sharding import PartitionSpec as P

W_DEV = 16
FG = 128
NB = 4
SB = 32
T_CAP = 1024

EDGE = 0.6
STEEP = 3.0
EPS = 1e-05

ROWS = NB * SB
VMEM_BYTES = 48 * 1024 * 1024


def sin_half_turn(turns):
    angle = turns * math.pi
    square = angle * angle
    sine = 1.0 / 6227020800.0
    for factorial in (-39916800.0, 362880.0, -5040.0, 120.0, -6.0, 1.0):
        sine = sine * square + 1.0 / factorial
    cosine = 1.0 / 479001600.0
    for factorial in (-3628800.0, 40320.0, -720.0, 24.0, -2.0, 1.0):
        cosine = cosine * square + 1.0 / factorial
    return sine * angle, cosine


def sincos_turns(turns):
    rest = turns - jnp.floor(turns + 0.5)
    sine, cosine = sin_half_turn(rest)
    return 2.0 * sine * cosine, 1.0 - 2.0 * sine * sine


def dot(left, right, contract):
    return lax.dot_general(
        left, right, (contract, ((), ())), preferred_element_type=jnp.float32
    )


def slot_order(slots):
    row = lax.broadcasted_iota(jnp.int32, (FG, FG), 0)
    column = lax.broadcasted_iota(jnp.int32, (FG, FG), 1)
    if slots > 1:
        row = row ^ (lax.axis_index("freq") * (FG // slots))
    return row == column


def delay_pieces(channel_ref, delay_ref, elements):
    channel_sel = (
        (
            lax.broadcasted_iota(jnp.int32, (delay_ref.shape[0], elements), 0)
            == channel_ref[...]
        )
        .astype(jnp.float32)
        .T.astype(jnp.bfloat16)
    )
    rest = delay_ref[...]
    pieces = []
    for _ in range(3):
        piece = rest.astype(jnp.bfloat16)
        rest = rest - piece.astype(jnp.float32)
        pieces.append(dot(channel_sel, piece, ((1,), (0,))).astype(jnp.bfloat16))
    return pieces


def prepare(freq_total, slots, which, pieces, cells_ref, size_ref, slope_ref, blocks_ref):
    sites = cells_ref.shape[1]
    first_freq = lax.axis_index("freq") * W_DEV
    order = slot_order(slots)
    cells = jnp.where(which == 0, cells_ref[:, :FG], cells_ref[:, FG:])
    cell_sel = lax.broadcasted_iota(jnp.int32, (sites, FG), 0) == cells
    pick = dot(
        order.astype(jnp.bfloat16), cell_sel.astype(jnp.bfloat16), ((1,), (1,))
    ).astype(jnp.bfloat16)
    size = size_ref[pl.ds(which, 1), :]
    turn = size * slope_ref[pl.ds(which, 1), :] * (1.0 / freq_total)
    size = jnp.sum(jnp.where(order, size, 0.0), axis=1, keepdims=True)
    turn = jnp.sum(jnp.where(order, turn, 0.0), axis=1, keepdims=True)
    freq = first_freq + lax.broadcasted_iota(jnp.int32, (FG, FG), 1)
    sine, cosine = sincos_turns(turn * freq.astype(jnp.float32))
    k_real = size * (1.0 + EDGE) * cosine
    k_imag = size * (EDGE - 1.0) * sine
    lane = lax.broadcasted_iota(jnp.int32, (1, ROWS), 1)
    position = lane & (SB - 1)
    for j in range(NB):
        block = blocks_ref[which * NB + j]
        position = position + jnp.where((lane >> 5) == j, block * SB, 0)
    scan_sel = (
        lax.broadcasted_iota(jnp.int32, (pieces[0].shape[1], ROWS), 0) == position
    ).astype(jnp.bfloat16)
    delays = None
    for piece in pieces:
        moved = dot(piece, scan_sel, ((1,), (0,)))
        delays = moved if delays is None else delays + moved
    phase = delays * (0.5 / freq_total)
    step_sin, step_cos = sincos_turns(phase)
    sin, cos = sincos_turns(phase * first_freq.astype(jnp.float32))
    return cos, sin, step_cos, step_sin, pick, k_real, k_imag


def plane(w, k):
    return (w % 2) * W_DEV + (w // 2) * 2 + k


def store_spectra(pick, law_ref, k_real, k_imag, field_ref, wait, out_refs, scratch):
    picked_ref, rows_ref = scratch
    elements, sites = field_ref.shape[2:]
    flaws = pick.shape[0]
    planes = 2 * W_DEV
    for w in range(W_DEV):
        wait(w)
        picked_ref[w] = dot(
            pick, field_ref[w].reshape(2 * elements, sites), ((1,), (1,))
        ).astype(jnp.bfloat16)
    for w in range(W_DEV):
        product = dot(picked_ref[w], law_ref[w], ((1,), (0,)))
        real_part = product[:, :ROWS]
        imag_part = product[:, ROWS:]
        kr = k_real[:, w : w + 1]
        ki = k_imag[:, w : w + 1]
        rows_ref[pl.ds(plane(w, 0), flaws, stride=planes), :] = (
            kr * real_part - ki * imag_part
        )
        rows_ref[pl.ds(plane(w, 1), flaws, stride=planes), :] = (
            kr * imag_part + ki * real_part
        )
    size = flaws // len(out_refs)
    for i, out_ref in enumerate(out_refs):
        out_ref[...] = (
            rows_ref[pl.ds(i * size * planes, size * planes), :]
            .reshape(size, planes, ROWS)
            .astype(jnp.bfloat16)
        )


def far_spectra(values, field_ref, wait, out_ref, kept, scratch):
    cosine, sine, step_cos, step_sin, pick, k_real, k_imag = values
    law_ref, pick_ref, k_real_ref, k_imag_ref = kept
    elements = field_ref.shape[2]
    for w in range(W_DEV):
        c = cosine.astype(jnp.bfloat16)
        s = sine.astype(jnp.bfloat16)
        law_ref[w, :elements, :ROWS] = c
        law_ref[w, :elements, ROWS:] = -s
        law_ref[w, elements:, :ROWS] = s
        law_ref[w, elements:, ROWS:] = c
        if w < W_DEV - 1:
            cosine, sine = (
                cosine * step_cos - sine * step_sin,
                sine * step_cos + cosine * step_sin,
            )
    near = pick_ref.shape[0]
    pick_ref[...] = pick[:near]
    k_real_ref[...] = k_real[:near]
    k_imag_ref[...] = k_imag[:near]
    store_spectra(
        pick[near:],
        law_ref,
        k_real[near:],
        k_imag[near:],
        field_ref,
        wait,
        [out_ref],
        scratch,
    )


def other_far_kernel(freq_total, slots, *refs):
    field_hbm, *small_hbm = refs[:7]
    out_ref, field_ref, cells_ref, size_ref, slope_ref, pieces_ref, *kept = refs[7:17]
    channel_ref, delay_ref, blocks_ref, field_sem, small_sem, *scratch = refs[17:]
    small = (cells_ref, size_ref, slope_ref, channel_ref, delay_ref, blocks_ref)
    copies = [
        pltpu.make_async_copy(source, target, small_sem.at[i])
        for i, (source, target) in enumerate(zip(small_hbm, small))
    ]
    for copy in copies:
        copy.start()
    parts = field_sem.shape[0]
    size = W_DEV // parts
    field_copies = [
        pltpu.make_async_copy(
            field_hbm.at[pl.ds(i * size, size)],
            field_ref.at[pl.ds(i * size, size)],
            field_sem.at[i],
        )
        for i in range(parts)
    ]
    for copy in field_copies:
        copy.start()
    for copy in copies:
        copy.wait()
    pieces = delay_pieces(channel_ref, delay_ref, field_ref.shape[2])
    for i, piece in enumerate(pieces):
        pieces_ref[i] = piece
    other = 1 - lax.axis_index("elem")
    values = prepare(
        freq_total, slots, other, pieces, cells_ref, size_ref, slope_ref, blocks_ref
    )

    def wait(w):
        if w % size == 0:
            field_copies[w // size].wait()

    far_spectra(values, field_ref, wait, out_ref, kept, scratch)


def own_far_kernel(freq_total, slots, field_ref, cells_ref, size_ref, slope_ref, *refs):
    pieces_ref, blocks_ref, out_ref, *refs = refs
    kept, scratch = refs[:4], refs[4:]
    pieces = [pieces_ref[i] for i in range(pieces_ref.shape[0])]
    group = lax.axis_index("elem")
    values = prepare(
        freq_total, slots, group, pieces, cells_ref, size_ref, slope_ref, blocks_ref
    )
    far_spectra(values, field_ref, lambda w: None, out_ref, kept, scratch)


def near_kernel(field_ref, law_ref, pick_ref, k_real_ref, k_imag_ref, _, *refs):
    out_refs, scratch = refs[:-2], refs[-2:]
    store_spectra(
        pick_ref[...],
        law_ref,
        k_real_ref,
        k_imag_ref,
        field_ref,
        lambda w: None,
        out_refs,
        scratch,
    )


def call(kernel, name, in_specs, out_shape, scratch):
    vmem = pl.BlockSpec(memory_space=pltpu.VMEM)
    return pl.pallas_call(
        kernel,
        in_specs=in_specs,
        out_specs=[vmem] * len(out_shape),
        out_shape=out_shape,
        scratch_shapes=scratch,
        compiler_params=pltpu.CompilerParams(vmem_limit_bytes=VMEM_BYTES),
        cost_estimate=pl.CostEstimate(flops=1000, bytes_accessed=1000, transcendentals=0),
        name=name,
    )


def spectra_of(field, small, swap, freq_total, slots):
    elements, sites = field.shape[2:]
    vmem = pl.BlockSpec(memory_space=pltpu.VMEM)
    hbm = pl.BlockSpec(memory_space=pltpu.HBM)
    smem = pl.BlockSpec(memory_space=pltpu.SMEM)
    size = FG // slots
    far = FG // 2
    out = jax.ShapeDtypeStruct((far, 2 * W_DEV, ROWS), jnp.bfloat16)
    near_count = slots // 2 if slots > 1 else 1
    near_out = jax.ShapeDtypeStruct((far // near_count, *out.shape[1:]), jnp.bfloat16)
    work = [
        pltpu.VMEM((W_DEV, far, 2 * elements), jnp.bfloat16),
        pltpu.VMEM((far * 2 * W_DEV, ROWS), jnp.float32),
    ]

    def like(array):
        return jax.ShapeDtypeStruct(array.shape, array.dtype)

    cells, length, slope, channel, delay, blocks = small
    pinned = [pltpu.with_memory_space_constraint(a, pltpu.HBM) for a in (field, *small)]
    pieces = jax.ShapeDtypeStruct((3, elements, delay.shape[1]), jnp.bfloat16)
    kept = [
        jax.ShapeDtypeStruct((W_DEV, 2 * elements, 2 * ROWS), jnp.bfloat16),
        jax.ShapeDtypeStruct((far, sites), jnp.bfloat16),
        jax.ShapeDtypeStruct((far, FG), jnp.float32),
        jax.ShapeDtypeStruct((far, FG), jnp.float32),
    ]
    other, field, cells, length, slope, pieces, *other_kept = call(
        functools.partial(other_far_kernel, freq_total, slots),
        "other_far",
        [hbm] * len(pinned),
        [out, like(field), like(cells), like(length), like(slope), pieces, *kept],
        [
            pltpu.VMEM(channel.shape, channel.dtype),
            pltpu.VMEM(delay.shape, delay.dtype),
            pltpu.SMEM(blocks.shape, blocks.dtype),
            pltpu.SemaphoreType.DMA((4,)),
            pltpu.SemaphoreType.DMA((len(small),)),
            *work,
        ],
    )(*pinned)
    moved = lax.ppermute(other, "elem", swap)
    own, *own_kept = call(
        functools.partial(own_far_kernel, freq_total, slots),
        "own_far",
        [vmem] * 5 + [smem],
        [out, *kept],
        work,
    )(field, cells, length, slope, pieces, blocks)
    far_sums = add(own, moved, [far - size, size] if slots > 1 else [far])
    specs = [vmem] * 5 + [pl.BlockSpec(memory_space=pl.ANY)]
    other, own = (
        call(near_kernel, name, specs, [near_out] * near_count, work)(
            field, *kept, far_sums[-1]
        )
        for name, kept in (("other_near", other_kept), ("own_near", own_kept))
    )
    moved = [lax.ppermute(array, "elem", swap) for array in other]
    return far_sums, add_each(own, moved)


def add_each_kernel(*refs):
    count = len(refs) // 3
    for own_ref, moved_ref, ref in zip(refs, refs[count:], refs[2 * count :]):
        ref[...] = (
            own_ref[...].astype(jnp.float32) + moved_ref[...].astype(jnp.float32)
        ).astype(jnp.bfloat16)


def add_each(own, moved):
    vmem = pl.BlockSpec(memory_space=pltpu.VMEM)
    shapes = [jax.ShapeDtypeStruct(array.shape, array.dtype) for array in own]
    specs = [vmem] * (2 * len(own))
    return call(add_each_kernel, "add_near", specs, shapes, [])(*own, *moved)


def add_kernel(own_ref, moved_ref, *refs):
    first = 0
    for ref in refs:
        rows = pl.ds(first, ref.shape[0])
        first += ref.shape[0]
        ref[...] = (
            own_ref[rows].astype(jnp.float32) + moved_ref[rows].astype(jnp.float32)
        ).astype(jnp.bfloat16)


def add(own, moved, sizes):
    vmem = pl.BlockSpec(memory_space=pltpu.VMEM)
    shapes = [jax.ShapeDtypeStruct((size, *own.shape[1:]), own.dtype) for size in sizes]
    return call(add_kernel, "add_far", [vmem] * 2, shapes, [])(own, moved)


def split_kernel(after, source_ref, last_ref, *refs):
    *refs, out_ref = refs[after:]
    out_ref[...] = last_ref[...]
    for i, ref in enumerate(refs):
        ref[...] = source_ref[pl.ds((i + 1) * ref.shape[0], ref.shape[0])]


def split(array, last, after):
    vmem = pl.BlockSpec(memory_space=pltpu.VMEM)
    shape = jax.ShapeDtypeStruct(last.shape, last.dtype)
    count = array.shape[0] // last.shape[0]
    return call(
        functools.partial(split_kernel, len(after)),
        "split",
        [vmem] * 2 + [pl.BlockSpec(memory_space=pl.ANY)] * len(after),
        [shape] * count,
        [],
    )(array, last, *after)


def table_kernel(freq_total, slots, table_ref):
    height, depth = table_ref.shape[2:]
    time_block = height // 2
    row = lax.broadcasted_iota(jnp.int32, (height, depth // 2), 0)
    column = lax.broadcasted_iota(jnp.int32, (height, depth // 2), 1)
    out_imag = (row >= time_block).astype(jnp.int32)
    time = pl.program_id(0) * time_block + row - out_imag * time_block
    for parity in range(2):
        freq = (column >> 1) * 2 + parity
        if slots > 1:
            freq = freq ^ (lax.axis_index("freq") * W_DEV)
        steps = freq * time + ((column & 1) - out_imag) * (freq_total // 2)
        steps = (steps + 2 * freq_total) & (2 * freq_total - 1)
        _, value = sincos_turns(steps.astype(jnp.float32) * (0.5 / freq_total))
        high = value.astype(jnp.bfloat16)
        table_ref[0, parity, :, : depth // 2] = high
        table_ref[0, parity, :, depth // 2 :] = (
            value - high.astype(jnp.float32)
        ).astype(jnp.bfloat16)


def table(freq_total, slots, times, time_block):
    blocks = times // time_block
    shape = (blocks, 2, 2 * time_block, 2 * freq_total)
    return pl.pallas_call(
        functools.partial(table_kernel, freq_total, slots),
        grid=(blocks,),
        out_specs=pl.BlockSpec((1, *shape[1:]), lambda i: (i, 0, 0, 0)),
        out_shape=jax.ShapeDtypeStruct(shape, jnp.bfloat16),
        compiler_params=pltpu.CompilerParams(vmem_limit_bytes=VMEM_BYTES),
        name="table",
    )()


def peak_kernel(freq_total, folded, sources, *refs):
    count = len(refs) - 5
    table_ref, noise_ref, peak_ref, found_ref, best_ref = refs[count:]
    step = pl.program_id(0)
    columns = peak_ref.shape[1]
    time_block = table_ref.shape[2] // 2

    @pl.when(step == 0)
    def _():
        best_ref[...] = jnp.zeros_like(best_ref)

    width = min(2, columns)
    for first in range(0, columns, width):
        parts = []
        for parity in range(2):
            planes = slice(parity * W_DEV, (parity + 1) * W_DEV)
            spectra = jnp.concatenate(
                [
                    jnp.concatenate(
                        [refs[i][row + first + k, planes, :] for i, row in sources] * 2,
                        axis=0,
                    )
                    for k in range(width)
                ],
                axis=1,
            )
            parts.append(dot(table_ref[0, parity], spectra, ((1,), (0,))))
        powers = []
        for signal in [parts[0] + parts[1]] + [parts[0] - parts[1]] * folded:
            real_part = signal[:time_block]
            imag_part = signal[time_block:]
            powers.append(real_part * real_part + imag_part * imag_part)
        power = jnp.maximum(powers[0], powers[-1]) if folded else powers[0]
        power = jnp.max(power, axis=0, keepdims=True)
        for k in range(width):
            row = pl.ds(first + k, 1)
            best_ref[row, :] = jnp.maximum(
                best_ref[row, :], power[:, k * ROWS : (k + 1) * ROWS]
            )

    @pl.when(step == pl.num_programs(0) - 1)
    def _():
        largest = jnp.max(best_ref[...], axis=1, keepdims=True)
        shape = best_ref.shape
        diagonal = lax.broadcasted_iota(jnp.int32, shape, 0) == lax.broadcasted_iota(
            jnp.int32, shape, 1
        )
        largest = jnp.max(jnp.where(diagonal, largest, 0.0), axis=0, keepdims=True)
        peak = jnp.sqrt(largest[:, :columns]) * (1.0 / math.sqrt(freq_total))
        score = STEEP * (jnp.log(peak + EPS) - jnp.log(noise_ref[...]))
        peak_ref[...] = peak
        found_ref[...] = 1.0 / (1.0 + jnp.exp(-score))


def peaks(spectra, sources, twiddles, noise_level, freq_total, folded):
    columns = noise_level.shape[1]
    out_spec = pl.BlockSpec((1, columns), lambda i: (0, 0))
    return pl.pallas_call(
        functools.partial(peak_kernel, freq_total, folded, sources),
        grid=(twiddles.shape[0],),
        in_specs=[pl.BlockSpec(a.shape, lambda i: (0, 0, 0)) for a in spectra]
        + [pl.BlockSpec((1, *twiddles.shape[1:]), lambda i: (i, 0, 0, 0)), out_spec],
        out_specs=[out_spec, out_spec],
        out_shape=[jax.ShapeDtypeStruct((1, columns), jnp.float32)] * 2,
        scratch_shapes=[pltpu.VMEM((max(8, columns), ROWS), jnp.float32)],
        compiler_params=pltpu.CompilerParams(vmem_limit_bytes=VMEM_BYTES),
        name="peaks",
    )(*spectra, twiddles, noise_level)


def body(
    flaw_cells,
    flaw_blocks,
    element_channel,
    focal_delay,
    beam_field,
    flaw_size,
    flaw_slope,
    noise_level,
):
    freq_count = lax.axis_size("freq")
    freq_total = W_DEV * freq_count
    sample_count = min(T_CAP, 2 * freq_total)
    swap = [(0, 1), (1, 0)]
    slots = freq_count if freq_count in (4, 8) else 1
    small = (
        flaw_cells.reshape(1, -1),
        flaw_size,
        flaw_slope,
        element_channel.reshape(1, -1),
        focal_delay,
        flaw_blocks,
    )
    far, near = spectra_of(beam_field, small, swap, freq_total, slots)
    folded = sample_count == 2 * freq_total
    times = sample_count // 2 if folded else sample_count
    twiddles = table(freq_total, slots, times, min(128, times))
    if slots > 1:

        def send(array, mask):
            pairs = [(a, a ^ mask) for a in range(slots)]
            return lax.ppermute(array, "freq", pairs)

        half = slots // 2
        across = send(far[0], half)
        spectra = [across, *(send(near[s], s) for s in (*range(2, half), 1))]
        *passed, last = split(across, far[1], spectra[1:half])
        sends = {slots - 1: send(last, slots - 1)}
        sends.update({half + 1 + i: send(array, 1 + i) for i, array in enumerate(passed)})
        final = (half + 1, slots - 1, *range(half + 2, slots - 1))
        spectra += [sends[slot] for slot in final]
        spectra.append(near[0])
        operands = [len(spectra) - 1, half - 1, *range(1, half - 1), 0]
        operands += [half + final.index(slot) for slot in range(half + 1, slots)]
        sources = [(i, 0) for i in operands]
    else:
        moved = jnp.concatenate([near[0], far[0]], axis=0)
        moved = lax.all_to_all(moved, "freq", split_axis=0, concat_axis=0, tiled=True)
        spectra = [moved]
        sources = [(0, s * (FG // freq_count)) for s in range(freq_count)]
    return tuple(peaks(spectra, sources, twiddles, noise_level, freq_total, folded))


def solution(mesh):
    in_specs = (
        P("batch"),
        P("batch"),
        P("elem"),
        P(),
        P("freq", None, "elem", None),
        P("batch", None),
        P("batch", None),
        P(("batch", "elem"), "freq"),
    )
    out_specs = (P(("batch", "elem"), "freq"), P(("batch", "elem"), "freq"))
    return jax.shard_map(body, mesh=mesh, in_specs=in_specs, out_specs=out_specs, check_vma=False)
```

```python
import functools
import math

import jax
import jax.numpy as jnp
from jax import lax
from jax.experimental import pallas as pl
from jax.experimental.pallas import tpu as pltpu
from jax.sharding import PartitionSpec as P

W_DEV = 16
W_HALF = W_DEV // 2
FG = 128
NB = 4
SB = 32
T_CAP = 1024

EDGE = 0.6
STEEP = 3.0
EPS = 1e-05

ROWS = NB * SB
VMEM_BYTES = 48 * 1024 * 1024


def sin_half_turn(turns):
    angle = turns * math.pi
    square = angle * angle
    sine = 1.0 / 6227020800.0
    for factorial in (-39916800.0, 362880.0, -5040.0, 120.0, -6.0, 1.0):
        sine = sine * square + 1.0 / factorial
    cosine = 1.0 / 479001600.0
    for factorial in (-3628800.0, 40320.0, -720.0, 24.0, -2.0, 1.0):
        cosine = cosine * square + 1.0 / factorial
    return sine * angle, cosine


def sincos_turns(turns):
    rest = turns - jnp.floor(turns + 0.5)
    sine, cosine = sin_half_turn(rest)
    return 2.0 * sine * cosine, 1.0 - 2.0 * sine * sine


def dot(left, right, contract):
    return lax.dot_general(
        left, right, (contract, ((), ())), preferred_element_type=jnp.float32
    )


def slot_masks(slots):
    half = slots // 2
    between = (2, half, half + 1, 3, slots - 1)
    return (0, 1, *between, slots - 2), (0, slots - 2, *between, 1)


def partner(slots, slot):
    index = lax.axis_index("freq")
    inner = ((index * 2) ^ index) & (slots // 2) != 0
    outer_masks, inner_masks = slot_masks(slots)
    mask = jnp.zeros_like(slot)
    for s in range(1, slots):
        mask = jnp.where(slot == s, jnp.where(inner, inner_masks[s], outer_masks[s]), mask)
    return mask ^ index


def slot_order(slots):
    size = FG // slots
    row = lax.broadcasted_iota(jnp.int32, (FG, 1), 0)
    column = lax.broadcasted_iota(jnp.int32, (FG, FG), 1)
    if slots > 1:
        row = partner(slots, row // size) * size + row % size
    return row == column


def flaw_pick(slots, which, cells_ref):
    cells = jnp.where(which == 0, cells_ref[:, :FG], cells_ref[:, FG:])
    cell_sel = lax.broadcasted_iota(jnp.int32, (cells_ref.shape[1], FG), 0) == cells
    return dot(
        slot_order(slots).astype(jnp.bfloat16), cell_sel.astype(jnp.bfloat16), ((1,), (1,))
    ).astype(jnp.bfloat16)


def delay_pieces(channel_ref, delay_ref, elements):
    channel_sel = (
        (
            lax.broadcasted_iota(jnp.int32, (delay_ref.shape[0], elements), 0)
            == channel_ref[...]
        )
        .astype(jnp.float32)
        .T.astype(jnp.bfloat16)
    )
    rest = delay_ref[...]
    pieces = []
    for _ in range(3):
        piece = rest.astype(jnp.bfloat16)
        rest = rest - piece.astype(jnp.float32)
        pieces.append(dot(channel_sel, piece, ((1,), (0,))).astype(jnp.bfloat16))
    return pieces


def turned(law, step):
    return law[0] * step[0] - law[1] * step[1], law[1] * step[0] + law[0] * step[1]


def prepare(freq_total, slots, which, pieces, size_ref, slope_ref, blocks_ref):
    first_freq = lax.axis_index("freq") * W_DEV
    order = slot_order(slots)
    size = size_ref[pl.ds(which, 1), :]
    turn = size * slope_ref[pl.ds(which, 1), :] * (1.0 / freq_total)
    size = jnp.sum(jnp.where(order, size, 0.0), axis=1, keepdims=True)
    turn = jnp.sum(jnp.where(order, turn, 0.0), axis=1, keepdims=True)
    freq = first_freq + lax.broadcasted_iota(jnp.int32, (FG, FG), 1)
    sine, cosine = sincos_turns(turn * freq.astype(jnp.float32))
    k_real = size * (1.0 + EDGE) * cosine
    k_imag = size * (EDGE - 1.0) * sine
    lane = lax.broadcasted_iota(jnp.int32, (1, ROWS), 1)
    position = lane & (SB - 1)
    for j in range(NB):
        block = blocks_ref[which * NB + j]
        position = position + jnp.where((lane >> 5) == j, block * SB, 0)
    scan_sel = (
        lax.broadcasted_iota(jnp.int32, (pieces[0].shape[1], ROWS), 0) == position
    ).astype(jnp.bfloat16)
    delays = None
    for piece in pieces:
        moved = dot(piece, scan_sel, ((1,), (0,)))
        delays = moved if delays is None else delays + moved
    phase = delays * (0.5 / freq_total)
    unit = sincos_turns(phase)[::-1]
    base = sincos_turns(phase * first_freq.astype(jnp.float32))[::-1]
    return base, turned(unit, unit), turned(base, unit), k_real, k_imag


def store_law(law_ref, law, step):
    elements = law_ref.shape[1] // 2
    for w in range(W_HALF):
        c = law[0].astype(jnp.bfloat16)
        s = law[1].astype(jnp.bfloat16)
        law_ref[w, :elements, :ROWS] = c
        law_ref[w, :elements, ROWS:] = -s
        law_ref[w, elements:, :ROWS] = s
        law_ref[w, elements:, ROWS:] = c
        if w < W_HALF - 1:
            law = turned(law, step)


def pick_fields(parity, picks, field_ref, wait, picked_refs):
    elements, sites = field_ref.shape[3:]
    for w in range(W_HALF):
        wait(w)
        picked = dot(
            picks, field_ref[w, parity].reshape(2 * elements, sites), ((1,), (1,))
        ).astype(jnp.bfloat16)
        for i, ref in enumerate(picked_refs):
            ref[w] = picked[i * FG : (i + 1) * FG]


def store_spectra(parity, picked_ref, law_ref, k_real, k_imag, rows_ref, first, planes):
    for w in range(W_HALF):
        product = dot(picked_ref[w], law_ref[w], ((1,), (0,)))
        real_part = product[:, :ROWS]
        imag_part = product[:, ROWS:]
        kr = k_real[:, 2 * w + parity : 2 * w + parity + 1]
        ki = k_imag[:, 2 * w + parity : 2 * w + parity + 1]
        rows_ref[pl.ds(first + 2 * w, FG, stride=planes), :] = (
            kr * real_part - ki * imag_part
        )
        rows_ref[pl.ds(first + 2 * w + 1, FG, stride=planes), :] = (
            kr * imag_part + ki * real_part
        )


def other_even_kernel(freq_total, slots, *refs):
    field_hbm, *small_hbm = refs[:7]
    out_ref, own_picked_ref, field_ref, size_ref, slope_ref, pieces_ref, *kept = refs[7:20]
    cells_ref, channel_ref, delay_ref, blocks_ref, field_sem, small_sem, *scratch = refs[20:]
    picked_ref, law_ref, rows_ref = scratch
    small = (cells_ref, size_ref, slope_ref, channel_ref, delay_ref, blocks_ref)
    copies = [
        pltpu.make_async_copy(source, target, small_sem.at[i])
        for i, (source, target) in enumerate(zip(small_hbm, small))
    ]
    for copy in copies:
        copy.start()
    part = W_HALF // 2
    field_copies = [
        pltpu.make_async_copy(
            field_hbm.at[pl.ds(i * part, part), parity],
            field_ref.at[pl.ds(i * part, part), parity],
            field_sem.at[parity, i],
        )
        for parity in range(2)
        for i in range(2)
    ]
    for copy in field_copies:
        copy.start()
    for copy in copies:
        copy.wait()
    group = lax.axis_index("elem")
    other = 1 - group
    pieces = delay_pieces(channel_ref, delay_ref, field_ref.shape[3])
    for i, piece in enumerate(pieces):
        pieces_ref[i] = piece
    picks = jnp.concatenate(
        [flaw_pick(slots, which, cells_ref) for which in (other, group)], axis=0
    )
    even, step, odd, k_real, k_imag = prepare(
        freq_total, slots, other, pieces, size_ref, slope_ref, blocks_ref
    )
    for ref, value in zip(kept, (*step, *odd, picks, k_real, k_imag)):
        ref[...] = value
    store_law(law_ref, even, step)

    def wait(w):
        if w % part == 0:
            field_copies[w // part].wait()

    pick_fields(0, picks, field_ref, wait, (picked_ref, own_picked_ref))
    store_spectra(0, picked_ref, law_ref, k_real, k_imag, rows_ref, 0, W_DEV)
    out_ref[...] = rows_ref[...].reshape(out_ref.shape).astype(jnp.bfloat16)
    for copy in field_copies[2:]:
        copy.wait()


def other_odd_kernel(field_ref, *refs):
    step, odd, (picks_ref, k_real_ref, k_imag_ref) = refs[:2], refs[2:4], refs[4:7]
    out_ref, own_picked_ref, picked_ref, law_ref, rows_ref = refs[7:]
    store_law(law_ref, [ref[...] for ref in odd], [ref[...] for ref in step])
    pick_fields(
        1, picks_ref[...], field_ref, lambda w: None, (picked_ref, own_picked_ref)
    )
    store_spectra(1, picked_ref, law_ref, k_real_ref, k_imag_ref, rows_ref, 0, W_DEV)
    out_ref[...] = rows_ref[...].reshape(out_ref.shape).astype(jnp.bfloat16)


def own_kernel(freq_total, slots, *refs):
    *picked_refs, size_ref, slope_ref, pieces_ref, blocks_ref = refs[:6]
    out_ref, law_ref, rows_ref = refs[6:]
    pieces = [pieces_ref[i] for i in range(pieces_ref.shape[0])]
    group = lax.axis_index("elem")
    even, step, odd, k_real, k_imag = prepare(
        freq_total, slots, group, pieces, size_ref, slope_ref, blocks_ref
    )
    for parity, law in enumerate((even, odd)):
        store_law(law_ref.at[parity], law, step)
    for parity in range(2):
        store_spectra(
            parity,
            picked_refs[parity],
            law_ref.at[parity],
            k_real,
            k_imag,
            rows_ref,
            parity * W_DEV,
            2 * W_DEV,
        )
    out_ref[...] = rows_ref[...].reshape(out_ref.shape).astype(jnp.bfloat16)


def call(kernel, name, in_specs, out_shape, scratch):
    vmem = pl.BlockSpec(memory_space=pltpu.VMEM)
    return pl.pallas_call(
        kernel,
        in_specs=in_specs,
        out_specs=[vmem] * len(out_shape),
        out_shape=out_shape,
        scratch_shapes=scratch,
        compiler_params=pltpu.CompilerParams(vmem_limit_bytes=VMEM_BYTES),
        cost_estimate=pl.CostEstimate(flops=1000, bytes_accessed=1000, transcendentals=0),
        name=name,
    )


def partials(field, small, swap, freq_total, slots):
    elements, sites = field.shape[3:]
    vmem = pl.BlockSpec(memory_space=pltpu.VMEM)
    hbm = pl.BlockSpec(memory_space=pltpu.HBM)
    smem = pl.BlockSpec(memory_space=pltpu.SMEM)
    cells, size, slope, channel, delay, blocks = small
    pinned = [pltpu.with_memory_space_constraint(a, pltpu.HBM) for a in (field, *small)]
    out = jax.ShapeDtypeStruct((FG, W_DEV, ROWS), jnp.bfloat16)
    picked = jax.ShapeDtypeStruct((W_HALF, FG, 2 * elements), jnp.bfloat16)
    pieces = jax.ShapeDtypeStruct((3, elements, delay.shape[1]), jnp.bfloat16)
    kept = [jax.ShapeDtypeStruct((elements, ROWS), jnp.float32)] * 4
    kept += [jax.ShapeDtypeStruct((2 * FG, sites), jnp.bfloat16)]
    kept += [jax.ShapeDtypeStruct((FG, FG), jnp.float32)] * 2
    copied = [jax.ShapeDtypeStruct(a.shape, a.dtype) for a in (field, size, slope)]
    law = (W_HALF, 2 * elements, 2 * ROWS)
    work = [
        pltpu.VMEM(picked.shape, picked.dtype),
        pltpu.VMEM(law, jnp.bfloat16),
        pltpu.VMEM((FG * W_DEV, ROWS), jnp.float32),
    ]
    even, even_picked, field, size, slope, pieces, *kept = call(
        functools.partial(other_even_kernel, freq_total, slots),
        "other_even",
        [hbm] * len(pinned),
        [out, picked, *copied, pieces, *kept],
        [
            pltpu.VMEM(cells.shape, cells.dtype),
            pltpu.VMEM(channel.shape, channel.dtype),
            pltpu.VMEM(delay.shape, delay.dtype),
            pltpu.SMEM(blocks.shape, blocks.dtype),
            pltpu.SemaphoreType.DMA((2, 2)),
            pltpu.SemaphoreType.DMA((len(small),)),
            *work,
        ],
    )(*pinned)
    even = lax.ppermute(even, "elem", swap)
    odd, odd_picked = call(
        other_odd_kernel, "other_odd", [vmem] * 8, [out, picked], work
    )(field, *kept)
    odd = lax.ppermute(odd, "elem", swap)
    (own,) = call(
        functools.partial(own_kernel, freq_total, slots),
        "own",
        [vmem] * 5 + [smem],
        [jax.ShapeDtypeStruct((FG, 2 * W_DEV, ROWS), jnp.bfloat16)],
        [
            pltpu.VMEM((2, *law), jnp.bfloat16),
            pltpu.VMEM((FG * 2 * W_DEV, ROWS), jnp.float32),
        ],
    )(even_picked, odd_picked, size, slope, pieces, blocks)
    return own, even, odd


def add_kernel(own_ref, even_ref, odd_ref, *refs):
    size = refs[0].shape[0]
    for slot, ref in enumerate(refs):
        rows = pl.ds(slot * size, size)
        for parity, moved_ref in enumerate((even_ref, odd_ref)):
            planes = slice(parity * W_DEV, (parity + 1) * W_DEV)
            ref[:, planes] = (
                own_ref[rows, planes].astype(jnp.float32)
                + moved_ref[rows].astype(jnp.float32)
            ).astype(jnp.bfloat16)


def add(own, even, odd, slots):
    vmem = pl.BlockSpec(memory_space=pltpu.VMEM)
    shape = jax.ShapeDtypeStruct((FG // slots, *own.shape[1:]), own.dtype)
    return call(add_kernel, "add", [vmem] * 3, [shape] * slots, [])(own, even, odd)


def table_kernel(freq_total, slots, table_ref):
    height, depth = table_ref.shape[2:]
    time_block = height // 2
    row = lax.broadcasted_iota(jnp.int32, (height, depth // 2), 0)
    column = lax.broadcasted_iota(jnp.int32, (height, depth // 2), 1)
    out_imag = (row >= time_block).astype(jnp.int32)
    time = pl.program_id(0) * time_block + row - out_imag * time_block
    for parity in range(2):
        freq = (column >> 1) * 2 + parity
        if slots > 1:
            lane = lax.broadcasted_iota(jnp.int32, (1, depth // 2), 1)
            lane = (lane >> 1) * 2 + parity
            freq = partner(slots, lane // W_DEV) * W_DEV + lane % W_DEV
        steps = freq * time + ((column & 1) - out_imag) * (freq_total // 2)
        steps = (steps + 2 * freq_total) & (2 * freq_total - 1)
        _, value = sincos_turns(steps.astype(jnp.float32) * (0.5 / freq_total))
        high = value.astype(jnp.bfloat16)
        table_ref[0, parity, :, : depth // 2] = high
        table_ref[0, parity, :, depth // 2 :] = (
            value - high.astype(jnp.float32)
        ).astype(jnp.bfloat16)


def table(freq_total, slots, times, time_block):
    blocks = times // time_block
    shape = (blocks, 2, 2 * time_block, 2 * freq_total)
    return pl.pallas_call(
        functools.partial(table_kernel, freq_total, slots),
        grid=(blocks,),
        out_specs=pl.BlockSpec((1, *shape[1:]), lambda i: (i, 0, 0, 0)),
        out_shape=jax.ShapeDtypeStruct(shape, jnp.bfloat16),
        compiler_params=pltpu.CompilerParams(vmem_limit_bytes=VMEM_BYTES),
        name="table",
    )()


def peak_kernel(freq_total, folded, sources, *refs):
    count = len(refs) - 5
    table_ref, noise_ref, peak_ref, found_ref, best_ref = refs[count:]
    step = pl.program_id(0)
    columns = peak_ref.shape[1]
    time_block = table_ref.shape[2] // 2

    @pl.when(step == 0)
    def _():
        best_ref[...] = jnp.zeros_like(best_ref)

    width = min(2, columns)
    for first in range(0, columns, width):
        parts = []
        for parity in range(2):
            planes = slice(parity * W_DEV, (parity + 1) * W_DEV)
            spectra = jnp.concatenate(
                [
                    jnp.concatenate(
                        [
                            refs[i][row + first + k, planes, :]
                            for i, row in sources
                        ]
                        * 2,
                        axis=0,
                    )
                    for k in range(width)
                ],
                axis=1,
            )
            parts.append(dot(table_ref[0, parity], spectra, ((1,), (0,))))
        powers = []
        for signal in [parts[0] + parts[1]] + [parts[0] - parts[1]] * folded:
            real_part = signal[:time_block]
            imag_part = signal[time_block:]
            powers.append(real_part * real_part + imag_part * imag_part)
        power = jnp.maximum(powers[0], powers[-1]) if folded else powers[0]
        power = jnp.max(power, axis=0, keepdims=True)
        for k in range(width):
            row = pl.ds(first + k, 1)
            best_ref[row, :] = jnp.maximum(
                best_ref[row, :], power[:, k * ROWS : (k + 1) * ROWS]
            )

    @pl.when(step == pl.num_programs(0) - 1)
    def _():
        largest = jnp.max(best_ref[...], axis=1, keepdims=True)
        shape = best_ref.shape
        diagonal = lax.broadcasted_iota(jnp.int32, shape, 0) == lax.broadcasted_iota(
            jnp.int32, shape, 1
        )
        largest = jnp.max(jnp.where(diagonal, largest, 0.0), axis=0, keepdims=True)
        peak = jnp.sqrt(largest[:, :columns]) * (1.0 / math.sqrt(freq_total))
        score = STEEP * (jnp.log(peak + EPS) - jnp.log(noise_ref[...]))
        peak_ref[...] = peak
        found_ref[...] = 1.0 / (1.0 + jnp.exp(-score))


def peaks(spectra, sources, twiddles, noise_level, freq_total, folded):
    columns = noise_level.shape[1]
    out_spec = pl.BlockSpec((1, columns), lambda i: (0, 0))
    return pl.pallas_call(
        functools.partial(peak_kernel, freq_total, folded, sources),
        grid=(twiddles.shape[0],),
        in_specs=[pl.BlockSpec(a.shape, lambda i: (0, 0, 0)) for a in spectra]
        + [pl.BlockSpec((1, *twiddles.shape[1:]), lambda i: (i, 0, 0, 0)), out_spec],
        out_specs=[out_spec, out_spec],
        out_shape=[jax.ShapeDtypeStruct((1, columns), jnp.float32)] * 2,
        scratch_shapes=[pltpu.VMEM((max(8, columns), ROWS), jnp.float32)],
        compiler_params=pltpu.CompilerParams(vmem_limit_bytes=VMEM_BYTES),
        name="peaks",
    )(*spectra, twiddles, noise_level)


def body(
    flaw_cells,
    flaw_blocks,
    element_channel,
    focal_delay,
    beam_field,
    flaw_size,
    flaw_slope,
    noise_level,
):
    freq_count = lax.axis_size("freq")
    freq_total = W_DEV * freq_count
    sample_count = min(T_CAP, 2 * freq_total)
    swap = [(0, 1), (1, 0)]
    direct = freq_count == 8
    slots = freq_count if direct else 1
    small = (
        flaw_cells.reshape(1, -1),
        flaw_size,
        flaw_slope,
        element_channel.reshape(1, -1),
        focal_delay,
        flaw_blocks,
    )
    folded = sample_count == 2 * freq_total
    times = sample_count // 2 if folded else sample_count
    twiddles = table(freq_total, slots, times, min(128, times))
    field = beam_field.reshape(W_HALF, 2, *beam_field.shape[1:])
    parts = add(*partials(field, small, swap, freq_total, slots), slots)
    if direct:
        half = slots // 2
        spectra = []
        for slot, masks in enumerate(zip(*slot_masks(slots))):
            pairs = [(a, a ^ masks[((2 * a) ^ a) & half != 0]) for a in range(slots)]
            spectra.append(lax.ppermute(parts[slot], "freq", pairs) if slot else parts[slot])
        spectra = [*spectra[1:], spectra[0]]
        sources = [((slot - 1) % slots, 0) for slot in range(slots)]
    else:
        spectra = [
            lax.all_to_all(parts[0], "freq", split_axis=0, concat_axis=0, tiled=True)
        ]
        sources = [(0, s * (FG // freq_count)) for s in range(freq_count)]
    return tuple(peaks(spectra, sources, twiddles, noise_level, freq_total, folded))


def solution(mesh):
    in_specs = (
        P("batch"),
        P("batch"),
        P("elem"),
        P(),
        P("freq", None, "elem", None),
        P("batch", None),
        P("batch", None),
        P(("batch", "elem"), "freq"),
    )
    out_specs = (P(("batch", "elem"), "freq"), P(("batch", "elem"), "freq"))
    return jax.shard_map(body, mesh=mesh, in_specs=in_specs, out_specs=out_specs, check_vma=False)
```

```python
import functools
import math

import jax
import jax.numpy as jnp
from jax import lax
from jax.experimental import pallas as pl
from jax.experimental.pallas import tpu as pltpu
from jax.sharding import PartitionSpec as P

W_DEV = 16
W_HALF = W_DEV // 2
FG = 128
NB = 4
SB = 32
T_CAP = 1024

EDGE = 0.6
STEEP = 3.0
EPS = 1e-05

ROWS = NB * SB
VMEM_BYTES = 48 * 1024 * 1024


def sin_half_turn(turns):
    angle = turns * math.pi
    square = angle * angle
    sine = 1.0 / 6227020800.0
    for factorial in (-39916800.0, 362880.0, -5040.0, 120.0, -6.0, 1.0):
        sine = sine * square + 1.0 / factorial
    cosine = 1.0 / 479001600.0
    for factorial in (-3628800.0, 40320.0, -720.0, 24.0, -2.0, 1.0):
        cosine = cosine * square + 1.0 / factorial
    return sine * angle, cosine


def sincos_turns(turns):
    rest = turns - jnp.floor(turns + 0.5)
    sine, cosine = sin_half_turn(rest)
    return 2.0 * sine * cosine, 1.0 - 2.0 * sine * sine


def dot(left, right, contract):
    return lax.dot_general(
        left, right, (contract, ((), ())), preferred_element_type=jnp.float32
    )


def slot_masks(slots):
    half = slots // 2
    first, last = (2, half, half + 1), (3, slots - 1)
    return (0, *first, 1, *last, slots - 2), (0, *first, slots - 2, *last, 1)


def partner(slots, slot):
    index = lax.axis_index("freq")
    inner = ((index * 2) ^ index) & (slots // 2) != 0
    outer_masks, inner_masks = slot_masks(slots)
    mask = jnp.zeros_like(slot)
    for s in range(1, slots):
        mask = jnp.where(slot == s, jnp.where(inner, inner_masks[s], outer_masks[s]), mask)
    return mask ^ index


def slot_order(slots):
    size = FG // slots
    row = lax.broadcasted_iota(jnp.int32, (FG, 1), 0)
    column = lax.broadcasted_iota(jnp.int32, (FG, FG), 1)
    if slots > 1:
        row = partner(slots, row // size) * size + row % size
    return row == column


def flaw_pick(slots, which, cells_ref):
    cells = jnp.where(which == 0, cells_ref[:, :FG], cells_ref[:, FG:])
    cell_sel = lax.broadcasted_iota(jnp.int32, (cells_ref.shape[1], FG), 0) == cells
    return dot(
        slot_order(slots).astype(jnp.bfloat16), cell_sel.astype(jnp.bfloat16), ((1,), (1,))
    ).astype(jnp.bfloat16)


def delay_pieces(channel_ref, delay_ref, elements):
    channel_sel = (
        (
            lax.broadcasted_iota(jnp.int32, (delay_ref.shape[0], elements), 0)
            == channel_ref[...]
        )
        .astype(jnp.float32)
        .T.astype(jnp.bfloat16)
    )
    rest = delay_ref[...]
    pieces = []
    for _ in range(3):
        piece = rest.astype(jnp.bfloat16)
        rest = rest - piece.astype(jnp.float32)
        pieces.append(dot(channel_sel, piece, ((1,), (0,))).astype(jnp.bfloat16))
    return pieces


def turned(law, step):
    return law[0] * step[0] - law[1] * step[1], law[1] * step[0] + law[0] * step[1]


def prepare(freq_total, slots, which, pieces, size_ref, slope_ref, blocks_ref):
    first_freq = lax.axis_index("freq") * W_DEV
    order = slot_order(slots)
    size = size_ref[pl.ds(which, 1), :]
    turn = size * slope_ref[pl.ds(which, 1), :] * (1.0 / freq_total)
    size = jnp.sum(jnp.where(order, size, 0.0), axis=1, keepdims=True)
    turn = jnp.sum(jnp.where(order, turn, 0.0), axis=1, keepdims=True)
    freq = first_freq + lax.broadcasted_iota(jnp.int32, (FG, FG), 1)
    sine, cosine = sincos_turns(turn * freq.astype(jnp.float32))
    k_real = size * (1.0 + EDGE) * cosine
    k_imag = size * (EDGE - 1.0) * sine
    lane = lax.broadcasted_iota(jnp.int32, (1, ROWS), 1)
    position = lane & (SB - 1)
    for j in range(NB):
        block = blocks_ref[which * NB + j]
        position = position + jnp.where((lane >> 5) == j, block * SB, 0)
    scan_sel = (
        lax.broadcasted_iota(jnp.int32, (pieces[0].shape[1], ROWS), 0) == position
    ).astype(jnp.bfloat16)
    delays = None
    for piece in pieces:
        moved = dot(piece, scan_sel, ((1,), (0,)))
        delays = moved if delays is None else delays + moved
    phase = delays * (0.5 / freq_total)
    unit = sincos_turns(phase)[::-1]
    base = sincos_turns(phase * first_freq.astype(jnp.float32))[::-1]
    return base, turned(unit, unit), turned(base, unit), k_real, k_imag


def store_law(law_ref, law, step):
    elements = law_ref.shape[1] // 2
    for w in range(W_HALF):
        c = law[0].astype(jnp.bfloat16)
        s = law[1].astype(jnp.bfloat16)
        law_ref[w, :elements, :ROWS] = c
        law_ref[w, :elements, ROWS:] = -s
        law_ref[w, elements:, :ROWS] = s
        law_ref[w, elements:, ROWS:] = c
        if w < W_HALF - 1:
            law = turned(law, step)


def pick_fields(parity, picks, field_ref, wait, picked_refs):
    elements, sites = field_ref.shape[3:]
    for w in range(W_HALF):
        wait(w)
        picked = dot(
            picks, field_ref[w, parity].reshape(2 * elements, sites), ((1,), (1,))
        ).astype(jnp.bfloat16)
        for i, ref in enumerate(picked_refs):
            ref[w] = picked[i * FG : (i + 1) * FG]


def store_spectra(parity, picked_ref, law_ref, k_real, k_imag, out_ref, first):
    for w in range(W_HALF):
        product = dot(picked_ref[w], law_ref[w], ((1,), (0,)))
        real_part = product[:, :ROWS]
        imag_part = product[:, ROWS:]
        kr = k_real[:, 2 * w + parity : 2 * w + parity + 1]
        ki = k_imag[:, 2 * w + parity : 2 * w + parity + 1]
        out_ref[first + 2 * w] = (kr * real_part - ki * imag_part).astype(jnp.bfloat16)
        out_ref[first + 2 * w + 1] = (kr * imag_part + ki * real_part).astype(jnp.bfloat16)


def other_even_kernel(freq_total, slots, *refs):
    field_hbm, *small_hbm = refs[:7]
    out_ref, own_picked_ref, field_ref, size_ref, slope_ref, pieces_ref, *kept = refs[7:20]
    cells_ref, channel_ref, delay_ref, blocks_ref, field_sem, small_sem, *scratch = refs[20:]
    picked_ref, law_ref = scratch
    small = (cells_ref, size_ref, slope_ref, channel_ref, delay_ref, blocks_ref)
    copies = [
        pltpu.make_async_copy(source, target, small_sem.at[i])
        for i, (source, target) in enumerate(zip(small_hbm, small))
    ]
    for copy in copies:
        copy.start()
    part = W_HALF // 2
    field_copies = [
        pltpu.make_async_copy(
            field_hbm.at[pl.ds(i * part, part), parity],
            field_ref.at[pl.ds(i * part, part), parity],
            field_sem.at[parity, i],
        )
        for parity in range(2)
        for i in range(2)
    ]
    for copy in field_copies:
        copy.start()
    for copy in copies:
        copy.wait()
    group = lax.axis_index("elem")
    other = 1 - group
    pieces = delay_pieces(channel_ref, delay_ref, field_ref.shape[3])
    for i, piece in enumerate(pieces):
        pieces_ref[i] = piece
    picks = jnp.concatenate(
        [flaw_pick(slots, which, cells_ref) for which in (other, group)], axis=0
    )
    even, step, odd, k_real, k_imag = prepare(
        freq_total, slots, other, pieces, size_ref, slope_ref, blocks_ref
    )
    for ref, value in zip(kept, (*step, *odd, picks, k_real, k_imag)):
        ref[...] = value
    store_law(law_ref, even, step)

    def wait(w):
        if w % part == 0:
            field_copies[w // part].wait()

    pick_fields(0, picks, field_ref, wait, (picked_ref, own_picked_ref))
    store_spectra(0, picked_ref, law_ref, k_real, k_imag, out_ref, 0)
    for copy in field_copies[2:]:
        copy.wait()


def other_odd_kernel(field_ref, *refs):
    step, odd, (picks_ref, k_real_ref, k_imag_ref) = refs[:2], refs[2:4], refs[4:7]
    out_ref, own_picked_ref, picked_ref, law_ref = refs[7:]
    store_law(law_ref, [ref[...] for ref in odd], [ref[...] for ref in step])
    pick_fields(
        1, picks_ref[...], field_ref, lambda w: None, (picked_ref, own_picked_ref)
    )
    store_spectra(1, picked_ref, law_ref, k_real_ref, k_imag_ref, out_ref, 0)


def own_kernel(freq_total, slots, *refs):
    *picked_refs, size_ref, slope_ref, pieces_ref, blocks_ref = refs[:6]
    out_ref, law_ref = refs[6:]
    pieces = [pieces_ref[i] for i in range(pieces_ref.shape[0])]
    group = lax.axis_index("elem")
    even, step, odd, k_real, k_imag = prepare(
        freq_total, slots, group, pieces, size_ref, slope_ref, blocks_ref
    )
    for parity, law in enumerate((even, odd)):
        store_law(law_ref.at[parity], law, step)
    for parity in range(2):
        store_spectra(
            parity,
            picked_refs[parity],
            law_ref.at[parity],
            k_real,
            k_imag,
            out_ref,
            parity * W_DEV,
        )


def call(kernel, name, in_specs, out_shape, scratch):
    vmem = pl.BlockSpec(memory_space=pltpu.VMEM)
    return pl.pallas_call(
        kernel,
        in_specs=in_specs,
        out_specs=[vmem] * len(out_shape),
        out_shape=out_shape,
        scratch_shapes=scratch,
        compiler_params=pltpu.CompilerParams(vmem_limit_bytes=VMEM_BYTES),
        cost_estimate=pl.CostEstimate(flops=1000, bytes_accessed=1000, transcendentals=0),
        name=name,
    )


def partials(field, small, swap, freq_total, slots):
    elements, sites = field.shape[3:]
    vmem = pl.BlockSpec(memory_space=pltpu.VMEM)
    hbm = pl.BlockSpec(memory_space=pltpu.HBM)
    smem = pl.BlockSpec(memory_space=pltpu.SMEM)
    cells, size, slope, channel, delay, blocks = small
    pinned = [pltpu.with_memory_space_constraint(a, pltpu.HBM) for a in (field, *small)]
    out = jax.ShapeDtypeStruct((W_DEV, FG, ROWS), jnp.bfloat16)
    picked = jax.ShapeDtypeStruct((W_HALF, FG, 2 * elements), jnp.bfloat16)
    pieces = jax.ShapeDtypeStruct((3, elements, delay.shape[1]), jnp.bfloat16)
    kept = [jax.ShapeDtypeStruct((elements, ROWS), jnp.float32)] * 4
    kept += [jax.ShapeDtypeStruct((2 * FG, sites), jnp.bfloat16)]
    kept += [jax.ShapeDtypeStruct((FG, FG), jnp.float32)] * 2
    copied = [jax.ShapeDtypeStruct(a.shape, a.dtype) for a in (field, size, slope)]
    law = (W_HALF, 2 * elements, 2 * ROWS)
    work = [
        pltpu.VMEM(picked.shape, picked.dtype),
        pltpu.VMEM(law, jnp.bfloat16),
    ]
    even, even_picked, field, size, slope, pieces, *kept = call(
        functools.partial(other_even_kernel, freq_total, slots),
        "other_even",
        [hbm] * len(pinned),
        [out, picked, *copied, pieces, *kept],
        [
            pltpu.VMEM(cells.shape, cells.dtype),
            pltpu.VMEM(channel.shape, channel.dtype),
            pltpu.VMEM(delay.shape, delay.dtype),
            pltpu.SMEM(blocks.shape, blocks.dtype),
            pltpu.SemaphoreType.DMA((2, 2)),
            pltpu.SemaphoreType.DMA((len(small),)),
            *work,
        ],
    )(*pinned)
    even = lax.ppermute(even, "elem", swap)
    odd, odd_picked = call(
        other_odd_kernel, "other_odd", [vmem] * 8, [out, picked], work
    )(field, *kept)
    odd = lax.ppermute(odd, "elem", swap)
    (own,) = call(
        functools.partial(own_kernel, freq_total, slots),
        "own",
        [vmem] * 5 + [smem],
        [jax.ShapeDtypeStruct((2 * W_DEV, FG, ROWS), jnp.bfloat16)],
        [pltpu.VMEM((2, *law), jnp.bfloat16)],
    )(even_picked, odd_picked, size, slope, pieces, blocks)
    return own, even, odd


def add_kernel(own_ref, even_ref, odd_ref, *refs):
    size = refs[0].shape[0]
    for slot, ref in enumerate(refs):
        rows = pl.ds(slot * size, size)
        for parity, moved_ref in enumerate((even_ref, odd_ref)):
            planes = slice(parity * W_DEV, (parity + 1) * W_DEV)
            value = own_ref[planes, rows].astype(jnp.float32) + moved_ref[
                :, rows
            ].astype(jnp.float32)
            ref[:, planes] = jnp.swapaxes(value, 0, 1).astype(jnp.bfloat16)


def add(own, even, odd, slots):
    vmem = pl.BlockSpec(memory_space=pltpu.VMEM)
    planes, flaws, rows = own.shape
    shape = jax.ShapeDtypeStruct((flaws // slots, planes, rows), own.dtype)
    return call(add_kernel, "add", [vmem] * 3, [shape] * slots, [])(own, even, odd)


def table_kernel(freq_total, slots, table_ref):
    height, depth = table_ref.shape[2:]
    time_block = height // 2
    row = lax.broadcasted_iota(jnp.int32, (height, depth // 2), 0)
    column = lax.broadcasted_iota(jnp.int32, (height, depth // 2), 1)
    out_imag = (row >= time_block).astype(jnp.int32)
    time = pl.program_id(0) * time_block + row - out_imag * time_block
    for parity in range(2):
        freq = (column >> 1) * 2 + parity
        if slots > 1:
            lane = lax.broadcasted_iota(jnp.int32, (1, depth // 2), 1)
            lane = (lane >> 1) * 2 + parity
            freq = partner(slots, lane // W_DEV) * W_DEV + lane % W_DEV
        steps = freq * time + ((column & 1) - out_imag) * (freq_total // 2)
        steps = (steps + 2 * freq_total) & (2 * freq_total - 1)
        _, value = sincos_turns(steps.astype(jnp.float32) * (0.5 / freq_total))
        high = value.astype(jnp.bfloat16)
        table_ref[0, parity, :, : depth // 2] = high
        table_ref[0, parity, :, depth // 2 :] = (
            value - high.astype(jnp.float32)
        ).astype(jnp.bfloat16)


def table(freq_total, slots, times, time_block):
    blocks = times // time_block
    shape = (blocks, 2, 2 * time_block, 2 * freq_total)
    return pl.pallas_call(
        functools.partial(table_kernel, freq_total, slots),
        grid=(blocks,),
        out_specs=pl.BlockSpec((1, *shape[1:]), lambda i: (i, 0, 0, 0)),
        out_shape=jax.ShapeDtypeStruct(shape, jnp.bfloat16),
        compiler_params=pltpu.CompilerParams(vmem_limit_bytes=VMEM_BYTES),
        name="table",
    )()


def peak_kernel(freq_total, folded, sources, *refs):
    count = len(refs) - 5
    table_ref, noise_ref, peak_ref, found_ref, best_ref = refs[count:]
    step = pl.program_id(0)
    columns = peak_ref.shape[1]
    time_block = table_ref.shape[2] // 2

    @pl.when(step == 0)
    def _():
        best_ref[...] = jnp.zeros_like(best_ref)

    width = min(2, columns)
    for first in range(0, columns, width):
        parts = []
        for parity in range(2):
            planes = slice(parity * W_DEV, (parity + 1) * W_DEV)
            spectra = jnp.concatenate(
                [
                    jnp.concatenate(
                        [
                            refs[i][row + first + k, planes, :]
                            for i, row in sources
                        ]
                        * 2,
                        axis=0,
                    )
                    for k in range(width)
                ],
                axis=1,
            )
            parts.append(dot(table_ref[0, parity], spectra, ((1,), (0,))))
        powers = []
        for signal in [parts[0] + parts[1]] + [parts[0] - parts[1]] * folded:
            real_part = signal[:time_block]
            imag_part = signal[time_block:]
            powers.append(real_part * real_part + imag_part * imag_part)
        power = jnp.maximum(powers[0], powers[-1]) if folded else powers[0]
        power = jnp.max(power, axis=0, keepdims=True)
        for k in range(width):
            row = pl.ds(first + k, 1)
            best_ref[row, :] = jnp.maximum(
                best_ref[row, :], power[:, k * ROWS : (k + 1) * ROWS]
            )

    @pl.when(step == pl.num_programs(0) - 1)
    def _():
        largest = jnp.max(best_ref[...], axis=1, keepdims=True)
        shape = best_ref.shape
        diagonal = lax.broadcasted_iota(jnp.int32, shape, 0) == lax.broadcasted_iota(
            jnp.int32, shape, 1
        )
        largest = jnp.max(jnp.where(diagonal, largest, 0.0), axis=0, keepdims=True)
        peak = jnp.sqrt(largest[:, :columns]) * (1.0 / math.sqrt(freq_total))
        score = STEEP * (jnp.log(peak + EPS) - jnp.log(noise_ref[...]))
        peak_ref[...] = peak
        found_ref[...] = 1.0 / (1.0 + jnp.exp(-score))


def peaks(spectra, sources, twiddles, noise_level, freq_total, folded):
    columns = noise_level.shape[1]
    out_spec = pl.BlockSpec((1, columns), lambda i: (0, 0))
    return pl.pallas_call(
        functools.partial(peak_kernel, freq_total, folded, sources),
        grid=(twiddles.shape[0],),
        in_specs=[pl.BlockSpec(a.shape, lambda i: (0, 0, 0)) for a in spectra]
        + [pl.BlockSpec((1, *twiddles.shape[1:]), lambda i: (i, 0, 0, 0)), out_spec],
        out_specs=[out_spec, out_spec],
        out_shape=[jax.ShapeDtypeStruct((1, columns), jnp.float32)] * 2,
        scratch_shapes=[pltpu.VMEM((max(8, columns), ROWS), jnp.float32)],
        compiler_params=pltpu.CompilerParams(vmem_limit_bytes=VMEM_BYTES),
        name="peaks",
    )(*spectra, twiddles, noise_level)


def body(
    flaw_cells,
    flaw_blocks,
    element_channel,
    focal_delay,
    beam_field,
    flaw_size,
    flaw_slope,
    noise_level,
):
    freq_count = lax.axis_size("freq")
    freq_total = W_DEV * freq_count
    sample_count = min(T_CAP, 2 * freq_total)
    swap = [(0, 1), (1, 0)]
    direct = freq_count == 8
    slots = freq_count if direct else 1
    small = (
        flaw_cells.reshape(1, -1),
        flaw_size,
        flaw_slope,
        element_channel.reshape(1, -1),
        focal_delay,
        flaw_blocks,
    )
    folded = sample_count == 2 * freq_total
    times = sample_count // 2 if folded else sample_count
    twiddles = table(freq_total, slots, times, min(128, times))
    field = beam_field.reshape(W_HALF, 2, *beam_field.shape[1:])
    parts = add(*partials(field, small, swap, freq_total, slots), slots)
    if direct:
        half = slots // 2
        spectra = []
        for slot, masks in enumerate(zip(*slot_masks(slots))):
            pairs = [(a, a ^ masks[((2 * a) ^ a) & half != 0]) for a in range(slots)]
            spectra.append(lax.ppermute(parts[slot], "freq", pairs) if slot else parts[slot])
        spectra = [*spectra[1:], spectra[0]]
        sources = [((slot - 1) % slots, 0) for slot in range(slots)]
    else:
        spectra = [
            lax.all_to_all(parts[0], "freq", split_axis=0, concat_axis=0, tiled=True)
        ]
        sources = [(0, s * (FG // freq_count)) for s in range(freq_count)]
    return tuple(peaks(spectra, sources, twiddles, noise_level, freq_total, folded))


def solution(mesh):
    in_specs = (
        P("batch"),
        P("batch"),
        P("elem"),
        P(),
        P("freq", None, "elem", None),
        P("batch", None),
        P("batch", None),
        P(("batch", "elem"), "freq"),
    )
    out_specs = (P(("batch", "elem"), "freq"), P(("batch", "elem"), "freq"))
    return jax.shard_map(body, mesh=mesh, in_specs=in_specs, out_specs=out_specs, check_vma=False)
```

```python
import functools
import math

import jax
import jax.numpy as jnp
from jax import lax
from jax.experimental import pallas as pl
from jax.experimental.pallas import tpu as pltpu
from jax.sharding import PartitionSpec as P

W_DEV = 16
W_HALF = W_DEV // 2
FG = 128
NB = 4
SB = 32
T_CAP = 1024

EDGE = 0.6
STEEP = 3.0
EPS = 1e-05

ROWS = NB * SB
VMEM_BYTES = 48 * 1024 * 1024


def sin_half_turn(turns):
    angle = turns * math.pi
    square = angle * angle
    sine = 1.0 / 6227020800.0
    for factorial in (-39916800.0, 362880.0, -5040.0, 120.0, -6.0, 1.0):
        sine = sine * square + 1.0 / factorial
    cosine = 1.0 / 479001600.0
    for factorial in (-3628800.0, 40320.0, -720.0, 24.0, -2.0, 1.0):
        cosine = cosine * square + 1.0 / factorial
    return sine * angle, cosine


def sincos_turns(turns):
    rest = turns - jnp.floor(turns + 0.5)
    sine, cosine = sin_half_turn(rest)
    return 2.0 * sine * cosine, 1.0 - 2.0 * sine * sine


def dot(left, right, contract):
    return lax.dot_general(
        left, right, (contract, ((), ())), preferred_element_type=jnp.float32
    )


def slot_masks(slots):
    half = slots // 2
    between = (2, half, half + 1, 3, slots - 1)
    return (0, 1, *between, slots - 2), (0, slots - 2, *between, 1)


def partner(slots, slot):
    index = lax.axis_index("freq")
    inner = ((index * 2) ^ index) & (slots // 2) != 0
    outer_masks, inner_masks = slot_masks(slots)
    mask = jnp.zeros_like(slot)
    for s in range(1, slots):
        mask = jnp.where(slot == s, jnp.where(inner, inner_masks[s], outer_masks[s]), mask)
    return mask ^ index


def slot_order(slots):
    size = FG // slots
    row = lax.broadcasted_iota(jnp.int32, (FG, 1), 0)
    column = lax.broadcasted_iota(jnp.int32, (FG, FG), 1)
    if slots > 1:
        row = partner(slots, row // size) * size + row % size
    return row == column


def flaw_pick(slots, which, cells_ref):
    cells = jnp.where(which == 0, cells_ref[:, :FG], cells_ref[:, FG:])
    cell_sel = lax.broadcasted_iota(jnp.int32, (cells_ref.shape[1], FG), 0) == cells
    return dot(
        slot_order(slots).astype(jnp.bfloat16), cell_sel.astype(jnp.bfloat16), ((1,), (1,))
    ).astype(jnp.bfloat16)


def delays_of(channel_ref, delay_ref, blocks_ref, groups, elements):
    lane = lax.broadcasted_iota(jnp.int32, (1, 2 * ROWS), 1)
    position = lane & (SB - 1)
    for j in range(2 * NB):
        block = blocks_ref[groups[j // NB] * NB + j % NB]
        position = position + jnp.where((lane >> 5) == j, block * SB, 0)
    channels, positions = delay_ref.shape
    scan_sel = (
        lax.broadcasted_iota(jnp.int32, (positions, 2 * ROWS), 0) == position
    ).astype(jnp.bfloat16)
    channel_sel = (
        (lax.broadcasted_iota(jnp.int32, (channels, elements), 0) == channel_ref[...])
        .astype(jnp.float32)
        .T.astype(jnp.bfloat16)
    )
    rest = delay_ref[...]
    pieces = []
    for _ in range(3):
        pieces.append(rest.astype(jnp.bfloat16))
        rest = rest - pieces[-1].astype(jnp.float32)
    moved = dot(jnp.concatenate(pieces, axis=0), scan_sel, ((1,), (0,))).astype(jnp.bfloat16)
    delays = None
    for i in range(3):
        piece = dot(channel_sel, moved[i * channels : (i + 1) * channels], ((1,), (0,)))
        delays = piece if delays is None else delays + piece
    return delays


def turned(law, step):
    return law[0] * step[0] - law[1] * step[1], law[1] * step[0] + law[0] * step[1]


def focal_base(freq_total, delays):
    first_freq = lax.axis_index("freq") * W_DEV
    phase = delays * (0.5 / freq_total)
    unit = sincos_turns(phase)[::-1]
    base = sincos_turns(phase * first_freq.astype(jnp.float32))[::-1]
    return base, turned(unit, unit), turned(base, unit)


def kirchhoff(freq_total, slots, which, size_ref, slope_ref):
    first_freq = lax.axis_index("freq") * W_DEV
    order = slot_order(slots)
    size = size_ref[pl.ds(which, 1), :]
    turn = size * slope_ref[pl.ds(which, 1), :] * (1.0 / freq_total)
    size = jnp.sum(jnp.where(order, size, 0.0), axis=1, keepdims=True)
    turn = jnp.sum(jnp.where(order, turn, 0.0), axis=1, keepdims=True)
    freq = first_freq + lax.broadcasted_iota(jnp.int32, (FG, FG), 1)
    sine, cosine = sincos_turns(turn * freq.astype(jnp.float32))
    return size * (1.0 + EDGE) * cosine, size * (EDGE - 1.0) * sine


def store_law(law_ref, law, step):
    elements = law_ref.shape[1] // 2
    for w in range(W_HALF):
        c = law[0].astype(jnp.bfloat16)
        s = law[1].astype(jnp.bfloat16)
        law_ref[w, :elements, :ROWS] = c
        law_ref[w, :elements, ROWS:] = -s
        law_ref[w, elements:, :ROWS] = s
        law_ref[w, elements:, ROWS:] = c
        if w < W_HALF - 1:
            law = turned(law, step)


def pick_fields(parity, picks, field_ref, wait, picked_refs):
    elements, sites = field_ref.shape[3:]
    for w in range(W_HALF):
        wait(w)
        picked = dot(
            picks, field_ref[w, parity].reshape(2 * elements, sites), ((1,), (1,))
        ).astype(jnp.bfloat16)
        for i, ref in enumerate(picked_refs):
            ref[w] = picked[i * FG : (i + 1) * FG]


def store_spectra(parity, picked_ref, law_ref, k_real, k_imag, out_ref, first):
    for w in range(W_HALF):
        product = dot(picked_ref[w], law_ref[w], ((1,), (0,)))
        real_part = product[:, :ROWS]
        imag_part = product[:, ROWS:]
        kr = k_real[:, 2 * w + parity : 2 * w + parity + 1]
        ki = k_imag[:, 2 * w + parity : 2 * w + parity + 1]
        out_ref[first + 2 * w] = (kr * real_part - ki * imag_part).astype(jnp.bfloat16)
        out_ref[first + 2 * w + 1] = (kr * imag_part + ki * real_part).astype(jnp.bfloat16)


def other_even_kernel(freq_total, slots, *refs):
    field_hbm, *small_hbm = refs[:7]
    out_ref, own_picked_ref, field_ref, *kept = refs[7:25]
    small, (field_sem, small_sem, *scratch) = refs[25:31], refs[31:]
    delay_ref, channel_ref, blocks_ref, cells_ref, size_ref, slope_ref = small
    picked_ref, law_ref = scratch
    copies = [
        pltpu.make_async_copy(source, target, small_sem.at[i])
        for i, (source, target) in enumerate(zip(small_hbm, small))
    ]
    for copy in copies:
        copy.start()
    part = W_HALF // 2
    field_copies = [
        pltpu.make_async_copy(
            field_hbm.at[pl.ds(i * part, part), parity],
            field_ref.at[pl.ds(i * part, part), parity],
            field_sem.at[parity, i],
        )
        for parity in range(2)
        for i in range(2)
    ]
    for copy in field_copies:
        copy.start()
    for copy in copies:
        copy.wait()
    group = lax.axis_index("elem")
    groups = (1 - group, group)
    picks = jnp.concatenate(
        [flaw_pick(slots, which, cells_ref) for which in groups], axis=0
    )
    factors = [
        kirchhoff(freq_total, slots, which, size_ref, slope_ref) for which in groups
    ]
    delays = delays_of(channel_ref, delay_ref, blocks_ref, groups, field_ref.shape[3])
    laws = [
        focal_base(freq_total, delays[:, i * ROWS : (i + 1) * ROWS]) for i in range(2)
    ]
    values = [picks]
    for (even, step, odd), factor in zip(laws, factors):
        values += [*even, *step, *odd, *factor]
    for ref, value in zip(kept, [*values[:1], *values[3:]]):
        ref[...] = value
    even, step, _ = laws[0]
    store_law(law_ref, even, step)

    def wait(w):
        if w % part == 0:
            field_copies[w // part].wait()

    pick_fields(0, picks, field_ref, wait, (picked_ref, own_picked_ref))
    store_spectra(0, picked_ref, law_ref, *factors[0], out_ref, 0)
    for copy in field_copies[2:]:
        copy.wait()


def other_odd_kernel(field_ref, picks_ref, *refs):
    step, odd, k_refs = refs[:2], refs[2:4], refs[4:6]
    out_ref, own_picked_ref, picked_ref, law_ref = refs[6:]
    store_law(law_ref, [ref[...] for ref in odd], [ref[...] for ref in step])
    pick_fields(
        1, picks_ref[...], field_ref, lambda w: None, (picked_ref, own_picked_ref)
    )
    store_spectra(1, picked_ref, law_ref, *k_refs, out_ref, 0)


def own_kernel(*refs):
    picked_refs, refs = refs[:2], refs[2:]
    even, step, odd, k_refs = (refs[2 * i : 2 * i + 2] for i in range(4))
    out_ref, law_ref = refs[8:]
    step = [ref[...] for ref in step]
    for parity, law in enumerate((even, odd)):
        store_law(law_ref.at[parity], [ref[...] for ref in law], step)
    for parity in range(2):
        store_spectra(
            parity, picked_refs[parity], law_ref.at[parity], *k_refs, out_ref, parity * W_DEV
        )


def call(kernel, name, in_specs, out_shape, scratch):
    vmem = pl.BlockSpec(memory_space=pltpu.VMEM)
    return pl.pallas_call(
        kernel,
        in_specs=in_specs,
        out_specs=[vmem] * len(out_shape),
        out_shape=out_shape,
        scratch_shapes=scratch,
        compiler_params=pltpu.CompilerParams(vmem_limit_bytes=VMEM_BYTES),
        cost_estimate=pl.CostEstimate(flops=1000, bytes_accessed=1000, transcendentals=0),
        name=name,
    )


def partials(field, small, swap, freq_total, slots):
    elements, sites = field.shape[3:]
    vmem = pl.BlockSpec(memory_space=pltpu.VMEM)
    hbm = pl.BlockSpec(memory_space=pltpu.HBM)
    pinned = [pltpu.with_memory_space_constraint(a, pltpu.HBM) for a in (field, *small)]
    out = jax.ShapeDtypeStruct((W_DEV, FG, ROWS), jnp.bfloat16)
    picked = jax.ShapeDtypeStruct((W_HALF, FG, 2 * elements), jnp.bfloat16)
    law = (W_HALF, 2 * elements, 2 * ROWS)
    base = [jax.ShapeDtypeStruct((elements, ROWS), jnp.float32)] * 2
    factors = [jax.ShapeDtypeStruct((FG, FG), jnp.float32)] * 2
    kept = [jax.ShapeDtypeStruct((2 * FG, sites), jnp.bfloat16)]
    kept += [*base, *base, *factors, *base, *base, *base, *factors]
    work = [pltpu.VMEM(picked.shape, picked.dtype), pltpu.VMEM(law, jnp.bfloat16)]
    even, even_picked, field, picks, *kept = call(
        functools.partial(other_even_kernel, freq_total, slots),
        "other_even",
        [hbm] * len(pinned),
        [out, picked, jax.ShapeDtypeStruct(field.shape, field.dtype), *kept],
        [
            pltpu.SMEM(a.shape, a.dtype) if a.ndim == 1 else pltpu.VMEM(a.shape, a.dtype)
            for a in small
        ]
        + [pltpu.SemaphoreType.DMA((2, 2)), pltpu.SemaphoreType.DMA((len(small),)), *work],
    )(*pinned)
    even = lax.ppermute(even, "elem", swap)
    odd, odd_picked = call(
        other_odd_kernel, "other_odd", [vmem] * 8, [out, picked], work
    )(field, picks, *kept[:6])
    odd = lax.ppermute(odd, "elem", swap)
    (own,) = call(
        own_kernel,
        "own",
        [vmem] * 10,
        [jax.ShapeDtypeStruct((2 * W_DEV, FG, ROWS), jnp.bfloat16)],
        [pltpu.VMEM((2, *law), jnp.bfloat16)],
    )(even_picked, odd_picked, *kept[6:])
    return own, even, odd


def total(own_ref, moved_ref, parity, rows):
    own = own_ref[parity * W_DEV : (parity + 1) * W_DEV, rows]
    both = own.astype(jnp.float32) + moved_ref[:, rows].astype(jnp.float32)
    return jnp.swapaxes(both, 0, 1).astype(jnp.bfloat16)


def add_even_kernel(size, own_ref, even_ref, held_ref):
    for first in range(0, held_ref.shape[0], size):
        rows = pl.ds(first, size)
        held_ref[rows] = total(own_ref, even_ref, 0, rows)


def add_odd_kernel(own_ref, odd_ref, held_ref, *refs):
    size = refs[0].shape[0]
    for slot, ref in enumerate(refs):
        rows = pl.ds(slot * size, size)
        ref[:, :W_DEV] = held_ref[rows]
        ref[:, W_DEV:] = total(own_ref, odd_ref, 1, rows)


def add(own, even, odd, slots):
    vmem = pl.BlockSpec(memory_space=pltpu.VMEM)
    planes, flaws, rows = own.shape
    size = flaws // slots
    shape = jax.ShapeDtypeStruct((flaws, planes // 2, rows), own.dtype)
    kernel = functools.partial(add_even_kernel, min(size, 16))
    (held,) = call(kernel, "add_even", [vmem] * 2, [shape], [])(own, even)
    shapes = [jax.ShapeDtypeStruct((size, planes, rows), own.dtype)] * slots
    return call(add_odd_kernel, "add_odd", [vmem] * 3, shapes, [])(own, odd, held)


def table_kernel(freq_total, slots, table_ref):
    height, depth = table_ref.shape[2:]
    time_block = height // 2
    row = lax.broadcasted_iota(jnp.int32, (height, depth // 2), 0)
    column = lax.broadcasted_iota(jnp.int32, (height, depth // 2), 1)
    out_imag = (row >= time_block).astype(jnp.int32)
    time = pl.program_id(0) * time_block + row - out_imag * time_block
    for parity in range(2):
        freq = (column >> 1) * 2 + parity
        if slots > 1:
            lane = lax.broadcasted_iota(jnp.int32, (1, depth // 2), 1)
            lane = (lane >> 1) * 2 + parity
            freq = partner(slots, lane // W_DEV) * W_DEV + lane % W_DEV
        steps = freq * time + ((column & 1) - out_imag) * (freq_total // 2)
        steps = (steps + 2 * freq_total) & (2 * freq_total - 1)
        _, value = sincos_turns(steps.astype(jnp.float32) * (0.5 / freq_total))
        high = value.astype(jnp.bfloat16)
        table_ref[0, parity, :, : depth // 2] = high
        table_ref[0, parity, :, depth // 2 :] = (
            value - high.astype(jnp.float32)
        ).astype(jnp.bfloat16)


def table(freq_total, slots, times, time_block):
    blocks = times // time_block
    shape = (blocks, 2, 2 * time_block, 2 * freq_total)
    return pl.pallas_call(
        functools.partial(table_kernel, freq_total, slots),
        grid=(blocks,),
        out_specs=pl.BlockSpec((1, *shape[1:]), lambda i: (i, 0, 0, 0)),
        out_shape=jax.ShapeDtypeStruct(shape, jnp.bfloat16),
        compiler_params=pltpu.CompilerParams(vmem_limit_bytes=VMEM_BYTES),
        name="table",
    )()


def peak_kernel(freq_total, folded, sources, *refs):
    count = len(refs) - 5
    table_ref, noise_ref, peak_ref, found_ref, best_ref = refs[count:]
    step = pl.program_id(0)
    columns = peak_ref.shape[1]
    time_block = table_ref.shape[2] // 2

    @pl.when(step == 0)
    def _():
        best_ref[...] = jnp.zeros_like(best_ref)

    width = min(2, columns)
    for first in range(0, columns, width):
        parts = []
        for parity in range(2):
            planes = slice(parity * W_DEV, (parity + 1) * W_DEV)
            spectra = jnp.concatenate(
                [
                    jnp.concatenate(
                        [
                            refs[i][row + first + k, planes, :]
                            for i, row in sources
                        ]
                        * 2,
                        axis=0,
                    )
                    for k in range(width)
                ],
                axis=1,
            )
            parts.append(dot(table_ref[0, parity], spectra, ((1,), (0,))))
        powers = []
        for signal in [parts[0] + parts[1]] + [parts[0] - parts[1]] * folded:
            real_part = signal[:time_block]
            imag_part = signal[time_block:]
            powers.append(real_part * real_part + imag_part * imag_part)
        power = jnp.maximum(powers[0], powers[-1]) if folded else powers[0]
        power = jnp.max(power, axis=0, keepdims=True)
        for k in range(width):
            row = pl.ds(first + k, 1)
            best_ref[row, :] = jnp.maximum(
                best_ref[row, :], power[:, k * ROWS : (k + 1) * ROWS]
            )

    @pl.when(step == pl.num_programs(0) - 1)
    def _():
        largest = jnp.max(best_ref[...], axis=1, keepdims=True)
        shape = best_ref.shape
        diagonal = lax.broadcasted_iota(jnp.int32, shape, 0) == lax.broadcasted_iota(
            jnp.int32, shape, 1
        )
        largest = jnp.max(jnp.where(diagonal, largest, 0.0), axis=0, keepdims=True)
        peak = jnp.sqrt(largest[:, :columns]) * (1.0 / math.sqrt(freq_total))
        score = STEEP * (jnp.log(peak + EPS) - jnp.log(noise_ref[...]))
        peak_ref[...] = peak
        found_ref[...] = 1.0 / (1.0 + jnp.exp(-score))


def peaks(spectra, sources, twiddles, noise_level, freq_total, folded):
    columns = noise_level.shape[1]
    out_spec = pl.BlockSpec((1, columns), lambda i: (0, 0))
    return pl.pallas_call(
        functools.partial(peak_kernel, freq_total, folded, sources),
        grid=(twiddles.shape[0],),
        in_specs=[pl.BlockSpec(a.shape, lambda i: (0, 0, 0)) for a in spectra]
        + [pl.BlockSpec((1, *twiddles.shape[1:]), lambda i: (i, 0, 0, 0)), out_spec],
        out_specs=[out_spec, out_spec],
        out_shape=[jax.ShapeDtypeStruct((1, columns), jnp.float32)] * 2,
        scratch_shapes=[pltpu.VMEM((max(8, columns), ROWS), jnp.float32)],
        compiler_params=pltpu.CompilerParams(vmem_limit_bytes=VMEM_BYTES),
        name="peaks",
    )(*spectra, twiddles, noise_level)


def body(
    flaw_cells,
    flaw_blocks,
    element_channel,
    focal_delay,
    beam_field,
    flaw_size,
    flaw_slope,
    noise_level,
):
    freq_count = lax.axis_size("freq")
    freq_total = W_DEV * freq_count
    sample_count = min(T_CAP, 2 * freq_total)
    swap = [(0, 1), (1, 0)]
    direct = freq_count == 8
    slots = freq_count if direct else 1
    small = (
        focal_delay,
        element_channel.reshape(1, -1),
        flaw_blocks,
        flaw_cells.reshape(1, -1),
        flaw_size,
        flaw_slope,
    )
    folded = sample_count == 2 * freq_total
    times = sample_count // 2 if folded else sample_count
    twiddles = table(freq_total, slots, times, min(128, times))
    field = beam_field.reshape(W_HALF, 2, *beam_field.shape[1:])
    parts = add(*partials(field, small, swap, freq_total, slots), slots)
    if direct:
        half = slots // 2
        spectra = []
        for slot, masks in enumerate(zip(*slot_masks(slots))):
            pairs = [(a, a ^ masks[((2 * a) ^ a) & half != 0]) for a in range(slots)]
            spectra.append(lax.ppermute(parts[slot], "freq", pairs) if slot else parts[slot])
        spectra = [*spectra[1:], spectra[0]]
        sources = [((slot - 1) % slots, 0) for slot in range(slots)]
    else:
        spectra = [
            lax.all_to_all(parts[0], "freq", split_axis=0, concat_axis=0, tiled=True)
        ]
        sources = [(0, s * (FG // freq_count)) for s in range(freq_count)]
    return tuple(peaks(spectra, sources, twiddles, noise_level, freq_total, folded))


def solution(mesh):
    in_specs = (
        P("batch"),
        P("batch"),
        P("elem"),
        P(),
        P("freq", None, "elem", None),
        P("batch", None),
        P("batch", None),
        P(("batch", "elem"), "freq"),
    )
    out_specs = (P(("batch", "elem"), "freq"), P(("batch", "elem"), "freq"))
    return jax.shard_map(body, mesh=mesh, in_specs=in_specs, out_specs=out_specs, check_vma=False)
```

```python
import functools
import math

import jax
import jax.numpy as jnp
from jax import lax
from jax.experimental import pallas as pl
from jax.experimental.pallas import tpu as pltpu
from jax.sharding import PartitionSpec as P

W_DEV = 16
W_HALF = W_DEV // 2
FG = 128
NB = 4
SB = 32
T_CAP = 1024

EDGE = 0.6
STEEP = 3.0
EPS = 1e-05

ROWS = NB * SB
VMEM_BYTES = 48 * 1024 * 1024


def sin_half_turn(turns):
    angle = turns * math.pi
    square = angle * angle
    sine = 1.0 / 6227020800.0
    for factorial in (-39916800.0, 362880.0, -5040.0, 120.0, -6.0, 1.0):
        sine = sine * square + 1.0 / factorial
    cosine = 1.0 / 479001600.0
    for factorial in (-3628800.0, 40320.0, -720.0, 24.0, -2.0, 1.0):
        cosine = cosine * square + 1.0 / factorial
    return sine * angle, cosine


def sincos_turns(turns):
    rest = turns - jnp.floor(turns + 0.5)
    sine, cosine = sin_half_turn(rest)
    return 2.0 * sine * cosine, 1.0 - 2.0 * sine * sine


def dot(left, right, contract):
    return lax.dot_general(
        left, right, (contract, ((), ())), preferred_element_type=jnp.float32
    )


def slot_masks(slots):
    half = slots // 2
    first, last = (half, half + 1, 2), (3, slots - 1)
    return (0, *first, 1, *last, slots - 2), (0, *first, slots - 2, *last, 1)


def partner(slots, slot):
    index = lax.axis_index("freq")
    inner = ((index * 2) ^ index) & (slots // 2) != 0
    outer_masks, inner_masks = slot_masks(slots)
    mask = jnp.zeros_like(slot)
    for s in range(1, slots):
        mask = jnp.where(slot == s, jnp.where(inner, inner_masks[s], outer_masks[s]), mask)
    return mask ^ index


def slot_order(slots):
    size = FG // slots
    row = lax.broadcasted_iota(jnp.int32, (FG, 1), 0)
    column = lax.broadcasted_iota(jnp.int32, (FG, FG), 1)
    if slots > 1:
        row = partner(slots, row // size) * size + row % size
    return row == column


def flaw_pick(slots, which, cells_ref):
    cells = jnp.where(which == 0, cells_ref[:, :FG], cells_ref[:, FG:])
    cell_sel = lax.broadcasted_iota(jnp.int32, (cells_ref.shape[1], FG), 0) == cells
    return dot(
        slot_order(slots).astype(jnp.bfloat16), cell_sel.astype(jnp.bfloat16), ((1,), (1,))
    ).astype(jnp.bfloat16)


def delays_of(channel_ref, delay_ref, blocks_ref, groups, elements):
    lane = lax.broadcasted_iota(jnp.int32, (1, 2 * ROWS), 1)
    position = lane & (SB - 1)
    for j in range(2 * NB):
        block = blocks_ref[groups[j // NB] * NB + j % NB]
        position = position + jnp.where((lane >> 5) == j, block * SB, 0)
    channels, positions = delay_ref.shape
    scan_sel = (
        lax.broadcasted_iota(jnp.int32, (positions, 2 * ROWS), 0) == position
    ).astype(jnp.bfloat16)
    channel_sel = (
        (lax.broadcasted_iota(jnp.int32, (channels, elements), 0) == channel_ref[...])
        .astype(jnp.float32)
        .T.astype(jnp.bfloat16)
    )
    rest = delay_ref[...]
    pieces = []
    for _ in range(3):
        pieces.append(rest.astype(jnp.bfloat16))
        rest = rest - pieces[-1].astype(jnp.float32)
    moved = dot(jnp.concatenate(pieces, axis=0), scan_sel, ((1,), (0,))).astype(jnp.bfloat16)
    delays = None
    for i in range(3):
        piece = dot(channel_sel, moved[i * channels : (i + 1) * channels], ((1,), (0,)))
        delays = piece if delays is None else delays + piece
    return delays


def turned(law, step):
    return law[0] * step[0] - law[1] * step[1], law[1] * step[0] + law[0] * step[1]


def focal_base(freq_total, delays):
    first_freq = lax.axis_index("freq") * W_DEV
    phase = delays * (0.5 / freq_total)
    unit = sincos_turns(phase)[::-1]
    base = sincos_turns(phase * first_freq.astype(jnp.float32))[::-1]
    return base, turned(unit, unit), turned(base, unit)


def kirchhoff(freq_total, slots, which, size_ref, slope_ref):
    first_freq = lax.axis_index("freq") * W_DEV
    order = slot_order(slots)
    size = size_ref[pl.ds(which, 1), :]
    turn = size * slope_ref[pl.ds(which, 1), :] * (1.0 / freq_total)
    size = jnp.sum(jnp.where(order, size, 0.0), axis=1, keepdims=True)
    turn = jnp.sum(jnp.where(order, turn, 0.0), axis=1, keepdims=True)
    freq = first_freq + lax.broadcasted_iota(jnp.int32, (FG, FG), 1)
    sine, cosine = sincos_turns(turn * freq.astype(jnp.float32))
    return size * (1.0 + EDGE) * cosine, size * (EDGE - 1.0) * sine


def store_law(law_ref, law, step):
    elements = law_ref.shape[1] // 2
    for w in range(W_HALF):
        c = law[0].astype(jnp.bfloat16)
        s = law[1].astype(jnp.bfloat16)
        law_ref[w, :elements, :ROWS] = c
        law_ref[w, :elements, ROWS:] = -s
        law_ref[w, elements:, :ROWS] = s
        law_ref[w, elements:, ROWS:] = c
        if w < W_HALF - 1:
            law = turned(law, step)


def pick_fields(parity, picks, field_ref, wait, picked_refs):
    elements, sites = field_ref.shape[3:]
    for w in range(W_HALF):
        wait(w)
        picked = dot(
            picks, field_ref[w, parity].reshape(2 * elements, sites), ((1,), (1,))
        ).astype(jnp.bfloat16)
        for i, ref in enumerate(picked_refs):
            ref[w] = picked[i * FG : (i + 1) * FG]


def store_spectra(parity, picked_ref, law_ref, k_real, k_imag, out_ref, first):
    for w in range(W_HALF):
        product = dot(picked_ref[w], law_ref[w], ((1,), (0,)))
        real_part = product[:, :ROWS]
        imag_part = product[:, ROWS:]
        kr = k_real[:, 2 * w + parity : 2 * w + parity + 1]
        ki = k_imag[:, 2 * w + parity : 2 * w + parity + 1]
        out_ref[first + 2 * w] = (kr * real_part - ki * imag_part).astype(jnp.bfloat16)
        out_ref[first + 2 * w + 1] = (kr * imag_part + ki * real_part).astype(jnp.bfloat16)


def other_even_kernel(freq_total, slots, *refs):
    field_hbm, *small_hbm = refs[:7]
    out_ref, own_picked_ref, field_ref, *kept = refs[7:25]
    small, (field_sem, small_sem, *scratch) = refs[25:31], refs[31:]
    delay_ref, channel_ref, blocks_ref, cells_ref, size_ref, slope_ref = small
    picked_ref, law_ref = scratch
    copies = [
        pltpu.make_async_copy(source, target, small_sem.at[i])
        for i, (source, target) in enumerate(zip(small_hbm, small))
    ]
    for copy in copies:
        copy.start()
    part = W_HALF // 2
    field_copies = [
        pltpu.make_async_copy(
            field_hbm.at[pl.ds(i * part, part), parity],
            field_ref.at[pl.ds(i * part, part), parity],
            field_sem.at[parity, i],
        )
        for parity in range(2)
        for i in range(2)
    ]
    for copy in field_copies:
        copy.start()
    for copy in copies:
        copy.wait()
    group = lax.axis_index("elem")
    groups = (1 - group, group)
    picks = jnp.concatenate(
        [flaw_pick(slots, which, cells_ref) for which in groups], axis=0
    )
    factors = [
        kirchhoff(freq_total, slots, which, size_ref, slope_ref) for which in groups
    ]
    delays = delays_of(channel_ref, delay_ref, blocks_ref, groups, field_ref.shape[3])
    laws = [
        focal_base(freq_total, delays[:, i * ROWS : (i + 1) * ROWS]) for i in range(2)
    ]
    values = [picks]
    for (even, step, odd), factor in zip(laws, factors):
        values += [*even, *step, *odd, *factor]
    for ref, value in zip(kept, [*values[:1], *values[3:]]):
        ref[...] = value
    even, step, _ = laws[0]
    store_law(law_ref, even, step)

    def wait(w):
        if w % part == 0:
            field_copies[w // part].wait()

    pick_fields(0, picks, field_ref, wait, (picked_ref, own_picked_ref))
    store_spectra(0, picked_ref, law_ref, *factors[0], out_ref, 0)
    for copy in field_copies[2:]:
        copy.wait()


def other_odd_kernel(field_ref, picks_ref, *refs):
    step, odd, k_refs = refs[:2], refs[2:4], refs[4:6]
    out_ref, own_picked_ref, picked_ref, law_ref = refs[6:]
    store_law(law_ref, [ref[...] for ref in odd], [ref[...] for ref in step])
    pick_fields(
        1, picks_ref[...], field_ref, lambda w: None, (picked_ref, own_picked_ref)
    )
    store_spectra(1, picked_ref, law_ref, *k_refs, out_ref, 0)


def own_kernel(parity, picked_ref, *refs):
    law, step, k_refs = (refs[2 * i : 2 * i + 2] for i in range(3))
    out_ref, law_ref = refs[-2:]
    store_law(law_ref, [ref[...] for ref in law], [ref[...] for ref in step])
    store_spectra(parity, picked_ref, law_ref, *k_refs, out_ref, 0)


def call(kernel, name, in_specs, out_shape, scratch):
    vmem = pl.BlockSpec(memory_space=pltpu.VMEM)
    return pl.pallas_call(
        kernel,
        in_specs=in_specs,
        out_specs=[vmem] * len(out_shape),
        out_shape=out_shape,
        scratch_shapes=scratch,
        compiler_params=pltpu.CompilerParams(vmem_limit_bytes=VMEM_BYTES),
        cost_estimate=pl.CostEstimate(flops=1000, bytes_accessed=1000, transcendentals=0),
        name=name,
    )


def partials(field, small, swap, freq_total, slots):
    elements, sites = field.shape[3:]
    vmem = pl.BlockSpec(memory_space=pltpu.VMEM)
    hbm = pl.BlockSpec(memory_space=pltpu.HBM)
    pinned = [pltpu.with_memory_space_constraint(a, pltpu.HBM) for a in (field, *small)]
    out = jax.ShapeDtypeStruct((W_DEV, FG, ROWS), jnp.bfloat16)
    picked = jax.ShapeDtypeStruct((W_HALF, FG, 2 * elements), jnp.bfloat16)
    law = (W_HALF, 2 * elements, 2 * ROWS)
    base = [jax.ShapeDtypeStruct((elements, ROWS), jnp.float32)] * 2
    factors = [jax.ShapeDtypeStruct((FG, FG), jnp.float32)] * 2
    kept = [jax.ShapeDtypeStruct((2 * FG, sites), jnp.bfloat16)]
    kept += [*base, *base, *factors, *base, *base, *base, *factors]
    work = [pltpu.VMEM(picked.shape, picked.dtype), pltpu.VMEM(law, jnp.bfloat16)]
    even, even_picked, field, picks, *kept = call(
        functools.partial(other_even_kernel, freq_total, slots),
        "other_even",
        [hbm] * len(pinned),
        [out, picked, jax.ShapeDtypeStruct(field.shape, field.dtype), *kept],
        [
            pltpu.SMEM(a.shape, a.dtype) if a.ndim == 1 else pltpu.VMEM(a.shape, a.dtype)
            for a in small
        ]
        + [pltpu.SemaphoreType.DMA((2, 2)), pltpu.SemaphoreType.DMA((len(small),)), *work],
    )(*pinned)
    even = lax.ppermute(even, "elem", swap)
    odd, odd_picked = call(
        other_odd_kernel, "other_odd", [vmem] * 8, [out, picked], work
    )(field, picks, *kept[:6])
    odd = lax.ppermute(odd, "elem", swap)
    law_even, step, law_odd, factors = (kept[6 + 2 * i : 8 + 2 * i] for i in range(4))

    def own(parity, *after):
        name, array, base = (
            ("own_even", even_picked, law_even),
            ("own_odd", odd_picked, law_odd),
        )[parity]
        return call(
            functools.partial(own_kernel, parity),
            name,
            [vmem] * 7 + [pl.BlockSpec(memory_space=pl.ANY)] * len(after),
            [out],
            [pltpu.VMEM(law, jnp.bfloat16)],
        )(array, *base, *step, *factors, *after)[0]

    return own, (even, odd)


def total(own_ref, moved_ref, first, size):
    rows = pl.ds(first, size)
    both = own_ref[:, rows].astype(jnp.float32) + moved_ref[:, rows].astype(jnp.float32)
    return jnp.swapaxes(both, 0, 1).astype(jnp.bfloat16)


def add_even_kernel(size, early, own_ref, moved_ref, held_ref, *refs):
    slots = range(own_ref.shape[1] // size)
    for slot, ref in zip(early, refs):
        ref[...] = total(own_ref, moved_ref, slot * size, size)
    for i, slot in enumerate([s for s in slots if s not in early]):
        held_ref[pl.ds(i * size, size)] = total(own_ref, moved_ref, slot * size, size)


def add_even(own, moved, size, early):
    vmem = pl.BlockSpec(memory_space=pltpu.VMEM)
    planes, flaws, rows = own.shape
    shapes = [jax.ShapeDtypeStruct((flaws - size * len(early), planes, rows), own.dtype)]
    shapes += [jax.ShapeDtypeStruct((size, planes, rows), own.dtype)] * len(early)
    return call(
        functools.partial(add_even_kernel, size, early), "add_even", [vmem] * 2, shapes, []
    )(own, moved)


def add_odd_kernel(size, early, late, own_ref, moved_ref, held_ref, *refs):
    held = sorted(late)
    for slot, ref in zip((*early, *late), refs):
        value = total(own_ref, moved_ref, slot * size, size)
        if slot in early:
            ref[...] = value
        else:
            ref[:, :W_DEV] = held_ref[pl.ds(held.index(slot) * size, size)]
            ref[:, W_DEV:] = value


def add_odd(own, moved, held, size, early, late):
    vmem = pl.BlockSpec(memory_space=pltpu.VMEM)
    planes, _, rows = own.shape
    shapes = [
        jax.ShapeDtypeStruct((size, planes * (1 if slot in early else 2), rows), own.dtype)
        for slot in (*early, *late)
    ]
    return call(
        functools.partial(add_odd_kernel, size, early, late), "add_odd", [vmem] * 3, shapes, []
    )(own, moved, held)


def table_kernel(freq_total, slots, table_ref):
    height, depth = table_ref.shape[2:]
    time_block = height // 2
    row = lax.broadcasted_iota(jnp.int32, (height, depth // 2), 0)
    column = lax.broadcasted_iota(jnp.int32, (height, depth // 2), 1)
    out_imag = (row >= time_block).astype(jnp.int32)
    time = pl.program_id(0) * time_block + row - out_imag * time_block
    for parity in range(2):
        freq = (column >> 1) * 2 + parity
        if slots > 1:
            lane = lax.broadcasted_iota(jnp.int32, (1, depth // 2), 1)
            lane = (lane >> 1) * 2 + parity
            freq = partner(slots, lane // W_DEV) * W_DEV + lane % W_DEV
        steps = freq * time + ((column & 1) - out_imag) * (freq_total // 2)
        steps = (steps + 2 * freq_total) & (2 * freq_total - 1)
        _, value = sincos_turns(steps.astype(jnp.float32) * (0.5 / freq_total))
        high = value.astype(jnp.bfloat16)
        table_ref[0, parity, :, : depth // 2] = high
        table_ref[0, parity, :, depth // 2 :] = (
            value - high.astype(jnp.float32)
        ).astype(jnp.bfloat16)


def table(freq_total, slots, times, time_block):
    blocks = times // time_block
    shape = (blocks, 2, 2 * time_block, 2 * freq_total)
    return pl.pallas_call(
        functools.partial(table_kernel, freq_total, slots),
        grid=(blocks,),
        out_specs=pl.BlockSpec((1, *shape[1:]), lambda i: (i, 0, 0, 0)),
        out_shape=jax.ShapeDtypeStruct(shape, jnp.bfloat16),
        compiler_params=pltpu.CompilerParams(vmem_limit_bytes=VMEM_BYTES),
        name="table",
    )()


def peak_kernel(freq_total, folded, sources, *refs):
    count = len(refs) - 5
    table_ref, noise_ref, peak_ref, found_ref, best_ref = refs[count:]
    step = pl.program_id(0)
    columns = peak_ref.shape[1]
    time_block = table_ref.shape[2] // 2

    @pl.when(step == 0)
    def _():
        best_ref[...] = jnp.zeros_like(best_ref)

    width = min(2, columns)
    for first in range(0, columns, width):
        parts = []
        for parity in range(2):
            spectra = jnp.concatenate(
                [
                    jnp.concatenate(
                        [
                            refs[i][row + first + k, plane : plane + W_DEV, :]
                            for i, row, plane in sources[parity]
                        ]
                        * 2,
                        axis=0,
                    )
                    for k in range(width)
                ],
                axis=1,
            )
            parts.append(dot(table_ref[0, parity], spectra, ((1,), (0,))))
        powers = []
        for signal in [parts[0] + parts[1]] + [parts[0] - parts[1]] * folded:
            real_part = signal[:time_block]
            imag_part = signal[time_block:]
            powers.append(real_part * real_part + imag_part * imag_part)
        power = jnp.maximum(powers[0], powers[-1]) if folded else powers[0]
        power = jnp.max(power, axis=0, keepdims=True)
        for k in range(width):
            row = pl.ds(first + k, 1)
            best_ref[row, :] = jnp.maximum(
                best_ref[row, :], power[:, k * ROWS : (k + 1) * ROWS]
            )

    @pl.when(step == pl.num_programs(0) - 1)
    def _():
        largest = jnp.max(best_ref[...], axis=1, keepdims=True)
        shape = best_ref.shape
        diagonal = lax.broadcasted_iota(jnp.int32, shape, 0) == lax.broadcasted_iota(
            jnp.int32, shape, 1
        )
        largest = jnp.max(jnp.where(diagonal, largest, 0.0), axis=0, keepdims=True)
        peak = jnp.sqrt(largest[:, :columns]) * (1.0 / math.sqrt(freq_total))
        score = STEEP * (jnp.log(peak + EPS) - jnp.log(noise_ref[...]))
        peak_ref[...] = peak
        found_ref[...] = 1.0 / (1.0 + jnp.exp(-score))


def peaks(spectra, sources, twiddles, noise_level, freq_total, folded):
    columns = noise_level.shape[1]
    out_spec = pl.BlockSpec((1, columns), lambda i: (0, 0))
    return pl.pallas_call(
        functools.partial(peak_kernel, freq_total, folded, sources),
        grid=(twiddles.shape[0],),
        in_specs=[pl.BlockSpec(a.shape, lambda i: (0, 0, 0)) for a in spectra]
        + [pl.BlockSpec((1, *twiddles.shape[1:]), lambda i: (i, 0, 0, 0)), out_spec],
        out_specs=[out_spec, out_spec],
        out_shape=[jax.ShapeDtypeStruct((1, columns), jnp.float32)] * 2,
        scratch_shapes=[pltpu.VMEM((max(8, columns), ROWS), jnp.float32)],
        compiler_params=pltpu.CompilerParams(vmem_limit_bytes=VMEM_BYTES),
        name="peaks",
    )(*spectra, twiddles, noise_level)


def body(
    flaw_cells,
    flaw_blocks,
    element_channel,
    focal_delay,
    beam_field,
    flaw_size,
    flaw_slope,
    noise_level,
):
    freq_count = lax.axis_size("freq")
    freq_total = W_DEV * freq_count
    sample_count = min(T_CAP, 2 * freq_total)
    swap = [(0, 1), (1, 0)]
    direct = freq_count == 8
    slots = freq_count if direct else 1
    small = (
        focal_delay,
        element_channel.reshape(1, -1),
        flaw_blocks,
        flaw_cells.reshape(1, -1),
        flaw_size,
        flaw_slope,
    )
    folded = sample_count == 2 * freq_total
    times = sample_count // 2 if folded else sample_count
    twiddles = table(freq_total, slots, times, min(128, times))
    field = beam_field.reshape(W_HALF, 2, *beam_field.shape[1:])
    own, moved = partials(field, small, swap, freq_total, slots)
    size = FG // slots
    early = (1, 2) if direct else ()
    late = tuple(slot for slot in range(slots) if slot not in early)
    held, *even = add_even(own(0), moved[0], size, early)
    odd = add_odd(own(1, held), moved[1], held, size, early, late)
    if direct:
        half = slots // 2

        def send(array, slot):
            masks = [masks[slot] for masks in slot_masks(slots)]
            pairs = [(a, a ^ masks[((2 * a) ^ a) & half != 0]) for a in range(slots)]
            return lax.ppermute(array, "freq", pairs) if slot else array

        even = {slot: send(array, slot) for slot, array in zip(early, even)}
        rest = {slot: send(array, slot) for slot, array in zip((*early, *late), odd)}
        order = (4, 3, 6, 5, 7, 1, 2, 0)
        spectra = [*even.values(), *(rest[slot] for slot in order)]
        sources = [
            [
                (early.index(slot), 0, 0)
                if slot in early and parity == 0
                else (len(early) + order.index(slot), 0, 0 if slot in early else plane)
                for slot in range(slots)
            ]
            for parity, plane in enumerate((0, W_DEV))
        ]
    else:
        spectra = [
            lax.all_to_all(odd[0], "freq", split_axis=0, concat_axis=0, tiled=True)
        ]
        columns = FG // freq_count
        sources = [
            [(0, s * columns, plane) for s in range(freq_count)] for plane in (0, W_DEV)
        ]
    return tuple(peaks(spectra, sources, twiddles, noise_level, freq_total, folded))


def solution(mesh):
    in_specs = (
        P("batch"),
        P("batch"),
        P("elem"),
        P(),
        P("freq", None, "elem", None),
        P("batch", None),
        P("batch", None),
        P(("batch", "elem"), "freq"),
    )
    out_specs = (P(("batch", "elem"), "freq"), P(("batch", "elem"), "freq"))
    return jax.shard_map(body, mesh=mesh, in_specs=in_specs, out_specs=out_specs, check_vma=False)
```

```python
import functools
import math

import jax
import jax.numpy as jnp
from jax import lax
from jax.experimental import pallas as pl
from jax.experimental.pallas import tpu as pltpu
from jax.sharding import PartitionSpec as P

W_DEV = 16
W_HALF = W_DEV // 2
FG = 128
NB = 4
SB = 32
T_CAP = 1024

EDGE = 0.6
STEEP = 3.0
EPS = 1e-05

ROWS = NB * SB
VMEM_BYTES = 48 * 1024 * 1024


def sin_half_turn(turns):
    angle = turns * math.pi
    square = angle * angle
    sine = 1.0 / 6227020800.0
    for factorial in (-39916800.0, 362880.0, -5040.0, 120.0, -6.0, 1.0):
        sine = sine * square + 1.0 / factorial
    cosine = 1.0 / 479001600.0
    for factorial in (-3628800.0, 40320.0, -720.0, 24.0, -2.0, 1.0):
        cosine = cosine * square + 1.0 / factorial
    return sine * angle, cosine


def sincos_turns(turns):
    rest = turns - jnp.floor(turns + 0.5)
    sine, cosine = sin_half_turn(rest)
    return 2.0 * sine * cosine, 1.0 - 2.0 * sine * sine


def dot(left, right, contract):
    return lax.dot_general(
        left, right, (contract, ((), ())), preferred_element_type=jnp.float32
    )


def slot_masks(slots):
    half = slots // 2
    between = (half, 2, half + 1, 3)
    return (0, 1, slots - 2, *between, slots - 1), (0, slots - 2, slots - 1, *between, 1)


def partner(slots, slot):
    index = lax.axis_index("freq")
    inner = ((index * 2) ^ index) & (slots // 2) != 0
    outer_masks, inner_masks = slot_masks(slots)
    mask = jnp.zeros_like(slot)
    for s in range(1, slots):
        mask = jnp.where(slot == s, jnp.where(inner, inner_masks[s], outer_masks[s]), mask)
    return mask ^ index


def slot_order(slots):
    size = FG // slots
    row = lax.broadcasted_iota(jnp.int32, (FG, 1), 0)
    column = lax.broadcasted_iota(jnp.int32, (FG, FG), 1)
    if slots > 1:
        row = partner(slots, row // size) * size + row % size
    return row == column


def flaw_pick(slots, which, cells_ref):
    cells = jnp.where(which == 0, cells_ref[:, :FG], cells_ref[:, FG:])
    cell_sel = lax.broadcasted_iota(jnp.int32, (cells_ref.shape[1], FG), 0) == cells
    return dot(
        slot_order(slots).astype(jnp.bfloat16), cell_sel.astype(jnp.bfloat16), ((1,), (1,))
    ).astype(jnp.bfloat16)


def delays_of(channel_ref, delay_ref, blocks_ref, groups, elements):
    lane = lax.broadcasted_iota(jnp.int32, (1, 2 * ROWS), 1)
    position = lane & (SB - 1)
    for j in range(2 * NB):
        block = blocks_ref[groups[j // NB] * NB + j % NB]
        position = position + jnp.where((lane >> 5) == j, block * SB, 0)
    channels, positions = delay_ref.shape
    scan_sel = (
        lax.broadcasted_iota(jnp.int32, (positions, 2 * ROWS), 0) == position
    ).astype(jnp.bfloat16)
    channel_sel = (
        (lax.broadcasted_iota(jnp.int32, (channels, elements), 0) == channel_ref[...])
        .astype(jnp.float32)
        .T.astype(jnp.bfloat16)
    )
    rest = delay_ref[...]
    pieces = []
    for _ in range(3):
        pieces.append(rest.astype(jnp.bfloat16))
        rest = rest - pieces[-1].astype(jnp.float32)
    moved = dot(jnp.concatenate(pieces, axis=0), scan_sel, ((1,), (0,))).astype(jnp.bfloat16)
    delays = None
    for i in range(3):
        piece = dot(channel_sel, moved[i * channels : (i + 1) * channels], ((1,), (0,)))
        delays = piece if delays is None else delays + piece
    return delays


def turned(law, step):
    return law[0] * step[0] - law[1] * step[1], law[1] * step[0] + law[0] * step[1]


def focal_base(freq_total, delays):
    first_freq = lax.axis_index("freq") * W_DEV
    phase = delays * (0.5 / freq_total)
    unit = sincos_turns(phase)[::-1]
    base = sincos_turns(phase * first_freq.astype(jnp.float32))[::-1]
    return base, turned(unit, unit), turned(base, unit)


def kirchhoff(freq_total, slots, which, size_ref, slope_ref):
    first_freq = lax.axis_index("freq") * W_DEV
    order = slot_order(slots)
    size = size_ref[pl.ds(which, 1), :]
    turn = size * slope_ref[pl.ds(which, 1), :] * (1.0 / freq_total)
    size = jnp.sum(jnp.where(order, size, 0.0), axis=1, keepdims=True)
    turn = jnp.sum(jnp.where(order, turn, 0.0), axis=1, keepdims=True)
    freq = first_freq + lax.broadcasted_iota(jnp.int32, (FG, FG), 1)
    sine, cosine = sincos_turns(turn * freq.astype(jnp.float32))
    return size * (1.0 + EDGE) * cosine, size * (EDGE - 1.0) * sine


def store_law(law_ref, law, step):
    elements = law_ref.shape[1] // 2
    for w in range(W_HALF):
        c = law[0].astype(jnp.bfloat16)
        s = law[1].astype(jnp.bfloat16)
        law_ref[w, :elements, :ROWS] = c
        law_ref[w, :elements, ROWS:] = -s
        law_ref[w, elements:, :ROWS] = s
        law_ref[w, elements:, ROWS:] = c
        if w < W_HALF - 1:
            law = turned(law, step)


def pick_fields(parity, picks, field_ref, wait, picked_refs):
    elements, sites = field_ref.shape[3:]
    for w in range(W_HALF):
        wait(w)
        picked = dot(
            picks, field_ref[w, parity].reshape(2 * elements, sites), ((1,), (1,))
        ).astype(jnp.bfloat16)
        for i, ref in enumerate(picked_refs):
            ref[w] = picked[i * FG : (i + 1) * FG]


def store_spectra(parity, picked_ref, law_ref, k_real, k_imag, out_ref, first):
    for w in range(W_HALF):
        product = dot(picked_ref[w], law_ref[w], ((1,), (0,)))
        real_part = product[:, :ROWS]
        imag_part = product[:, ROWS:]
        kr = k_real[:, 2 * w + parity : 2 * w + parity + 1]
        ki = k_imag[:, 2 * w + parity : 2 * w + parity + 1]
        out_ref[first + 2 * w] = (kr * real_part - ki * imag_part).astype(jnp.bfloat16)
        out_ref[first + 2 * w + 1] = (kr * imag_part + ki * real_part).astype(jnp.bfloat16)


def other_even_kernel(freq_total, slots, *refs):
    field_hbm, *small_hbm = refs[:7]
    out_ref, own_picked_ref, field_ref, *kept = refs[7:25]
    small, (field_sem, small_sem, *scratch) = refs[25:31], refs[31:]
    cells_ref, size_ref, slope_ref, channel_ref, blocks_ref, delay_ref = small
    picked_ref, law_ref = scratch
    copies = [
        pltpu.make_async_copy(source, target, small_sem.at[i])
        for i, (source, target) in enumerate(zip(small_hbm, small))
    ]
    for copy in copies:
        copy.start()
    part = W_HALF // 2
    field_copies = [
        pltpu.make_async_copy(
            field_hbm.at[pl.ds(i * part, part), parity],
            field_ref.at[pl.ds(i * part, part), parity],
            field_sem.at[parity, i],
        )
        for parity in range(2)
        for i in range(2)
    ]
    for copy in field_copies:
        copy.start()
    group = lax.axis_index("elem")
    groups = (1 - group, group)
    for copy in copies[:3]:
        copy.wait()
    picks = jnp.concatenate(
        [flaw_pick(slots, which, cells_ref) for which in groups], axis=0
    )
    factors = [
        kirchhoff(freq_total, slots, which, size_ref, slope_ref) for which in groups
    ]
    for copy in copies[3:]:
        copy.wait()
    delays = delays_of(channel_ref, delay_ref, blocks_ref, groups, field_ref.shape[3])
    laws = [
        focal_base(freq_total, delays[:, i * ROWS : (i + 1) * ROWS]) for i in range(2)
    ]
    values = [picks]
    for (even, step, odd), factor in zip(laws, factors):
        values += [*even, *step, *odd, *factor]
    for ref, value in zip(kept, [*values[:1], *values[3:]]):
        ref[...] = value
    even, step, _ = laws[0]
    store_law(law_ref, even, step)

    def wait(w):
        if w % part == 0:
            field_copies[w // part].wait()

    pick_fields(0, picks, field_ref, wait, (picked_ref, own_picked_ref))
    store_spectra(0, picked_ref, law_ref, *factors[0], out_ref, 0)
    for copy in field_copies[2:]:
        copy.wait()


def other_odd_kernel(field_ref, picks_ref, *refs):
    step, odd, k_refs = refs[:2], refs[2:4], refs[4:6]
    out_ref, own_picked_ref, picked_ref, law_ref = refs[6:]
    store_law(law_ref, [ref[...] for ref in odd], [ref[...] for ref in step])
    pick_fields(
        1, picks_ref[...], field_ref, lambda w: None, (picked_ref, own_picked_ref)
    )
    store_spectra(1, picked_ref, law_ref, *k_refs, out_ref, 0)


def own_kernel(*refs):
    picked_refs, refs = refs[:2], refs[2:]
    even, step, odd, k_refs = (refs[2 * i : 2 * i + 2] for i in range(4))
    out_ref, law_ref = refs[8:]
    step = [ref[...] for ref in step]
    for parity, law in enumerate((even, odd)):
        store_law(law_ref.at[parity], [ref[...] for ref in law], step)
    for parity in range(2):
        store_spectra(
            parity, picked_refs[parity], law_ref.at[parity], *k_refs, out_ref, parity * W_DEV
        )


def call(kernel, name, in_specs, out_shape, scratch):
    vmem = pl.BlockSpec(memory_space=pltpu.VMEM)
    return pl.pallas_call(
        kernel,
        in_specs=in_specs,
        out_specs=[vmem] * len(out_shape),
        out_shape=out_shape,
        scratch_shapes=scratch,
        compiler_params=pltpu.CompilerParams(vmem_limit_bytes=VMEM_BYTES),
        cost_estimate=pl.CostEstimate(flops=1000, bytes_accessed=1000, transcendentals=0),
        name=name,
    )


def partials(field, small, swap, freq_total, slots):
    elements, sites = field.shape[3:]
    vmem = pl.BlockSpec(memory_space=pltpu.VMEM)
    hbm = pl.BlockSpec(memory_space=pltpu.HBM)
    pinned = [pltpu.with_memory_space_constraint(a, pltpu.HBM) for a in (field, *small)]
    out = jax.ShapeDtypeStruct((W_DEV, FG, ROWS), jnp.bfloat16)
    picked = jax.ShapeDtypeStruct((W_HALF, FG, 2 * elements), jnp.bfloat16)
    law = (W_HALF, 2 * elements, 2 * ROWS)
    base = [jax.ShapeDtypeStruct((elements, ROWS), jnp.float32)] * 2
    factors = [jax.ShapeDtypeStruct((FG, FG), jnp.float32)] * 2
    kept = [jax.ShapeDtypeStruct((2 * FG, sites), jnp.bfloat16)]
    kept += [*base, *base, *factors, *base, *base, *base, *factors]
    work = [pltpu.VMEM(picked.shape, picked.dtype), pltpu.VMEM(law, jnp.bfloat16)]
    even, even_picked, field, picks, *kept = call(
        functools.partial(other_even_kernel, freq_total, slots),
        "other_even",
        [hbm] * len(pinned),
        [out, picked, jax.ShapeDtypeStruct(field.shape, field.dtype), *kept],
        [
            pltpu.SMEM(a.shape, a.dtype) if a.ndim == 1 else pltpu.VMEM(a.shape, a.dtype)
            for a in small
        ]
        + [pltpu.SemaphoreType.DMA((2, 2)), pltpu.SemaphoreType.DMA((len(small),)), *work],
    )(*pinned)
    even = lax.ppermute(even, "elem", swap)
    odd, odd_picked = call(
        other_odd_kernel, "other_odd", [vmem] * 8, [out, picked], work
    )(field, picks, *kept[:6])
    odd = lax.ppermute(odd, "elem", swap)
    (own,) = call(
        own_kernel,
        "own",
        [vmem] * 10,
        [jax.ShapeDtypeStruct((2 * W_DEV, FG, ROWS), jnp.bfloat16)],
        [pltpu.VMEM((2, *law), jnp.bfloat16)],
    )(even_picked, odd_picked, *kept[6:])
    return own, even, odd


def total(own_ref, moved_ref, parity, rows):
    own = own_ref[parity * W_DEV : (parity + 1) * W_DEV, rows]
    both = own.astype(jnp.float32) + moved_ref[:, rows].astype(jnp.float32)
    return jnp.swapaxes(both, 0, 1).astype(jnp.bfloat16)


def add_even_kernel(size, own_ref, even_ref, held_ref):
    for first in range(0, held_ref.shape[0], size):
        rows = pl.ds(first, size)
        held_ref[rows] = total(own_ref, even_ref, 0, rows)


def add_odd_kernel(own_ref, odd_ref, held_ref, *refs):
    size = refs[0].shape[0]
    for slot, ref in enumerate(refs):
        rows = pl.ds(slot * size, size)
        ref[:, :W_DEV] = held_ref[rows]
        ref[:, W_DEV:] = total(own_ref, odd_ref, 1, rows)


def add(own, even, odd, slots):
    vmem = pl.BlockSpec(memory_space=pltpu.VMEM)
    planes, flaws, rows = own.shape
    size = flaws // slots
    shape = jax.ShapeDtypeStruct((flaws, planes // 2, rows), own.dtype)
    kernel = functools.partial(add_even_kernel, min(size, 16))
    (held,) = call(kernel, "add_even", [vmem] * 2, [shape], [])(own, even)
    shapes = [jax.ShapeDtypeStruct((size, planes, rows), own.dtype)] * slots
    return call(add_odd_kernel, "add_odd", [vmem] * 3, shapes, [])(own, odd, held)


def table_kernel(freq_total, slots, table_ref):
    height, depth = table_ref.shape[2:]
    time_block = height // 2
    row = lax.broadcasted_iota(jnp.int32, (height, depth // 2), 0)
    column = lax.broadcasted_iota(jnp.int32, (height, depth // 2), 1)
    out_imag = (row >= time_block).astype(jnp.int32)
    time = pl.program_id(0) * time_block + row - out_imag * time_block
    for parity in range(2):
        freq = (column >> 1) * 2 + parity
        if slots > 1:
            lane = lax.broadcasted_iota(jnp.int32, (1, depth // 2), 1)
            lane = (lane >> 1) * 2 + parity
            freq = partner(slots, lane // W_DEV) * W_DEV + lane % W_DEV
        steps = freq * time + ((column & 1) - out_imag) * (freq_total // 2)
        steps = (steps + 2 * freq_total) & (2 * freq_total - 1)
        _, value = sincos_turns(steps.astype(jnp.float32) * (0.5 / freq_total))
        high = value.astype(jnp.bfloat16)
        table_ref[0, parity, :, : depth // 2] = high
        table_ref[0, parity, :, depth // 2 :] = (
            value - high.astype(jnp.float32)
        ).astype(jnp.bfloat16)


def table(freq_total, slots, times, time_block):
    blocks = times // time_block
    shape = (blocks, 2, 2 * time_block, 2 * freq_total)
    return pl.pallas_call(
        functools.partial(table_kernel, freq_total, slots),
        grid=(blocks,),
        out_specs=pl.BlockSpec((1, *shape[1:]), lambda i: (i, 0, 0, 0)),
        out_shape=jax.ShapeDtypeStruct(shape, jnp.bfloat16),
        compiler_params=pltpu.CompilerParams(vmem_limit_bytes=VMEM_BYTES),
        name="table",
    )()


def peak_kernel(freq_total, folded, sources, *refs):
    count = len(refs) - 5
    table_ref, noise_ref, peak_ref, found_ref, best_ref = refs[count:]
    step = pl.program_id(0)
    columns = peak_ref.shape[1]
    time_block = table_ref.shape[2] // 2

    @pl.when(step == 0)
    def _():
        best_ref[...] = jnp.zeros_like(best_ref)

    width = min(2, columns)
    for first in range(0, columns, width):
        parts = []
        for parity in range(2):
            planes = slice(parity * W_DEV, (parity + 1) * W_DEV)
            spectra = jnp.concatenate(
                [
                    jnp.concatenate(
                        [
                            refs[i][row + first + k, planes, :]
                            for i, row in sources
                        ]
                        * 2,
                        axis=0,
                    )
                    for k in range(width)
                ],
                axis=1,
            )
            parts.append(dot(table_ref[0, parity], spectra, ((1,), (0,))))
        powers = []
        for signal in [parts[0] + parts[1]] + [parts[0] - parts[1]] * folded:
            real_part = signal[:time_block]
            imag_part = signal[time_block:]
            powers.append(real_part * real_part + imag_part * imag_part)
        power = jnp.maximum(powers[0], powers[-1]) if folded else powers[0]
        power = jnp.max(power, axis=0, keepdims=True)
        for k in range(width):
            row = pl.ds(first + k, 1)
            best_ref[row, :] = jnp.maximum(
                best_ref[row, :], power[:, k * ROWS : (k + 1) * ROWS]
            )

    @pl.when(step == pl.num_programs(0) - 1)
    def _():
        largest = jnp.max(best_ref[...], axis=1, keepdims=True)
        shape = best_ref.shape
        diagonal = lax.broadcasted_iota(jnp.int32, shape, 0) == lax.broadcasted_iota(
            jnp.int32, shape, 1
        )
        largest = jnp.max(jnp.where(diagonal, largest, 0.0), axis=0, keepdims=True)
        peak = jnp.sqrt(largest[:, :columns]) * (1.0 / math.sqrt(freq_total))
        score = STEEP * (jnp.log(peak + EPS) - jnp.log(noise_ref[...]))
        peak_ref[...] = peak
        found_ref[...] = 1.0 / (1.0 + jnp.exp(-score))


def peaks(spectra, sources, twiddles, noise_level, freq_total, folded):
    columns = noise_level.shape[1]
    out_spec = pl.BlockSpec((1, columns), lambda i: (0, 0))
    return pl.pallas_call(
        functools.partial(peak_kernel, freq_total, folded, sources),
        grid=(twiddles.shape[0],),
        in_specs=[pl.BlockSpec(a.shape, lambda i: (0, 0, 0)) for a in spectra]
        + [pl.BlockSpec((1, *twiddles.shape[1:]), lambda i: (i, 0, 0, 0)), out_spec],
        out_specs=[out_spec, out_spec],
        out_shape=[jax.ShapeDtypeStruct((1, columns), jnp.float32)] * 2,
        scratch_shapes=[pltpu.VMEM((max(8, columns), ROWS), jnp.float32)],
        compiler_params=pltpu.CompilerParams(vmem_limit_bytes=VMEM_BYTES),
        name="peaks",
    )(*spectra, twiddles, noise_level)


def body(
    flaw_cells,
    flaw_blocks,
    element_channel,
    focal_delay,
    beam_field,
    flaw_size,
    flaw_slope,
    noise_level,
):
    freq_count = lax.axis_size("freq")
    freq_total = W_DEV * freq_count
    sample_count = min(T_CAP, 2 * freq_total)
    swap = [(0, 1), (1, 0)]
    direct = freq_count == 8
    slots = freq_count if direct else 1
    small = (
        flaw_cells.reshape(1, -1),
        flaw_size,
        flaw_slope,
        element_channel.reshape(1, -1),
        flaw_blocks,
        focal_delay,
    )
    folded = sample_count == 2 * freq_total
    times = sample_count // 2 if folded else sample_count
    twiddles = table(freq_total, slots, times, min(128, times))
    field = beam_field.reshape(W_HALF, 2, *beam_field.shape[1:])
    parts = add(*partials(field, small, swap, freq_total, slots), slots)
    if direct:
        half = slots // 2
        spectra = []
        for slot, masks in enumerate(zip(*slot_masks(slots))):
            pairs = [(a, a ^ masks[((2 * a) ^ a) & half != 0]) for a in range(slots)]
            spectra.append(lax.ppermute(parts[slot], "freq", pairs) if slot else parts[slot])
        spectra = [*spectra[1:], spectra[0]]
        sources = [((slot - 1) % slots, 0) for slot in range(slots)]
    else:
        spectra = [
            lax.all_to_all(parts[0], "freq", split_axis=0, concat_axis=0, tiled=True)
        ]
        sources = [(0, s * (FG // freq_count)) for s in range(freq_count)]
    return tuple(peaks(spectra, sources, twiddles, noise_level, freq_total, folded))


def solution(mesh):
    in_specs = (
        P("batch"),
        P("batch"),
        P("elem"),
        P(),
        P("freq", None, "elem", None),
        P("batch", None),
        P("batch", None),
        P(("batch", "elem"), "freq"),
    )
    out_specs = (P(("batch", "elem"), "freq"), P(("batch", "elem"), "freq"))
    return jax.shard_map(body, mesh=mesh, in_specs=in_specs, out_specs=out_specs, check_vma=False)
```

```python
import functools
import math

import jax
import jax.numpy as jnp
from jax import lax
from jax.experimental import pallas as pl
from jax.experimental.pallas import tpu as pltpu
from jax.sharding import PartitionSpec as P

W_DEV = 16
W_HALF = W_DEV // 2
FG = 128
NB = 4
SB = 32
T_CAP = 1024

EDGE = 0.6
STEEP = 3.0
EPS = 1e-05

ROWS = NB * SB
VMEM_BYTES = 48 * 1024 * 1024


def sin_half_turn(turns):
    angle = turns * math.pi
    square = angle * angle
    sine = 1.0 / 6227020800.0
    for factorial in (-39916800.0, 362880.0, -5040.0, 120.0, -6.0, 1.0):
        sine = sine * square + 1.0 / factorial
    cosine = 1.0 / 479001600.0
    for factorial in (-3628800.0, 40320.0, -720.0, 24.0, -2.0, 1.0):
        cosine = cosine * square + 1.0 / factorial
    return sine * angle, cosine


def sincos_turns(turns):
    rest = turns - jnp.floor(turns + 0.5)
    sine, cosine = sin_half_turn(rest)
    return 2.0 * sine * cosine, 1.0 - 2.0 * sine * sine


def dot(left, right, contract):
    return lax.dot_general(
        left, right, (contract, ((), ())), preferred_element_type=jnp.float32
    )


def slot_masks(slots):
    half = slots // 2
    between = (2, half, half + 1, 3, slots - 1)
    return (0, 1, *between, slots - 2), (0, slots - 2, *between, 1)


def partner(slots, slot):
    index = lax.axis_index("freq")
    inner = ((index * 2) ^ index) & (slots // 2) != 0
    outer_masks, inner_masks = slot_masks(slots)
    mask = jnp.zeros_like(slot)
    for s in range(1, slots):
        mask = jnp.where(slot == s, jnp.where(inner, inner_masks[s], outer_masks[s]), mask)
    return mask ^ index


def slot_order(slots):
    size = FG // slots
    row = lax.broadcasted_iota(jnp.int32, (FG, 1), 0)
    column = lax.broadcasted_iota(jnp.int32, (FG, FG), 1)
    if slots > 1:
        row = partner(slots, row // size) * size + row % size
    return row == column


def flaw_pick(slots, which, cells_ref):
    cells = jnp.where(which == 0, cells_ref[:, :FG], cells_ref[:, FG:])
    cell_sel = lax.broadcasted_iota(jnp.int32, (cells_ref.shape[1], FG), 0) == cells
    return dot(
        slot_order(slots).astype(jnp.bfloat16), cell_sel.astype(jnp.bfloat16), ((1,), (1,))
    ).astype(jnp.bfloat16)


def delays_of(channel_ref, delay_ref, blocks_ref, groups, elements):
    lane = lax.broadcasted_iota(jnp.int32, (1, 2 * ROWS), 1)
    position = lane & (SB - 1)
    for j in range(2 * NB):
        block = blocks_ref[groups[j // NB] * NB + j % NB]
        position = position + jnp.where((lane >> 5) == j, block * SB, 0)
    channels, positions = delay_ref.shape
    scan_sel = (
        lax.broadcasted_iota(jnp.int32, (positions, 2 * ROWS), 0) == position
    ).astype(jnp.bfloat16)
    channel_sel = (
        (lax.broadcasted_iota(jnp.int32, (channels, elements), 0) == channel_ref[...])
        .astype(jnp.float32)
        .T.astype(jnp.bfloat16)
    )
    rest = delay_ref[...]
    pieces = []
    for _ in range(3):
        pieces.append(rest.astype(jnp.bfloat16))
        rest = rest - pieces[-1].astype(jnp.float32)
    moved = dot(jnp.concatenate(pieces, axis=0), scan_sel, ((1,), (0,))).astype(jnp.bfloat16)
    delays = None
    for i in range(3):
        piece = dot(channel_sel, moved[i * channels : (i + 1) * channels], ((1,), (0,)))
        delays = piece if delays is None else delays + piece
    return delays


def turned(law, step):
    return law[0] * step[0] - law[1] * step[1], law[1] * step[0] + law[0] * step[1]


def focal_base(freq_total, delays):
    first_freq = lax.axis_index("freq") * W_DEV
    phase = delays * (0.5 / freq_total)
    unit = sincos_turns(phase)[::-1]
    base = sincos_turns(phase * first_freq.astype(jnp.float32))[::-1]
    return base, turned(unit, unit), turned(base, unit)


def kirchhoff(freq_total, slots, which, size_ref, slope_ref):
    first_freq = lax.axis_index("freq") * W_DEV
    order = slot_order(slots)
    size = size_ref[pl.ds(which, 1), :]
    turn = size * slope_ref[pl.ds(which, 1), :] * (1.0 / freq_total)
    size = jnp.sum(jnp.where(order, size, 0.0), axis=1, keepdims=True)
    turn = jnp.sum(jnp.where(order, turn, 0.0), axis=1, keepdims=True)
    freq = first_freq + lax.broadcasted_iota(jnp.int32, (FG, FG), 1)
    sine, cosine = sincos_turns(turn * freq.astype(jnp.float32))
    return size * (1.0 + EDGE) * cosine, size * (EDGE - 1.0) * sine


def store_law(law_ref, law, step):
    elements = law_ref.shape[1] // 2
    for w in range(W_HALF):
        c = law[0].astype(jnp.bfloat16)
        s = law[1].astype(jnp.bfloat16)
        law_ref[w, :elements, :ROWS] = c
        law_ref[w, :elements, ROWS:] = -s
        law_ref[w, elements:, :ROWS] = s
        law_ref[w, elements:, ROWS:] = c
        if w < W_HALF - 1:
            law = turned(law, step)


def pick_fields(parity, picks, field_ref, wait, picked_refs):
    elements, sites = field_ref.shape[3:]
    for w in range(W_HALF):
        wait(w)
        picked = dot(
            picks, field_ref[w, parity].reshape(2 * elements, sites), ((1,), (1,))
        ).astype(jnp.bfloat16)
        for i, ref in enumerate(picked_refs):
            ref[w] = picked[i * FG : (i + 1) * FG]


def store_spectra(parity, picked_ref, law_ref, k_real, k_imag, out_ref, first):
    for w in range(W_HALF):
        product = dot(picked_ref[w], law_ref[w], ((1,), (0,)))
        real_part = product[:, :ROWS]
        imag_part = product[:, ROWS:]
        kr = k_real[:, 2 * w + parity : 2 * w + parity + 1]
        ki = k_imag[:, 2 * w + parity : 2 * w + parity + 1]
        out_ref[first + 2 * w] = (kr * real_part - ki * imag_part).astype(jnp.bfloat16)
        out_ref[first + 2 * w + 1] = (kr * imag_part + ki * real_part).astype(jnp.bfloat16)


def other_even_kernel(freq_total, slots, *refs):
    field_hbm, *small_hbm = refs[:7]
    out_ref, own_picked_ref, field_ref, *kept = refs[7:25]
    small, (field_sem, small_sem, *scratch) = refs[25:31], refs[31:]
    delay_ref, channel_ref, blocks_ref, cells_ref, size_ref, slope_ref = small
    picked_ref, law_ref = scratch
    copies = [
        pltpu.make_async_copy(source, target, small_sem.at[i])
        for i, (source, target) in enumerate(zip(small_hbm, small))
    ]
    for copy in copies:
        copy.start()
    part = W_HALF // 2
    field_copies = [
        pltpu.make_async_copy(
            field_hbm.at[pl.ds(i * part, part), parity],
            field_ref.at[pl.ds(i * part, part), parity],
            field_sem.at[parity, i],
        )
        for parity in range(2)
        for i in range(2)
    ]
    for copy in field_copies:
        copy.start()
    for copy in copies:
        copy.wait()
    group = lax.axis_index("elem")
    groups = (1 - group, group)
    picks = jnp.concatenate(
        [flaw_pick(slots, which, cells_ref) for which in groups], axis=0
    )
    factors = [
        kirchhoff(freq_total, slots, which, size_ref, slope_ref) for which in groups
    ]
    delays = delays_of(channel_ref, delay_ref, blocks_ref, groups, field_ref.shape[3])
    laws = [
        focal_base(freq_total, delays[:, i * ROWS : (i + 1) * ROWS]) for i in range(2)
    ]
    values = [picks]
    for (even, step, odd), factor in zip(laws, factors):
        values += [*even, *step, *odd, *factor]
    for ref, value in zip(kept, [*values[:1], *values[3:]]):
        ref[...] = value
    even, step, _ = laws[0]
    store_law(law_ref, even, step)

    def wait(w):
        if w % part == 0:
            field_copies[w // part].wait()

    pick_fields(0, picks, field_ref, wait, (picked_ref, own_picked_ref))
    store_spectra(0, picked_ref, law_ref, *factors[0], out_ref, 0)
    for copy in field_copies[2:]:
        copy.wait()


def other_odd_kernel(field_ref, picks_ref, *refs):
    step, odd, k_refs = refs[:2], refs[2:4], refs[4:6]
    out_ref, own_picked_ref, picked_ref, law_ref = refs[6:]
    store_law(law_ref, [ref[...] for ref in odd], [ref[...] for ref in step])
    pick_fields(
        1, picks_ref[...], field_ref, lambda w: None, (picked_ref, own_picked_ref)
    )
    store_spectra(1, picked_ref, law_ref, *k_refs, out_ref, 0)


def own_kernel(*refs):
    picked_refs, refs = refs[:2], refs[2:]
    even, step, odd, k_refs = (refs[2 * i : 2 * i + 2] for i in range(4))
    out_ref, law_ref = refs[8:]
    step = [ref[...] for ref in step]
    for parity, law in enumerate((even, odd)):
        store_law(law_ref.at[parity], [ref[...] for ref in law], step)
    for parity in range(2):
        store_spectra(
            parity, picked_refs[parity], law_ref.at[parity], *k_refs, out_ref, parity * W_DEV
        )


def call(kernel, name, in_specs, out_shape, scratch):
    vmem = pl.BlockSpec(memory_space=pltpu.VMEM)
    return pl.pallas_call(
        kernel,
        in_specs=in_specs,
        out_specs=[vmem] * len(out_shape),
        out_shape=out_shape,
        scratch_shapes=scratch,
        compiler_params=pltpu.CompilerParams(vmem_limit_bytes=VMEM_BYTES),
        cost_estimate=pl.CostEstimate(flops=1000, bytes_accessed=1000, transcendentals=0),
        name=name,
    )


def partials(field, small, swap, freq_total, slots):
    elements, sites = field.shape[3:]
    vmem = pl.BlockSpec(memory_space=pltpu.VMEM)
    hbm = pl.BlockSpec(memory_space=pltpu.HBM)
    pinned = [pltpu.with_memory_space_constraint(a, pltpu.HBM) for a in (field, *small)]
    out = jax.ShapeDtypeStruct((W_DEV, FG, ROWS), jnp.bfloat16)
    picked = jax.ShapeDtypeStruct((W_HALF, FG, 2 * elements), jnp.bfloat16)
    law = (W_HALF, 2 * elements, 2 * ROWS)
    base = [jax.ShapeDtypeStruct((elements, ROWS), jnp.float32)] * 2
    factors = [jax.ShapeDtypeStruct((FG, FG), jnp.float32)] * 2
    kept = [jax.ShapeDtypeStruct((2 * FG, sites), jnp.bfloat16)]
    kept += [*base, *base, *factors, *base, *base, *base, *factors]
    work = [pltpu.VMEM(picked.shape, picked.dtype), pltpu.VMEM(law, jnp.bfloat16)]
    even, even_picked, field, picks, *kept = call(
        functools.partial(other_even_kernel, freq_total, slots),
        "other_even",
        [hbm] * len(pinned),
        [out, picked, jax.ShapeDtypeStruct(field.shape, field.dtype), *kept],
        [
            pltpu.SMEM(a.shape, a.dtype) if a.ndim == 1 else pltpu.VMEM(a.shape, a.dtype)
            for a in small
        ]
        + [pltpu.SemaphoreType.DMA((2, 2)), pltpu.SemaphoreType.DMA((len(small),)), *work],
    )(*pinned)
    even = lax.ppermute(even, "elem", swap)
    odd, odd_picked = call(
        other_odd_kernel, "other_odd", [vmem] * 8, [out, picked], work
    )(field, picks, *kept[:6])
    odd = lax.ppermute(odd, "elem", swap)
    (own,) = call(
        own_kernel,
        "own",
        [vmem] * 10,
        [jax.ShapeDtypeStruct((2 * W_DEV, FG, ROWS), jnp.bfloat16)],
        [pltpu.VMEM((2, *law), jnp.bfloat16)],
    )(even_picked, odd_picked, *kept[6:])
    return own, even, odd


def total(own_ref, moved_ref, parity, rows):
    own = own_ref[parity * W_DEV : (parity + 1) * W_DEV, rows]
    both = own.astype(jnp.float32) + moved_ref[:, rows].astype(jnp.float32)
    return jnp.swapaxes(both, 0, 1).astype(jnp.bfloat16)


def add_even_kernel(size, own_ref, even_ref, held_ref):
    for first in range(0, held_ref.shape[0], size):
        rows = pl.ds(first, size)
        held_ref[rows] = total(own_ref, even_ref, 0, rows)


def add_odd_kernel(own_ref, odd_ref, held_ref, *refs):
    size = refs[0].shape[0]
    for slot, ref in enumerate(refs):
        rows = pl.ds(slot * size, size)
        ref[:, :W_DEV] = held_ref[rows]
        ref[:, W_DEV:] = total(own_ref, odd_ref, 1, rows)


def add(own, even, odd, slots):
    vmem = pl.BlockSpec(memory_space=pltpu.VMEM)
    planes, flaws, rows = own.shape
    size = flaws // slots
    shape = jax.ShapeDtypeStruct((flaws, planes // 2, rows), own.dtype)
    kernel = functools.partial(add_even_kernel, min(size, 16))
    (held,) = call(kernel, "add_even", [vmem] * 2, [shape], [])(own, even)
    shapes = [jax.ShapeDtypeStruct((size, planes, rows), own.dtype)] * slots
    return call(add_odd_kernel, "add_odd", [vmem] * 3, shapes, [])(own, odd, held)


def table_kernel(freq_total, slots, table_ref):
    height, depth = table_ref.shape[2:]
    time_block = height // 2
    row = lax.broadcasted_iota(jnp.int32, (height, depth // 2), 0)
    column = lax.broadcasted_iota(jnp.int32, (height, depth // 2), 1)
    out_imag = (row >= time_block).astype(jnp.int32)
    time = pl.program_id(0) * time_block + row - out_imag * time_block
    for parity in range(2):
        freq = (column >> 1) * 2 + parity
        if slots > 1:
            lane = lax.broadcasted_iota(jnp.int32, (1, depth // 2), 1)
            lane = (lane >> 1) * 2 + parity
            freq = partner(slots, lane // W_DEV) * W_DEV + lane % W_DEV
        steps = freq * time + ((column & 1) - out_imag) * (freq_total // 2)
        steps = (steps + 2 * freq_total) & (2 * freq_total - 1)
        _, value = sincos_turns(steps.astype(jnp.float32) * (0.5 / freq_total))
        high = value.astype(jnp.bfloat16)
        table_ref[0, parity, :, : depth // 2] = high
        table_ref[0, parity, :, depth // 2 :] = (
            value - high.astype(jnp.float32)
        ).astype(jnp.bfloat16)


def table(freq_total, slots, times, time_block):
    blocks = times // time_block
    shape = (blocks, 2, 2 * time_block, 2 * freq_total)
    return pl.pallas_call(
        functools.partial(table_kernel, freq_total, slots),
        grid=(blocks,),
        out_specs=pl.BlockSpec((1, *shape[1:]), lambda i: (i, 0, 0, 0)),
        out_shape=jax.ShapeDtypeStruct(shape, jnp.bfloat16),
        compiler_params=pltpu.CompilerParams(vmem_limit_bytes=VMEM_BYTES),
        name="table",
    )()


def peak_kernel(freq_total, folded, sources, blocks, *refs):
    def first_step():
        return blocks == 1 or pl.program_id(0) == 0

    def last_step():
        return blocks == 1 or pl.program_id(0) == blocks - 1

    count = len(refs) - 5
    table_ref, noise_ref, peak_ref, found_ref, best_ref = refs[count:]
    columns = peak_ref.shape[1]
    time_block = table_ref.shape[2] // 2

    @pl.when(first_step())
    def _():
        best_ref[...] = jnp.zeros_like(best_ref)

    width = min(2, columns)
    for first in range(0, columns, width):
        parts = []
        for parity in range(2):
            planes = slice(parity * W_DEV, (parity + 1) * W_DEV)
            spectra = jnp.concatenate(
                [
                    jnp.concatenate(
                        [
                            refs[i][row + first + k, planes, :]
                            for i, row in sources
                        ]
                        * 2,
                        axis=0,
                    )
                    for k in range(width)
                ],
                axis=1,
            )
            parts.append(dot(table_ref[0, parity], spectra, ((1,), (0,))))
        powers = []
        for signal in [parts[0] + parts[1]] + [parts[0] - parts[1]] * folded:
            real_part = signal[:time_block]
            imag_part = signal[time_block:]
            powers.append(real_part * real_part + imag_part * imag_part)
        power = jnp.maximum(powers[0], powers[-1]) if folded else powers[0]
        power = jnp.max(power, axis=0, keepdims=True)
        for k in range(width):
            row = pl.ds(first + k, 1)
            best_ref[row, :] = jnp.maximum(
                best_ref[row, :], power[:, k * ROWS : (k + 1) * ROWS]
            )

    @pl.when(last_step())
    def _():
        largest = jnp.max(best_ref[...], axis=1, keepdims=True)
        shape = best_ref.shape
        diagonal = lax.broadcasted_iota(jnp.int32, shape, 0) == lax.broadcasted_iota(
            jnp.int32, shape, 1
        )
        largest = jnp.max(jnp.where(diagonal, largest, 0.0), axis=0, keepdims=True)
        peak = jnp.sqrt(largest[:, :columns]) * (1.0 / math.sqrt(freq_total))
        score = STEEP * (jnp.log(peak + EPS) - jnp.log(noise_ref[...]))
        peak_ref[...] = peak
        found_ref[...] = 1.0 / (1.0 + jnp.exp(-score))


def peaks(spectra, sources, twiddles, noise_level, freq_total, folded):
    columns = noise_level.shape[1]
    blocks = twiddles.shape[0]
    if blocks == 1:
        vmem = pl.BlockSpec(memory_space=pltpu.VMEM)
        grid, in_specs, out_spec = (), [vmem] * (len(spectra) + 2), vmem
    else:
        grid = (blocks,)
        out_spec = pl.BlockSpec((1, columns), lambda i: (0, 0))
        in_specs = [pl.BlockSpec(a.shape, lambda i: (0, 0, 0)) for a in spectra]
        in_specs += [
            pl.BlockSpec((1, *twiddles.shape[1:]), lambda i: (i, 0, 0, 0)),
            out_spec,
        ]
    return pl.pallas_call(
        functools.partial(peak_kernel, freq_total, folded, sources, blocks),
        grid=grid,
        in_specs=in_specs,
        out_specs=[out_spec, out_spec],
        out_shape=[jax.ShapeDtypeStruct((1, columns), jnp.float32)] * 2,
        scratch_shapes=[pltpu.VMEM((max(8, columns), ROWS), jnp.float32)],
        compiler_params=pltpu.CompilerParams(vmem_limit_bytes=VMEM_BYTES),
        name="peaks",
    )(*spectra, twiddles, noise_level)


def body(
    flaw_cells,
    flaw_blocks,
    element_channel,
    focal_delay,
    beam_field,
    flaw_size,
    flaw_slope,
    noise_level,
):
    freq_count = lax.axis_size("freq")
    freq_total = W_DEV * freq_count
    sample_count = min(T_CAP, 2 * freq_total)
    swap = [(0, 1), (1, 0)]
    direct = freq_count == 8
    slots = freq_count if direct else 1
    small = (
        focal_delay,
        element_channel.reshape(1, -1),
        flaw_blocks,
        flaw_cells.reshape(1, -1),
        flaw_size,
        flaw_slope,
    )
    folded = sample_count == 2 * freq_total
    times = sample_count // 2 if folded else sample_count
    twiddles = table(freq_total, slots, times, min(128, times))
    field = beam_field.reshape(W_HALF, 2, *beam_field.shape[1:])
    parts = add(*partials(field, small, swap, freq_total, slots), slots)
    if direct:
        half = slots // 2
        spectra = []
        for slot, masks in enumerate(zip(*slot_masks(slots))):
            pairs = [(a, a ^ masks[((2 * a) ^ a) & half != 0]) for a in range(slots)]
            spectra.append(lax.ppermute(parts[slot], "freq", pairs) if slot else parts[slot])
        spectra = [*spectra[1:], spectra[0]]
        sources = [((slot - 1) % slots, 0) for slot in range(slots)]
    else:
        spectra = [
            lax.all_to_all(parts[0], "freq", split_axis=0, concat_axis=0, tiled=True)
        ]
        sources = [(0, s * (FG // freq_count)) for s in range(freq_count)]
    return tuple(peaks(spectra, sources, twiddles, noise_level, freq_total, folded))


def solution(mesh):
    in_specs = (
        P("batch"),
        P("batch"),
        P("elem"),
        P(),
        P("freq", None, "elem", None),
        P("batch", None),
        P("batch", None),
        P(("batch", "elem"), "freq"),
    )
    out_specs = (P(("batch", "elem"), "freq"), P(("batch", "elem"), "freq"))
    return jax.shard_map(body, mesh=mesh, in_specs=in_specs, out_specs=out_specs, check_vma=False)
```

```python
import functools
import math

import jax
import jax.numpy as jnp
from jax import lax
from jax.experimental import pallas as pl
from jax.experimental.pallas import tpu as pltpu
from jax.sharding import PartitionSpec as P

W_DEV = 16
W_HALF = W_DEV // 2
FG = 128
NB = 4
SB = 32
T_CAP = 1024
TIME_BLOCK = 128

EDGE = 0.6
STEEP = 3.0
EPS = 1e-05

ROWS = NB * SB
VMEM_BYTES = 48 * 1024 * 1024


def sin_half_turn(turns):
    angle = turns * math.pi
    square = angle * angle
    sine = 1.0 / 6227020800.0
    for factorial in (-39916800.0, 362880.0, -5040.0, 120.0, -6.0, 1.0):
        sine = sine * square + 1.0 / factorial
    cosine = 1.0 / 479001600.0
    for factorial in (-3628800.0, 40320.0, -720.0, 24.0, -2.0, 1.0):
        cosine = cosine * square + 1.0 / factorial
    return sine * angle, cosine


def sincos_turns(turns):
    rest = turns - jnp.floor(turns + 0.5)
    sine, cosine = sin_half_turn(rest)
    return 2.0 * sine * cosine, 1.0 - 2.0 * sine * sine


def dot(left, right, contract):
    return lax.dot_general(
        left, right, (contract, ((), ())), preferred_element_type=jnp.float32
    )


def slot_masks(slots):
    half = slots // 2
    between = (2, half, half + 1, 3, slots - 1)
    return (0, 1, *between, slots - 2), (0, slots - 2, *between, 1)


def partner(slots, slot):
    index = lax.axis_index("freq")
    inner = ((index * 2) ^ index) & (slots // 2) != 0
    outer_masks, inner_masks = slot_masks(slots)
    mask = jnp.zeros_like(slot)
    for s in range(1, slots):
        mask = jnp.where(slot == s, jnp.where(inner, inner_masks[s], outer_masks[s]), mask)
    return mask ^ index


def slot_order(slots):
    size = FG // slots
    row = lax.broadcasted_iota(jnp.int32, (FG, 1), 0)
    column = lax.broadcasted_iota(jnp.int32, (FG, FG), 1)
    if slots > 1:
        row = partner(slots, row // size) * size + row % size
    return row == column


def flaw_pick(slots, which, cells_ref):
    cells = jnp.where(which == 0, cells_ref[:, :FG], cells_ref[:, FG:])
    cell_sel = lax.broadcasted_iota(jnp.int32, (cells_ref.shape[1], FG), 0) == cells
    return dot(
        slot_order(slots).astype(jnp.bfloat16), cell_sel.astype(jnp.bfloat16), ((1,), (1,))
    ).astype(jnp.bfloat16)


def delays_of(channel_ref, delay_ref, blocks_ref, groups, elements):
    lane = lax.broadcasted_iota(jnp.int32, (1, 2 * ROWS), 1)
    position = lane & (SB - 1)
    for j in range(2 * NB):
        block = blocks_ref[groups[j // NB] * NB + j % NB]
        position = position + jnp.where((lane >> 5) == j, block * SB, 0)
    channels, positions = delay_ref.shape
    scan_sel = (
        lax.broadcasted_iota(jnp.int32, (positions, 2 * ROWS), 0) == position
    ).astype(jnp.bfloat16)
    channel_sel = (
        (lax.broadcasted_iota(jnp.int32, (channels, elements), 0) == channel_ref[...])
        .astype(jnp.float32)
        .T.astype(jnp.bfloat16)
    )
    rest = delay_ref[...]
    pieces = []
    for _ in range(3):
        pieces.append(rest.astype(jnp.bfloat16))
        rest = rest - pieces[-1].astype(jnp.float32)
    moved = dot(jnp.concatenate(pieces, axis=0), scan_sel, ((1,), (0,))).astype(jnp.bfloat16)
    delays = None
    for i in range(3):
        piece = dot(channel_sel, moved[i * channels : (i + 1) * channels], ((1,), (0,)))
        delays = piece if delays is None else delays + piece
    return delays


def turned(law, step):
    return law[0] * step[0] - law[1] * step[1], law[1] * step[0] + law[0] * step[1]


def focal_base(freq_total, delays):
    first_freq = lax.axis_index("freq") * W_DEV
    phase = delays * (0.5 / freq_total)
    unit = sincos_turns(phase)[::-1]
    base = sincos_turns(phase * first_freq.astype(jnp.float32))[::-1]
    return base, turned(unit, unit), turned(base, unit)


def kirchhoff(freq_total, slots, which, size_ref, slope_ref):
    first_freq = lax.axis_index("freq") * W_DEV
    order = slot_order(slots)
    size = size_ref[pl.ds(which, 1), :]
    turn = size * slope_ref[pl.ds(which, 1), :] * (1.0 / freq_total)
    size = jnp.sum(jnp.where(order, size, 0.0), axis=1, keepdims=True)
    turn = jnp.sum(jnp.where(order, turn, 0.0), axis=1, keepdims=True)
    freq = first_freq + lax.broadcasted_iota(jnp.int32, (FG, FG), 1)
    sine, cosine = sincos_turns(turn * freq.astype(jnp.float32))
    return size * (1.0 + EDGE) * cosine, size * (EDGE - 1.0) * sine


def store_law(law_ref, law, step):
    elements = law_ref.shape[1] // 2
    for w in range(W_HALF):
        c = law[0].astype(jnp.bfloat16)
        s = law[1].astype(jnp.bfloat16)
        law_ref[w, :elements, :ROWS] = c
        law_ref[w, :elements, ROWS:] = -s
        law_ref[w, elements:, :ROWS] = s
        law_ref[w, elements:, ROWS:] = c
        if w < W_HALF - 1:
            law = turned(law, step)


def pick_fields(parity, picks, field_ref, wait, picked_refs):
    elements, sites = field_ref.shape[3:]
    for w in range(W_HALF):
        wait(w)
        picked = dot(
            picks, field_ref[w, parity].reshape(2 * elements, sites), ((1,), (1,))
        ).astype(jnp.bfloat16)
        for i, ref in enumerate(picked_refs):
            ref[w] = picked[i * FG : (i + 1) * FG]


def store_spectra(parity, picked_ref, law_ref, k_real, k_imag, out_ref, first):
    for w in range(W_HALF):
        product = dot(picked_ref[w], law_ref[w], ((1,), (0,)))
        real_part = product[:, :ROWS]
        imag_part = product[:, ROWS:]
        kr = k_real[:, 2 * w + parity : 2 * w + parity + 1]
        ki = k_imag[:, 2 * w + parity : 2 * w + parity + 1]
        out_ref[first + 2 * w] = (kr * real_part - ki * imag_part).astype(jnp.bfloat16)
        out_ref[first + 2 * w + 1] = (kr * imag_part + ki * real_part).astype(jnp.bfloat16)


def other_even_kernel(freq_total, slots, *refs):
    field_hbm, *small_hbm = refs[:7]
    out_ref, own_picked_ref, field_ref, size_ref, slope_ref, *kept = refs[7:20]
    delay_ref, channel_ref, blocks_ref, cells_ref = refs[20:24]
    field_sem, small_sem, *scratch = refs[24:]
    small = (delay_ref, channel_ref, blocks_ref, cells_ref, size_ref, slope_ref)
    picked_ref, law_ref = scratch
    copies = [
        pltpu.make_async_copy(source, target, small_sem.at[i])
        for i, (source, target) in enumerate(zip(small_hbm, small))
    ]
    for copy in copies:
        copy.start()
    part = W_HALF // 2
    field_copies = [
        pltpu.make_async_copy(
            field_hbm.at[pl.ds(i * part, part), parity],
            field_ref.at[pl.ds(i * part, part), parity],
            field_sem.at[parity, i],
        )
        for parity in range(2)
        for i in range(2)
    ]
    for copy in field_copies:
        copy.start()
    for copy in copies:
        copy.wait()
    group = lax.axis_index("elem")
    groups = (1 - group, group)
    picks = jnp.concatenate(
        [flaw_pick(slots, which, cells_ref) for which in groups], axis=0
    )
    factors = kirchhoff(freq_total, slots, groups[0], size_ref, slope_ref)
    delays = delays_of(channel_ref, delay_ref, blocks_ref, groups, field_ref.shape[3])
    even, step, odd = focal_base(freq_total, delays[:, :ROWS])
    values = (picks, *step, *odd, *factors, delays[:, ROWS:])
    for ref, value in zip(kept, values):
        ref[...] = value
    store_law(law_ref, even, step)

    def wait(w):
        if w % part == 0:
            field_copies[w // part].wait()

    pick_fields(0, picks, field_ref, wait, (picked_ref, own_picked_ref))
    store_spectra(0, picked_ref, law_ref, *factors, out_ref, 0)
    for copy in field_copies[2:]:
        copy.wait()


def other_odd_kernel(field_ref, picks_ref, *refs):
    step, odd, k_refs = refs[:2], refs[2:4], refs[4:6]
    out_ref, own_picked_ref, picked_ref, law_ref = refs[6:]
    store_law(law_ref, [ref[...] for ref in odd], [ref[...] for ref in step])
    pick_fields(
        1, picks_ref[...], field_ref, lambda w: None, (picked_ref, own_picked_ref)
    )
    store_spectra(1, picked_ref, law_ref, *k_refs, out_ref, 0)


def own_kernel(freq_total, slots, *refs):
    picked_refs, (delays_ref, size_ref, slope_ref, out_ref, law_ref) = refs[:2], refs[2:]
    even, step, odd = focal_base(freq_total, delays_ref[...])
    for parity, law in enumerate((even, odd)):
        store_law(law_ref.at[parity], law, step)
    group = lax.axis_index("elem")
    factors = kirchhoff(freq_total, slots, group, size_ref, slope_ref)
    for parity in range(2):
        store_spectra(
            parity, picked_refs[parity], law_ref.at[parity], *factors, out_ref, parity * W_DEV
        )


def call(kernel, name, in_specs, out_shape, scratch):
    vmem = pl.BlockSpec(memory_space=pltpu.VMEM)
    return pl.pallas_call(
        kernel,
        in_specs=in_specs,
        out_specs=[vmem] * len(out_shape),
        out_shape=out_shape,
        scratch_shapes=scratch,
        compiler_params=pltpu.CompilerParams(vmem_limit_bytes=VMEM_BYTES),
        cost_estimate=pl.CostEstimate(flops=1000, bytes_accessed=1000, transcendentals=0),
        name=name,
    )


def partials(field, small, swap, freq_total, slots):
    elements, sites = field.shape[3:]
    vmem = pl.BlockSpec(memory_space=pltpu.VMEM)
    hbm = pl.BlockSpec(memory_space=pltpu.HBM)
    pinned = [pltpu.with_memory_space_constraint(a, pltpu.HBM) for a in (field, *small)]
    out = jax.ShapeDtypeStruct((W_DEV, FG, ROWS), jnp.bfloat16)
    picked = jax.ShapeDtypeStruct((W_HALF, FG, 2 * elements), jnp.bfloat16)
    law = (W_HALF, 2 * elements, 2 * ROWS)
    base = [jax.ShapeDtypeStruct((elements, ROWS), jnp.float32)] * 2
    factors = [jax.ShapeDtypeStruct((FG, FG), jnp.float32)] * 2
    kept = [jax.ShapeDtypeStruct((2 * FG, sites), jnp.bfloat16), *base, *base, *factors]
    copied = [jax.ShapeDtypeStruct(a.shape, a.dtype) for a in (field, *small[4:])]
    work = [pltpu.VMEM(picked.shape, picked.dtype), pltpu.VMEM(law, jnp.bfloat16)]
    even, even_picked, field, size, slope, *kept, delays = call(
        functools.partial(other_even_kernel, freq_total, slots),
        "other_even",
        [hbm] * len(pinned),
        [out, picked, *copied, *kept, base[0]],
        [
            pltpu.SMEM(a.shape, a.dtype) if a.ndim == 1 else pltpu.VMEM(a.shape, a.dtype)
            for a in small[:4]
        ]
        + [pltpu.SemaphoreType.DMA((2, 2)), pltpu.SemaphoreType.DMA((len(small),)), *work],
    )(*pinned)
    even = lax.ppermute(even, "elem", swap)
    odd, odd_picked = call(
        other_odd_kernel, "other_odd", [vmem] * 8, [out, picked], work
    )(field, *kept)
    odd = lax.ppermute(odd, "elem", swap)
    (own,) = call(
        functools.partial(own_kernel, freq_total, slots),
        "own",
        [vmem] * 5,
        [jax.ShapeDtypeStruct((2 * W_DEV, FG, ROWS), jnp.bfloat16)],
        [pltpu.VMEM((2, *law), jnp.bfloat16)],
    )(even_picked, odd_picked, delays, size, slope)
    return own, even, odd


def total(own_ref, moved_ref, parity, rows):
    own = own_ref[parity * W_DEV : (parity + 1) * W_DEV, rows]
    both = own.astype(jnp.float32) + moved_ref[:, rows].astype(jnp.float32)
    return jnp.swapaxes(both, 0, 1).astype(jnp.bfloat16)


def add_even_kernel(size, own_ref, even_ref, held_ref):
    for first in range(0, held_ref.shape[0], size):
        rows = pl.ds(first, size)
        held_ref[rows] = total(own_ref, even_ref, 0, rows)


def add_odd_kernel(own_ref, odd_ref, held_ref, *refs):
    size = refs[0].shape[0]
    for slot, ref in enumerate(refs):
        rows = pl.ds(slot * size, size)
        ref[:, :W_DEV] = held_ref[rows]
        ref[:, W_DEV:] = total(own_ref, odd_ref, 1, rows)


def add(own, even, odd, slots):
    vmem = pl.BlockSpec(memory_space=pltpu.VMEM)
    planes, flaws, rows = own.shape
    size = flaws // slots
    shape = jax.ShapeDtypeStruct((flaws, planes // 2, rows), own.dtype)
    kernel = functools.partial(add_even_kernel, min(size, 16))
    (held,) = call(kernel, "add_even", [vmem] * 2, [shape], [])(own, even)
    shapes = [jax.ShapeDtypeStruct((size, planes, rows), own.dtype)] * slots
    return call(add_odd_kernel, "add_odd", [vmem] * 3, shapes, [])(own, odd, held)


def table_kernel(freq_total, slots, table_ref):
    _, height, depth = table_ref.shape
    time_block = TIME_BLOCK
    row = lax.broadcasted_iota(jnp.int32, (height, depth), 0)
    column = lax.broadcasted_iota(jnp.int32, (height, depth), 1)
    out_imag = (row // time_block) % 2
    time = pl.program_id(0) * time_block + row % time_block
    later = row // (2 * time_block)
    parity = (column >= depth // 2).astype(jnp.int32)
    freq = ((column - parity * (depth // 2)) >> 1) * 2 + parity
    if slots > 1:
        lane = lax.broadcasted_iota(jnp.int32, (1, depth), 1)
        odd = (lane >= depth // 2).astype(jnp.int32)
        lane = ((lane - odd * (depth // 2)) >> 1) * 2 + odd
        freq = partner(slots, lane // W_DEV) * W_DEV + lane % W_DEV
    steps = freq * time + ((column & 1) - out_imag) * (freq_total // 2)
    steps = (steps + (2 + later * freq) * freq_total) & (2 * freq_total - 1)
    _, value = sincos_turns(steps.astype(jnp.float32) * (0.5 / freq_total))
    table_ref[0] = value.astype(jnp.bfloat16)


def table(freq_total, slots, times, folded):
    blocks = times // TIME_BLOCK
    shape = (blocks, (4 if folded else 2) * TIME_BLOCK, 2 * freq_total)
    return pl.pallas_call(
        functools.partial(table_kernel, freq_total, slots),
        grid=(blocks,),
        out_specs=pl.BlockSpec((1, *shape[1:]), lambda i: (i, 0, 0)),
        out_shape=jax.ShapeDtypeStruct(shape, jnp.bfloat16),
        compiler_params=pltpu.CompilerParams(vmem_limit_bytes=VMEM_BYTES),
        name="table",
    )()


def peak_kernel(freq_total, sources, blocks, *refs):
    def first_step():
        return blocks == 1 or pl.program_id(0) == 0

    def last_step():
        return blocks == 1 or pl.program_id(0) == blocks - 1

    count = len(refs) - 5
    table_ref, noise_ref, peak_ref, found_ref, best_ref = refs[count:]
    columns = peak_ref.shape[1]

    @pl.when(first_step())
    def _():
        best_ref[...] = jnp.zeros_like(best_ref)

    width = min(2, columns)
    for first in range(0, columns, width):
        spectra = jnp.concatenate(
            [
                jnp.concatenate(
                    [
                        refs[i][row + first + k, plane : plane + W_DEV, :]
                        for plane in (0, W_DEV)
                        for i, row in sources
                    ],
                    axis=0,
                )
                for k in range(width)
            ],
            axis=1,
        )
        signal = dot(table_ref[0], spectra, ((1,), (0,)))
        power = None
        for top in range(0, signal.shape[0], 2 * TIME_BLOCK):
            real_part = signal[top : top + TIME_BLOCK]
            imag_part = signal[top + TIME_BLOCK : top + 2 * TIME_BLOCK]
            value = real_part * real_part + imag_part * imag_part
            power = value if power is None else jnp.maximum(power, value)
        power = jnp.max(power, axis=0, keepdims=True)
        for k in range(width):
            row = pl.ds(first + k, 1)
            best_ref[row, :] = jnp.maximum(
                best_ref[row, :], power[:, k * ROWS : (k + 1) * ROWS]
            )

    @pl.when(last_step())
    def _():
        largest = jnp.max(best_ref[...], axis=1, keepdims=True)
        shape = best_ref.shape
        diagonal = lax.broadcasted_iota(jnp.int32, shape, 0) == lax.broadcasted_iota(
            jnp.int32, shape, 1
        )
        largest = jnp.max(jnp.where(diagonal, largest, 0.0), axis=0, keepdims=True)
        peak = jnp.sqrt(largest[:, :columns]) * (1.0 / math.sqrt(freq_total))
        score = STEEP * (jnp.log(peak + EPS) - jnp.log(noise_ref[...]))
        peak_ref[...] = peak
        found_ref[...] = 1.0 / (1.0 + jnp.exp(-score))


def peaks(spectra, sources, twiddles, noise_level, freq_total):
    columns = noise_level.shape[1]
    blocks = twiddles.shape[0]
    if blocks == 1:
        vmem = pl.BlockSpec(memory_space=pltpu.VMEM)
        grid, in_specs, out_spec = (), [vmem] * (len(spectra) + 2), vmem
    else:
        grid = (blocks,)
        out_spec = pl.BlockSpec((1, columns), lambda i: (0, 0))
        in_specs = [pl.BlockSpec(a.shape, lambda i: (0, 0, 0)) for a in spectra]
        in_specs += [
            pl.BlockSpec((1, *twiddles.shape[1:]), lambda i: (i, 0, 0)),
            out_spec,
        ]
    return pl.pallas_call(
        functools.partial(peak_kernel, freq_total, sources, blocks),
        grid=grid,
        in_specs=in_specs,
        out_specs=[out_spec, out_spec],
        out_shape=[jax.ShapeDtypeStruct((1, columns), jnp.float32)] * 2,
        scratch_shapes=[pltpu.VMEM((max(8, columns), ROWS), jnp.float32)],
        compiler_params=pltpu.CompilerParams(vmem_limit_bytes=VMEM_BYTES),
        name="peaks",
    )(*spectra, twiddles, noise_level)


def body(
    flaw_cells,
    flaw_blocks,
    element_channel,
    focal_delay,
    beam_field,
    flaw_size,
    flaw_slope,
    noise_level,
):
    freq_count = lax.axis_size("freq")
    freq_total = W_DEV * freq_count
    sample_count = min(T_CAP, 2 * freq_total)
    swap = [(0, 1), (1, 0)]
    direct = freq_count == 8
    slots = freq_count if direct else 1
    small = (
        focal_delay,
        element_channel.reshape(1, -1),
        flaw_blocks,
        flaw_cells.reshape(1, -1),
        flaw_size,
        flaw_slope,
    )
    folded = sample_count == 2 * freq_total
    times = sample_count // 2 if folded else sample_count
    twiddles = table(freq_total, slots, times, folded)
    field = beam_field.reshape(W_HALF, 2, *beam_field.shape[1:])
    parts = add(*partials(field, small, swap, freq_total, slots), slots)
    if direct:
        half = slots // 2
        spectra = []
        for slot, masks in enumerate(zip(*slot_masks(slots))):
            pairs = [(a, a ^ masks[((2 * a) ^ a) & half != 0]) for a in range(slots)]
            spectra.append(lax.ppermute(parts[slot], "freq", pairs) if slot else parts[slot])
        spectra = [*spectra[1:], spectra[0]]
        sources = [((slot - 1) % slots, 0) for slot in range(slots)]
    else:
        spectra = [
            lax.all_to_all(parts[0], "freq", split_axis=0, concat_axis=0, tiled=True)
        ]
        sources = [(0, s * (FG // freq_count)) for s in range(freq_count)]
    return tuple(peaks(spectra, sources, twiddles, noise_level, freq_total))


def solution(mesh):
    in_specs = (
        P("batch"),
        P("batch"),
        P("elem"),
        P(),
        P("freq", None, "elem", None),
        P("batch", None),
        P("batch", None),
        P(("batch", "elem"), "freq"),
    )
    out_specs = (P(("batch", "elem"), "freq"), P(("batch", "elem"), "freq"))
    return jax.shard_map(body, mesh=mesh, in_specs=in_specs, out_specs=out_specs, check_vma=False)
```

```python
import functools
import math

import jax
import jax.numpy as jnp
from jax import lax
from jax.experimental import pallas as pl
from jax.experimental.pallas import tpu as pltpu
from jax.sharding import PartitionSpec as P

W_DEV = 16
W_HALF = W_DEV // 2
FG = 128
NB = 4
SB = 32
T_CAP = 1024

EDGE = 0.6
STEEP = 3.0
EPS = 1e-05

ROWS = NB * SB
VMEM_BYTES = 48 * 1024 * 1024


def sin_half_turn(turns):
    angle = turns * math.pi
    square = angle * angle
    sine = 1.0 / 6227020800.0
    for factorial in (-39916800.0, 362880.0, -5040.0, 120.0, -6.0, 1.0):
        sine = sine * square + 1.0 / factorial
    cosine = 1.0 / 479001600.0
    for factorial in (-3628800.0, 40320.0, -720.0, 24.0, -2.0, 1.0):
        cosine = cosine * square + 1.0 / factorial
    return sine * angle, cosine


def sincos_turns(turns):
    rest = turns - jnp.floor(turns + 0.5)
    sine, cosine = sin_half_turn(rest)
    return 2.0 * sine * cosine, 1.0 - 2.0 * sine * sine


def dot(left, right, contract):
    return lax.dot_general(
        left, right, (contract, ((), ())), preferred_element_type=jnp.float32
    )


def slot_masks(slots):
    half = slots // 2
    between = (half, half + 1, 3)
    return (
        (0, 1, 2, slots - 2, *between, slots - 1),
        (0, slots - 2, 2, slots - 1, *between, 1),
    )


def partner(slots, slot):
    index = lax.axis_index("freq")
    inner = ((index * 2) ^ index) & (slots // 2) != 0
    outer_masks, inner_masks = slot_masks(slots)
    mask = jnp.zeros_like(slot)
    for s in range(1, slots):
        mask = jnp.where(slot == s, jnp.where(inner, inner_masks[s], outer_masks[s]), mask)
    return mask ^ index


def slot_order(slots):
    size = FG // slots
    row = lax.broadcasted_iota(jnp.int32, (FG, 1), 0)
    column = lax.broadcasted_iota(jnp.int32, (FG, FG), 1)
    if slots > 1:
        row = partner(slots, row // size) * size + row % size
    return row == column


def flaw_pick(slots, which, cells_ref):
    cells = jnp.where(which == 0, cells_ref[:, :FG], cells_ref[:, FG:])
    cell_sel = lax.broadcasted_iota(jnp.int32, (cells_ref.shape[1], FG), 0) == cells
    return dot(
        slot_order(slots).astype(jnp.bfloat16), cell_sel.astype(jnp.bfloat16), ((1,), (1,))
    ).astype(jnp.bfloat16)


def delays_of(channel_ref, delay_ref, blocks_ref, groups, elements):
    lane = lax.broadcasted_iota(jnp.int32, (1, 2 * ROWS), 1)
    position = lane & (SB - 1)
    for j in range(2 * NB):
        block = blocks_ref[groups[j // NB] * NB + j % NB]
        position = position + jnp.where((lane >> 5) == j, block * SB, 0)
    channels, positions = delay_ref.shape
    scan_sel = (
        lax.broadcasted_iota(jnp.int32, (positions, 2 * ROWS), 0) == position
    ).astype(jnp.bfloat16)
    channel_sel = (
        (lax.broadcasted_iota(jnp.int32, (channels, elements), 0) == channel_ref[...])
        .astype(jnp.float32)
        .T.astype(jnp.bfloat16)
    )
    rest = delay_ref[...]
    pieces = []
    for _ in range(3):
        pieces.append(rest.astype(jnp.bfloat16))
        rest = rest - pieces[-1].astype(jnp.float32)
    moved = dot(jnp.concatenate(pieces, axis=0), scan_sel, ((1,), (0,))).astype(jnp.bfloat16)
    delays = None
    for i in range(3):
        piece = dot(channel_sel, moved[i * channels : (i + 1) * channels], ((1,), (0,)))
        delays = piece if delays is None else delays + piece
    return delays


def turned(law, step):
    return law[0] * step[0] - law[1] * step[1], law[1] * step[0] + law[0] * step[1]


def focal_base(freq_total, delays):
    first_freq = lax.axis_index("freq") * W_DEV
    phase = delays * (0.5 / freq_total)
    unit = sincos_turns(phase)[::-1]
    base = sincos_turns(phase * first_freq.astype(jnp.float32))[::-1]
    return base, turned(unit, unit), turned(base, unit)


def kirchhoff(freq_total, slots, which, size_ref, slope_ref):
    first_freq = lax.axis_index("freq") * W_DEV
    order = slot_order(slots)
    size = size_ref[pl.ds(which, 1), :]
    turn = size * slope_ref[pl.ds(which, 1), :] * (1.0 / freq_total)
    size = jnp.sum(jnp.where(order, size, 0.0), axis=1, keepdims=True)
    turn = jnp.sum(jnp.where(order, turn, 0.0), axis=1, keepdims=True)
    freq = first_freq + lax.broadcasted_iota(jnp.int32, (FG, FG), 1)
    sine, cosine = sincos_turns(turn * freq.astype(jnp.float32))
    return size * (1.0 + EDGE) * cosine, size * (EDGE - 1.0) * sine


def store_law(law_ref, law, step):
    elements = law_ref.shape[1] // 2
    for w in range(W_HALF):
        c = law[0].astype(jnp.bfloat16)
        s = law[1].astype(jnp.bfloat16)
        law_ref[w, :elements, :ROWS] = c
        law_ref[w, :elements, ROWS:] = -s
        law_ref[w, elements:, :ROWS] = s
        law_ref[w, elements:, ROWS:] = c
        if w < W_HALF - 1:
            law = turned(law, step)


def pick_fields(parity, picks, field_ref, wait, picked_refs):
    elements, sites = field_ref.shape[3:]
    for w in range(W_HALF):
        wait(w)
        picked = dot(
            picks, field_ref[w, parity].reshape(2 * elements, sites), ((1,), (1,))
        ).astype(jnp.bfloat16)
        for i, ref in enumerate(picked_refs):
            ref[w] = picked[i * FG : (i + 1) * FG]


def store_spectra(parity, picked_ref, law_ref, k_real, k_imag, out_ref, first):
    for w in range(W_HALF):
        product = dot(picked_ref[w], law_ref[w], ((1,), (0,)))
        real_part = product[:, :ROWS]
        imag_part = product[:, ROWS:]
        kr = k_real[:, 2 * w + parity : 2 * w + parity + 1]
        ki = k_imag[:, 2 * w + parity : 2 * w + parity + 1]
        out_ref[first + 2 * w] = (kr * real_part - ki * imag_part).astype(jnp.bfloat16)
        out_ref[first + 2 * w + 1] = (kr * imag_part + ki * real_part).astype(jnp.bfloat16)


def other_even_kernel(freq_total, slots, *refs):
    field_hbm, *small_hbm = refs[:7]
    out_ref, own_picked_ref, field_ref, size_ref, slope_ref, *kept = refs[7:20]
    delay_ref, channel_ref, blocks_ref, cells_ref = refs[20:24]
    field_sem, small_sem, *scratch = refs[24:]
    small = (delay_ref, channel_ref, blocks_ref, cells_ref, size_ref, slope_ref)
    picked_ref, law_ref = scratch
    copies = [
        pltpu.make_async_copy(source, target, small_sem.at[i])
        for i, (source, target) in enumerate(zip(small_hbm, small))
    ]
    for copy in copies:
        copy.start()
    part = W_HALF // 2
    field_copies = [
        pltpu.make_async_copy(
            field_hbm.at[pl.ds(i * part, part), parity],
            field_ref.at[pl.ds(i * part, part), parity],
            field_sem.at[parity, i],
        )
        for parity in range(2)
        for i in range(2)
    ]
    for copy in field_copies:
        copy.start()
    for copy in copies:
        copy.wait()
    group = lax.axis_index("elem")
    groups = (1 - group, group)
    picks = jnp.concatenate(
        [flaw_pick(slots, which, cells_ref) for which in groups], axis=0
    )
    factors = kirchhoff(freq_total, slots, groups[0], size_ref, slope_ref)
    delays = delays_of(channel_ref, delay_ref, blocks_ref, groups, field_ref.shape[3])
    even, step, odd = focal_base(freq_total, delays[:, :ROWS])
    values = (picks, *step, *odd, *factors, delays[:, ROWS:])
    for ref, value in zip(kept, values):
        ref[...] = value
    store_law(law_ref, even, step)

    def wait(w):
        if w % part == 0:
            field_copies[w // part].wait()

    pick_fields(0, picks, field_ref, wait, (picked_ref, own_picked_ref))
    store_spectra(0, picked_ref, law_ref, *factors, out_ref, 0)
    for copy in field_copies[2:]:
        copy.wait()


def other_odd_kernel(field_ref, picks_ref, *refs):
    step, odd, k_refs = refs[:2], refs[2:4], refs[4:6]
    out_ref, own_picked_ref, picked_ref, law_ref = refs[6:]
    store_law(law_ref, [ref[...] for ref in odd], [ref[...] for ref in step])
    pick_fields(
        1, picks_ref[...], field_ref, lambda w: None, (picked_ref, own_picked_ref)
    )
    store_spectra(1, picked_ref, law_ref, *k_refs, out_ref, 0)


def own_kernel(freq_total, slots, *refs):
    picked_refs, (delays_ref, size_ref, slope_ref, out_ref, law_ref) = refs[:2], refs[2:]
    even, step, odd = focal_base(freq_total, delays_ref[...])
    for parity, law in enumerate((even, odd)):
        store_law(law_ref.at[parity], law, step)
    group = lax.axis_index("elem")
    factors = kirchhoff(freq_total, slots, group, size_ref, slope_ref)
    for parity in range(2):
        store_spectra(
            parity, picked_refs[parity], law_ref.at[parity], *factors, out_ref, parity * W_DEV
        )


def call(kernel, name, in_specs, out_shape, scratch):
    vmem = pl.BlockSpec(memory_space=pltpu.VMEM)
    return pl.pallas_call(
        kernel,
        in_specs=in_specs,
        out_specs=[vmem] * len(out_shape),
        out_shape=out_shape,
        scratch_shapes=scratch,
        compiler_params=pltpu.CompilerParams(vmem_limit_bytes=VMEM_BYTES),
        cost_estimate=pl.CostEstimate(flops=1000, bytes_accessed=1000, transcendentals=0),
        name=name,
    )


def partials(field, small, swap, freq_total, slots):
    elements, sites = field.shape[3:]
    vmem = pl.BlockSpec(memory_space=pltpu.VMEM)
    hbm = pl.BlockSpec(memory_space=pltpu.HBM)
    pinned = [pltpu.with_memory_space_constraint(a, pltpu.HBM) for a in (field, *small)]
    out = jax.ShapeDtypeStruct((W_DEV, FG, ROWS), jnp.bfloat16)
    picked = jax.ShapeDtypeStruct((W_HALF, FG, 2 * elements), jnp.bfloat16)
    law = (W_HALF, 2 * elements, 2 * ROWS)
    base = [jax.ShapeDtypeStruct((elements, ROWS), jnp.float32)] * 2
    factors = [jax.ShapeDtypeStruct((FG, FG), jnp.float32)] * 2
    kept = [jax.ShapeDtypeStruct((2 * FG, sites), jnp.bfloat16), *base, *base, *factors]
    copied = [jax.ShapeDtypeStruct(a.shape, a.dtype) for a in (field, *small[4:])]
    work = [pltpu.VMEM(picked.shape, picked.dtype), pltpu.VMEM(law, jnp.bfloat16)]
    even, even_picked, field, size, slope, *kept, delays = call(
        functools.partial(other_even_kernel, freq_total, slots),
        "other_even",
        [hbm] * len(pinned),
        [out, picked, *copied, *kept, base[0]],
        [
            pltpu.SMEM(a.shape, a.dtype) if a.ndim == 1 else pltpu.VMEM(a.shape, a.dtype)
            for a in small[:4]
        ]
        + [pltpu.SemaphoreType.DMA((2, 2)), pltpu.SemaphoreType.DMA((len(small),)), *work],
    )(*pinned)
    even = lax.ppermute(even, "elem", swap)
    odd, odd_picked = call(
        other_odd_kernel, "other_odd", [vmem] * 8, [out, picked], work
    )(field, *kept)
    odd = lax.ppermute(odd, "elem", swap)
    (own,) = call(
        functools.partial(own_kernel, freq_total, slots),
        "own",
        [vmem] * 5,
        [jax.ShapeDtypeStruct((2 * W_DEV, FG, ROWS), jnp.bfloat16)],
        [pltpu.VMEM((2, *law), jnp.bfloat16)],
    )(even_picked, odd_picked, delays, size, slope)
    return own, even, odd


def total(own_ref, moved_ref, parity, rows):
    own = own_ref[parity * W_DEV : (parity + 1) * W_DEV, rows]
    both = own.astype(jnp.float32) + moved_ref[:, rows].astype(jnp.float32)
    return jnp.swapaxes(both, 0, 1).astype(jnp.bfloat16)


def add_even_kernel(size, own_ref, even_ref, held_ref):
    for first in range(0, held_ref.shape[0], size):
        rows = pl.ds(first, size)
        held_ref[rows] = total(own_ref, even_ref, 0, rows)


def add_odd_kernel(own_ref, odd_ref, held_ref, *refs):
    size = refs[0].shape[0]
    for slot, ref in enumerate(refs):
        rows = pl.ds(slot * size, size)
        ref[:, :W_DEV] = held_ref[rows]
        ref[:, W_DEV:] = total(own_ref, odd_ref, 1, rows)


def add(own, even, odd, slots):
    vmem = pl.BlockSpec(memory_space=pltpu.VMEM)
    planes, flaws, rows = own.shape
    size = flaws // slots
    shape = jax.ShapeDtypeStruct((flaws, planes // 2, rows), own.dtype)
    kernel = functools.partial(add_even_kernel, min(size, 16))
    (held,) = call(kernel, "add_even", [vmem] * 2, [shape], [])(own, even)
    shapes = [jax.ShapeDtypeStruct((size, planes, rows), own.dtype)] * slots
    return call(add_odd_kernel, "add_odd", [vmem] * 3, shapes, [])(own, odd, held)


def table_kernel(freq_total, slots, table_ref):
    height, depth = table_ref.shape[2:]
    time_block = height // 2
    row = lax.broadcasted_iota(jnp.int32, (height, depth // 2), 0)
    column = lax.broadcasted_iota(jnp.int32, (height, depth // 2), 1)
    out_imag = (row >= time_block).astype(jnp.int32)
    time = pl.program_id(0) * time_block + row - out_imag * time_block
    for parity in range(2):
        freq = (column >> 1) * 2 + parity
        if slots > 1:
            lane = lax.broadcasted_iota(jnp.int32, (1, depth // 2), 1)
            lane = (lane >> 1) * 2 + parity
            freq = partner(slots, lane // W_DEV) * W_DEV + lane % W_DEV
        steps = freq * time + ((column & 1) - out_imag) * (freq_total // 2)
        steps = (steps + 2 * freq_total) & (2 * freq_total - 1)
        _, value = sincos_turns(steps.astype(jnp.float32) * (0.5 / freq_total))
        high = value.astype(jnp.bfloat16)
        table_ref[0, parity, :, : depth // 2] = high
        table_ref[0, parity, :, depth // 2 :] = (
            value - high.astype(jnp.float32)
        ).astype(jnp.bfloat16)


def table(freq_total, slots, times, time_block):
    blocks = times // time_block
    shape = (blocks, 2, 2 * time_block, 2 * freq_total)
    return pl.pallas_call(
        functools.partial(table_kernel, freq_total, slots),
        grid=(blocks,),
        out_specs=pl.BlockSpec((1, *shape[1:]), lambda i: (i, 0, 0, 0)),
        out_shape=jax.ShapeDtypeStruct(shape, jnp.bfloat16),
        compiler_params=pltpu.CompilerParams(vmem_limit_bytes=VMEM_BYTES),
        name="table",
    )()


def peak_kernel(freq_total, folded, sources, blocks, *refs):
    def first_step():
        return blocks == 1 or pl.program_id(0) == 0

    def last_step():
        return blocks == 1 or pl.program_id(0) == blocks - 1

    count = len(refs) - 5
    table_ref, noise_ref, peak_ref, found_ref, best_ref = refs[count:]
    columns = peak_ref.shape[1]
    time_block = table_ref.shape[2] // 2

    @pl.when(first_step())
    def _():
        best_ref[...] = jnp.zeros_like(best_ref)

    width = min(2, columns)
    for first in range(0, columns, width):
        parts = []
        for parity in range(2):
            planes = slice(parity * W_DEV, (parity + 1) * W_DEV)
            spectra = jnp.concatenate(
                [
                    jnp.concatenate(
                        [
                            refs[i][row + first + k, planes, :]
                            for i, row in sources
                        ]
                        * 2,
                        axis=0,
                    )
                    for k in range(width)
                ],
                axis=1,
            )
            parts.append(dot(table_ref[0, parity], spectra, ((1,), (0,))))
        powers = []
        for signal in [parts[0] + parts[1]] + [parts[0] - parts[1]] * folded:
            real_part = signal[:time_block]
            imag_part = signal[time_block:]
            powers.append(real_part * real_part + imag_part * imag_part)
        power = jnp.maximum(powers[0], powers[-1]) if folded else powers[0]
        power = jnp.max(power, axis=0, keepdims=True)
        for k in range(width):
            row = pl.ds(first + k, 1)
            best_ref[row, :] = jnp.maximum(
                best_ref[row, :], power[:, k * ROWS : (k + 1) * ROWS]
            )

    @pl.when(last_step())
    def _():
        largest = jnp.max(best_ref[...], axis=1, keepdims=True)
        shape = best_ref.shape
        diagonal = lax.broadcasted_iota(jnp.int32, shape, 0) == lax.broadcasted_iota(
            jnp.int32, shape, 1
        )
        largest = jnp.max(jnp.where(diagonal, largest, 0.0), axis=0, keepdims=True)
        peak = jnp.sqrt(largest[:, :columns]) * (1.0 / math.sqrt(freq_total))
        score = STEEP * (jnp.log(peak + EPS) - jnp.log(noise_ref[...]))
        peak_ref[...] = peak
        found_ref[...] = 1.0 / (1.0 + jnp.exp(-score))


def peaks(spectra, sources, twiddles, noise_level, freq_total, folded):
    columns = noise_level.shape[1]
    blocks = twiddles.shape[0]
    if blocks == 1:
        vmem = pl.BlockSpec(memory_space=pltpu.VMEM)
        grid, in_specs, out_spec = (), [vmem] * (len(spectra) + 2), vmem
    else:
        grid = (blocks,)
        out_spec = pl.BlockSpec((1, columns), lambda i: (0, 0))
        in_specs = [pl.BlockSpec(a.shape, lambda i: (0, 0, 0)) for a in spectra]
        in_specs += [
            pl.BlockSpec((1, *twiddles.shape[1:]), lambda i: (i, 0, 0, 0)),
            out_spec,
        ]
    return pl.pallas_call(
        functools.partial(peak_kernel, freq_total, folded, sources, blocks),
        grid=grid,
        in_specs=in_specs,
        out_specs=[out_spec, out_spec],
        out_shape=[jax.ShapeDtypeStruct((1, columns), jnp.float32)] * 2,
        scratch_shapes=[pltpu.VMEM((max(8, columns), ROWS), jnp.float32)],
        compiler_params=pltpu.CompilerParams(vmem_limit_bytes=VMEM_BYTES),
        name="peaks",
    )(*spectra, twiddles, noise_level)


def body(
    flaw_cells,
    flaw_blocks,
    element_channel,
    focal_delay,
    beam_field,
    flaw_size,
    flaw_slope,
    noise_level,
):
    freq_count = lax.axis_size("freq")
    freq_total = W_DEV * freq_count
    sample_count = min(T_CAP, 2 * freq_total)
    swap = [(0, 1), (1, 0)]
    direct = freq_count == 8
    slots = freq_count if direct else 1
    small = (
        focal_delay,
        element_channel.reshape(1, -1),
        flaw_blocks,
        flaw_cells.reshape(1, -1),
        flaw_size,
        flaw_slope,
    )
    folded = sample_count == 2 * freq_total
    times = sample_count // 2 if folded else sample_count
    twiddles = table(freq_total, slots, times, min(128, times))
    field = beam_field.reshape(W_HALF, 2, *beam_field.shape[1:])
    parts = add(*partials(field, small, swap, freq_total, slots), slots)
    if direct:
        half = slots // 2
        spectra = []
        for slot, masks in enumerate(zip(*slot_masks(slots))):
            pairs = [(a, a ^ masks[((2 * a) ^ a) & half != 0]) for a in range(slots)]
            spectra.append(lax.ppermute(parts[slot], "freq", pairs) if slot else parts[slot])
        spectra = [*spectra[1:], spectra[0]]
        sources = [((slot - 1) % slots, 0) for slot in range(slots)]
    else:
        spectra = [
            lax.all_to_all(parts[0], "freq", split_axis=0, concat_axis=0, tiled=True)
        ]
        sources = [(0, s * (FG // freq_count)) for s in range(freq_count)]
    return tuple(peaks(spectra, sources, twiddles, noise_level, freq_total, folded))


def solution(mesh):
    in_specs = (
        P("batch"),
        P("batch"),
        P("elem"),
        P(),
        P("freq", None, "elem", None),
        P("batch", None),
        P("batch", None),
        P(("batch", "elem"), "freq"),
    )
    out_specs = (P(("batch", "elem"), "freq"), P(("batch", "elem"), "freq"))
    return jax.shard_map(body, mesh=mesh, in_specs=in_specs, out_specs=out_specs, check_vma=False)
```

```python
import functools
import math

import jax
import jax.numpy as jnp
from jax import lax
from jax.experimental import pallas as pl
from jax.experimental.pallas import tpu as pltpu
from jax.sharding import PartitionSpec as P

W_DEV = 16
W_HALF = W_DEV // 2
FG = 128
NB = 4
SB = 32
T_CAP = 1024

EDGE = 0.6
STEEP = 3.0
EPS = 1e-05

ROWS = NB * SB
VMEM_BYTES = 48 * 1024 * 1024


def sin_half_turn(turns):
    angle = turns * math.pi
    square = angle * angle
    sine = 1.0 / 6227020800.0
    for factorial in (-39916800.0, 362880.0, -5040.0, 120.0, -6.0, 1.0):
        sine = sine * square + 1.0 / factorial
    cosine = 1.0 / 479001600.0
    for factorial in (-3628800.0, 40320.0, -720.0, 24.0, -2.0, 1.0):
        cosine = cosine * square + 1.0 / factorial
    return sine * angle, cosine


def sincos_turns(turns):
    rest = turns - jnp.floor(turns + 0.5)
    sine, cosine = sin_half_turn(rest)
    return 2.0 * sine * cosine, 1.0 - 2.0 * sine * sine


def dot(left, right, contract):
    return lax.dot_general(
        left, right, (contract, ((), ())), preferred_element_type=jnp.float32
    )


def slot_masks(slots):
    half = slots // 2
    between = (2, half, half + 1, slots - 1, 3)
    return (0, 1, *between, slots - 2), (0, slots - 2, *between, 1)


def partner(slots, slot):
    index = lax.axis_index("freq")
    inner = ((index * 2) ^ index) & (slots // 2) != 0
    outer_masks, inner_masks = slot_masks(slots)
    mask = jnp.zeros_like(slot)
    for s in range(1, slots):
        mask = jnp.where(slot == s, jnp.where(inner, inner_masks[s], outer_masks[s]), mask)
    return mask ^ index


def slot_order(slots):
    size = FG // slots
    row = lax.broadcasted_iota(jnp.int32, (FG, 1), 0)
    column = lax.broadcasted_iota(jnp.int32, (FG, FG), 1)
    if slots > 1:
        row = partner(slots, row // size) * size + row % size
    return row == column


def flaw_pick(slots, which, cells_ref):
    cells = jnp.where(which == 0, cells_ref[:, :FG], cells_ref[:, FG:])
    cell_sel = lax.broadcasted_iota(jnp.int32, (cells_ref.shape[1], FG), 0) == cells
    return dot(
        slot_order(slots).astype(jnp.bfloat16), cell_sel.astype(jnp.bfloat16), ((1,), (1,))
    ).astype(jnp.bfloat16)


def delays_of(channel_ref, delay_ref, blocks_ref, groups, elements):
    lane = lax.broadcasted_iota(jnp.int32, (1, 2 * ROWS), 1)
    position = lane & (SB - 1)
    for j in range(2 * NB):
        block = blocks_ref[groups[j // NB] * NB + j % NB]
        position = position + jnp.where((lane >> 5) == j, block * SB, 0)
    channels, positions = delay_ref.shape
    scan_sel = (
        lax.broadcasted_iota(jnp.int32, (positions, 2 * ROWS), 0) == position
    ).astype(jnp.bfloat16)
    channel_sel = (
        (lax.broadcasted_iota(jnp.int32, (channels, elements), 0) == channel_ref[...])
        .astype(jnp.float32)
        .T.astype(jnp.bfloat16)
    )
    rest = delay_ref[...]
    pieces = []
    for _ in range(3):
        pieces.append(rest.astype(jnp.bfloat16))
        rest = rest - pieces[-1].astype(jnp.float32)
    moved = dot(jnp.concatenate(pieces, axis=0), scan_sel, ((1,), (0,))).astype(jnp.bfloat16)
    delays = None
    for i in range(3):
        piece = dot(channel_sel, moved[i * channels : (i + 1) * channels], ((1,), (0,)))
        delays = piece if delays is None else delays + piece
    return delays


def turned(law, step):
    return law[0] * step[0] - law[1] * step[1], law[1] * step[0] + law[0] * step[1]


def focal_base(freq_total, delays):
    first_freq = lax.axis_index("freq") * W_DEV
    phase = delays * (0.5 / freq_total)
    unit = sincos_turns(phase)[::-1]
    base = sincos_turns(phase * first_freq.astype(jnp.float32))[::-1]
    return base, turned(unit, unit), turned(base, unit)


def kirchhoff(freq_total, slots, which, size_ref, slope_ref):
    first_freq = lax.axis_index("freq") * W_DEV
    order = slot_order(slots)
    size = size_ref[pl.ds(which, 1), :]
    turn = size * slope_ref[pl.ds(which, 1), :] * (1.0 / freq_total)
    size = jnp.sum(jnp.where(order, size, 0.0), axis=1, keepdims=True)
    turn = jnp.sum(jnp.where(order, turn, 0.0), axis=1, keepdims=True)
    freq = first_freq + lax.broadcasted_iota(jnp.int32, (FG, FG), 1)
    sine, cosine = sincos_turns(turn * freq.astype(jnp.float32))
    return size * (1.0 + EDGE) * cosine, size * (EDGE - 1.0) * sine


def store_law(law_ref, law, step):
    elements = law_ref.shape[1] // 2
    for w in range(W_HALF):
        c = law[0].astype(jnp.bfloat16)
        s = law[1].astype(jnp.bfloat16)
        law_ref[w, :elements, :ROWS] = c
        law_ref[w, :elements, ROWS:] = -s
        law_ref[w, elements:, :ROWS] = s
        law_ref[w, elements:, ROWS:] = c
        if w < W_HALF - 1:
            law = turned(law, step)


def pick_fields(parity, picks, field_ref, wait, picked_refs):
    elements, sites = field_ref.shape[3:]
    for w in range(W_HALF):
        wait(w)
        picked = dot(
            picks, field_ref[w, parity].reshape(2 * elements, sites), ((1,), (1,))
        ).astype(jnp.bfloat16)
        for i, ref in enumerate(picked_refs):
            ref[w] = picked[i * FG : (i + 1) * FG]


def store_spectra(parity, picked_ref, law_ref, k_real, k_imag, out_ref, first):
    for w in range(W_HALF):
        product = dot(picked_ref[w], law_ref[w], ((1,), (0,)))
        real_part = product[:, :ROWS]
        imag_part = product[:, ROWS:]
        kr = k_real[:, 2 * w + parity : 2 * w + parity + 1]
        ki = k_imag[:, 2 * w + parity : 2 * w + parity + 1]
        out_ref[first + 2 * w] = (kr * real_part - ki * imag_part).astype(jnp.bfloat16)
        out_ref[first + 2 * w + 1] = (kr * imag_part + ki * real_part).astype(jnp.bfloat16)


def other_even_kernel(freq_total, slots, *refs):
    field_hbm, *small_hbm = refs[:7]
    out_ref, own_picked_ref, field_ref, size_ref, slope_ref, *kept = refs[7:20]
    delay_ref, channel_ref, blocks_ref, cells_ref = refs[20:24]
    field_sem, small_sem, *scratch = refs[24:]
    small = (delay_ref, channel_ref, blocks_ref, cells_ref, size_ref, slope_ref)
    picked_ref, law_ref = scratch
    copies = [
        pltpu.make_async_copy(source, target, small_sem.at[i])
        for i, (source, target) in enumerate(zip(small_hbm, small))
    ]
    for copy in copies:
        copy.start()
    part = W_HALF // 2
    field_copies = [
        pltpu.make_async_copy(
            field_hbm.at[pl.ds(i * part, part), parity],
            field_ref.at[pl.ds(i * part, part), parity],
            field_sem.at[parity, i],
        )
        for parity in range(2)
        for i in range(2)
    ]
    for copy in field_copies:
        copy.start()
    for copy in copies:
        copy.wait()
    group = lax.axis_index("elem")
    groups = (1 - group, group)
    picks = jnp.concatenate(
        [flaw_pick(slots, which, cells_ref) for which in groups], axis=0
    )
    factors = kirchhoff(freq_total, slots, groups[0], size_ref, slope_ref)
    delays = delays_of(channel_ref, delay_ref, blocks_ref, groups, field_ref.shape[3])
    even, step, odd = focal_base(freq_total, delays[:, :ROWS])
    values = (picks, *step, *odd, *factors, delays[:, ROWS:])
    for ref, value in zip(kept, values):
        ref[...] = value
    store_law(law_ref, even, step)

    def wait(w):
        if w % part == 0:
            field_copies[w // part].wait()

    pick_fields(0, picks, field_ref, wait, (picked_ref, own_picked_ref))
    store_spectra(0, picked_ref, law_ref, *factors, out_ref, 0)
    for copy in field_copies[2:]:
        copy.wait()


def other_odd_kernel(field_ref, picks_ref, *refs):
    step, odd, k_refs = refs[:2], refs[2:4], refs[4:6]
    out_ref, own_picked_ref, picked_ref, law_ref = refs[6:]
    store_law(law_ref, [ref[...] for ref in odd], [ref[...] for ref in step])
    pick_fields(
        1, picks_ref[...], field_ref, lambda w: None, (picked_ref, own_picked_ref)
    )
    store_spectra(1, picked_ref, law_ref, *k_refs, out_ref, 0)


def own_kernel(freq_total, slots, *refs):
    picked_refs, (delays_ref, size_ref, slope_ref, out_ref, law_ref) = refs[:2], refs[2:]
    even, step, odd = focal_base(freq_total, delays_ref[...])
    for parity, law in enumerate((even, odd)):
        store_law(law_ref.at[parity], law, step)
    group = lax.axis_index("elem")
    factors = kirchhoff(freq_total, slots, group, size_ref, slope_ref)
    for parity in range(2):
        store_spectra(
            parity, picked_refs[parity], law_ref.at[parity], *factors, out_ref, parity * W_DEV
        )


def call(kernel, name, in_specs, out_shape, scratch):
    vmem = pl.BlockSpec(memory_space=pltpu.VMEM)
    return pl.pallas_call(
        kernel,
        in_specs=in_specs,
        out_specs=[vmem] * len(out_shape),
        out_shape=out_shape,
        scratch_shapes=scratch,
        compiler_params=pltpu.CompilerParams(vmem_limit_bytes=VMEM_BYTES),
        cost_estimate=pl.CostEstimate(flops=1000, bytes_accessed=1000, transcendentals=0),
        name=name,
    )


def partials(field, small, swap, freq_total, slots):
    elements, sites = field.shape[3:]
    vmem = pl.BlockSpec(memory_space=pltpu.VMEM)
    hbm = pl.BlockSpec(memory_space=pltpu.HBM)
    pinned = [pltpu.with_memory_space_constraint(a, pltpu.HBM) for a in (field, *small)]
    out = jax.ShapeDtypeStruct((W_DEV, FG, ROWS), jnp.bfloat16)
    picked = jax.ShapeDtypeStruct((W_HALF, FG, 2 * elements), jnp.bfloat16)
    law = (W_HALF, 2 * elements, 2 * ROWS)
    base = [jax.ShapeDtypeStruct((elements, ROWS), jnp.float32)] * 2
    factors = [jax.ShapeDtypeStruct((FG, FG), jnp.float32)] * 2
    kept = [jax.ShapeDtypeStruct((2 * FG, sites), jnp.bfloat16), *base, *base, *factors]
    copied = [jax.ShapeDtypeStruct(a.shape, a.dtype) for a in (field, *small[4:])]
    work = [pltpu.VMEM(picked.shape, picked.dtype), pltpu.VMEM(law, jnp.bfloat16)]
    even, even_picked, field, size, slope, *kept, delays = call(
        functools.partial(other_even_kernel, freq_total, slots),
        "other_even",
        [hbm] * len(pinned),
        [out, picked, *copied, *kept, base[0]],
        [
            pltpu.SMEM(a.shape, a.dtype) if a.ndim == 1 else pltpu.VMEM(a.shape, a.dtype)
            for a in small[:4]
        ]
        + [pltpu.SemaphoreType.DMA((2, 2)), pltpu.SemaphoreType.DMA((len(small),)), *work],
    )(*pinned)
    even = lax.ppermute(even, "elem", swap)
    odd, odd_picked = call(
        other_odd_kernel, "other_odd", [vmem] * 8, [out, picked], work
    )(field, *kept)
    odd = lax.ppermute(odd, "elem", swap)
    (own,) = call(
        functools.partial(own_kernel, freq_total, slots),
        "own",
        [vmem] * 5,
        [jax.ShapeDtypeStruct((2 * W_DEV, FG, ROWS), jnp.bfloat16)],
        [pltpu.VMEM((2, *law), jnp.bfloat16)],
    )(even_picked, odd_picked, delays, size, slope)
    return own, even, odd


def total(own_ref, moved_ref, parity, rows):
    own = own_ref[parity * W_DEV : (parity + 1) * W_DEV, rows]
    both = own.astype(jnp.float32) + moved_ref[:, rows].astype(jnp.float32)
    return jnp.swapaxes(both, 0, 1).astype(jnp.bfloat16)


def add_even_kernel(size, own_ref, even_ref, held_ref):
    for first in range(0, held_ref.shape[0], size):
        rows = pl.ds(first, size)
        held_ref[rows] = total(own_ref, even_ref, 0, rows)


def add_odd_kernel(own_ref, odd_ref, held_ref, *refs):
    size = refs[0].shape[0]
    for slot, ref in enumerate(refs):
        rows = pl.ds(slot * size, size)
        ref[:, :W_DEV] = held_ref[rows]
        ref[:, W_DEV:] = total(own_ref, odd_ref, 1, rows)


def add(own, even, odd, slots):
    vmem = pl.BlockSpec(memory_space=pltpu.VMEM)
    planes, flaws, rows = own.shape
    size = flaws // slots
    shape = jax.ShapeDtypeStruct((flaws, planes // 2, rows), own.dtype)
    kernel = functools.partial(add_even_kernel, min(size, 16))
    (held,) = call(kernel, "add_even", [vmem] * 2, [shape], [])(own, even)
    shapes = [jax.ShapeDtypeStruct((size, planes, rows), own.dtype)] * slots
    return call(add_odd_kernel, "add_odd", [vmem] * 3, shapes, [])(own, odd, held)


def table_kernel(freq_total, slots, table_ref):
    height, depth = table_ref.shape[2:]
    time_block = height // 2
    row = lax.broadcasted_iota(jnp.int32, (height, depth // 2), 0)
    column = lax.broadcasted_iota(jnp.int32, (height, depth // 2), 1)
    out_imag = (row >= time_block).astype(jnp.int32)
    time = pl.program_id(0) * time_block + row - out_imag * time_block
    for parity in range(2):
        freq = (column >> 1) * 2 + parity
        if slots > 1:
            lane = lax.broadcasted_iota(jnp.int32, (1, depth // 2), 1)
            lane = (lane >> 1) * 2 + parity
            freq = partner(slots, lane // W_DEV) * W_DEV + lane % W_DEV
        steps = freq * time + ((column & 1) - out_imag) * (freq_total // 2)
        steps = (steps + 2 * freq_total) & (2 * freq_total - 1)
        _, value = sincos_turns(steps.astype(jnp.float32) * (0.5 / freq_total))
        high = value.astype(jnp.bfloat16)
        table_ref[0, parity, :, : depth // 2] = high
        table_ref[0, parity, :, depth // 2 :] = (
            value - high.astype(jnp.float32)
        ).astype(jnp.bfloat16)


def table(freq_total, slots, times, time_block):
    blocks = times // time_block
    shape = (blocks, 2, 2 * time_block, 2 * freq_total)
    return pl.pallas_call(
        functools.partial(table_kernel, freq_total, slots),
        grid=(blocks,),
        out_specs=pl.BlockSpec((1, *shape[1:]), lambda i: (i, 0, 0, 0)),
        out_shape=jax.ShapeDtypeStruct(shape, jnp.bfloat16),
        compiler_params=pltpu.CompilerParams(vmem_limit_bytes=VMEM_BYTES),
        name="table",
    )()


def peak_kernel(freq_total, folded, sources, blocks, *refs):
    def first_step():
        return blocks == 1 or pl.program_id(0) == 0

    def last_step():
        return blocks == 1 or pl.program_id(0) == blocks - 1

    count = len(refs) - 5
    table_ref, noise_ref, peak_ref, found_ref, best_ref = refs[count:]
    columns = peak_ref.shape[1]
    time_block = table_ref.shape[2] // 2

    @pl.when(first_step())
    def _():
        best_ref[...] = jnp.zeros_like(best_ref)

    width = min(2, columns)
    for first in range(0, columns, width):
        parts = []
        for parity in range(2):
            planes = slice(parity * W_DEV, (parity + 1) * W_DEV)
            spectra = jnp.concatenate(
                [
                    jnp.concatenate(
                        [
                            refs[i][row + first + k, planes, :]
                            for i, row in sources
                        ]
                        * 2,
                        axis=0,
                    )
                    for k in range(width)
                ],
                axis=1,
            )
            parts.append(dot(table_ref[0, parity], spectra, ((1,), (0,))))
        powers = []
        for signal in [parts[0] + parts[1]] + [parts[0] - parts[1]] * folded:
            real_part = signal[:time_block]
            imag_part = signal[time_block:]
            powers.append(real_part * real_part + imag_part * imag_part)
        power = jnp.maximum(powers[0], powers[-1]) if folded else powers[0]
        power = jnp.max(power, axis=0, keepdims=True)
        for k in range(width):
            row = pl.ds(first + k, 1)
            best_ref[row, :] = jnp.maximum(
                best_ref[row, :], power[:, k * ROWS : (k + 1) * ROWS]
            )

    @pl.when(last_step())
    def _():
        largest = jnp.max(best_ref[...], axis=1, keepdims=True)
        shape = best_ref.shape
        diagonal = lax.broadcasted_iota(jnp.int32, shape, 0) == lax.broadcasted_iota(
            jnp.int32, shape, 1
        )
        largest = jnp.max(jnp.where(diagonal, largest, 0.0), axis=0, keepdims=True)
        peak = jnp.sqrt(largest[:, :columns]) * (1.0 / math.sqrt(freq_total))
        score = STEEP * (jnp.log(peak + EPS) - jnp.log(noise_ref[...]))
        peak_ref[...] = peak
        found_ref[...] = 1.0 / (1.0 + jnp.exp(-score))


def peaks(spectra, sources, twiddles, noise_level, freq_total, folded):
    columns = noise_level.shape[1]
    blocks = twiddles.shape[0]
    if blocks == 1:
        vmem = pl.BlockSpec(memory_space=pltpu.VMEM)
        grid, in_specs, out_spec = (), [vmem] * (len(spectra) + 2), vmem
    else:
        grid = (blocks,)
        out_spec = pl.BlockSpec((1, columns), lambda i: (0, 0))
        in_specs = [pl.BlockSpec(a.shape, lambda i: (0, 0, 0)) for a in spectra]
        in_specs += [
            pl.BlockSpec((1, *twiddles.shape[1:]), lambda i: (i, 0, 0, 0)),
            out_spec,
        ]
    return pl.pallas_call(
        functools.partial(peak_kernel, freq_total, folded, sources, blocks),
        grid=grid,
        in_specs=in_specs,
        out_specs=[out_spec, out_spec],
        out_shape=[jax.ShapeDtypeStruct((1, columns), jnp.float32)] * 2,
        scratch_shapes=[pltpu.VMEM((max(8, columns), ROWS), jnp.float32)],
        compiler_params=pltpu.CompilerParams(vmem_limit_bytes=VMEM_BYTES),
        name="peaks",
    )(*spectra, twiddles, noise_level)


def body(
    flaw_cells,
    flaw_blocks,
    element_channel,
    focal_delay,
    beam_field,
    flaw_size,
    flaw_slope,
    noise_level,
):
    freq_count = lax.axis_size("freq")
    freq_total = W_DEV * freq_count
    sample_count = min(T_CAP, 2 * freq_total)
    swap = [(0, 1), (1, 0)]
    direct = freq_count == 8
    slots = freq_count if direct else 1
    small = (
        focal_delay,
        element_channel.reshape(1, -1),
        flaw_blocks,
        flaw_cells.reshape(1, -1),
        flaw_size,
        flaw_slope,
    )
    folded = sample_count == 2 * freq_total
    times = sample_count // 2 if folded else sample_count
    twiddles = table(freq_total, slots, times, min(128, times))
    field = beam_field.reshape(W_HALF, 2, *beam_field.shape[1:])
    parts = add(*partials(field, small, swap, freq_total, slots), slots)
    if direct:
        half = slots // 2
        spectra = []
        for slot, masks in enumerate(zip(*slot_masks(slots))):
            pairs = [(a, a ^ masks[((2 * a) ^ a) & half != 0]) for a in range(slots)]
            spectra.append(lax.ppermute(parts[slot], "freq", pairs) if slot else parts[slot])
        spectra = [*spectra[1:], spectra[0]]
        sources = [((slot - 1) % slots, 0) for slot in range(slots)]
    else:
        spectra = [
            lax.all_to_all(parts[0], "freq", split_axis=0, concat_axis=0, tiled=True)
        ]
        sources = [(0, s * (FG // freq_count)) for s in range(freq_count)]
    return tuple(peaks(spectra, sources, twiddles, noise_level, freq_total, folded))


def solution(mesh):
    in_specs = (
        P("batch"),
        P("batch"),
        P("elem"),
        P(),
        P("freq", None, "elem", None),
        P("batch", None),
        P("batch", None),
        P(("batch", "elem"), "freq"),
    )
    out_specs = (P(("batch", "elem"), "freq"), P(("batch", "elem"), "freq"))
    return jax.shard_map(body, mesh=mesh, in_specs=in_specs, out_specs=out_specs, check_vma=False)
```

```python
import functools
import math

import jax
import jax.numpy as jnp
from jax import lax
from jax.experimental import pallas as pl
from jax.experimental.pallas import tpu as pltpu
from jax.sharding import PartitionSpec as P

W_DEV = 16
W_HALF = W_DEV // 2
FG = 128
NB = 4
SB = 32
T_CAP = 1024

EDGE = 0.6
STEEP = 3.0
EPS = 1e-05

ROWS = NB * SB
VMEM_BYTES = 48 * 1024 * 1024


def sin_half_turn(turns):
    angle = turns * math.pi
    square = angle * angle
    sine = 1.0 / 6227020800.0
    for factorial in (-39916800.0, 362880.0, -5040.0, 120.0, -6.0, 1.0):
        sine = sine * square + 1.0 / factorial
    cosine = 1.0 / 479001600.0
    for factorial in (-3628800.0, 40320.0, -720.0, 24.0, -2.0, 1.0):
        cosine = cosine * square + 1.0 / factorial
    return sine * angle, cosine


def sincos_turns(turns):
    rest = turns - jnp.floor(turns + 0.5)
    sine, cosine = sin_half_turn(rest)
    return 2.0 * sine * cosine, 1.0 - 2.0 * sine * sine


def dot(left, right, contract):
    return lax.dot_general(
        left, right, (contract, ((), ())), preferred_element_type=jnp.float32
    )


def slot_masks(slots):
    half = slots // 2
    first, then = (half, 2), (half + 1, slots - 1, 3)
    return (0, *first, 1, *then, slots - 2), (0, *first, slots - 2, *then, 1)


def partner(slots, slot):
    index = lax.axis_index("freq")
    inner = ((index * 2) ^ index) & (slots // 2) != 0
    outer_masks, inner_masks = slot_masks(slots)
    mask = jnp.zeros_like(slot)
    for s in range(1, slots):
        mask = jnp.where(slot == s, jnp.where(inner, inner_masks[s], outer_masks[s]), mask)
    return mask ^ index


def slot_order(slots):
    size = FG // slots
    row = lax.broadcasted_iota(jnp.int32, (FG, 1), 0)
    column = lax.broadcasted_iota(jnp.int32, (FG, FG), 1)
    if slots > 1:
        row = partner(slots, row // size) * size + row % size
    return row == column


def flaw_pick(slots, which, cells_ref):
    cells = jnp.where(which == 0, cells_ref[:, :FG], cells_ref[:, FG:])
    cell_sel = lax.broadcasted_iota(jnp.int32, (cells_ref.shape[1], FG), 0) == cells
    return dot(
        slot_order(slots).astype(jnp.bfloat16), cell_sel.astype(jnp.bfloat16), ((1,), (1,))
    ).astype(jnp.bfloat16)


def delays_of(channel_ref, delay_ref, blocks_ref, groups, elements):
    lane = lax.broadcasted_iota(jnp.int32, (1, 2 * ROWS), 1)
    position = lane & (SB - 1)
    for j in range(2 * NB):
        block = blocks_ref[groups[j // NB] * NB + j % NB]
        position = position + jnp.where((lane >> 5) == j, block * SB, 0)
    channels, positions = delay_ref.shape
    scan_sel = (
        lax.broadcasted_iota(jnp.int32, (positions, 2 * ROWS), 0) == position
    ).astype(jnp.bfloat16)
    channel_sel = (
        (lax.broadcasted_iota(jnp.int32, (channels, elements), 0) == channel_ref[...])
        .astype(jnp.float32)
        .T.astype(jnp.bfloat16)
    )
    rest = delay_ref[...]
    pieces = []
    for _ in range(3):
        pieces.append(rest.astype(jnp.bfloat16))
        rest = rest - pieces[-1].astype(jnp.float32)
    moved = jnp.concatenate(
        [dot(channel_sel, piece, ((1,), (0,))).astype(jnp.bfloat16) for piece in pieces], axis=0
    )
    moved = dot(moved, scan_sel, ((1,), (0,)))
    return moved[:elements] + moved[elements : 2 * elements] + moved[2 * elements :]


def turned(law, step):
    return law[0] * step[0] - law[1] * step[1], law[1] * step[0] + law[0] * step[1]


def focal_base(freq_total, delays):
    first_freq = lax.axis_index("freq") * W_DEV
    phase = delays * (0.5 / freq_total)
    unit = sincos_turns(phase)[::-1]
    base = sincos_turns(phase * first_freq.astype(jnp.float32))[::-1]
    return base, turned(unit, unit), turned(base, unit)


def kirchhoff(freq_total, slots, which, size_ref, slope_ref):
    first_freq = lax.axis_index("freq") * W_DEV
    order = slot_order(slots)
    size = size_ref[pl.ds(which, 1), :]
    turn = size * slope_ref[pl.ds(which, 1), :] * (1.0 / freq_total)
    size = jnp.sum(jnp.where(order, size, 0.0), axis=1, keepdims=True)
    turn = jnp.sum(jnp.where(order, turn, 0.0), axis=1, keepdims=True)
    freq = first_freq + lax.broadcasted_iota(jnp.int32, (FG, FG), 1)
    sine, cosine = sincos_turns(turn * freq.astype(jnp.float32))
    return size * (1.0 + EDGE) * cosine, size * (EDGE - 1.0) * sine


def store_law(law_ref, law, step):
    elements = law_ref.shape[1] // 2
    for w in range(W_HALF):
        c = law[0].astype(jnp.bfloat16)
        s = law[1].astype(jnp.bfloat16)
        law_ref[w, :elements, :ROWS] = c
        law_ref[w, :elements, ROWS:] = -s
        law_ref[w, elements:, :ROWS] = s
        law_ref[w, elements:, ROWS:] = c
        if w < W_HALF - 1:
            law = turned(law, step)


def pick_fields(parity, picks, field_ref, wait, picked_refs):
    elements, sites = field_ref.shape[3:]
    for w in range(W_HALF):
        wait(w)
        picked = dot(
            picks, field_ref[w, parity].reshape(2 * elements, sites), ((1,), (1,))
        ).astype(jnp.bfloat16)
        for i, ref in enumerate(picked_refs):
            ref[w] = picked[i * FG : (i + 1) * FG]


def store_spectra(parity, picked_ref, law_ref, k_real, k_imag, out_ref, first):
    for w in range(W_HALF):
        product = dot(picked_ref[w], law_ref[w], ((1,), (0,)))
        real_part = product[:, :ROWS]
        imag_part = product[:, ROWS:]
        kr = k_real[:, 2 * w + parity : 2 * w + parity + 1]
        ki = k_imag[:, 2 * w + parity : 2 * w + parity + 1]
        out_ref[first + 2 * w] = (kr * real_part - ki * imag_part).astype(jnp.bfloat16)
        out_ref[first + 2 * w + 1] = (kr * imag_part + ki * real_part).astype(jnp.bfloat16)


def other_even_kernel(freq_total, slots, *refs):
    field_hbm, *small_hbm = refs[:7]
    out_ref, own_picked_ref, field_ref, size_ref, slope_ref, *kept = refs[7:20]
    delay_ref, channel_ref, blocks_ref, cells_ref = refs[20:24]
    field_sem, small_sem, *scratch = refs[24:]
    small = (delay_ref, channel_ref, blocks_ref, cells_ref, size_ref, slope_ref)
    picked_ref, law_ref = scratch
    copies = [
        pltpu.make_async_copy(source, target, small_sem.at[i])
        for i, (source, target) in enumerate(zip(small_hbm, small))
    ]
    for copy in copies:
        copy.start()
    part = W_HALF // 2
    field_copies = [
        pltpu.make_async_copy(
            field_hbm.at[pl.ds(i * part, part), parity],
            field_ref.at[pl.ds(i * part, part), parity],
            field_sem.at[parity, i],
        )
        for parity in range(2)
        for i in range(2)
    ]
    for copy in field_copies:
        copy.start()
    for copy in copies:
        copy.wait()
    group = lax.axis_index("elem")
    groups = (1 - group, group)
    picks = jnp.concatenate(
        [flaw_pick(slots, which, cells_ref) for which in groups], axis=0
    )
    factors = kirchhoff(freq_total, slots, groups[0], size_ref, slope_ref)
    delays = delays_of(channel_ref, delay_ref, blocks_ref, groups, field_ref.shape[3])
    even, step, odd = focal_base(freq_total, delays[:, :ROWS])
    values = (picks, *step, *odd, *factors, delays[:, ROWS:])
    for ref, value in zip(kept, values):
        ref[...] = value
    store_law(law_ref, even, step)

    def wait(w):
        if w % part == 0:
            field_copies[w // part].wait()

    pick_fields(0, picks, field_ref, wait, (picked_ref, own_picked_ref))
    store_spectra(0, picked_ref, law_ref, *factors, out_ref, 0)
    for copy in field_copies[2:]:
        copy.wait()


def other_odd_kernel(field_ref, picks_ref, *refs):
    step, odd, k_refs = refs[:2], refs[2:4], refs[4:6]
    out_ref, own_picked_ref, picked_ref, law_ref = refs[6:]
    store_law(law_ref, [ref[...] for ref in odd], [ref[...] for ref in step])
    pick_fields(
        1, picks_ref[...], field_ref, lambda w: None, (picked_ref, own_picked_ref)
    )
    store_spectra(1, picked_ref, law_ref, *k_refs, out_ref, 0)


def own_kernel(freq_total, slots, *refs):
    picked_refs, (delays_ref, size_ref, slope_ref, out_ref, law_ref) = refs[:2], refs[2:]
    even, step, odd = focal_base(freq_total, delays_ref[...])
    for parity, law in enumerate((even, odd)):
        store_law(law_ref.at[parity], law, step)
    group = lax.axis_index("elem")
    factors = kirchhoff(freq_total, slots, group, size_ref, slope_ref)
    for parity in range(2):
        store_spectra(
            parity, picked_refs[parity], law_ref.at[parity], *factors, out_ref, parity * W_DEV
        )


def call(kernel, name, in_specs, out_shape, scratch):
    vmem = pl.BlockSpec(memory_space=pltpu.VMEM)
    return pl.pallas_call(
        kernel,
        in_specs=in_specs,
        out_specs=[vmem] * len(out_shape),
        out_shape=out_shape,
        scratch_shapes=scratch,
        compiler_params=pltpu.CompilerParams(vmem_limit_bytes=VMEM_BYTES),
        cost_estimate=pl.CostEstimate(flops=1000, bytes_accessed=1000, transcendentals=0),
        name=name,
    )


def partials(field, small, swap, freq_total, slots):
    elements, sites = field.shape[3:]
    vmem = pl.BlockSpec(memory_space=pltpu.VMEM)
    hbm = pl.BlockSpec(memory_space=pltpu.HBM)
    pinned = [pltpu.with_memory_space_constraint(a, pltpu.HBM) for a in (field, *small)]
    out = jax.ShapeDtypeStruct((W_DEV, FG, ROWS), jnp.bfloat16)
    picked = jax.ShapeDtypeStruct((W_HALF, FG, 2 * elements), jnp.bfloat16)
    law = (W_HALF, 2 * elements, 2 * ROWS)
    base = [jax.ShapeDtypeStruct((elements, ROWS), jnp.float32)] * 2
    factors = [jax.ShapeDtypeStruct((FG, FG), jnp.float32)] * 2
    kept = [jax.ShapeDtypeStruct((2 * FG, sites), jnp.bfloat16), *base, *base, *factors]
    copied = [jax.ShapeDtypeStruct(a.shape, a.dtype) for a in (field, *small[4:])]
    work = [pltpu.VMEM(picked.shape, picked.dtype), pltpu.VMEM(law, jnp.bfloat16)]
    even, even_picked, field, size, slope, *kept, delays = call(
        functools.partial(other_even_kernel, freq_total, slots),
        "other_even",
        [hbm] * len(pinned),
        [out, picked, *copied, *kept, base[0]],
        [
            pltpu.SMEM(a.shape, a.dtype) if a.ndim == 1 else pltpu.VMEM(a.shape, a.dtype)
            for a in small[:4]
        ]
        + [pltpu.SemaphoreType.DMA((2, 2)), pltpu.SemaphoreType.DMA((len(small),)), *work],
    )(*pinned)
    even = lax.ppermute(even, "elem", swap)
    odd, odd_picked = call(
        other_odd_kernel, "other_odd", [vmem] * 8, [out, picked], work
    )(field, *kept)
    odd = lax.ppermute(odd, "elem", swap)
    (own,) = call(
        functools.partial(own_kernel, freq_total, slots),
        "own",
        [vmem] * 5,
        [jax.ShapeDtypeStruct((2 * W_DEV, FG, ROWS), jnp.bfloat16)],
        [pltpu.VMEM((2, *law), jnp.bfloat16)],
    )(even_picked, odd_picked, delays, size, slope)
    return own, even, odd


def total(own_ref, moved_ref, parity, rows):
    own = own_ref[parity * W_DEV : (parity + 1) * W_DEV, rows]
    both = own.astype(jnp.float32) + moved_ref[:, rows].astype(jnp.float32)
    return jnp.swapaxes(both, 0, 1).astype(jnp.bfloat16)


def add_even_kernel(size, own_ref, even_ref, held_ref):
    for first in range(0, held_ref.shape[0], size):
        rows = pl.ds(first, size)
        held_ref[rows] = total(own_ref, even_ref, 0, rows)


def add_odd_kernel(own_ref, odd_ref, held_ref, *refs):
    size = refs[0].shape[0]
    for slot, ref in enumerate(refs):
        rows = pl.ds(slot * size, size)
        ref[:, :W_DEV] = held_ref[rows]
        ref[:, W_DEV:] = total(own_ref, odd_ref, 1, rows)


def add(own, even, odd, slots):
    vmem = pl.BlockSpec(memory_space=pltpu.VMEM)
    planes, flaws, rows = own.shape
    size = flaws // slots
    shape = jax.ShapeDtypeStruct((flaws, planes // 2, rows), own.dtype)
    kernel = functools.partial(add_even_kernel, min(size, 16))
    (held,) = call(kernel, "add_even", [vmem] * 2, [shape], [])(own, even)
    shapes = [jax.ShapeDtypeStruct((size, planes, rows), own.dtype)] * slots
    return call(add_odd_kernel, "add_odd", [vmem] * 3, shapes, [])(own, odd, held)


def table_kernel(freq_total, slots, table_ref):
    height, depth = table_ref.shape[2:]
    time_block = height // 2
    row = lax.broadcasted_iota(jnp.int32, (height, depth // 2), 0)
    column = lax.broadcasted_iota(jnp.int32, (height, depth // 2), 1)
    out_imag = (row >= time_block).astype(jnp.int32)
    time = pl.program_id(0) * time_block + row - out_imag * time_block
    for parity in range(2):
        freq = (column >> 1) * 2 + parity
        if slots > 1:
            lane = lax.broadcasted_iota(jnp.int32, (1, depth // 2), 1)
            lane = (lane >> 1) * 2 + parity
            freq = partner(slots, lane // W_DEV) * W_DEV + lane % W_DEV
        steps = freq * time + ((column & 1) - out_imag) * (freq_total // 2)
        steps = (steps + 2 * freq_total) & (2 * freq_total - 1)
        _, value = sincos_turns(steps.astype(jnp.float32) * (0.5 / freq_total))
        high = value.astype(jnp.bfloat16)
        table_ref[0, parity, :, : depth // 2] = high
        table_ref[0, parity, :, depth // 2 :] = (
            value - high.astype(jnp.float32)
        ).astype(jnp.bfloat16)


def table(freq_total, slots, times, time_block):
    blocks = times // time_block
    shape = (blocks, 2, 2 * time_block, 2 * freq_total)
    return pl.pallas_call(
        functools.partial(table_kernel, freq_total, slots),
        grid=(blocks,),
        out_specs=pl.BlockSpec((1, *shape[1:]), lambda i: (i, 0, 0, 0)),
        out_shape=jax.ShapeDtypeStruct(shape, jnp.bfloat16),
        compiler_params=pltpu.CompilerParams(vmem_limit_bytes=VMEM_BYTES),
        name="table",
    )()


def peak_kernel(freq_total, folded, sources, blocks, *refs):
    def first_step():
        return blocks == 1 or pl.program_id(0) == 0

    def last_step():
        return blocks == 1 or pl.program_id(0) == blocks - 1

    count = len(refs) - 5
    table_ref, noise_ref, peak_ref, found_ref, best_ref = refs[count:]
    columns = peak_ref.shape[1]
    time_block = table_ref.shape[2] // 2

    @pl.when(first_step())
    def _():
        best_ref[...] = jnp.zeros_like(best_ref)

    width = min(2, columns)
    for first in range(0, columns, width):
        parts = []
        for parity in range(2):
            planes = slice(parity * W_DEV, (parity + 1) * W_DEV)
            spectra = jnp.concatenate(
                [
                    jnp.concatenate(
                        [
                            refs[i][row + first + k, planes, :]
                            for i, row in sources
                        ]
                        * 2,
                        axis=0,
                    )
                    for k in range(width)
                ],
                axis=1,
            )
            parts.append(dot(table_ref[0, parity], spectra, ((1,), (0,))))
        powers = []
        for signal in [parts[0] + parts[1]] + [parts[0] - parts[1]] * folded:
            real_part = signal[:time_block]
            imag_part = signal[time_block:]
            powers.append(real_part * real_part + imag_part * imag_part)
        power = jnp.maximum(powers[0], powers[-1]) if folded else powers[0]
        power = jnp.max(power, axis=0, keepdims=True)
        for k in range(width):
            row = pl.ds(first + k, 1)
            best_ref[row, :] = jnp.maximum(
                best_ref[row, :], power[:, k * ROWS : (k + 1) * ROWS]
            )

    @pl.when(last_step())
    def _():
        largest = jnp.max(best_ref[...], axis=1, keepdims=True)
        shape = best_ref.shape
        diagonal = lax.broadcasted_iota(jnp.int32, shape, 0) == lax.broadcasted_iota(
            jnp.int32, shape, 1
        )
        largest = jnp.max(jnp.where(diagonal, largest, 0.0), axis=0, keepdims=True)
        peak = jnp.sqrt(largest[:, :columns]) * (1.0 / math.sqrt(freq_total))
        score = STEEP * (jnp.log(peak + EPS) - jnp.log(noise_ref[...]))
        peak_ref[...] = peak
        found_ref[...] = 1.0 / (1.0 + jnp.exp(-score))


def peaks(spectra, sources, twiddles, noise_level, freq_total, folded):
    columns = noise_level.shape[1]
    blocks = twiddles.shape[0]
    if blocks == 1:
        vmem = pl.BlockSpec(memory_space=pltpu.VMEM)
        grid, in_specs, out_spec = (), [vmem] * (len(spectra) + 2), vmem
    else:
        grid = (blocks,)
        out_spec = pl.BlockSpec((1, columns), lambda i: (0, 0))
        in_specs = [pl.BlockSpec(a.shape, lambda i: (0, 0, 0)) for a in spectra]
        in_specs += [
            pl.BlockSpec((1, *twiddles.shape[1:]), lambda i: (i, 0, 0, 0)),
            out_spec,
        ]
    return pl.pallas_call(
        functools.partial(peak_kernel, freq_total, folded, sources, blocks),
        grid=grid,
        in_specs=in_specs,
        out_specs=[out_spec, out_spec],
        out_shape=[jax.ShapeDtypeStruct((1, columns), jnp.float32)] * 2,
        scratch_shapes=[pltpu.VMEM((max(8, columns), ROWS), jnp.float32)],
        compiler_params=pltpu.CompilerParams(vmem_limit_bytes=VMEM_BYTES),
        name="peaks",
    )(*spectra, twiddles, noise_level)


def body(
    flaw_cells,
    flaw_blocks,
    element_channel,
    focal_delay,
    beam_field,
    flaw_size,
    flaw_slope,
    noise_level,
):
    freq_count = lax.axis_size("freq")
    freq_total = W_DEV * freq_count
    sample_count = min(T_CAP, 2 * freq_total)
    swap = [(0, 1), (1, 0)]
    direct = freq_count == 8
    slots = freq_count if direct else 1
    small = (
        focal_delay,
        element_channel.reshape(1, -1),
        flaw_blocks,
        flaw_cells.reshape(1, -1),
        flaw_size,
        flaw_slope,
    )
    folded = sample_count == 2 * freq_total
    times = sample_count // 2 if folded else sample_count
    twiddles = table(freq_total, slots, times, min(128, times))
    field = beam_field.reshape(W_HALF, 2, *beam_field.shape[1:])
    parts = add(*partials(field, small, swap, freq_total, slots), slots)
    if direct:
        half = slots // 2
        spectra = []
        for slot, masks in enumerate(zip(*slot_masks(slots))):
            pairs = [(a, a ^ masks[((2 * a) ^ a) & half != 0]) for a in range(slots)]
            spectra.append(lax.ppermute(parts[slot], "freq", pairs) if slot else parts[slot])
        spectra = [*spectra[1:], spectra[0]]
        sources = [((slot - 1) % slots, 0) for slot in range(slots)]
    else:
        spectra = [
            lax.all_to_all(parts[0], "freq", split_axis=0, concat_axis=0, tiled=True)
        ]
        sources = [(0, s * (FG // freq_count)) for s in range(freq_count)]
    return tuple(peaks(spectra, sources, twiddles, noise_level, freq_total, folded))


def solution(mesh):
    in_specs = (
        P("batch"),
        P("batch"),
        P("elem"),
        P(),
        P("freq", None, "elem", None),
        P("batch", None),
        P("batch", None),
        P(("batch", "elem"), "freq"),
    )
    out_specs = (P(("batch", "elem"), "freq"), P(("batch", "elem"), "freq"))
    return jax.shard_map(body, mesh=mesh, in_specs=in_specs, out_specs=out_specs, check_vma=False)
```

```python
import functools
import math

import jax
import jax.numpy as jnp
from jax import lax
from jax.experimental import pallas as pl
from jax.experimental.pallas import tpu as pltpu
from jax.sharding import PartitionSpec as P

W_DEV = 16
W_HALF = W_DEV // 2
FG = 128
NB = 4
SB = 32
T_CAP = 1024

EDGE = 0.6
STEEP = 3.0
EPS = 1e-05

ROWS = NB * SB
VMEM_BYTES = 48 * 1024 * 1024


def sin_half_turn(turns):
    angle = turns * math.pi
    square = angle * angle
    sine = 1.0 / 6227020800.0
    for factorial in (-39916800.0, 362880.0, -5040.0, 120.0, -6.0, 1.0):
        sine = sine * square + 1.0 / factorial
    cosine = 1.0 / 479001600.0
    for factorial in (-3628800.0, 40320.0, -720.0, 24.0, -2.0, 1.0):
        cosine = cosine * square + 1.0 / factorial
    return sine * angle, cosine


def sincos_turns(turns):
    rest = turns - jnp.floor(turns + 0.5)
    sine, cosine = sin_half_turn(rest)
    return 2.0 * sine * cosine, 1.0 - 2.0 * sine * sine


def dot(left, right, contract):
    return lax.dot_general(
        left, right, (contract, ((), ())), preferred_element_type=jnp.float32
    )


def slot_masks(slots):
    half = slots // 2
    between = (2, half, half + 1, 3, slots - 1)
    return (0, 1, *between, slots - 2), (0, slots - 2, *between, 1)


def partner(slots, slot):
    index = lax.axis_index("freq")
    inner = ((index * 2) ^ index) & (slots // 2) != 0
    outer_masks, inner_masks = slot_masks(slots)
    mask = jnp.zeros_like(slot)
    for s in range(1, slots):
        mask = jnp.where(slot == s, jnp.where(inner, inner_masks[s], outer_masks[s]), mask)
    return mask ^ index


def slot_order(slots):
    size = FG // slots
    row = lax.broadcasted_iota(jnp.int32, (FG, 1), 0)
    column = lax.broadcasted_iota(jnp.int32, (FG, FG), 1)
    if slots > 1:
        row = partner(slots, row // size) * size + row % size
    return row == column


def flaw_pick(order, which, cells_ref):
    cells = jnp.where(which == 0, cells_ref[:, :FG], cells_ref[:, FG:])
    cell_sel = lax.broadcasted_iota(jnp.int32, (cells_ref.shape[1], FG), 0) == cells
    return dot(
        order.astype(jnp.bfloat16), cell_sel.astype(jnp.bfloat16), ((1,), (1,))
    ).astype(jnp.bfloat16)


def delays_of(channel_ref, delay_ref, blocks_ref, groups, elements):
    lane = lax.broadcasted_iota(jnp.int32, (1, 2 * ROWS), 1)
    position = lane & (SB - 1)
    for j in range(2 * NB):
        block = blocks_ref[groups[j // NB] * NB + j % NB]
        position = position + jnp.where((lane >> 5) == j, block * SB, 0)
    channels, positions = delay_ref.shape
    scan_sel = (
        lax.broadcasted_iota(jnp.int32, (positions, 2 * ROWS), 0) == position
    ).astype(jnp.bfloat16)
    channel_sel = (
        (lax.broadcasted_iota(jnp.int32, (channels, elements), 0) == channel_ref[...])
        .astype(jnp.float32)
        .T.astype(jnp.bfloat16)
    )
    rest = delay_ref[...]
    pieces = []
    for _ in range(3):
        pieces.append(rest.astype(jnp.bfloat16))
        rest = rest - pieces[-1].astype(jnp.float32)
    moved = jnp.concatenate(
        [dot(channel_sel, piece, ((1,), (0,))).astype(jnp.bfloat16) for piece in pieces], axis=0
    )
    moved = dot(moved, scan_sel, ((1,), (0,)))
    return moved[:elements] + moved[elements : 2 * elements] + moved[2 * elements :]


def turned(law, step):
    return law[0] * step[0] - law[1] * step[1], law[1] * step[0] + law[0] * step[1]


def focal_base(freq_total, delays):
    first_freq = lax.axis_index("freq") * W_DEV
    phase = delays * (0.5 / freq_total)
    unit = sincos_turns(phase)[::-1]
    base = sincos_turns(phase * first_freq.astype(jnp.float32))[::-1]
    return base, turned(unit, unit), turned(base, unit)


def kirchhoff(freq_total, order, which, size_ref, slope_ref):
    first_freq = lax.axis_index("freq") * W_DEV
    size = size_ref[pl.ds(which, 1), :]
    turn = size * slope_ref[pl.ds(which, 1), :] * (1.0 / freq_total)
    size = jnp.sum(jnp.where(order, size, 0.0), axis=1, keepdims=True)
    turn = jnp.sum(jnp.where(order, turn, 0.0), axis=1, keepdims=True)
    freq = first_freq + lax.broadcasted_iota(jnp.int32, (FG, FG), 1)
    sine, cosine = sincos_turns(turn * freq.astype(jnp.float32))
    return size * (1.0 + EDGE) * cosine, size * (EDGE - 1.0) * sine


def store_law(law_ref, law, step):
    elements = law_ref.shape[1] // 2
    for w in range(W_HALF):
        c = law[0].astype(jnp.bfloat16)
        s = law[1].astype(jnp.bfloat16)
        law_ref[w, :elements, :ROWS] = c
        law_ref[w, :elements, ROWS:] = -s
        law_ref[w, elements:, :ROWS] = s
        law_ref[w, elements:, ROWS:] = c
        if w < W_HALF - 1:
            law = turned(law, step)


def pick_fields(parity, picks, field_ref, picked_refs):
    elements, sites = field_ref.shape[3:]
    for w in range(W_HALF):
        picked = dot(
            picks, field_ref[w, parity].reshape(2 * elements, sites), ((1,), (1,))
        ).astype(jnp.bfloat16)
        for i, ref in enumerate(picked_refs):
            ref[w] = picked[i * FG : (i + 1) * FG]


def store_spectra(parity, picked_ref, law_ref, k_real, k_imag, out_ref, first):
    for w in range(W_HALF):
        product = dot(picked_ref[w], law_ref[w], ((1,), (0,)))
        real_part = product[:, :ROWS]
        imag_part = product[:, ROWS:]
        kr = k_real[:, 2 * w + parity : 2 * w + parity + 1]
        ki = k_imag[:, 2 * w + parity : 2 * w + parity + 1]
        out_ref[first + 2 * w] = (kr * real_part - ki * imag_part).astype(jnp.bfloat16)
        out_ref[first + 2 * w + 1] = (kr * imag_part + ki * real_part).astype(jnp.bfloat16)


def other_even_kernel(freq_total, slots, *refs):
    field_hbm, *small_hbm = refs[:7]
    out_ref, own_picked_ref, field_ref, size_ref, slope_ref, *kept = refs[7:20]
    delay_ref, channel_ref, blocks_ref, cells_ref = refs[20:24]
    field_sem, small_sem, *scratch = refs[24:]
    small = (delay_ref, channel_ref, blocks_ref, cells_ref, size_ref, slope_ref)
    picked_ref, law_ref = scratch
    copies = [
        pltpu.make_async_copy(source, target, small_sem.at[i])
        for i, (source, target) in enumerate(zip(small_hbm, small))
    ]
    for copy in copies:
        copy.start()
    field_copies = [
        pltpu.make_async_copy(
            field_hbm.at[:, parity], field_ref.at[:, parity], field_sem.at[parity]
        )
        for parity in range(2)
    ]
    for copy in field_copies:
        copy.start()
    order = slot_order(slots)
    for copy in copies:
        copy.wait()
    group = lax.axis_index("elem")
    groups = (1 - group, group)
    picks = jnp.concatenate(
        [flaw_pick(order, which, cells_ref) for which in groups], axis=0
    )
    factors = kirchhoff(freq_total, order, groups[0], size_ref, slope_ref)
    delays = delays_of(channel_ref, delay_ref, blocks_ref, groups, field_ref.shape[3])
    even, step, odd = focal_base(freq_total, delays[:, :ROWS])
    values = (picks, *step, *odd, *factors, delays[:, ROWS:])
    for ref, value in zip(kept, values):
        ref[...] = value
    store_law(law_ref, even, step)

    field_copies[0].wait()
    pick_fields(0, picks, field_ref, (picked_ref, own_picked_ref))
    store_spectra(0, picked_ref, law_ref, *factors, out_ref, 0)
    field_copies[1].wait()


def other_odd_kernel(field_ref, picks_ref, *refs):
    step, odd, k_refs = refs[:2], refs[2:4], refs[4:6]
    out_ref, own_picked_ref, picked_ref, law_ref = refs[6:]
    store_law(law_ref, [ref[...] for ref in odd], [ref[...] for ref in step])
    pick_fields(1, picks_ref[...], field_ref, (picked_ref, own_picked_ref))
    store_spectra(1, picked_ref, law_ref, *k_refs, out_ref, 0)


def own_kernel(freq_total, slots, *refs):
    picked_refs, (delays_ref, size_ref, slope_ref, out_ref, law_ref) = refs[:2], refs[2:]
    even, step, odd = focal_base(freq_total, delays_ref[...])
    for parity, law in enumerate((even, odd)):
        store_law(law_ref.at[parity], law, step)
    group = lax.axis_index("elem")
    factors = kirchhoff(freq_total, slot_order(slots), group, size_ref, slope_ref)
    for parity in range(2):
        store_spectra(
            parity, picked_refs[parity], law_ref.at[parity], *factors, out_ref, parity * W_DEV
        )


def call(kernel, name, in_specs, out_shape, scratch):
    vmem = pl.BlockSpec(memory_space=pltpu.VMEM)
    return pl.pallas_call(
        kernel,
        in_specs=in_specs,
        out_specs=[vmem] * len(out_shape),
        out_shape=out_shape,
        scratch_shapes=scratch,
        compiler_params=pltpu.CompilerParams(vmem_limit_bytes=VMEM_BYTES),
        cost_estimate=pl.CostEstimate(flops=1000, bytes_accessed=1000, transcendentals=0),
        name=name,
    )


def partials(field, small, swap, freq_total, slots):
    elements, sites = field.shape[3:]
    vmem = pl.BlockSpec(memory_space=pltpu.VMEM)
    hbm = pl.BlockSpec(memory_space=pltpu.HBM)
    pinned = [pltpu.with_memory_space_constraint(a, pltpu.HBM) for a in (field, *small)]
    out = jax.ShapeDtypeStruct((W_DEV, FG, ROWS), jnp.bfloat16)
    picked = jax.ShapeDtypeStruct((W_HALF, FG, 2 * elements), jnp.bfloat16)
    law = (W_HALF, 2 * elements, 2 * ROWS)
    base = [jax.ShapeDtypeStruct((elements, ROWS), jnp.float32)] * 2
    factors = [jax.ShapeDtypeStruct((FG, FG), jnp.float32)] * 2
    kept = [jax.ShapeDtypeStruct((2 * FG, sites), jnp.bfloat16), *base, *base, *factors]
    copied = [jax.ShapeDtypeStruct(a.shape, a.dtype) for a in (field, *small[4:])]
    work = [pltpu.VMEM(picked.shape, picked.dtype), pltpu.VMEM(law, jnp.bfloat16)]
    even, even_picked, field, size, slope, *kept, delays = call(
        functools.partial(other_even_kernel, freq_total, slots),
        "other_even",
        [hbm] * len(pinned),
        [out, picked, *copied, *kept, base[0]],
        [
            pltpu.SMEM(a.shape, a.dtype) if a.ndim == 1 else pltpu.VMEM(a.shape, a.dtype)
            for a in small[:4]
        ]
        + [pltpu.SemaphoreType.DMA((2,)), pltpu.SemaphoreType.DMA((len(small),)), *work],
    )(*pinned)
    even = lax.ppermute(even, "elem", swap)
    odd, odd_picked = call(
        other_odd_kernel, "other_odd", [vmem] * 8, [out, picked], work
    )(field, *kept)
    odd = lax.ppermute(odd, "elem", swap)
    (own,) = call(
        functools.partial(own_kernel, freq_total, slots),
        "own",
        [vmem] * 5,
        [jax.ShapeDtypeStruct((2 * W_DEV, FG, ROWS), jnp.bfloat16)],
        [pltpu.VMEM((2, *law), jnp.bfloat16)],
    )(even_picked, odd_picked, delays, size, slope)
    return own, even, odd


def total(own_ref, moved_ref, parity, rows):
    own = own_ref[parity * W_DEV : (parity + 1) * W_DEV, rows]
    both = own.astype(jnp.float32) + moved_ref[:, rows].astype(jnp.float32)
    return jnp.swapaxes(both, 0, 1).astype(jnp.bfloat16)


def add_even_kernel(size, own_ref, even_ref, held_ref):
    for first in range(0, held_ref.shape[0], size):
        rows = pl.ds(first, size)
        held_ref[rows] = total(own_ref, even_ref, 0, rows)


def add_odd_kernel(own_ref, odd_ref, held_ref, *refs):
    size = refs[0].shape[0]
    for slot, ref in enumerate(refs):
        rows = pl.ds(slot * size, size)
        ref[:, :W_DEV] = held_ref[rows]
        ref[:, W_DEV:] = total(own_ref, odd_ref, 1, rows)


def add(own, even, odd, slots):
    vmem = pl.BlockSpec(memory_space=pltpu.VMEM)
    planes, flaws, rows = own.shape
    size = flaws // slots
    shape = jax.ShapeDtypeStruct((flaws, planes // 2, rows), own.dtype)
    kernel = functools.partial(add_even_kernel, min(size, 16))
    (held,) = call(kernel, "add_even", [vmem] * 2, [shape], [])(own, even)
    shapes = [jax.ShapeDtypeStruct((size, planes, rows), own.dtype)] * slots
    return call(add_odd_kernel, "add_odd", [vmem] * 3, shapes, [])(own, odd, held)


def table_kernel(freq_total, slots, table_ref):
    height, depth = table_ref.shape[2:]
    time_block = height // 2
    row = lax.broadcasted_iota(jnp.int32, (height, depth // 2), 0)
    column = lax.broadcasted_iota(jnp.int32, (height, depth // 2), 1)
    out_imag = (row >= time_block).astype(jnp.int32)
    time = pl.program_id(0) * time_block + row - out_imag * time_block
    for parity in range(2):
        freq = (column >> 1) * 2 + parity
        if slots > 1:
            lane = lax.broadcasted_iota(jnp.int32, (1, depth // 2), 1)
            lane = (lane >> 1) * 2 + parity
            freq = partner(slots, lane // W_DEV) * W_DEV + lane % W_DEV
        steps = freq * time + ((column & 1) - out_imag) * (freq_total // 2)
        steps = (steps + 2 * freq_total) & (2 * freq_total - 1)
        _, value = sincos_turns(steps.astype(jnp.float32) * (0.5 / freq_total))
        high = value.astype(jnp.bfloat16)
        table_ref[0, parity, :, : depth // 2] = high
        table_ref[0, parity, :, depth // 2 :] = (
            value - high.astype(jnp.float32)
        ).astype(jnp.bfloat16)


def table(freq_total, slots, times, time_block):
    blocks = times // time_block
    shape = (blocks, 2, 2 * time_block, 2 * freq_total)
    return pl.pallas_call(
        functools.partial(table_kernel, freq_total, slots),
        grid=(blocks,),
        out_specs=pl.BlockSpec((1, *shape[1:]), lambda i: (i, 0, 0, 0)),
        out_shape=jax.ShapeDtypeStruct(shape, jnp.bfloat16),
        compiler_params=pltpu.CompilerParams(vmem_limit_bytes=VMEM_BYTES),
        name="table",
    )()


def peak_kernel(freq_total, folded, sources, blocks, *refs):
    def first_step():
        return blocks == 1 or pl.program_id(0) == 0

    def last_step():
        return blocks == 1 or pl.program_id(0) == blocks - 1

    count = len(refs) - 5
    table_ref, noise_ref, peak_ref, found_ref, best_ref = refs[count:]
    columns = peak_ref.shape[1]
    time_block = table_ref.shape[2] // 2

    @pl.when(first_step())
    def _():
        best_ref[...] = jnp.zeros_like(best_ref)

    width = min(2, columns)
    for first in range(0, columns, width):
        parts = []
        for parity in range(2):
            planes = slice(parity * W_DEV, (parity + 1) * W_DEV)
            spectra = jnp.concatenate(
                [
                    jnp.concatenate(
                        [
                            refs[i][row + first + k, planes, :]
                            for i, row in sources
                        ]
                        * 2,
                        axis=0,
                    )
                    for k in range(width)
                ],
                axis=1,
            )
            parts.append(dot(table_ref[0, parity], spectra, ((1,), (0,))))
        powers = []
        for signal in [parts[0] + parts[1]] + [parts[0] - parts[1]] * folded:
            real_part = signal[:time_block]
            imag_part = signal[time_block:]
            powers.append(real_part * real_part + imag_part * imag_part)
        power = jnp.maximum(powers[0], powers[-1]) if folded else powers[0]
        power = jnp.max(power, axis=0, keepdims=True)
        for k in range(width):
            row = pl.ds(first + k, 1)
            best_ref[row, :] = jnp.maximum(
                best_ref[row, :], power[:, k * ROWS : (k + 1) * ROWS]
            )

    @pl.when(last_step())
    def _():
        largest = jnp.max(best_ref[...], axis=1, keepdims=True)
        shape = best_ref.shape
        diagonal = lax.broadcasted_iota(jnp.int32, shape, 0) == lax.broadcasted_iota(
            jnp.int32, shape, 1
        )
        largest = jnp.max(jnp.where(diagonal, largest, 0.0), axis=0, keepdims=True)
        peak = jnp.sqrt(largest[:, :columns]) * (1.0 / math.sqrt(freq_total))
        score = STEEP * (jnp.log(peak + EPS) - jnp.log(noise_ref[...]))
        peak_ref[...] = peak
        found_ref[...] = 1.0 / (1.0 + jnp.exp(-score))


def peaks(spectra, sources, twiddles, noise_level, freq_total, folded):
    columns = noise_level.shape[1]
    blocks = twiddles.shape[0]
    if blocks == 1:
        vmem = pl.BlockSpec(memory_space=pltpu.VMEM)
        grid, in_specs, out_spec = (), [vmem] * (len(spectra) + 2), vmem
    else:
        grid = (blocks,)
        out_spec = pl.BlockSpec((1, columns), lambda i: (0, 0))
        in_specs = [pl.BlockSpec(a.shape, lambda i: (0, 0, 0)) for a in spectra]
        in_specs += [
            pl.BlockSpec((1, *twiddles.shape[1:]), lambda i: (i, 0, 0, 0)),
            out_spec,
        ]
    return pl.pallas_call(
        functools.partial(peak_kernel, freq_total, folded, sources, blocks),
        grid=grid,
        in_specs=in_specs,
        out_specs=[out_spec, out_spec],
        out_shape=[jax.ShapeDtypeStruct((1, columns), jnp.float32)] * 2,
        scratch_shapes=[pltpu.VMEM((max(8, columns), ROWS), jnp.float32)],
        compiler_params=pltpu.CompilerParams(vmem_limit_bytes=VMEM_BYTES),
        name="peaks",
    )(*spectra, twiddles, noise_level)


def body(
    flaw_cells,
    flaw_blocks,
    element_channel,
    focal_delay,
    beam_field,
    flaw_size,
    flaw_slope,
    noise_level,
):
    freq_count = lax.axis_size("freq")
    freq_total = W_DEV * freq_count
    sample_count = min(T_CAP, 2 * freq_total)
    swap = [(0, 1), (1, 0)]
    direct = freq_count == 8
    slots = freq_count if direct else 1
    small = (
        focal_delay,
        element_channel.reshape(1, -1),
        flaw_blocks,
        flaw_cells.reshape(1, -1),
        flaw_size,
        flaw_slope,
    )
    folded = sample_count == 2 * freq_total
    times = sample_count // 2 if folded else sample_count
    twiddles = table(freq_total, slots, times, min(128, times))
    field = beam_field.reshape(W_HALF, 2, *beam_field.shape[1:])
    parts = add(*partials(field, small, swap, freq_total, slots), slots)
    if direct:
        half = slots // 2
        spectra = []
        for slot, masks in enumerate(zip(*slot_masks(slots))):
            pairs = [(a, a ^ masks[((2 * a) ^ a) & half != 0]) for a in range(slots)]
            spectra.append(lax.ppermute(parts[slot], "freq", pairs) if slot else parts[slot])
        spectra = [*spectra[1:], spectra[0]]
        sources = [((slot - 1) % slots, 0) for slot in range(slots)]
    else:
        spectra = [
            lax.all_to_all(parts[0], "freq", split_axis=0, concat_axis=0, tiled=True)
        ]
        sources = [(0, s * (FG // freq_count)) for s in range(freq_count)]
    return tuple(peaks(spectra, sources, twiddles, noise_level, freq_total, folded))


def solution(mesh):
    in_specs = (
        P("batch"),
        P("batch"),
        P("elem"),
        P(),
        P("freq", None, "elem", None),
        P("batch", None),
        P("batch", None),
        P(("batch", "elem"), "freq"),
    )
    out_specs = (P(("batch", "elem"), "freq"), P(("batch", "elem"), "freq"))
    return jax.shard_map(body, mesh=mesh, in_specs=in_specs, out_specs=out_specs, check_vma=False)
```

```python
import functools
import math

import jax
import jax.numpy as jnp
from jax import lax
from jax.experimental import pallas as pl
from jax.experimental.pallas import tpu as pltpu
from jax.sharding import PartitionSpec as P

W_DEV = 16
W_HALF = W_DEV // 2
FG = 128
NB = 4
SB = 32
T_CAP = 1024

EDGE = 0.6
STEEP = 3.0
EPS = 1e-05

ROWS = NB * SB
VMEM_BYTES = 48 * 1024 * 1024


def sin_half_turn(turns):
    angle = turns * math.pi
    square = angle * angle
    sine = 1.0 / 6227020800.0
    for factorial in (-39916800.0, 362880.0, -5040.0, 120.0, -6.0, 1.0):
        sine = sine * square + 1.0 / factorial
    cosine = 1.0 / 479001600.0
    for factorial in (-3628800.0, 40320.0, -720.0, 24.0, -2.0, 1.0):
        cosine = cosine * square + 1.0 / factorial
    return sine * angle, cosine


def sincos_turns(turns):
    rest = turns - jnp.floor(turns + 0.5)
    sine, cosine = sin_half_turn(rest)
    return 2.0 * sine * cosine, 1.0 - 2.0 * sine * sine


def dot(left, right, contract):
    return lax.dot_general(
        left, right, (contract, ((), ())), preferred_element_type=jnp.float32
    )


def slot_masks(slots):
    half = slots // 2
    between = (2, half, half + 1, 3, slots - 1)
    return (1, *between, slots - 2, 0), (slots - 2, *between, 1, 0)


def partner(slots, slot):
    index = lax.axis_index("freq")
    inner = ((index * 2) ^ index) & (slots // 2) != 0
    mask = jnp.zeros_like(slot)
    for s, (outer_mask, inner_mask) in enumerate(zip(*slot_masks(slots))):
        mask = jnp.where(slot == s, jnp.where(inner, inner_mask, outer_mask), mask)
    return mask ^ index


def slot_order(slots):
    size = FG // slots
    row = lax.broadcasted_iota(jnp.int32, (FG, 1), 0)
    column = lax.broadcasted_iota(jnp.int32, (FG, FG), 1)
    if slots > 1:
        row = partner(slots, row // size) * size + row % size
    return row == column


def flaw_pick(order, which, cells_ref):
    cells = jnp.where(which == 0, cells_ref[:, :FG], cells_ref[:, FG:])
    cell_sel = lax.broadcasted_iota(jnp.int32, (cells_ref.shape[1], FG), 0) == cells
    return dot(
        order.astype(jnp.bfloat16), cell_sel.astype(jnp.bfloat16), ((1,), (1,))
    ).astype(jnp.bfloat16)


def delays_of(channel_ref, delay_ref, blocks_ref, groups, elements):
    lane = lax.broadcasted_iota(jnp.int32, (1, 2 * ROWS), 1)
    position = lane & (SB - 1)
    for j in range(2 * NB):
        block = blocks_ref[groups[j // NB] * NB + j % NB]
        position = position + jnp.where((lane >> 5) == j, block * SB, 0)
    channels, positions = delay_ref.shape
    scan_sel = (
        lax.broadcasted_iota(jnp.int32, (positions, 2 * ROWS), 0) == position
    ).astype(jnp.bfloat16)
    channel_sel = (
        (lax.broadcasted_iota(jnp.int32, (channels, elements), 0) == channel_ref[...])
        .astype(jnp.float32)
        .T.astype(jnp.bfloat16)
    )
    rest = delay_ref[...]
    pieces = []
    for _ in range(3):
        pieces.append(rest.astype(jnp.bfloat16))
        rest = rest - pieces[-1].astype(jnp.float32)
    moved = jnp.concatenate(
        [dot(channel_sel, piece, ((1,), (0,))).astype(jnp.bfloat16) for piece in pieces], axis=0
    )
    moved = dot(moved, scan_sel, ((1,), (0,)))
    return moved[:elements] + moved[elements : 2 * elements] + moved[2 * elements :]


def turned(law, step):
    return law[0] * step[0] - law[1] * step[1], law[1] * step[0] + law[0] * step[1]


def focal_base(freq_total, delays):
    first_freq = lax.axis_index("freq") * W_DEV
    phase = delays * (0.5 / freq_total)
    unit = sincos_turns(phase)[::-1]
    base = sincos_turns(phase * first_freq.astype(jnp.float32))[::-1]
    return base, turned(unit, unit), turned(base, unit)


def kirchhoff(freq_total, order, which, size_ref, slope_ref):
    first_freq = lax.axis_index("freq") * W_DEV
    size = size_ref[pl.ds(which, 1), :]
    turn = size * slope_ref[pl.ds(which, 1), :] * (1.0 / freq_total)
    size = jnp.sum(jnp.where(order, size, 0.0), axis=1, keepdims=True)
    turn = jnp.sum(jnp.where(order, turn, 0.0), axis=1, keepdims=True)
    freq = first_freq + lax.broadcasted_iota(jnp.int32, (FG, FG), 1)
    sine, cosine = sincos_turns(turn * freq.astype(jnp.float32))
    return size * (1.0 + EDGE) * cosine, size * (EDGE - 1.0) * sine


def store_law(law_ref, law, step):
    elements = law_ref.shape[1] // 2
    for w in range(W_HALF):
        c = law[0].astype(jnp.bfloat16)
        s = law[1].astype(jnp.bfloat16)
        law_ref[w, :elements, :ROWS] = c
        law_ref[w, :elements, ROWS:] = -s
        law_ref[w, elements:, :ROWS] = s
        law_ref[w, elements:, ROWS:] = c
        if w < W_HALF - 1:
            law = turned(law, step)


def pick_fields(parity, picks, field_ref, picked_refs):
    elements, sites = field_ref.shape[3:]
    for w in range(W_HALF):
        picked = dot(
            picks, field_ref[w, parity].reshape(2 * elements, sites), ((1,), (1,))
        ).astype(jnp.bfloat16)
        for i, ref in enumerate(picked_refs):
            ref[parity, w] = picked[i * FG : (i + 1) * FG]


def store_spectra(picked_ref, law_ref, k_real, k_imag, out_refs):
    size = out_refs[0].shape[1]
    for parity in range(2):
        for w in range(W_HALF):
            product = dot(picked_ref[parity, w], law_ref[parity, w], ((1,), (0,)))
            real_part = product[:, :ROWS]
            imag_part = product[:, ROWS:]
            kr = k_real[:, 2 * w + parity : 2 * w + parity + 1]
            ki = k_imag[:, 2 * w + parity : 2 * w + parity + 1]
            parts = (kr * real_part - ki * imag_part, kr * imag_part + ki * real_part)
            for k, part in enumerate(parts):
                part = part.astype(jnp.bfloat16)
                for i, out_ref in enumerate(out_refs):
                    out_ref[parity * W_DEV + 2 * w + k] = part[i * size : (i + 1) * size]


def other_kernel(freq_total, slots, *refs):
    field_hbm, *small_hbm = refs[:7]
    first_ref, second_ref, own_picked_ref, size_ref, slope_ref, delays_ref = refs[7:13]
    delay_ref, channel_ref, blocks_ref, cells_ref = refs[13:17]
    field_ref, field_sem, small_sem, picked_ref, law_ref = refs[17:]
    small = (delay_ref, channel_ref, blocks_ref, cells_ref, size_ref, slope_ref)
    copies = [
        pltpu.make_async_copy(source, target, small_sem.at[i])
        for i, (source, target) in enumerate(zip(small_hbm, small))
    ]
    for copy in copies:
        copy.start()
    field_copies = [
        pltpu.make_async_copy(
            field_hbm.at[:, parity], field_ref.at[:, parity], field_sem.at[parity]
        )
        for parity in range(2)
    ]
    for copy in field_copies:
        copy.start()
    order = slot_order(slots)
    for copy in copies:
        copy.wait()
    group = lax.axis_index("elem")
    groups = (1 - group, group)
    picks = jnp.concatenate(
        [flaw_pick(order, which, cells_ref) for which in groups], axis=0
    )
    factors = kirchhoff(freq_total, order, groups[0], size_ref, slope_ref)
    delays = delays_of(channel_ref, delay_ref, blocks_ref, groups, field_ref.shape[3])
    delays_ref[...] = delays[:, ROWS:]
    even, step, odd = focal_base(freq_total, delays[:, :ROWS])
    for parity, law in enumerate((even, odd)):
        store_law(law_ref.at[parity], law, step)
        field_copies[parity].wait()
        pick_fields(parity, picks, field_ref, (picked_ref, own_picked_ref))
    store_spectra(picked_ref, law_ref, *factors, (first_ref, second_ref))


def own_kernel(freq_total, slots, *refs):
    picked_ref, delays_ref, size_ref, slope_ref, out_ref, law_ref = refs
    even, step, odd = focal_base(freq_total, delays_ref[...])
    for parity, law in enumerate((even, odd)):
        store_law(law_ref.at[parity], law, step)
    group = lax.axis_index("elem")
    factors = kirchhoff(freq_total, slot_order(slots), group, size_ref, slope_ref)
    store_spectra(picked_ref, law_ref, *factors, (out_ref,))


def call(kernel, name, in_specs, out_shape, scratch):
    vmem = pl.BlockSpec(memory_space=pltpu.VMEM)
    return pl.pallas_call(
        kernel,
        in_specs=in_specs,
        out_specs=[vmem] * len(out_shape),
        out_shape=out_shape,
        scratch_shapes=scratch,
        compiler_params=pltpu.CompilerParams(vmem_limit_bytes=VMEM_BYTES),
        cost_estimate=pl.CostEstimate(flops=1000, bytes_accessed=1000, transcendentals=0),
        name=name,
    )


def partials(field, small, swap, freq_total, slots):
    elements, sites = field.shape[3:]
    vmem = pl.BlockSpec(memory_space=pltpu.VMEM)
    hbm = pl.BlockSpec(memory_space=pltpu.HBM)
    pinned = [pltpu.with_memory_space_constraint(a, pltpu.HBM) for a in (field, *small)]
    out = jax.ShapeDtypeStruct((2 * W_DEV, FG, ROWS), jnp.bfloat16)
    half = jax.ShapeDtypeStruct((2 * W_DEV, FG // 2, ROWS), jnp.bfloat16)
    picked = jax.ShapeDtypeStruct((2, W_HALF, FG, 2 * elements), jnp.bfloat16)
    law = pltpu.VMEM((2, W_HALF, 2 * elements, 2 * ROWS), jnp.bfloat16)
    copied = [jax.ShapeDtypeStruct(a.shape, a.dtype) for a in small[4:]]
    delays = jax.ShapeDtypeStruct((elements, ROWS), jnp.float32)
    first, second, own_picked, size, slope, delays = call(
        functools.partial(other_kernel, freq_total, slots),
        "other",
        [hbm] * len(pinned),
        [half, half, picked, *copied, delays],
        [
            pltpu.SMEM(a.shape, a.dtype) if a.ndim == 1 else pltpu.VMEM(a.shape, a.dtype)
            for a in small[:4]
        ]
        + [
            pltpu.VMEM(field.shape, field.dtype),
            pltpu.SemaphoreType.DMA((2,)),
            pltpu.SemaphoreType.DMA((len(small),)),
            pltpu.VMEM(picked.shape, picked.dtype),
            law,
        ],
    )(*pinned)
    first = lax.ppermute(first, "elem", swap)
    second = lax.ppermute(second, "elem", swap)
    (own,) = call(
        functools.partial(own_kernel, freq_total, slots), "own", [vmem] * 4, [out], [law]
    )(own_picked, delays, size, slope)
    return own, first, second


def add_kernel(first, own_ref, moved_ref, *refs):
    size = refs[0].shape[0]
    for slot, ref in enumerate(refs):
        own = own_ref[:, pl.ds(first + slot * size, size)].astype(jnp.float32)
        both = own + moved_ref[:, pl.ds(slot * size, size)].astype(jnp.float32)
        ref[...] = jnp.swapaxes(both, 0, 1).astype(jnp.bfloat16)


def add(own, first, second, slots):
    vmem = pl.BlockSpec(memory_space=pltpu.VMEM)
    planes, flaws, rows = own.shape
    count = max(1, slots // 2)
    shape = jax.ShapeDtypeStruct((flaws // 2 // count, planes, rows), own.dtype)
    parts = []
    for name, start, moved in (("add_first", 0, first), ("add_second", flaws // 2, second)):
        kernel = functools.partial(add_kernel, start)
        parts += call(kernel, name, [vmem] * 2, [shape] * count, [])(own, moved)
    return parts


def table_kernel(freq_total, slots, table_ref):
    height, depth = table_ref.shape[2:]
    time_block = height // 2
    row = lax.broadcasted_iota(jnp.int32, (height, depth // 2), 0)
    column = lax.broadcasted_iota(jnp.int32, (height, depth // 2), 1)
    out_imag = (row >= time_block).astype(jnp.int32)
    time = pl.program_id(0) * time_block + row - out_imag * time_block
    for parity in range(2):
        freq = (column >> 1) * 2 + parity
        if slots > 1:
            lane = lax.broadcasted_iota(jnp.int32, (1, depth // 2), 1)
            lane = (lane >> 1) * 2 + parity
            freq = partner(slots, lane // W_DEV) * W_DEV + lane % W_DEV
        steps = freq * time + ((column & 1) - out_imag) * (freq_total // 2)
        steps = (steps + 2 * freq_total) & (2 * freq_total - 1)
        _, value = sincos_turns(steps.astype(jnp.float32) * (0.5 / freq_total))
        high = value.astype(jnp.bfloat16)
        table_ref[0, parity, :, : depth // 2] = high
        table_ref[0, parity, :, depth // 2 :] = (
            value - high.astype(jnp.float32)
        ).astype(jnp.bfloat16)


def table(freq_total, slots, times, time_block):
    blocks = times // time_block
    shape = (blocks, 2, 2 * time_block, 2 * freq_total)
    return pl.pallas_call(
        functools.partial(table_kernel, freq_total, slots),
        grid=(blocks,),
        out_specs=pl.BlockSpec((1, *shape[1:]), lambda i: (i, 0, 0, 0)),
        out_shape=jax.ShapeDtypeStruct(shape, jnp.bfloat16),
        compiler_params=pltpu.CompilerParams(vmem_limit_bytes=VMEM_BYTES),
        name="table",
    )()


def peak_kernel(freq_total, folded, sources, blocks, *refs):
    def first_step():
        return blocks == 1 or pl.program_id(0) == 0

    def last_step():
        return blocks == 1 or pl.program_id(0) == blocks - 1

    count = len(refs) - 5
    table_ref, noise_ref, peak_ref, found_ref, best_ref = refs[count:]
    columns = peak_ref.shape[1]
    time_block = table_ref.shape[2] // 2

    @pl.when(first_step())
    def _():
        best_ref[...] = jnp.zeros_like(best_ref)

    width = min(2, columns)
    for first in range(0, columns, width):
        parts = []
        for parity in range(2):
            planes = slice(parity * W_DEV, (parity + 1) * W_DEV)
            spectra = jnp.concatenate(
                [
                    jnp.concatenate(
                        [
                            refs[i][row + first + k, planes, :]
                            for i, row in sources
                        ]
                        * 2,
                        axis=0,
                    )
                    for k in range(width)
                ],
                axis=1,
            )
            parts.append(dot(table_ref[0, parity], spectra, ((1,), (0,))))
        powers = []
        for signal in [parts[0] + parts[1]] + [parts[0] - parts[1]] * folded:
            real_part = signal[:time_block]
            imag_part = signal[time_block:]
            powers.append(real_part * real_part + imag_part * imag_part)
        power = jnp.maximum(powers[0], powers[-1]) if folded else powers[0]
        power = jnp.max(power, axis=0, keepdims=True)
        for k in range(width):
            row = pl.ds(first + k, 1)
            best_ref[row, :] = jnp.maximum(
                best_ref[row, :], power[:, k * ROWS : (k + 1) * ROWS]
            )

    @pl.when(last_step())
    def _():
        largest = jnp.max(best_ref[...], axis=1, keepdims=True)
        shape = best_ref.shape
        diagonal = lax.broadcasted_iota(jnp.int32, shape, 0) == lax.broadcasted_iota(
            jnp.int32, shape, 1
        )
        largest = jnp.max(jnp.where(diagonal, largest, 0.0), axis=0, keepdims=True)
        peak = jnp.sqrt(largest[:, :columns]) * (1.0 / math.sqrt(freq_total))
        score = STEEP * (jnp.log(peak + EPS) - jnp.log(noise_ref[...]))
        peak_ref[...] = peak
        found_ref[...] = 1.0 / (1.0 + jnp.exp(-score))


def peaks(spectra, sources, twiddles, noise_level, freq_total, folded):
    columns = noise_level.shape[1]
    blocks = twiddles.shape[0]
    if blocks == 1:
        vmem = pl.BlockSpec(memory_space=pltpu.VMEM)
        grid, in_specs, out_spec = (), [vmem] * (len(spectra) + 2), vmem
    else:
        grid = (blocks,)
        out_spec = pl.BlockSpec((1, columns), lambda i: (0, 0))
        in_specs = [pl.BlockSpec(a.shape, lambda i: (0, 0, 0)) for a in spectra]
        in_specs += [
            pl.BlockSpec((1, *twiddles.shape[1:]), lambda i: (i, 0, 0, 0)),
            out_spec,
        ]
    return pl.pallas_call(
        functools.partial(peak_kernel, freq_total, folded, sources, blocks),
        grid=grid,
        in_specs=in_specs,
        out_specs=[out_spec, out_spec],
        out_shape=[jax.ShapeDtypeStruct((1, columns), jnp.float32)] * 2,
        scratch_shapes=[pltpu.VMEM((max(8, columns), ROWS), jnp.float32)],
        compiler_params=pltpu.CompilerParams(vmem_limit_bytes=VMEM_BYTES),
        name="peaks",
    )(*spectra, twiddles, noise_level)


def body(
    flaw_cells,
    flaw_blocks,
    element_channel,
    focal_delay,
    beam_field,
    flaw_size,
    flaw_slope,
    noise_level,
):
    freq_count = lax.axis_size("freq")
    freq_total = W_DEV * freq_count
    sample_count = min(T_CAP, 2 * freq_total)
    swap = [(0, 1), (1, 0)]
    direct = freq_count == 8
    slots = freq_count if direct else 1
    small = (
        focal_delay,
        element_channel.reshape(1, -1),
        flaw_blocks,
        flaw_cells.reshape(1, -1),
        flaw_size,
        flaw_slope,
    )
    folded = sample_count == 2 * freq_total
    times = sample_count // 2 if folded else sample_count
    twiddles = table(freq_total, slots, times, min(128, times))
    field = beam_field.reshape(W_HALF, 2, *beam_field.shape[1:])
    parts = add(*partials(field, small, swap, freq_total, slots), slots)
    if direct:
        half = slots // 2
        spectra = []
        for slot, masks in enumerate(zip(*slot_masks(slots))):
            pairs = [(a, a ^ masks[((2 * a) ^ a) & half != 0]) for a in range(slots)]
            own = slot == slots - 1
            spectra.append(parts[slot] if own else lax.ppermute(parts[slot], "freq", pairs))
        order = (*range(half, slots - 1), *range(half), slots - 1)
        spectra = [spectra[slot] for slot in order]
        sources = [(order.index(slot), 0) for slot in range(slots)]
    else:
        whole = jnp.concatenate(parts, axis=0)
        spectra = [
            lax.all_to_all(whole, "freq", split_axis=0, concat_axis=0, tiled=True)
        ]
        sources = [(0, s * (FG // freq_count)) for s in range(freq_count)]
    return tuple(peaks(spectra, sources, twiddles, noise_level, freq_total, folded))


def solution(mesh):
    in_specs = (
        P("batch"),
        P("batch"),
        P("elem"),
        P(),
        P("freq", None, "elem", None),
        P("batch", None),
        P("batch", None),
        P(("batch", "elem"), "freq"),
    )
    out_specs = (P(("batch", "elem"), "freq"), P(("batch", "elem"), "freq"))
    return jax.shard_map(body, mesh=mesh, in_specs=in_specs, out_specs=out_specs, check_vma=False)
```

```python
import functools
import math

import jax
import jax.numpy as jnp
from jax import lax
from jax.experimental import pallas as pl
from jax.experimental.pallas import tpu as pltpu
from jax.sharding import PartitionSpec as P

W_DEV = 16
W_HALF = W_DEV // 2
FG = 128
NB = 4
SB = 32
T_CAP = 1024

EDGE = 0.6
STEEP = 3.0
EPS = 1e-05

ROWS = NB * SB
VMEM_BYTES = 48 * 1024 * 1024


def sin_half_turn(turns):
    angle = turns * math.pi
    square = angle * angle
    sine = 1.0 / 6227020800.0
    for factorial in (-39916800.0, 362880.0, -5040.0, 120.0, -6.0, 1.0):
        sine = sine * square + 1.0 / factorial
    cosine = 1.0 / 479001600.0
    for factorial in (-3628800.0, 40320.0, -720.0, 24.0, -2.0, 1.0):
        cosine = cosine * square + 1.0 / factorial
    return sine * angle, cosine


def sincos_turns(turns):
    rest = turns - jnp.floor(turns + 0.5)
    sine, cosine = sin_half_turn(rest)
    return 2.0 * sine * cosine, 1.0 - 2.0 * sine * sine


def dot(left, right, contract):
    return lax.dot_general(
        left, right, (contract, ((), ())), preferred_element_type=jnp.float32
    )


def slot_masks(slots):
    half = slots // 2
    between = (2, half, half + 1, 3, slots - 1)
    return (1, *between, slots - 2, 0), (slots - 2, *between, 1, 0)


def partner(slots, slot):
    index = lax.axis_index("freq")
    inner = ((index * 2) ^ index) & (slots // 2) != 0
    mask = jnp.zeros_like(slot)
    for s, (outer_mask, inner_mask) in enumerate(zip(*slot_masks(slots))):
        mask = jnp.where(slot == s, jnp.where(inner, inner_mask, outer_mask), mask)
    return mask ^ index


def slot_order(slots):
    size = FG // slots
    row = lax.broadcasted_iota(jnp.int32, (FG, 1), 0)
    column = lax.broadcasted_iota(jnp.int32, (FG, FG), 1)
    if slots > 1:
        row = partner(slots, row // size) * size + row % size
    return row == column


def flaw_pick(order, which, cells_ref):
    cells = jnp.where(which == 0, cells_ref[:, :FG], cells_ref[:, FG:])
    cell_sel = lax.broadcasted_iota(jnp.int32, (cells_ref.shape[1], FG), 0) == cells
    return dot(
        order.astype(jnp.bfloat16), cell_sel.astype(jnp.bfloat16), ((1,), (1,))
    ).astype(jnp.bfloat16)


def delays_of(channel_ref, delay_ref, blocks_ref, groups, elements):
    lane = lax.broadcasted_iota(jnp.int32, (1, 2 * ROWS), 1)
    position = lane & (SB - 1)
    for j in range(2 * NB):
        block = blocks_ref[groups[j // NB] * NB + j % NB]
        position = position + jnp.where((lane >> 5) == j, block * SB, 0)
    channels, positions = delay_ref.shape
    scan_sel = (
        lax.broadcasted_iota(jnp.int32, (positions, 2 * ROWS), 0) == position
    ).astype(jnp.bfloat16)
    channel_sel = (
        (lax.broadcasted_iota(jnp.int32, (channels, elements), 0) == channel_ref[...])
        .astype(jnp.float32)
        .T.astype(jnp.bfloat16)
    )
    rest = delay_ref[...]
    pieces = []
    for _ in range(3):
        pieces.append(rest.astype(jnp.bfloat16))
        rest = rest - pieces[-1].astype(jnp.float32)
    moved = jnp.concatenate(
        [dot(channel_sel, piece, ((1,), (0,))).astype(jnp.bfloat16) for piece in pieces], axis=0
    )
    moved = dot(moved, scan_sel, ((1,), (0,)))
    return moved[:elements] + moved[elements : 2 * elements] + moved[2 * elements :]


def turned(law, step):
    return law[0] * step[0] - law[1] * step[1], law[1] * step[0] + law[0] * step[1]


def focal_base(freq_total, delays):
    first_freq = lax.axis_index("freq") * W_DEV
    phase = delays * (0.5 / freq_total)
    unit = sincos_turns(phase)[::-1]
    base = sincos_turns(phase * first_freq.astype(jnp.float32))[::-1]
    return base, turned(unit, unit), turned(base, unit)


def kirchhoff(freq_total, order, which, size_ref, slope_ref):
    first_freq = lax.axis_index("freq") * W_DEV
    size = size_ref[pl.ds(which, 1), :]
    turn = size * slope_ref[pl.ds(which, 1), :] * (1.0 / freq_total)
    size = jnp.sum(jnp.where(order, size, 0.0), axis=1, keepdims=True)
    turn = jnp.sum(jnp.where(order, turn, 0.0), axis=1, keepdims=True)
    freq = first_freq + lax.broadcasted_iota(jnp.int32, (FG, FG), 1)
    sine, cosine = sincos_turns(turn * freq.astype(jnp.float32))
    return size * (1.0 + EDGE) * cosine, size * (EDGE - 1.0) * sine


def store_law(law_ref, law, step):
    elements = law_ref.shape[1] // 2
    double = 2.0 * step[0]
    following = turned(law, step)
    for w in range(W_HALF):
        c = law[0].astype(jnp.bfloat16)
        s = law[1].astype(jnp.bfloat16)
        law_ref[w, :elements, :ROWS] = c
        law_ref[w, :elements, ROWS:] = -s
        law_ref[w, elements:, :ROWS] = s
        law_ref[w, elements:, ROWS:] = c
        law, following = following, [double * x - y for x, y in zip(following, law)]


def pick_fields(parity, picks, field_ref, picked_refs):
    elements, sites = field_ref.shape[3:]
    for w in range(W_HALF):
        picked = dot(
            picks, field_ref[w, parity].reshape(2 * elements, sites), ((1,), (1,))
        ).astype(jnp.bfloat16)
        for i, ref in enumerate(picked_refs):
            ref[parity, w] = picked[i * FG : (i + 1) * FG]


def store_spectra(picked_ref, law_ref, k_real, k_imag, out_refs):
    size = out_refs[0].shape[1]
    for parity in range(2):
        for w in range(W_HALF):
            product = dot(picked_ref[parity, w], law_ref[parity, w], ((1,), (0,)))
            real_part = product[:, :ROWS]
            imag_part = product[:, ROWS:]
            kr = k_real[:, 2 * w + parity : 2 * w + parity + 1]
            ki = k_imag[:, 2 * w + parity : 2 * w + parity + 1]
            parts = (kr * real_part - ki * imag_part, kr * imag_part + ki * real_part)
            for k, part in enumerate(parts):
                part = part.astype(jnp.bfloat16)
                for i, out_ref in enumerate(out_refs):
                    out_ref[parity * W_DEV + 2 * w + k] = part[i * size : (i + 1) * size]


def other_kernel(freq_total, slots, *refs):
    field_hbm, *small_hbm = refs[:7]
    first_ref, second_ref, own_picked_ref, size_ref, slope_ref, delays_ref = refs[7:13]
    delay_ref, channel_ref, blocks_ref, cells_ref = refs[13:17]
    field_ref, field_sem, small_sem, picked_ref, law_ref = refs[17:]
    small = (delay_ref, channel_ref, blocks_ref, cells_ref, size_ref, slope_ref)
    copies = [
        pltpu.make_async_copy(source, target, small_sem.at[i])
        for i, (source, target) in enumerate(zip(small_hbm, small))
    ]
    for copy in copies:
        copy.start()
    field_copies = [
        pltpu.make_async_copy(
            field_hbm.at[:, parity], field_ref.at[:, parity], field_sem.at[parity]
        )
        for parity in range(2)
    ]
    field_copies[0].start()
    order = slot_order(slots)
    for copy in copies:
        copy.wait()
    field_copies[1].start()
    group = lax.axis_index("elem")
    groups = (1 - group, group)
    picks = jnp.concatenate(
        [flaw_pick(order, which, cells_ref) for which in groups], axis=0
    )
    factors = kirchhoff(freq_total, order, groups[0], size_ref, slope_ref)
    delays = delays_of(channel_ref, delay_ref, blocks_ref, groups, field_ref.shape[3])
    delays_ref[...] = delays[:, ROWS:]
    even, step, odd = focal_base(freq_total, delays[:, :ROWS])
    for parity, law in enumerate((even, odd)):
        store_law(law_ref.at[parity], law, step)
        field_copies[parity].wait()
        pick_fields(parity, picks, field_ref, (picked_ref, own_picked_ref))
    store_spectra(picked_ref, law_ref, *factors, (first_ref, second_ref))


def own_kernel(freq_total, slots, *refs):
    picked_ref, delays_ref, size_ref, slope_ref, out_ref, law_ref = refs
    even, step, odd = focal_base(freq_total, delays_ref[...])
    for parity, law in enumerate((even, odd)):
        store_law(law_ref.at[parity], law, step)
    group = lax.axis_index("elem")
    factors = kirchhoff(freq_total, slot_order(slots), group, size_ref, slope_ref)
    store_spectra(picked_ref, law_ref, *factors, (out_ref,))


def call(kernel, name, in_specs, out_shape, scratch):
    vmem = pl.BlockSpec(memory_space=pltpu.VMEM)
    return pl.pallas_call(
        kernel,
        in_specs=in_specs,
        out_specs=[vmem] * len(out_shape),
        out_shape=out_shape,
        scratch_shapes=scratch,
        compiler_params=pltpu.CompilerParams(vmem_limit_bytes=VMEM_BYTES),
        cost_estimate=pl.CostEstimate(flops=1000, bytes_accessed=1000, transcendentals=0),
        name=name,
    )


def partials(field, small, swap, freq_total, slots):
    elements, sites = field.shape[3:]
    vmem = pl.BlockSpec(memory_space=pltpu.VMEM)
    hbm = pl.BlockSpec(memory_space=pltpu.HBM)
    pinned = [pltpu.with_memory_space_constraint(a, pltpu.HBM) for a in (field, *small)]
    out = jax.ShapeDtypeStruct((2 * W_DEV, FG, ROWS), jnp.bfloat16)
    half = jax.ShapeDtypeStruct((2 * W_DEV, FG // 2, ROWS), jnp.bfloat16)
    picked = jax.ShapeDtypeStruct((2, W_HALF, FG, 2 * elements), jnp.bfloat16)
    law = pltpu.VMEM((2, W_HALF, 2 * elements, 2 * ROWS), jnp.bfloat16)
    copied = [jax.ShapeDtypeStruct(a.shape, a.dtype) for a in small[4:]]
    delays = jax.ShapeDtypeStruct((elements, ROWS), jnp.float32)
    first, second, own_picked, size, slope, delays = call(
        functools.partial(other_kernel, freq_total, slots),
        "other",
        [hbm] * len(pinned),
        [half, half, picked, *copied, delays],
        [
            pltpu.SMEM(a.shape, a.dtype) if a.ndim == 1 else pltpu.VMEM(a.shape, a.dtype)
            for a in small[:4]
        ]
        + [
            pltpu.VMEM(field.shape, field.dtype),
            pltpu.SemaphoreType.DMA((2,)),
            pltpu.SemaphoreType.DMA((len(small),)),
            pltpu.VMEM(picked.shape, picked.dtype),
            law,
        ],
    )(*pinned)
    first = lax.ppermute(first, "elem", swap)
    second = lax.ppermute(second, "elem", swap)
    (own,) = call(
        functools.partial(own_kernel, freq_total, slots), "own", [vmem] * 4, [out], [law]
    )(own_picked, delays, size, slope)
    return own, first, second


def add_kernel(first, own_ref, moved_ref, *refs):
    size = refs[0].shape[0]
    for slot, ref in enumerate(refs):
        own = own_ref[:, pl.ds(first + slot * size, size)].astype(jnp.float32)
        both = own + moved_ref[:, pl.ds(slot * size, size)].astype(jnp.float32)
        ref[...] = jnp.swapaxes(both, 0, 1).astype(jnp.bfloat16)


def add(own, first, second, slots):
    vmem = pl.BlockSpec(memory_space=pltpu.VMEM)
    planes, flaws, rows = own.shape
    count = max(1, slots // 2)
    shape = jax.ShapeDtypeStruct((flaws // 2 // count, planes, rows), own.dtype)
    parts = []
    for name, start, moved in (("add_first", 0, first), ("add_second", flaws // 2, second)):
        kernel = functools.partial(add_kernel, start)
        parts += call(kernel, name, [vmem] * 2, [shape] * count, [])(own, moved)
    return parts


def table_kernel(freq_total, slots, table_ref):
    height, depth = table_ref.shape[2:]
    time_block = height // 2
    row = lax.broadcasted_iota(jnp.int32, (height, depth // 2), 0)
    column = lax.broadcasted_iota(jnp.int32, (height, depth // 2), 1)
    out_imag = (row >= time_block).astype(jnp.int32)
    time = pl.program_id(0) * time_block + row - out_imag * time_block
    for parity in range(2):
        freq = (column >> 1) * 2 + parity
        if slots > 1:
            lane = lax.broadcasted_iota(jnp.int32, (1, depth // 2), 1)
            lane = (lane >> 1) * 2 + parity
            freq = partner(slots, lane // W_DEV) * W_DEV + lane % W_DEV
        steps = freq * time + ((column & 1) - out_imag) * (freq_total // 2)
        steps = (steps + 2 * freq_total) & (2 * freq_total - 1)
        _, value = sincos_turns(steps.astype(jnp.float32) * (0.5 / freq_total))
        high = value.astype(jnp.bfloat16)
        table_ref[0, parity, :, : depth // 2] = high
        table_ref[0, parity, :, depth // 2 :] = (
            value - high.astype(jnp.float32)
        ).astype(jnp.bfloat16)


def table(freq_total, slots, times, time_block):
    blocks = times // time_block
    shape = (blocks, 2, 2 * time_block, 2 * freq_total)
    return pl.pallas_call(
        functools.partial(table_kernel, freq_total, slots),
        grid=(blocks,),
        out_specs=pl.BlockSpec((1, *shape[1:]), lambda i: (i, 0, 0, 0)),
        out_shape=jax.ShapeDtypeStruct(shape, jnp.bfloat16),
        compiler_params=pltpu.CompilerParams(vmem_limit_bytes=VMEM_BYTES),
        name="table",
    )()


def peak_kernel(freq_total, folded, sources, blocks, *refs):
    def first_step():
        return blocks == 1 or pl.program_id(0) == 0

    def last_step():
        return blocks == 1 or pl.program_id(0) == blocks - 1

    count = len(refs) - 5
    table_ref, noise_ref, peak_ref, found_ref, best_ref = refs[count:]
    columns = peak_ref.shape[1]
    time_block = table_ref.shape[2] // 2

    @pl.when(first_step())
    def _():
        best_ref[...] = jnp.zeros_like(best_ref)

    width = min(2, columns)
    for first in range(0, columns, width):
        parts = []
        for parity in range(2):
            planes = slice(parity * W_DEV, (parity + 1) * W_DEV)
            spectra = jnp.concatenate(
                [
                    jnp.concatenate(
                        [
                            refs[i][row + first + k, planes, :]
                            for i, row in sources
                        ]
                        * 2,
                        axis=0,
                    )
                    for k in range(width)
                ],
                axis=1,
            )
            parts.append(dot(table_ref[0, parity], spectra, ((1,), (0,))))
        powers = []
        for signal in [parts[0] + parts[1]] + [parts[0] - parts[1]] * folded:
            real_part = signal[:time_block]
            imag_part = signal[time_block:]
            powers.append(real_part * real_part + imag_part * imag_part)
        power = jnp.maximum(powers[0], powers[-1]) if folded else powers[0]
        power = jnp.max(power, axis=0, keepdims=True)
        for k in range(width):
            row = pl.ds(first + k, 1)
            best_ref[row, :] = jnp.maximum(
                best_ref[row, :], power[:, k * ROWS : (k + 1) * ROWS]
            )

    @pl.when(last_step())
    def _():
        largest = jnp.max(best_ref[...], axis=1, keepdims=True)
        shape = best_ref.shape
        diagonal = lax.broadcasted_iota(jnp.int32, shape, 0) == lax.broadcasted_iota(
            jnp.int32, shape, 1
        )
        largest = jnp.max(jnp.where(diagonal, largest, 0.0), axis=0, keepdims=True)
        peak = jnp.sqrt(largest[:, :columns]) * (1.0 / math.sqrt(freq_total))
        score = STEEP * (jnp.log(peak + EPS) - jnp.log(noise_ref[...]))
        peak_ref[...] = peak
        found_ref[...] = 1.0 / (1.0 + jnp.exp(-score))


def peaks(spectra, sources, twiddles, noise_level, freq_total, folded):
    columns = noise_level.shape[1]
    blocks = twiddles.shape[0]
    if blocks == 1:
        vmem = pl.BlockSpec(memory_space=pltpu.VMEM)
        grid, in_specs, out_spec = (), [vmem] * (len(spectra) + 2), vmem
    else:
        grid = (blocks,)
        out_spec = pl.BlockSpec((1, columns), lambda i: (0, 0))
        in_specs = [pl.BlockSpec(a.shape, lambda i: (0, 0, 0)) for a in spectra]
        in_specs += [
            pl.BlockSpec((1, *twiddles.shape[1:]), lambda i: (i, 0, 0, 0)),
            out_spec,
        ]
    return pl.pallas_call(
        functools.partial(peak_kernel, freq_total, folded, sources, blocks),
        grid=grid,
        in_specs=in_specs,
        out_specs=[out_spec, out_spec],
        out_shape=[jax.ShapeDtypeStruct((1, columns), jnp.float32)] * 2,
        scratch_shapes=[pltpu.VMEM((max(8, columns), ROWS), jnp.float32)],
        compiler_params=pltpu.CompilerParams(vmem_limit_bytes=VMEM_BYTES),
        name="peaks",
    )(*spectra, twiddles, noise_level)


def body(
    flaw_cells,
    flaw_blocks,
    element_channel,
    focal_delay,
    beam_field,
    flaw_size,
    flaw_slope,
    noise_level,
):
    freq_count = lax.axis_size("freq")
    freq_total = W_DEV * freq_count
    sample_count = min(T_CAP, 2 * freq_total)
    swap = [(0, 1), (1, 0)]
    direct = freq_count == 8
    slots = freq_count if direct else 1
    small = (
        focal_delay,
        element_channel.reshape(1, -1),
        flaw_blocks,
        flaw_cells.reshape(1, -1),
        flaw_size,
        flaw_slope,
    )
    folded = sample_count == 2 * freq_total
    times = sample_count // 2 if folded else sample_count
    twiddles = table(freq_total, slots, times, min(128, times))
    field = beam_field.reshape(W_HALF, 2, *beam_field.shape[1:])
    parts = add(*partials(field, small, swap, freq_total, slots), slots)
    if direct:
        half = slots // 2
        spectra = []
        for slot, masks in enumerate(zip(*slot_masks(slots))):
            pairs = [(a, a ^ masks[((2 * a) ^ a) & half != 0]) for a in range(slots)]
            own = slot == slots - 1
            spectra.append(parts[slot] if own else lax.ppermute(parts[slot], "freq", pairs))
        order = (*range(half, slots - 1), *range(half), slots - 1)
        spectra = [spectra[slot] for slot in order]
        sources = [(order.index(slot), 0) for slot in range(slots)]
    else:
        whole = jnp.concatenate(parts, axis=0)
        spectra = [
            lax.all_to_all(whole, "freq", split_axis=0, concat_axis=0, tiled=True)
        ]
        sources = [(0, s * (FG // freq_count)) for s in range(freq_count)]
    return tuple(peaks(spectra, sources, twiddles, noise_level, freq_total, folded))


def solution(mesh):
    in_specs = (
        P("batch"),
        P("batch"),
        P("elem"),
        P(),
        P("freq", None, "elem", None),
        P("batch", None),
        P("batch", None),
        P(("batch", "elem"), "freq"),
    )
    out_specs = (P(("batch", "elem"), "freq"), P(("batch", "elem"), "freq"))
    return jax.shard_map(body, mesh=mesh, in_specs=in_specs, out_specs=out_specs, check_vma=False)
```

```python
import functools
import math

import jax
import jax.numpy as jnp
from jax import lax
from jax.experimental import pallas as pl
from jax.experimental.pallas import tpu as pltpu
from jax.sharding import PartitionSpec as P

W_DEV = 16
W_HALF = W_DEV // 2
FG = 128
NB = 4
SB = 32
T_CAP = 1024
FIRST_SLOTS = 3

EDGE = 0.6
STEEP = 3.0
EPS = 1e-05

ROWS = NB * SB
VMEM_BYTES = 48 * 1024 * 1024


def sin_half_turn(turns):
    angle = turns * math.pi
    square = angle * angle
    sine = 1.0 / 6227020800.0
    for factorial in (-39916800.0, 362880.0, -5040.0, 120.0, -6.0, 1.0):
        sine = sine * square + 1.0 / factorial
    cosine = 1.0 / 479001600.0
    for factorial in (-3628800.0, 40320.0, -720.0, 24.0, -2.0, 1.0):
        cosine = cosine * square + 1.0 / factorial
    return sine * angle, cosine


def sincos_turns(turns):
    rest = turns - jnp.floor(turns + 0.5)
    sine, cosine = sin_half_turn(rest)
    return 2.0 * sine * cosine, 1.0 - 2.0 * sine * sine


def dot(left, right, contract):
    return lax.dot_general(
        left, right, (contract, ((), ())), preferred_element_type=jnp.float32
    )


def slot_masks(slots):
    half = slots // 2
    between = (2, half, half + 1, 3, slots - 1)
    return (1, *between, slots - 2, 0), (slots - 2, *between, 1, 0)


def partner(slots, slot):
    index = lax.axis_index("freq")
    inner = ((index * 2) ^ index) & (slots // 2) != 0
    mask = jnp.zeros_like(slot)
    for s, (outer_mask, inner_mask) in enumerate(zip(*slot_masks(slots))):
        mask = jnp.where(slot == s, jnp.where(inner, inner_mask, outer_mask), mask)
    return mask ^ index


def slot_order(slots):
    size = FG // slots
    row = lax.broadcasted_iota(jnp.int32, (FG, 1), 0)
    column = lax.broadcasted_iota(jnp.int32, (FG, FG), 1)
    if slots > 1:
        row = partner(slots, row // size) * size + row % size
    return row == column


def flaw_pick(order, which, cells_ref):
    cells = jnp.where(which == 0, cells_ref[:, :FG], cells_ref[:, FG:])
    cell_sel = lax.broadcasted_iota(jnp.int32, (cells_ref.shape[1], FG), 0) == cells
    return dot(
        order.astype(jnp.bfloat16), cell_sel.astype(jnp.bfloat16), ((1,), (1,))
    ).astype(jnp.bfloat16)


def delays_of(channel_ref, delay_ref, blocks_ref, groups, elements):
    lane = lax.broadcasted_iota(jnp.int32, (1, 2 * ROWS), 1)
    position = lane & (SB - 1)
    for j in range(2 * NB):
        block = blocks_ref[groups[j // NB] * NB + j % NB]
        position = position + jnp.where((lane >> 5) == j, block * SB, 0)
    channels, positions = delay_ref.shape
    scan_sel = (
        lax.broadcasted_iota(jnp.int32, (positions, 2 * ROWS), 0) == position
    ).astype(jnp.bfloat16)
    channel_sel = (
        (lax.broadcasted_iota(jnp.int32, (channels, elements), 0) == channel_ref[...])
        .astype(jnp.float32)
        .T.astype(jnp.bfloat16)
    )
    rest = delay_ref[...]
    pieces = []
    for _ in range(3):
        pieces.append(rest.astype(jnp.bfloat16))
        rest = rest - pieces[-1].astype(jnp.float32)
    moved = jnp.concatenate(
        [dot(channel_sel, piece, ((1,), (0,))).astype(jnp.bfloat16) for piece in pieces], axis=0
    )
    moved = dot(moved, scan_sel, ((1,), (0,)))
    return moved[:elements] + moved[elements : 2 * elements] + moved[2 * elements :]


def turned(law, step):
    return law[0] * step[0] - law[1] * step[1], law[1] * step[0] + law[0] * step[1]


def focal_base(freq_total, delays):
    first_freq = lax.axis_index("freq") * W_DEV
    phase = delays * (0.5 / freq_total)
    unit = sincos_turns(phase)[::-1]
    base = sincos_turns(phase * first_freq.astype(jnp.float32))[::-1]
    return base, turned(unit, unit), turned(base, unit)


def kirchhoff(freq_total, order, which, size_ref, slope_ref):
    first_freq = lax.axis_index("freq") * W_DEV
    size = size_ref[pl.ds(which, 1), :]
    turn = size * slope_ref[pl.ds(which, 1), :] * (1.0 / freq_total)
    size = jnp.sum(jnp.where(order, size, 0.0), axis=1, keepdims=True)
    turn = jnp.sum(jnp.where(order, turn, 0.0), axis=1, keepdims=True)
    freq = first_freq + lax.broadcasted_iota(jnp.int32, (FG, FG), 1)
    sine, cosine = sincos_turns(turn * freq.astype(jnp.float32))
    return size * (1.0 + EDGE) * cosine, size * (EDGE - 1.0) * sine


def store_law(law_ref, law, step):
    elements = law_ref.shape[1] // 2
    double = 2.0 * step[0]
    following = turned(law, step)
    for w in range(W_HALF):
        c = law[0].astype(jnp.bfloat16)
        s = law[1].astype(jnp.bfloat16)
        law_ref[w, :elements, :ROWS] = c
        law_ref[w, :elements, ROWS:] = -s
        law_ref[w, elements:, :ROWS] = s
        law_ref[w, elements:, ROWS:] = c
        law, following = following, [double * x - y for x, y in zip(following, law)]


def pick_fields(parity, picks, field_ref, picked_refs):
    elements, sites = field_ref.shape[3:]
    for w in range(W_HALF):
        picked = dot(
            picks, field_ref[w, parity].reshape(2 * elements, sites), ((1,), (1,))
        ).astype(jnp.bfloat16)
        for i, ref in enumerate(picked_refs):
            ref[parity, w] = picked[i * FG : (i + 1) * FG]


def store_spectra(picked_ref, law_ref, k_real, k_imag, out_refs):
    for parity in range(2):
        for w in range(W_HALF):
            product = dot(picked_ref[parity, w], law_ref[parity, w], ((1,), (0,)))
            real_part = product[:, :ROWS]
            imag_part = product[:, ROWS:]
            kr = k_real[:, 2 * w + parity : 2 * w + parity + 1]
            ki = k_imag[:, 2 * w + parity : 2 * w + parity + 1]
            parts = (kr * real_part - ki * imag_part, kr * imag_part + ki * real_part)
            for k, part in enumerate(parts):
                part = part.astype(jnp.bfloat16)
                first = 0
                for out_ref in out_refs:
                    last = first + out_ref.shape[1]
                    out_ref[parity * W_DEV + 2 * w + k] = part[first:last]
                    first = last


def other_kernel(freq_total, slots, *refs):
    field_hbm, *small_hbm = refs[:7]
    first_ref, second_ref, own_picked_ref, size_ref, slope_ref, delays_ref = refs[7:13]
    delay_ref, channel_ref, blocks_ref, cells_ref = refs[13:17]
    field_ref, field_sem, small_sem, picked_ref, law_ref = refs[17:]
    small = (delay_ref, channel_ref, blocks_ref, cells_ref, size_ref, slope_ref)
    copies = [
        pltpu.make_async_copy(source, target, small_sem.at[i])
        for i, (source, target) in enumerate(zip(small_hbm, small))
    ]
    for copy in copies:
        copy.start()
    field_copies = [
        pltpu.make_async_copy(
            field_hbm.at[:, parity], field_ref.at[:, parity], field_sem.at[parity]
        )
        for parity in range(2)
    ]
    field_copies[0].start()
    order = slot_order(slots)
    for copy in copies:
        copy.wait()
    field_copies[1].start()
    group = lax.axis_index("elem")
    groups = (1 - group, group)
    picks = jnp.concatenate(
        [flaw_pick(order, which, cells_ref) for which in groups], axis=0
    )
    factors = kirchhoff(freq_total, order, groups[0], size_ref, slope_ref)
    delays = delays_of(channel_ref, delay_ref, blocks_ref, groups, field_ref.shape[3])
    delays_ref[...] = delays[:, ROWS:]
    even, step, odd = focal_base(freq_total, delays[:, :ROWS])
    for parity, law in enumerate((even, odd)):
        store_law(law_ref.at[parity], law, step)
        field_copies[parity].wait()
        pick_fields(parity, picks, field_ref, (picked_ref, own_picked_ref))
    store_spectra(picked_ref, law_ref, *factors, (first_ref, second_ref))


def own_kernel(freq_total, slots, *refs):
    picked_ref, delays_ref, size_ref, slope_ref, out_ref, law_ref = refs
    even, step, odd = focal_base(freq_total, delays_ref[...])
    for parity, law in enumerate((even, odd)):
        store_law(law_ref.at[parity], law, step)
    group = lax.axis_index("elem")
    factors = kirchhoff(freq_total, slot_order(slots), group, size_ref, slope_ref)
    store_spectra(picked_ref, law_ref, *factors, (out_ref,))


def call(kernel, name, in_specs, out_shape, scratch):
    vmem = pl.BlockSpec(memory_space=pltpu.VMEM)
    return pl.pallas_call(
        kernel,
        in_specs=in_specs,
        out_specs=[vmem] * len(out_shape),
        out_shape=out_shape,
        scratch_shapes=scratch,
        compiler_params=pltpu.CompilerParams(vmem_limit_bytes=VMEM_BYTES),
        cost_estimate=pl.CostEstimate(flops=1000, bytes_accessed=1000, transcendentals=0),
        name=name,
    )


def partials(field, small, swap, freq_total, slots):
    elements, sites = field.shape[3:]
    vmem = pl.BlockSpec(memory_space=pltpu.VMEM)
    hbm = pl.BlockSpec(memory_space=pltpu.HBM)
    pinned = [pltpu.with_memory_space_constraint(a, pltpu.HBM) for a in (field, *small)]
    out = jax.ShapeDtypeStruct((2 * W_DEV, FG, ROWS), jnp.bfloat16)
    flaws = FG // 2 if slots == 1 else FG // slots * FIRST_SLOTS
    halves = [
        jax.ShapeDtypeStruct((2 * W_DEV, count, ROWS), jnp.bfloat16)
        for count in (flaws, FG - flaws)
    ]
    picked = jax.ShapeDtypeStruct((2, W_HALF, FG, 2 * elements), jnp.bfloat16)
    law = pltpu.VMEM((2, W_HALF, 2 * elements, 2 * ROWS), jnp.bfloat16)
    copied = [jax.ShapeDtypeStruct(a.shape, a.dtype) for a in small[4:]]
    delays = jax.ShapeDtypeStruct((elements, ROWS), jnp.float32)
    first, second, own_picked, size, slope, delays = call(
        functools.partial(other_kernel, freq_total, slots),
        "other",
        [hbm] * len(pinned),
        [*halves, picked, *copied, delays],
        [
            pltpu.SMEM(a.shape, a.dtype) if a.ndim == 1 else pltpu.VMEM(a.shape, a.dtype)
            for a in small[:4]
        ]
        + [
            pltpu.VMEM(field.shape, field.dtype),
            pltpu.SemaphoreType.DMA((2,)),
            pltpu.SemaphoreType.DMA((len(small),)),
            pltpu.VMEM(picked.shape, picked.dtype),
            law,
        ],
    )(*pinned)
    first = lax.ppermute(first, "elem", swap)
    second = lax.ppermute(second, "elem", swap)
    (own,) = call(
        functools.partial(own_kernel, freq_total, slots), "own", [vmem] * 4, [out], [law]
    )(own_picked, delays, size, slope)
    return own, first, second


def add_kernel(first, own_ref, moved_ref, *refs):
    size = refs[0].shape[0]
    for slot, ref in enumerate(refs):
        own = own_ref[:, pl.ds(first + slot * size, size)].astype(jnp.float32)
        both = own + moved_ref[:, pl.ds(slot * size, size)].astype(jnp.float32)
        ref[...] = jnp.swapaxes(both, 0, 1).astype(jnp.bfloat16)


def add(own, first, second, slots):
    vmem = pl.BlockSpec(memory_space=pltpu.VMEM)
    planes, flaws, rows = own.shape
    size = min(flaws // slots, first.shape[1])
    shape = jax.ShapeDtypeStruct((size, planes, rows), own.dtype)
    parts = []
    for name, start, moved in (
        ("add_first", 0, first),
        ("add_second", first.shape[1], second),
    ):
        kernel = functools.partial(add_kernel, start)
        shapes = [shape] * (moved.shape[1] // size)
        parts += call(kernel, name, [vmem] * 2, shapes, [])(own, moved)
    return parts


def table_kernel(freq_total, slots, table_ref):
    height, depth = table_ref.shape[2:]
    time_block = height // 2
    row = lax.broadcasted_iota(jnp.int32, (height, depth // 2), 0)
    column = lax.broadcasted_iota(jnp.int32, (height, depth // 2), 1)
    out_imag = (row >= time_block).astype(jnp.int32)
    time = pl.program_id(0) * time_block + row - out_imag * time_block
    for parity in range(2):
        freq = (column >> 1) * 2 + parity
        if slots > 1:
            lane = lax.broadcasted_iota(jnp.int32, (1, depth // 2), 1)
            lane = (lane >> 1) * 2 + parity
            freq = partner(slots, lane // W_DEV) * W_DEV + lane % W_DEV
        steps = freq * time + ((column & 1) - out_imag) * (freq_total // 2)
        steps = (steps + 2 * freq_total) & (2 * freq_total - 1)
        _, value = sincos_turns(steps.astype(jnp.float32) * (0.5 / freq_total))
        high = value.astype(jnp.bfloat16)
        table_ref[0, parity, :, : depth // 2] = high
        table_ref[0, parity, :, depth // 2 :] = (
            value - high.astype(jnp.float32)
        ).astype(jnp.bfloat16)


def table(freq_total, slots, times, time_block):
    blocks = times // time_block
    shape = (blocks, 2, 2 * time_block, 2 * freq_total)
    return pl.pallas_call(
        functools.partial(table_kernel, freq_total, slots),
        grid=(blocks,),
        out_specs=pl.BlockSpec((1, *shape[1:]), lambda i: (i, 0, 0, 0)),
        out_shape=jax.ShapeDtypeStruct(shape, jnp.bfloat16),
        compiler_params=pltpu.CompilerParams(vmem_limit_bytes=VMEM_BYTES),
        name="table",
    )()


def peak_kernel(freq_total, folded, sources, blocks, *refs):
    def first_step():
        return blocks == 1 or pl.program_id(0) == 0

    def last_step():
        return blocks == 1 or pl.program_id(0) == blocks - 1

    count = len(refs) - 5
    table_ref, noise_ref, peak_ref, found_ref, best_ref = refs[count:]
    columns = peak_ref.shape[1]
    time_block = table_ref.shape[2] // 2

    @pl.when(first_step())
    def _():
        best_ref[...] = jnp.zeros_like(best_ref)

    width = min(2, columns)
    for first in range(0, columns, width):
        parts = []
        for parity in range(2):
            planes = slice(parity * W_DEV, (parity + 1) * W_DEV)
            spectra = jnp.concatenate(
                [
                    jnp.concatenate(
                        [
                            refs[i][row + first + k, planes, :]
                            for i, row in sources
                        ]
                        * 2,
                        axis=0,
                    )
                    for k in range(width)
                ],
                axis=1,
            )
            parts.append(dot(table_ref[0, parity], spectra, ((1,), (0,))))
        powers = []
        for signal in [parts[0] + parts[1]] + [parts[0] - parts[1]] * folded:
            real_part = signal[:time_block]
            imag_part = signal[time_block:]
            powers.append(real_part * real_part + imag_part * imag_part)
        power = jnp.maximum(powers[0], powers[-1]) if folded else powers[0]
        power = jnp.max(power, axis=0, keepdims=True)
        for k in range(width):
            row = pl.ds(first + k, 1)
            best_ref[row, :] = jnp.maximum(
                best_ref[row, :], power[:, k * ROWS : (k + 1) * ROWS]
            )

    @pl.when(last_step())
    def _():
        largest = jnp.max(best_ref[...], axis=1, keepdims=True)
        shape = best_ref.shape
        diagonal = lax.broadcasted_iota(jnp.int32, shape, 0) == lax.broadcasted_iota(
            jnp.int32, shape, 1
        )
        largest = jnp.max(jnp.where(diagonal, largest, 0.0), axis=0, keepdims=True)
        peak = jnp.sqrt(largest[:, :columns]) * (1.0 / math.sqrt(freq_total))
        score = STEEP * (jnp.log(peak + EPS) - jnp.log(noise_ref[...]))
        peak_ref[...] = peak
        found_ref[...] = 1.0 / (1.0 + jnp.exp(-score))


def peaks(spectra, sources, twiddles, noise_level, freq_total, folded):
    columns = noise_level.shape[1]
    blocks = twiddles.shape[0]
    if blocks == 1:
        vmem = pl.BlockSpec(memory_space=pltpu.VMEM)
        grid, in_specs, out_spec = (), [vmem] * (len(spectra) + 2), vmem
    else:
        grid = (blocks,)
        out_spec = pl.BlockSpec((1, columns), lambda i: (0, 0))
        in_specs = [pl.BlockSpec(a.shape, lambda i: (0, 0, 0)) for a in spectra]
        in_specs += [
            pl.BlockSpec((1, *twiddles.shape[1:]), lambda i: (i, 0, 0, 0)),
            out_spec,
        ]
    return pl.pallas_call(
        functools.partial(peak_kernel, freq_total, folded, sources, blocks),
        grid=grid,
        in_specs=in_specs,
        out_specs=[out_spec, out_spec],
        out_shape=[jax.ShapeDtypeStruct((1, columns), jnp.float32)] * 2,
        scratch_shapes=[pltpu.VMEM((max(8, columns), ROWS), jnp.float32)],
        compiler_params=pltpu.CompilerParams(vmem_limit_bytes=VMEM_BYTES),
        name="peaks",
    )(*spectra, twiddles, noise_level)


def body(
    flaw_cells,
    flaw_blocks,
    element_channel,
    focal_delay,
    beam_field,
    flaw_size,
    flaw_slope,
    noise_level,
):
    freq_count = lax.axis_size("freq")
    freq_total = W_DEV * freq_count
    sample_count = min(T_CAP, 2 * freq_total)
    swap = [(0, 1), (1, 0)]
    direct = freq_count == 8
    slots = freq_count if direct else 1
    small = (
        focal_delay,
        element_channel.reshape(1, -1),
        flaw_blocks,
        flaw_cells.reshape(1, -1),
        flaw_size,
        flaw_slope,
    )
    folded = sample_count == 2 * freq_total
    times = sample_count // 2 if folded else sample_count
    twiddles = table(freq_total, slots, times, min(128, times))
    field = beam_field.reshape(W_HALF, 2, *beam_field.shape[1:])
    parts = add(*partials(field, small, swap, freq_total, slots), slots)
    if direct:
        half = slots // 2
        spectra = []
        for slot, masks in enumerate(zip(*slot_masks(slots))):
            pairs = [(a, a ^ masks[((2 * a) ^ a) & half != 0]) for a in range(slots)]
            own = slot == slots - 1
            spectra.append(parts[slot] if own else lax.ppermute(parts[slot], "freq", pairs))
        order = (*range(FIRST_SLOTS, slots - 1), *range(FIRST_SLOTS), slots - 1)
        spectra = [spectra[slot] for slot in order]
        sources = [(order.index(slot), 0) for slot in range(slots)]
    else:
        whole = jnp.concatenate(parts, axis=0)
        spectra = [
            lax.all_to_all(whole, "freq", split_axis=0, concat_axis=0, tiled=True)
        ]
        sources = [(0, s * (FG // freq_count)) for s in range(freq_count)]
    return tuple(peaks(spectra, sources, twiddles, noise_level, freq_total, folded))


def solution(mesh):
    in_specs = (
        P("batch"),
        P("batch"),
        P("elem"),
        P(),
        P("freq", None, "elem", None),
        P("batch", None),
        P("batch", None),
        P(("batch", "elem"), "freq"),
    )
    out_specs = (P(("batch", "elem"), "freq"), P(("batch", "elem"), "freq"))
    return jax.shard_map(body, mesh=mesh, in_specs=in_specs, out_specs=out_specs, check_vma=False)
```

```python
import functools
import math

import jax
import jax.numpy as jnp
from jax import lax
from jax.experimental import pallas as pl
from jax.experimental.pallas import tpu as pltpu
from jax.sharding import PartitionSpec as P

W_DEV = 16
W_HALF = W_DEV // 2
FG = 128
NB = 4
SB = 32
T_CAP = 1024
FIRST_SLOTS = 3

EDGE = 0.6
STEEP = 3.0
EPS = 1e-05

ROWS = NB * SB
VMEM_BYTES = 48 * 1024 * 1024


def sin_half_turn(turns):
    angle = turns * math.pi
    square = angle * angle
    sine = 1.0 / 6227020800.0
    for factorial in (-39916800.0, 362880.0, -5040.0, 120.0, -6.0, 1.0):
        sine = sine * square + 1.0 / factorial
    cosine = 1.0 / 479001600.0
    for factorial in (-3628800.0, 40320.0, -720.0, 24.0, -2.0, 1.0):
        cosine = cosine * square + 1.0 / factorial
    return sine * angle, cosine


def sincos_turns(turns):
    rest = turns - jnp.floor(turns + 0.5)
    sine, cosine = sin_half_turn(rest)
    return 2.0 * sine * cosine, 1.0 - 2.0 * sine * sine


def dot(left, right, contract):
    return lax.dot_general(
        left, right, (contract, ((), ())), preferred_element_type=jnp.float32
    )


def slot_masks(slots):
    half = slots // 2
    between = (2, half, half + 1, 3, slots - 1)
    return (1, *between, slots - 2, 0), (slots - 2, *between, 1, 0)


def partner(slots, slot):
    index = lax.axis_index("freq")
    inner = ((index * 2) ^ index) & (slots // 2) != 0
    mask = jnp.zeros_like(slot)
    for s, (outer_mask, inner_mask) in enumerate(zip(*slot_masks(slots))):
        mask = jnp.where(slot == s, jnp.where(inner, inner_mask, outer_mask), mask)
    return mask ^ index


def slot_order(slots):
    size = FG // slots
    row = lax.broadcasted_iota(jnp.int32, (FG, 1), 0)
    column = lax.broadcasted_iota(jnp.int32, (FG, FG), 1)
    if slots > 1:
        row = partner(slots, row // size) * size + row % size
    return row == column


def flaw_pick(order, which, cells_ref):
    cells = jnp.where(which == 0, cells_ref[:, :FG], cells_ref[:, FG:])
    cell_sel = lax.broadcasted_iota(jnp.int32, (cells_ref.shape[1], FG), 0) == cells
    return dot(
        order.astype(jnp.bfloat16), cell_sel.astype(jnp.bfloat16), ((1,), (1,))
    ).astype(jnp.bfloat16)


def delays_of(channel_ref, delay_ref, blocks_ref, groups, elements):
    lane = lax.broadcasted_iota(jnp.int32, (1, 2 * ROWS), 1)
    position = lane & (SB - 1)
    for j in range(2 * NB):
        block = blocks_ref[groups[j // NB] * NB + j % NB]
        position = position + jnp.where((lane >> 5) == j, block * SB, 0)
    channels, positions = delay_ref.shape
    scan_sel = (
        lax.broadcasted_iota(jnp.int32, (positions, 2 * ROWS), 0) == position
    ).astype(jnp.bfloat16)
    channel_sel = (
        (lax.broadcasted_iota(jnp.int32, (channels, elements), 0) == channel_ref[...])
        .astype(jnp.float32)
        .T.astype(jnp.bfloat16)
    )
    rest = delay_ref[...]
    pieces = []
    for _ in range(3):
        pieces.append(rest.astype(jnp.bfloat16))
        rest = rest - pieces[-1].astype(jnp.float32)
    moved = jnp.concatenate(
        [dot(channel_sel, piece, ((1,), (0,))).astype(jnp.bfloat16) for piece in pieces], axis=0
    )
    moved = dot(moved, scan_sel, ((1,), (0,)))
    return moved[:elements] + moved[elements : 2 * elements] + moved[2 * elements :]


def turned(law, step):
    return law[0] * step[0] - law[1] * step[1], law[1] * step[0] + law[0] * step[1]


def focal_base(freq_total, delays):
    first_freq = lax.axis_index("freq") * W_DEV
    phase = delays * (0.5 / freq_total)
    unit = sincos_turns(phase)[::-1]
    base = sincos_turns(phase * first_freq.astype(jnp.float32))[::-1]
    return base, turned(unit, unit), turned(base, unit)


def kirchhoff(freq_total, order, which, size_ref, slope_ref):
    first_freq = lax.axis_index("freq") * W_DEV
    size = size_ref[pl.ds(which, 1), :]
    turn = size * slope_ref[pl.ds(which, 1), :] * (1.0 / freq_total)
    size = jnp.sum(jnp.where(order, size, 0.0), axis=1, keepdims=True)
    turn = jnp.sum(jnp.where(order, turn, 0.0), axis=1, keepdims=True)
    freq = first_freq + lax.broadcasted_iota(jnp.int32, (FG, FG), 1)
    sine, cosine = sincos_turns(turn * freq.astype(jnp.float32))
    return size * (1.0 + EDGE) * cosine, size * (EDGE - 1.0) * sine


def store_law(law_ref, law, step):
    elements = law_ref.shape[1] // 2
    double = 2.0 * step[0]
    following = turned(law, step)
    for w in range(W_HALF):
        c = law[0].astype(jnp.bfloat16)
        s = law[1].astype(jnp.bfloat16)
        law_ref[w, :elements, :ROWS] = c
        law_ref[w, :elements, ROWS:] = -s
        law_ref[w, elements:, :ROWS] = s
        law_ref[w, elements:, ROWS:] = c
        law, following = following, [double * x - y for x, y in zip(following, law)]


def pick_fields(parity, picks, field_ref, picked_refs):
    elements, sites = field_ref.shape[3:]
    for w in range(W_HALF):
        picked = dot(
            picks, field_ref[w, parity].reshape(2 * elements, sites), ((1,), (1,))
        ).astype(jnp.bfloat16)
        for i, ref in enumerate(picked_refs):
            ref[parity, w] = picked[i * FG : (i + 1) * FG]


def store_spectra(picked_ref, law_ref, k_real, k_imag, out_refs):
    for parity in range(2):
        for w in range(W_HALF):
            product = dot(picked_ref[parity, w], law_ref[parity, w], ((1,), (0,)))
            real_part = product[:, :ROWS]
            imag_part = product[:, ROWS:]
            kr = k_real[:, 2 * w + parity : 2 * w + parity + 1]
            ki = k_imag[:, 2 * w + parity : 2 * w + parity + 1]
            parts = (kr * real_part - ki * imag_part, kr * imag_part + ki * real_part)
            for k, part in enumerate(parts):
                part = part.astype(jnp.bfloat16)
                first = 0
                for out_ref in out_refs:
                    last = first + out_ref.shape[1]
                    out_ref[parity * W_DEV + 2 * w + k] = part[first:last]
                    first = last


def other_kernel(freq_total, slots, *refs):
    field_hbm, *small_hbm = refs[:7]
    first_ref, second_ref, own_picked_ref, size_ref, slope_ref, delays_ref = refs[7:13]
    delay_ref, channel_ref, blocks_ref, cells_ref = refs[13:17]
    field_ref, field_sem, small_sem, picked_ref, law_ref = refs[17:]
    small = (delay_ref, channel_ref, blocks_ref, cells_ref, size_ref, slope_ref)
    copies = [
        pltpu.make_async_copy(source, target, small_sem.at[i])
        for i, (source, target) in enumerate(zip(small_hbm, small))
    ]
    for copy in copies:
        copy.start()
    field_copies = [
        pltpu.make_async_copy(
            field_hbm.at[:, parity], field_ref.at[:, parity], field_sem.at[parity]
        )
        for parity in range(2)
    ]
    field_copies[0].start()
    order = slot_order(slots)
    for copy in copies:
        copy.wait()
    field_copies[1].start()
    group = lax.axis_index("elem")
    groups = (1 - group, group)
    picks = jnp.concatenate(
        [flaw_pick(order, which, cells_ref) for which in groups], axis=0
    )
    factors = kirchhoff(freq_total, order, groups[0], size_ref, slope_ref)
    delays = delays_of(channel_ref, delay_ref, blocks_ref, groups, field_ref.shape[3])
    delays_ref[...] = delays[:, ROWS:]
    even, step, odd = focal_base(freq_total, delays[:, :ROWS])
    for parity, law in enumerate((even, odd)):
        store_law(law_ref.at[parity], law, step)
        field_copies[parity].wait()
        pick_fields(parity, picks, field_ref, (picked_ref, own_picked_ref))
    store_spectra(picked_ref, law_ref, *factors, (first_ref, second_ref))


def own_kernel(freq_total, slots, *refs):
    picked_ref, delays_ref, size_ref, slope_ref, out_ref, law_ref = refs
    even, step, odd = focal_base(freq_total, delays_ref[...])
    for parity, law in enumerate((even, odd)):
        store_law(law_ref.at[parity], law, step)
    group = lax.axis_index("elem")
    factors = kirchhoff(freq_total, slot_order(slots), group, size_ref, slope_ref)
    store_spectra(picked_ref, law_ref, *factors, (out_ref,))


def call(kernel, name, in_specs, out_shape, scratch):
    vmem = pl.BlockSpec(memory_space=pltpu.VMEM)
    return pl.pallas_call(
        kernel,
        in_specs=in_specs,
        out_specs=[vmem] * len(out_shape),
        out_shape=out_shape,
        scratch_shapes=scratch,
        compiler_params=pltpu.CompilerParams(vmem_limit_bytes=VMEM_BYTES),
        cost_estimate=pl.CostEstimate(flops=1000, bytes_accessed=1000, transcendentals=0),
        name=name,
    )


def partials(field, small, swap, freq_total, slots):
    elements, sites = field.shape[3:]
    vmem = pl.BlockSpec(memory_space=pltpu.VMEM)
    hbm = pl.BlockSpec(memory_space=pltpu.HBM)
    pinned = [pltpu.with_memory_space_constraint(a, pltpu.HBM) for a in (field, *small)]
    out = jax.ShapeDtypeStruct((2 * W_DEV, FG, ROWS), jnp.bfloat16)
    flaws = FG // 2 if slots == 1 else FG // slots * FIRST_SLOTS
    halves = [
        jax.ShapeDtypeStruct((2 * W_DEV, count, ROWS), jnp.bfloat16)
        for count in (flaws, FG - flaws)
    ]
    picked = jax.ShapeDtypeStruct((2, W_HALF, FG, 2 * elements), jnp.bfloat16)
    law = pltpu.VMEM((2, W_HALF, 2 * elements, 2 * ROWS), jnp.bfloat16)
    copied = [jax.ShapeDtypeStruct(a.shape, a.dtype) for a in small[4:]]
    delays = jax.ShapeDtypeStruct((elements, ROWS), jnp.float32)
    first, second, own_picked, size, slope, delays = call(
        functools.partial(other_kernel, freq_total, slots),
        "other",
        [hbm] * len(pinned),
        [*halves, picked, *copied, delays],
        [
            pltpu.SMEM(a.shape, a.dtype) if a.ndim == 1 else pltpu.VMEM(a.shape, a.dtype)
            for a in small[:4]
        ]
        + [
            pltpu.VMEM(field.shape, field.dtype),
            pltpu.SemaphoreType.DMA((2,)),
            pltpu.SemaphoreType.DMA((len(small),)),
            pltpu.VMEM(picked.shape, picked.dtype),
            law,
        ],
    )(*pinned)
    first = lax.ppermute(first, "elem", swap)
    (own,) = call(
        functools.partial(own_kernel, freq_total, slots), "own", [vmem] * 4, [out], [law]
    )(own_picked, delays, size, slope)
    return own, first, second


def add_kernel(first, passed, own_ref, moved_ref, *refs):
    if passed:
        source_ref, *refs, target_ref = refs
        target_ref[...] = source_ref[...]
    size = refs[0].shape[0]
    for slot, ref in enumerate(refs):
        own = own_ref[:, pl.ds(first + slot * size, size)].astype(jnp.float32)
        both = own + moved_ref[:, pl.ds(slot * size, size)].astype(jnp.float32)
        ref[...] = jnp.swapaxes(both, 0, 1).astype(jnp.bfloat16)


def add(own, first, second, swap, slots):
    vmem = pl.BlockSpec(memory_space=pltpu.VMEM)
    planes, flaws, rows = own.shape
    size = min(flaws // slots, first.shape[1])
    shape = jax.ShapeDtypeStruct((size, planes, rows), own.dtype)
    early = first.shape[1]
    *parts, second = call(
        functools.partial(add_kernel, 0, 1),
        "add_first",
        [vmem] * 3,
        [shape] * (early // size) + [jax.ShapeDtypeStruct(second.shape, second.dtype)],
        [],
    )(own, first, second)
    second = lax.ppermute(second, "elem", swap)
    kernel = functools.partial(add_kernel, early, 0)
    shapes = [shape] * ((flaws - early) // size)
    return parts + [*call(kernel, "add_second", [vmem] * 2, shapes, [])(own, second)]


def table_kernel(freq_total, slots, table_ref):
    height, depth = table_ref.shape[2:]
    time_block = height // 2
    row = lax.broadcasted_iota(jnp.int32, (height, depth // 2), 0)
    column = lax.broadcasted_iota(jnp.int32, (height, depth // 2), 1)
    out_imag = (row >= time_block).astype(jnp.int32)
    time = pl.program_id(0) * time_block + row - out_imag * time_block
    for parity in range(2):
        freq = (column >> 1) * 2 + parity
        if slots > 1:
            lane = lax.broadcasted_iota(jnp.int32, (1, depth // 2), 1)
            lane = (lane >> 1) * 2 + parity
            freq = partner(slots, lane // W_DEV) * W_DEV + lane % W_DEV
        steps = freq * time + ((column & 1) - out_imag) * (freq_total // 2)
        steps = (steps + 2 * freq_total) & (2 * freq_total - 1)
        _, value = sincos_turns(steps.astype(jnp.float32) * (0.5 / freq_total))
        high = value.astype(jnp.bfloat16)
        table_ref[0, parity, :, : depth // 2] = high
        table_ref[0, parity, :, depth // 2 :] = (
            value - high.astype(jnp.float32)
        ).astype(jnp.bfloat16)


def table(freq_total, slots, times, time_block):
    blocks = times // time_block
    shape = (blocks, 2, 2 * time_block, 2 * freq_total)
    return pl.pallas_call(
        functools.partial(table_kernel, freq_total, slots),
        grid=(blocks,),
        out_specs=pl.BlockSpec((1, *shape[1:]), lambda i: (i, 0, 0, 0)),
        out_shape=jax.ShapeDtypeStruct(shape, jnp.bfloat16),
        compiler_params=pltpu.CompilerParams(vmem_limit_bytes=VMEM_BYTES),
        name="table",
    )()


def peak_kernel(freq_total, folded, sources, blocks, *refs):
    def first_step():
        return blocks == 1 or pl.program_id(0) == 0

    def last_step():
        return blocks == 1 or pl.program_id(0) == blocks - 1

    count = len(refs) - 5
    table_ref, noise_ref, peak_ref, found_ref, best_ref = refs[count:]
    columns = peak_ref.shape[1]
    time_block = table_ref.shape[2] // 2

    @pl.when(first_step())
    def _():
        best_ref[...] = jnp.zeros_like(best_ref)

    width = min(2, columns)
    for first in range(0, columns, width):
        parts = []
        for parity in range(2):
            planes = slice(parity * W_DEV, (parity + 1) * W_DEV)
            spectra = jnp.concatenate(
                [
                    jnp.concatenate(
                        [
                            refs[i][row + first + k, planes, :]
                            for i, row in sources
                        ]
                        * 2,
                        axis=0,
                    )
                    for k in range(width)
                ],
                axis=1,
            )
            parts.append(dot(table_ref[0, parity], spectra, ((1,), (0,))))
        powers = []
        for signal in [parts[0] + parts[1]] + [parts[0] - parts[1]] * folded:
            real_part = signal[:time_block]
            imag_part = signal[time_block:]
            powers.append(real_part * real_part + imag_part * imag_part)
        power = jnp.maximum(powers[0], powers[-1]) if folded else powers[0]
        power = jnp.max(power, axis=0, keepdims=True)
        for k in range(width):
            row = pl.ds(first + k, 1)
            best_ref[row, :] = jnp.maximum(
                best_ref[row, :], power[:, k * ROWS : (k + 1) * ROWS]
            )

    @pl.when(last_step())
    def _():
        largest = jnp.max(best_ref[...], axis=1, keepdims=True)
        shape = best_ref.shape
        diagonal = lax.broadcasted_iota(jnp.int32, shape, 0) == lax.broadcasted_iota(
            jnp.int32, shape, 1
        )
        largest = jnp.max(jnp.where(diagonal, largest, 0.0), axis=0, keepdims=True)
        peak = jnp.sqrt(largest[:, :columns]) * (1.0 / math.sqrt(freq_total))
        score = STEEP * (jnp.log(peak + EPS) - jnp.log(noise_ref[...]))
        peak_ref[...] = peak
        found_ref[...] = 1.0 / (1.0 + jnp.exp(-score))


def peaks(spectra, sources, twiddles, noise_level, freq_total, folded):
    columns = noise_level.shape[1]
    blocks = twiddles.shape[0]
    if blocks == 1:
        vmem = pl.BlockSpec(memory_space=pltpu.VMEM)
        grid, in_specs, out_spec = (), [vmem] * (len(spectra) + 2), vmem
    else:
        grid = (blocks,)
        out_spec = pl.BlockSpec((1, columns), lambda i: (0, 0))
        in_specs = [pl.BlockSpec(a.shape, lambda i: (0, 0, 0)) for a in spectra]
        in_specs += [
            pl.BlockSpec((1, *twiddles.shape[1:]), lambda i: (i, 0, 0, 0)),
            out_spec,
        ]
    return pl.pallas_call(
        functools.partial(peak_kernel, freq_total, folded, sources, blocks),
        grid=grid,
        in_specs=in_specs,
        out_specs=[out_spec, out_spec],
        out_shape=[jax.ShapeDtypeStruct((1, columns), jnp.float32)] * 2,
        scratch_shapes=[pltpu.VMEM((max(8, columns), ROWS), jnp.float32)],
        compiler_params=pltpu.CompilerParams(vmem_limit_bytes=VMEM_BYTES),
        name="peaks",
    )(*spectra, twiddles, noise_level)


def body(
    flaw_cells,
    flaw_blocks,
    element_channel,
    focal_delay,
    beam_field,
    flaw_size,
    flaw_slope,
    noise_level,
):
    freq_count = lax.axis_size("freq")
    freq_total = W_DEV * freq_count
    sample_count = min(T_CAP, 2 * freq_total)
    swap = [(0, 1), (1, 0)]
    direct = freq_count == 8
    slots = freq_count if direct else 1
    small = (
        focal_delay,
        element_channel.reshape(1, -1),
        flaw_blocks,
        flaw_cells.reshape(1, -1),
        flaw_size,
        flaw_slope,
    )
    folded = sample_count == 2 * freq_total
    times = sample_count // 2 if folded else sample_count
    twiddles = table(freq_total, slots, times, min(128, times))
    field = beam_field.reshape(W_HALF, 2, *beam_field.shape[1:])
    parts = add(*partials(field, small, swap, freq_total, slots), swap, slots)
    if direct:
        half = slots // 2
        spectra = []
        for slot, masks in enumerate(zip(*slot_masks(slots))):
            pairs = [(a, a ^ masks[((2 * a) ^ a) & half != 0]) for a in range(slots)]
            own = slot == slots - 1
            spectra.append(parts[slot] if own else lax.ppermute(parts[slot], "freq", pairs))
        order = (*range(FIRST_SLOTS, slots - 1), *range(FIRST_SLOTS), slots - 1)
        spectra = [spectra[slot] for slot in order]
        sources = [(order.index(slot), 0) for slot in range(slots)]
    else:
        whole = jnp.concatenate(parts, axis=0)
        spectra = [
            lax.all_to_all(whole, "freq", split_axis=0, concat_axis=0, tiled=True)
        ]
        sources = [(0, s * (FG // freq_count)) for s in range(freq_count)]
    return tuple(peaks(spectra, sources, twiddles, noise_level, freq_total, folded))


def solution(mesh):
    in_specs = (
        P("batch"),
        P("batch"),
        P("elem"),
        P(),
        P("freq", None, "elem", None),
        P("batch", None),
        P("batch", None),
        P(("batch", "elem"), "freq"),
    )
    out_specs = (P(("batch", "elem"), "freq"), P(("batch", "elem"), "freq"))
    return jax.shard_map(body, mesh=mesh, in_specs=in_specs, out_specs=out_specs, check_vma=False)
```

```python
import functools
import math

import jax
import jax.numpy as jnp
from jax import lax
from jax.experimental import pallas as pl
from jax.experimental.pallas import tpu as pltpu
from jax.sharding import PartitionSpec as P

W_DEV = 16
W_HALF = W_DEV // 2
FG = 128
NB = 4
SB = 32
T_CAP = 1024

EDGE = 0.6
STEEP = 3.0
EPS = 1e-05

ROWS = NB * SB
VMEM_BYTES = 48 * 1024 * 1024


def sin_half_turn(turns):
    angle = turns * math.pi
    square = angle * angle
    sine = 1.0 / 6227020800.0
    for factorial in (-39916800.0, 362880.0, -5040.0, 120.0, -6.0, 1.0):
        sine = sine * square + 1.0 / factorial
    cosine = 1.0 / 479001600.0
    for factorial in (-3628800.0, 40320.0, -720.0, 24.0, -2.0, 1.0):
        cosine = cosine * square + 1.0 / factorial
    return sine * angle, cosine


def sincos_turns(turns):
    rest = turns - jnp.floor(turns + 0.5)
    sine, cosine = sin_half_turn(rest)
    return 2.0 * sine * cosine, 1.0 - 2.0 * sine * sine


def dot(left, right, contract):
    return lax.dot_general(
        left, right, (contract, ((), ())), preferred_element_type=jnp.float32
    )


def slot_masks(slots):
    half = slots // 2
    between = (2, half, half + 1, 3, slots - 1)
    return (1, *between, slots - 2, 0), (slots - 2, *between, 1, 0)


def partner(slots, slot):
    index = lax.axis_index("freq")
    inner = ((index * 2) ^ index) & (slots // 2) != 0
    mask = jnp.zeros_like(slot)
    for s, (outer_mask, inner_mask) in enumerate(zip(*slot_masks(slots))):
        mask = jnp.where(slot == s, jnp.where(inner, inner_mask, outer_mask), mask)
    return mask ^ index


def slot_order(slots):
    size = FG // slots
    row = lax.broadcasted_iota(jnp.int32, (FG, 1), 0)
    column = lax.broadcasted_iota(jnp.int32, (FG, FG), 1)
    if slots > 1:
        row = partner(slots, row // size) * size + row % size
    return row == column


def flaw_pick(order, which, cells_ref):
    cells = jnp.where(which == 0, cells_ref[:, :FG], cells_ref[:, FG:])
    cell_sel = lax.broadcasted_iota(jnp.int32, (cells_ref.shape[1], FG), 0) == cells
    return dot(
        order.astype(jnp.bfloat16), cell_sel.astype(jnp.bfloat16), ((1,), (1,))
    ).astype(jnp.bfloat16)


def delays_of(channel_ref, delay_ref, blocks_ref, groups, elements):
    lane = lax.broadcasted_iota(jnp.int32, (1, 2 * ROWS), 1)
    position = lane & (SB - 1)
    for j in range(2 * NB):
        block = blocks_ref[groups[j // NB] * NB + j % NB]
        position = position + jnp.where((lane >> 5) == j, block * SB, 0)
    channels, positions = delay_ref.shape
    scan_sel = (
        lax.broadcasted_iota(jnp.int32, (positions, 2 * ROWS), 0) == position
    ).astype(jnp.bfloat16)
    channel_sel = (
        (lax.broadcasted_iota(jnp.int32, (channels, elements), 0) == channel_ref[...])
        .astype(jnp.float32)
        .T.astype(jnp.bfloat16)
    )
    rest = delay_ref[...]
    pieces = []
    for _ in range(3):
        pieces.append(rest.astype(jnp.bfloat16))
        rest = rest - pieces[-1].astype(jnp.float32)
    moved = jnp.concatenate(
        [dot(channel_sel, piece, ((1,), (0,))).astype(jnp.bfloat16) for piece in pieces], axis=0
    )
    moved = dot(moved, scan_sel, ((1,), (0,)))
    return moved[:elements] + moved[elements : 2 * elements] + moved[2 * elements :]


def turned(law, step):
    return law[0] * step[0] - law[1] * step[1], law[1] * step[0] + law[0] * step[1]


def focal_base(freq_total, delays):
    first_freq = lax.axis_index("freq") * W_DEV
    phase = delays * (0.5 / freq_total)
    unit = sincos_turns(phase)[::-1]
    base = sincos_turns(phase * first_freq.astype(jnp.float32))[::-1]
    return base, turned(unit, unit), turned(base, unit)


def kirchhoff(freq_total, order, which, size_ref, slope_ref):
    first_freq = lax.axis_index("freq") * W_DEV
    size = size_ref[pl.ds(which, 1), :]
    turn = size * slope_ref[pl.ds(which, 1), :] * (1.0 / freq_total)
    size = jnp.sum(jnp.where(order, size, 0.0), axis=1, keepdims=True)
    turn = jnp.sum(jnp.where(order, turn, 0.0), axis=1, keepdims=True)
    freq = first_freq + lax.broadcasted_iota(jnp.int32, (FG, FG), 1)
    sine, cosine = sincos_turns(turn * freq.astype(jnp.float32))
    return size * (1.0 + EDGE) * cosine, size * (EDGE - 1.0) * sine


def store_law(law_ref, law, step):
    elements = law_ref.shape[1] // 2
    double = 2.0 * step[0]
    following = turned(law, step)
    for w in range(W_HALF):
        c = law[0].astype(jnp.bfloat16)
        s = law[1].astype(jnp.bfloat16)
        law_ref[w, :elements, :ROWS] = c
        law_ref[w, :elements, ROWS:] = -s
        law_ref[w, elements:, :ROWS] = s
        law_ref[w, elements:, ROWS:] = c
        law, following = following, [double * x - y for x, y in zip(following, law)]


def pick_fields(parity, picks, field_ref, picked_refs):
    elements, sites = field_ref.shape[3:]
    width = 2
    for w in range(0, W_HALF, width):
        rows = field_ref[w : w + width, parity].reshape(width * 2 * elements, sites)
        picked = dot(picks, rows, ((1,), (1,))).astype(jnp.bfloat16)
        for k in range(width):
            columns = slice(k * 2 * elements, (k + 1) * 2 * elements)
            for i, ref in enumerate(picked_refs):
                ref[parity, w + k] = picked[i * FG : (i + 1) * FG, columns]


def store_spectra(picked_ref, law_ref, k_real, k_imag, out_refs):
    size = out_refs[0].shape[1]
    for parity in range(2):
        for w in range(W_HALF):
            product = dot(picked_ref[parity, w], law_ref[parity, w], ((1,), (0,)))
            real_part = product[:, :ROWS]
            imag_part = product[:, ROWS:]
            kr = k_real[:, 2 * w + parity : 2 * w + parity + 1]
            ki = k_imag[:, 2 * w + parity : 2 * w + parity + 1]
            parts = (kr * real_part - ki * imag_part, kr * imag_part + ki * real_part)
            for k, part in enumerate(parts):
                part = part.astype(jnp.bfloat16)
                for i, out_ref in enumerate(out_refs):
                    out_ref[parity * W_DEV + 2 * w + k] = part[i * size : (i + 1) * size]


def other_kernel(freq_total, slots, *refs):
    field_hbm, *small_hbm = refs[:7]
    first_ref, second_ref, own_picked_ref, size_ref, slope_ref, delays_ref = refs[7:13]
    delay_ref, channel_ref, blocks_ref, cells_ref = refs[13:17]
    field_ref, field_sem, small_sem, picked_ref, law_ref = refs[17:]
    small = (delay_ref, channel_ref, blocks_ref, cells_ref, size_ref, slope_ref)
    copies = [
        pltpu.make_async_copy(source, target, small_sem.at[i])
        for i, (source, target) in enumerate(zip(small_hbm, small))
    ]
    for copy in copies:
        copy.start()
    field_copies = [
        pltpu.make_async_copy(
            field_hbm.at[:, parity], field_ref.at[:, parity], field_sem.at[parity]
        )
        for parity in range(2)
    ]
    field_copies[0].start()
    order = slot_order(slots)
    for copy in copies:
        copy.wait()
    field_copies[1].start()
    group = lax.axis_index("elem")
    groups = (1 - group, group)
    picks = jnp.concatenate(
        [flaw_pick(order, which, cells_ref) for which in groups], axis=0
    )
    factors = kirchhoff(freq_total, order, groups[0], size_ref, slope_ref)
    delays = delays_of(channel_ref, delay_ref, blocks_ref, groups, field_ref.shape[3])
    delays_ref[...] = delays[:, ROWS:]
    even, step, odd = focal_base(freq_total, delays[:, :ROWS])
    for parity, law in enumerate((even, odd)):
        store_law(law_ref.at[parity], law, step)
        field_copies[parity].wait()
        pick_fields(parity, picks, field_ref, (picked_ref, own_picked_ref))
    store_spectra(picked_ref, law_ref, *factors, (first_ref, second_ref))


def own_kernel(freq_total, slots, *refs):
    picked_ref, delays_ref, size_ref, slope_ref, out_ref, law_ref = refs
    even, step, odd = focal_base(freq_total, delays_ref[...])
    for parity, law in enumerate((even, odd)):
        store_law(law_ref.at[parity], law, step)
    group = lax.axis_index("elem")
    factors = kirchhoff(freq_total, slot_order(slots), group, size_ref, slope_ref)
    store_spectra(picked_ref, law_ref, *factors, (out_ref,))


def call(kernel, name, in_specs, out_shape, scratch):
    vmem = pl.BlockSpec(memory_space=pltpu.VMEM)
    return pl.pallas_call(
        kernel,
        in_specs=in_specs,
        out_specs=[vmem] * len(out_shape),
        out_shape=out_shape,
        scratch_shapes=scratch,
        compiler_params=pltpu.CompilerParams(vmem_limit_bytes=VMEM_BYTES),
        cost_estimate=pl.CostEstimate(flops=1000, bytes_accessed=1000, transcendentals=0),
        name=name,
    )


def partials(field, small, swap, freq_total, slots):
    elements, sites = field.shape[3:]
    vmem = pl.BlockSpec(memory_space=pltpu.VMEM)
    hbm = pl.BlockSpec(memory_space=pltpu.HBM)
    pinned = [pltpu.with_memory_space_constraint(a, pltpu.HBM) for a in (field, *small)]
    out = jax.ShapeDtypeStruct((2 * W_DEV, FG, ROWS), jnp.bfloat16)
    half = jax.ShapeDtypeStruct((2 * W_DEV, FG // 2, ROWS), jnp.bfloat16)
    picked = jax.ShapeDtypeStruct((2, W_HALF, FG, 2 * elements), jnp.bfloat16)
    law = pltpu.VMEM((2, W_HALF, 2 * elements, 2 * ROWS), jnp.bfloat16)
    copied = [jax.ShapeDtypeStruct(a.shape, a.dtype) for a in small[4:]]
    delays = jax.ShapeDtypeStruct((elements, ROWS), jnp.float32)
    first, second, own_picked, size, slope, delays = call(
        functools.partial(other_kernel, freq_total, slots),
        "other",
        [hbm] * len(pinned),
        [half, half, picked, *copied, delays],
        [
            pltpu.SMEM(a.shape, a.dtype) if a.ndim == 1 else pltpu.VMEM(a.shape, a.dtype)
            for a in small[:4]
        ]
        + [
            pltpu.VMEM(field.shape, field.dtype),
            pltpu.SemaphoreType.DMA((2,)),
            pltpu.SemaphoreType.DMA((len(small),)),
            pltpu.VMEM(picked.shape, picked.dtype),
            law,
        ],
    )(*pinned)
    first = lax.ppermute(first, "elem", swap)
    second = lax.ppermute(second, "elem", swap)
    (own,) = call(
        functools.partial(own_kernel, freq_total, slots), "own", [vmem] * 4, [out], [law]
    )(own_picked, delays, size, slope)
    return own, first, second


def add_kernel(first, own_ref, moved_ref, *refs):
    size = refs[0].shape[0]
    for slot, ref in enumerate(refs):
        own = own_ref[:, pl.ds(first + slot * size, size)].astype(jnp.float32)
        both = own + moved_ref[:, pl.ds(slot * size, size)].astype(jnp.float32)
        ref[...] = jnp.swapaxes(both, 0, 1).astype(jnp.bfloat16)


def add(own, first, second, slots):
    vmem = pl.BlockSpec(memory_space=pltpu.VMEM)
    planes, flaws, rows = own.shape
    count = max(1, slots // 2)
    shape = jax.ShapeDtypeStruct((flaws // 2 // count, planes, rows), own.dtype)
    parts = []
    for name, start, moved in (("add_first", 0, first), ("add_second", flaws // 2, second)):
        kernel = functools.partial(add_kernel, start)
        parts += call(kernel, name, [vmem] * 2, [shape] * count, [])(own, moved)
    return parts


def table_kernel(freq_total, slots, table_ref):
    height, depth = table_ref.shape[2:]
    time_block = height // 2
    row = lax.broadcasted_iota(jnp.int32, (height, depth // 2), 0)
    column = lax.broadcasted_iota(jnp.int32, (height, depth // 2), 1)
    out_imag = (row >= time_block).astype(jnp.int32)
    time = pl.program_id(0) * time_block + row - out_imag * time_block
    for parity in range(2):
        freq = (column >> 1) * 2 + parity
        if slots > 1:
            lane = lax.broadcasted_iota(jnp.int32, (1, depth // 2), 1)
            lane = (lane >> 1) * 2 + parity
            freq = partner(slots, lane // W_DEV) * W_DEV + lane % W_DEV
        steps = freq * time + ((column & 1) - out_imag) * (freq_total // 2)
        steps = (steps + 2 * freq_total) & (2 * freq_total - 1)
        _, value = sincos_turns(steps.astype(jnp.float32) * (0.5 / freq_total))
        high = value.astype(jnp.bfloat16)
        table_ref[0, parity, :, : depth // 2] = high
        table_ref[0, parity, :, depth // 2 :] = (
            value - high.astype(jnp.float32)
        ).astype(jnp.bfloat16)


def table(freq_total, slots, times, time_block):
    blocks = times // time_block
    shape = (blocks, 2, 2 * time_block, 2 * freq_total)
    return pl.pallas_call(
        functools.partial(table_kernel, freq_total, slots),
        grid=(blocks,),
        out_specs=pl.BlockSpec((1, *shape[1:]), lambda i: (i, 0, 0, 0)),
        out_shape=jax.ShapeDtypeStruct(shape, jnp.bfloat16),
        compiler_params=pltpu.CompilerParams(vmem_limit_bytes=VMEM_BYTES),
        name="table",
    )()


def peak_kernel(freq_total, folded, sources, blocks, *refs):
    def first_step():
        return blocks == 1 or pl.program_id(0) == 0

    def last_step():
        return blocks == 1 or pl.program_id(0) == blocks - 1

    count = len(refs) - 5
    table_ref, noise_ref, peak_ref, found_ref, best_ref = refs[count:]
    columns = peak_ref.shape[1]
    time_block = table_ref.shape[2] // 2

    @pl.when(first_step())
    def _():
        best_ref[...] = jnp.zeros_like(best_ref)

    width = min(4, columns)
    for first in range(0, columns, width):
        parts = []
        for parity in range(2):
            planes = slice(parity * W_DEV, (parity + 1) * W_DEV)
            spectra = jnp.concatenate(
                [
                    jnp.concatenate(
                        [
                            refs[i][row + first + k, planes, :]
                            for i, row in sources
                        ]
                        * 2,
                        axis=0,
                    )
                    for k in range(width)
                ],
                axis=1,
            )
            parts.append(dot(table_ref[0, parity], spectra, ((1,), (0,))))
        powers = []
        for signal in [parts[0] + parts[1]] + [parts[0] - parts[1]] * folded:
            real_part = signal[:time_block]
            imag_part = signal[time_block:]
            powers.append(real_part * real_part + imag_part * imag_part)
        power = jnp.maximum(powers[0], powers[-1]) if folded else powers[0]
        power = jnp.max(power, axis=0, keepdims=True)
        for k in range(width):
            row = pl.ds(first + k, 1)
            best_ref[row, :] = jnp.maximum(
                best_ref[row, :], power[:, k * ROWS : (k + 1) * ROWS]
            )

    @pl.when(last_step())
    def _():
        largest = jnp.max(best_ref[...], axis=1, keepdims=True)
        shape = best_ref.shape
        diagonal = lax.broadcasted_iota(jnp.int32, shape, 0) == lax.broadcasted_iota(
            jnp.int32, shape, 1
        )
        largest = jnp.max(jnp.where(diagonal, largest, 0.0), axis=0, keepdims=True)
        peak = jnp.sqrt(largest[:, :columns]) * (1.0 / math.sqrt(freq_total))
        score = STEEP * (jnp.log(peak + EPS) - jnp.log(noise_ref[...]))
        peak_ref[...] = peak
        found_ref[...] = 1.0 / (1.0 + jnp.exp(-score))


def peaks(spectra, sources, twiddles, noise_level, freq_total, folded):
    columns = noise_level.shape[1]
    blocks = twiddles.shape[0]
    if blocks == 1:
        vmem = pl.BlockSpec(memory_space=pltpu.VMEM)
        grid, in_specs, out_spec = (), [vmem] * (len(spectra) + 2), vmem
    else:
        grid = (blocks,)
        out_spec = pl.BlockSpec((1, columns), lambda i: (0, 0))
        in_specs = [pl.BlockSpec(a.shape, lambda i: (0, 0, 0)) for a in spectra]
        in_specs += [
            pl.BlockSpec((1, *twiddles.shape[1:]), lambda i: (i, 0, 0, 0)),
            out_spec,
        ]
    return pl.pallas_call(
        functools.partial(peak_kernel, freq_total, folded, sources, blocks),
        grid=grid,
        in_specs=in_specs,
        out_specs=[out_spec, out_spec],
        out_shape=[jax.ShapeDtypeStruct((1, columns), jnp.float32)] * 2,
        scratch_shapes=[pltpu.VMEM((max(8, columns), ROWS), jnp.float32)],
        compiler_params=pltpu.CompilerParams(vmem_limit_bytes=VMEM_BYTES),
        name="peaks",
    )(*spectra, twiddles, noise_level)


def body(
    flaw_cells,
    flaw_blocks,
    element_channel,
    focal_delay,
    beam_field,
    flaw_size,
    flaw_slope,
    noise_level,
):
    freq_count = lax.axis_size("freq")
    freq_total = W_DEV * freq_count
    sample_count = min(T_CAP, 2 * freq_total)
    swap = [(0, 1), (1, 0)]
    direct = freq_count == 8
    slots = freq_count if direct else 1
    small = (
        focal_delay,
        element_channel.reshape(1, -1),
        flaw_blocks,
        flaw_cells.reshape(1, -1),
        flaw_size,
        flaw_slope,
    )
    folded = sample_count == 2 * freq_total
    times = sample_count // 2 if folded else sample_count
    twiddles = table(freq_total, slots, times, min(128, times))
    field = beam_field.reshape(W_HALF, 2, *beam_field.shape[1:])
    parts = add(*partials(field, small, swap, freq_total, slots), slots)
    if direct:
        half = slots // 2
        spectra = []
        for slot, masks in enumerate(zip(*slot_masks(slots))):
            pairs = [(a, a ^ masks[((2 * a) ^ a) & half != 0]) for a in range(slots)]
            own = slot == slots - 1
            spectra.append(parts[slot] if own else lax.ppermute(parts[slot], "freq", pairs))
        order = (*range(half, slots - 1), *range(half), slots - 1)
        spectra = [spectra[slot] for slot in order]
        sources = [(order.index(slot), 0) for slot in range(slots)]
    else:
        whole = jnp.concatenate(parts, axis=0)
        spectra = [
            lax.all_to_all(whole, "freq", split_axis=0, concat_axis=0, tiled=True)
        ]
        sources = [(0, s * (FG // freq_count)) for s in range(freq_count)]
    return tuple(peaks(spectra, sources, twiddles, noise_level, freq_total, folded))


def solution(mesh):
    in_specs = (
        P("batch"),
        P("batch"),
        P("elem"),
        P(),
        P("freq", None, "elem", None),
        P("batch", None),
        P("batch", None),
        P(("batch", "elem"), "freq"),
    )
    out_specs = (P(("batch", "elem"), "freq"), P(("batch", "elem"), "freq"))
    return jax.shard_map(body, mesh=mesh, in_specs=in_specs, out_specs=out_specs, check_vma=False)
```

```python
import functools
import math

import jax
import jax.numpy as jnp
from jax import lax
from jax.experimental import pallas as pl
from jax.experimental.pallas import tpu as pltpu
from jax.sharding import PartitionSpec as P

W_DEV = 16
W_HALF = W_DEV // 2
FG = 128
NB = 4
SB = 32
T_CAP = 1024

EDGE = 0.6
STEEP = 3.0
EPS = 1e-05

ROWS = NB * SB
VMEM_BYTES = 48 * 1024 * 1024


def sin_half_turn(turns):
    angle = turns * math.pi
    square = angle * angle
    sine = 1.0 / 6227020800.0
    for factorial in (-39916800.0, 362880.0, -5040.0, 120.0, -6.0, 1.0):
        sine = sine * square + 1.0 / factorial
    cosine = 1.0 / 479001600.0
    for factorial in (-3628800.0, 40320.0, -720.0, 24.0, -2.0, 1.0):
        cosine = cosine * square + 1.0 / factorial
    return sine * angle, cosine


def sincos_turns(turns):
    rest = turns - jnp.floor(turns + 0.5)
    sine, cosine = sin_half_turn(rest)
    return 2.0 * sine * cosine, 1.0 - 2.0 * sine * sine


def dot(left, right, contract):
    return lax.dot_general(
        left, right, (contract, ((), ())), preferred_element_type=jnp.float32
    )


def slot_masks(slots):
    half = slots // 2
    between = (2, half + 1, half, 3, slots - 1)
    return (1, *between, slots - 2, 0), (slots - 2, *between, 1, 0)


def partner(slots, slot):
    index = lax.axis_index("freq")
    inner = ((index * 2) ^ index) & (slots // 2) != 0
    mask = jnp.zeros_like(slot)
    for s, (outer_mask, inner_mask) in enumerate(zip(*slot_masks(slots))):
        mask = jnp.where(slot == s, jnp.where(inner, inner_mask, outer_mask), mask)
    return mask ^ index


def slot_order(slots):
    size = FG // slots
    row = lax.broadcasted_iota(jnp.int32, (FG, 1), 0)
    column = lax.broadcasted_iota(jnp.int32, (FG, FG), 1)
    if slots > 1:
        row = partner(slots, row // size) * size + row % size
    return row == column


def flaw_pick(order, which, cells_ref):
    cells = jnp.where(which == 0, cells_ref[:, :FG], cells_ref[:, FG:])
    cell_sel = lax.broadcasted_iota(jnp.int32, (cells_ref.shape[1], FG), 0) == cells
    return dot(
        order.astype(jnp.bfloat16), cell_sel.astype(jnp.bfloat16), ((1,), (1,))
    ).astype(jnp.bfloat16)


def delays_of(channel_ref, delay_ref, blocks_ref, groups, elements):
    lane = lax.broadcasted_iota(jnp.int32, (1, 2 * ROWS), 1)
    position = lane & (SB - 1)
    for j in range(2 * NB):
        block = blocks_ref[groups[j // NB] * NB + j % NB]
        position = position + jnp.where((lane >> 5) == j, block * SB, 0)
    channels, positions = delay_ref.shape
    scan_sel = (
        lax.broadcasted_iota(jnp.int32, (positions, 2 * ROWS), 0) == position
    ).astype(jnp.bfloat16)
    channel_sel = (
        (lax.broadcasted_iota(jnp.int32, (channels, elements), 0) == channel_ref[...])
        .astype(jnp.float32)
        .T.astype(jnp.bfloat16)
    )
    rest = delay_ref[...]
    pieces = []
    for _ in range(3):
        pieces.append(rest.astype(jnp.bfloat16))
        rest = rest - pieces[-1].astype(jnp.float32)
    moved = jnp.concatenate(
        [dot(channel_sel, piece, ((1,), (0,))).astype(jnp.bfloat16) for piece in pieces], axis=0
    )
    moved = dot(moved, scan_sel, ((1,), (0,)))
    return moved[:elements] + moved[elements : 2 * elements] + moved[2 * elements :]


def turned(law, step):
    return law[0] * step[0] - law[1] * step[1], law[1] * step[0] + law[0] * step[1]


def focal_base(freq_total, delays):
    first_freq = lax.axis_index("freq") * W_DEV
    phase = delays * (0.5 / freq_total)
    unit = sincos_turns(phase)[::-1]
    base = sincos_turns(phase * first_freq.astype(jnp.float32))[::-1]
    return base, turned(unit, unit), turned(base, unit)


def kirchhoff(freq_total, order, which, size_ref, slope_ref):
    first_freq = lax.axis_index("freq") * W_DEV
    size = size_ref[pl.ds(which, 1), :]
    turn = size * slope_ref[pl.ds(which, 1), :] * (1.0 / freq_total)
    size = jnp.sum(jnp.where(order, size, 0.0), axis=1, keepdims=True)
    turn = jnp.sum(jnp.where(order, turn, 0.0), axis=1, keepdims=True)
    freq = first_freq + lax.broadcasted_iota(jnp.int32, (FG, FG), 1)
    sine, cosine = sincos_turns(turn * freq.astype(jnp.float32))
    return size * (1.0 + EDGE) * cosine, size * (EDGE - 1.0) * sine


def store_law(law_ref, law, step):
    elements = law_ref.shape[1] // 2
    double = 2.0 * step[0]
    following = turned(law, step)
    for w in range(W_HALF):
        c = law[0].astype(jnp.bfloat16)
        s = law[1].astype(jnp.bfloat16)
        law_ref[w, :elements, :ROWS] = c
        law_ref[w, :elements, ROWS:] = -s
        law_ref[w, elements:, :ROWS] = s
        law_ref[w, elements:, ROWS:] = c
        law, following = following, [double * x - y for x, y in zip(following, law)]


def pick_fields(parity, picks, field_ref, picked_refs):
    elements, sites = field_ref.shape[3:]
    for w in range(W_HALF):
        picked = dot(
            picks, field_ref[w, parity].reshape(2 * elements, sites), ((1,), (1,))
        ).astype(jnp.bfloat16)
        for i, ref in enumerate(picked_refs):
            ref[parity, w] = picked[i * FG : (i + 1) * FG]


def store_spectra(picked_ref, law_ref, k_real, k_imag, out_refs):
    size = out_refs[0].shape[1]
    for parity in range(2):
        for w in range(W_HALF):
            product = dot(picked_ref[parity, w], law_ref[parity, w], ((1,), (0,)))
            real_part = product[:, :ROWS]
            imag_part = product[:, ROWS:]
            kr = k_real[:, 2 * w + parity : 2 * w + parity + 1]
            ki = k_imag[:, 2 * w + parity : 2 * w + parity + 1]
            parts = (kr * real_part - ki * imag_part, kr * imag_part + ki * real_part)
            for k, part in enumerate(parts):
                part = part.astype(jnp.bfloat16)
                for i, out_ref in enumerate(out_refs):
                    out_ref[parity * W_DEV + 2 * w + k] = part[i * size : (i + 1) * size]


def other_kernel(freq_total, slots, *refs):
    field_hbm, *small_hbm = refs[:7]
    first_ref, second_ref, own_picked_ref, size_ref, slope_ref, delays_ref = refs[7:13]
    delay_ref, channel_ref, blocks_ref, cells_ref = refs[13:17]
    field_ref, field_sem, small_sem, picked_ref, law_ref = refs[17:]
    small = (delay_ref, channel_ref, blocks_ref, cells_ref, size_ref, slope_ref)
    copies = [
        pltpu.make_async_copy(source, target, small_sem.at[i])
        for i, (source, target) in enumerate(zip(small_hbm, small))
    ]
    for copy in copies:
        copy.start()
    field_copies = [
        pltpu.make_async_copy(
            field_hbm.at[:, parity], field_ref.at[:, parity], field_sem.at[parity]
        )
        for parity in range(2)
    ]
    field_copies[0].start()
    order = slot_order(slots)
    for copy in copies:
        copy.wait()
    field_copies[1].start()
    group = lax.axis_index("elem")
    groups = (1 - group, group)
    picks = jnp.concatenate(
        [flaw_pick(order, which, cells_ref) for which in groups], axis=0
    )
    factors = kirchhoff(freq_total, order, groups[0], size_ref, slope_ref)
    delays = delays_of(channel_ref, delay_ref, blocks_ref, groups, field_ref.shape[3])
    delays_ref[...] = delays[:, ROWS:]
    even, step, odd = focal_base(freq_total, delays[:, :ROWS])
    for parity, law in enumerate((even, odd)):
        store_law(law_ref.at[parity], law, step)
        field_copies[parity].wait()
        pick_fields(parity, picks, field_ref, (picked_ref, own_picked_ref))
    store_spectra(picked_ref, law_ref, *factors, (first_ref, second_ref))


def own_kernel(freq_total, slots, *refs):
    picked_ref, delays_ref, size_ref, slope_ref, out_ref, law_ref = refs
    even, step, odd = focal_base(freq_total, delays_ref[...])
    for parity, law in enumerate((even, odd)):
        store_law(law_ref.at[parity], law, step)
    group = lax.axis_index("elem")
    factors = kirchhoff(freq_total, slot_order(slots), group, size_ref, slope_ref)
    store_spectra(picked_ref, law_ref, *factors, (out_ref,))


def call(kernel, name, in_specs, out_shape, scratch):
    vmem = pl.BlockSpec(memory_space=pltpu.VMEM)
    return pl.pallas_call(
        kernel,
        in_specs=in_specs,
        out_specs=[vmem] * len(out_shape),
        out_shape=out_shape,
        scratch_shapes=scratch,
        compiler_params=pltpu.CompilerParams(vmem_limit_bytes=VMEM_BYTES),
        cost_estimate=pl.CostEstimate(flops=1000, bytes_accessed=1000, transcendentals=0),
        name=name,
    )


def partials(field, small, swap, freq_total, slots):
    elements, sites = field.shape[3:]
    vmem = pl.BlockSpec(memory_space=pltpu.VMEM)
    hbm = pl.BlockSpec(memory_space=pltpu.HBM)
    pinned = [pltpu.with_memory_space_constraint(a, pltpu.HBM) for a in (field, *small)]
    out = jax.ShapeDtypeStruct((2 * W_DEV, FG, ROWS), jnp.bfloat16)
    half = jax.ShapeDtypeStruct((2 * W_DEV, FG // 2, ROWS), jnp.bfloat16)
    picked = jax.ShapeDtypeStruct((2, W_HALF, FG, 2 * elements), jnp.bfloat16)
    law = pltpu.VMEM((2, W_HALF, 2 * elements, 2 * ROWS), jnp.bfloat16)
    copied = [jax.ShapeDtypeStruct(a.shape, a.dtype) for a in small[4:]]
    delays = jax.ShapeDtypeStruct((elements, ROWS), jnp.float32)
    first, second, own_picked, size, slope, delays = call(
        functools.partial(other_kernel, freq_total, slots),
        "other",
        [hbm] * len(pinned),
        [half, half, picked, *copied, delays],
        [
            pltpu.SMEM(a.shape, a.dtype) if a.ndim == 1 else pltpu.VMEM(a.shape, a.dtype)
            for a in small[:4]
        ]
        + [
            pltpu.VMEM(field.shape, field.dtype),
            pltpu.SemaphoreType.DMA((2,)),
            pltpu.SemaphoreType.DMA((len(small),)),
            pltpu.VMEM(picked.shape, picked.dtype),
            law,
        ],
    )(*pinned)
    first = lax.ppermute(first, "elem", swap)
    second = lax.ppermute(second, "elem", swap)
    (own,) = call(
        functools.partial(own_kernel, freq_total, slots), "own", [vmem] * 4, [out], [law]
    )(own_picked, delays, size, slope)
    return own, first, second


def add_kernel(first, own_ref, moved_ref, *refs):
    size = refs[0].shape[0]
    for slot, ref in enumerate(refs):
        own = own_ref[:, pl.ds(first + slot * size, size)].astype(jnp.float32)
        both = own + moved_ref[:, pl.ds(slot * size, size)].astype(jnp.float32)
        ref[...] = jnp.swapaxes(both, 0, 1).astype(jnp.bfloat16)


def add(own, first, second, slots):
    vmem = pl.BlockSpec(memory_space=pltpu.VMEM)
    planes, flaws, rows = own.shape
    count = max(1, slots // 2)
    shape = jax.ShapeDtypeStruct((flaws // 2 // count, planes, rows), own.dtype)
    parts = []
    for name, start, moved in (("add_first", 0, first), ("add_second", flaws // 2, second)):
        kernel = functools.partial(add_kernel, start)
        parts += call(kernel, name, [vmem] * 2, [shape] * count, [])(own, moved)
    return parts


def table_kernel(freq_total, slots, table_ref):
    height, depth = table_ref.shape[2:]
    time_block = height // 2
    row = lax.broadcasted_iota(jnp.int32, (height, depth // 2), 0)
    column = lax.broadcasted_iota(jnp.int32, (height, depth // 2), 1)
    out_imag = (row >= time_block).astype(jnp.int32)
    time = pl.program_id(0) * time_block + row - out_imag * time_block
    for parity in range(2):
        freq = (column >> 1) * 2 + parity
        if slots > 1:
            lane = lax.broadcasted_iota(jnp.int32, (1, depth // 2), 1)
            lane = (lane >> 1) * 2 + parity
            freq = partner(slots, lane // W_DEV) * W_DEV + lane % W_DEV
        steps = freq * time + ((column & 1) - out_imag) * (freq_total // 2)
        steps = (steps + 2 * freq_total) & (2 * freq_total - 1)
        _, value = sincos_turns(steps.astype(jnp.float32) * (0.5 / freq_total))
        high = value.astype(jnp.bfloat16)
        table_ref[0, parity, :, : depth // 2] = high
        table_ref[0, parity, :, depth // 2 :] = (
            value - high.astype(jnp.float32)
        ).astype(jnp.bfloat16)


def table(freq_total, slots, times, time_block):
    blocks = times // time_block
    shape = (blocks, 2, 2 * time_block, 2 * freq_total)
    return pl.pallas_call(
        functools.partial(table_kernel, freq_total, slots),
        grid=(blocks,),
        out_specs=pl.BlockSpec((1, *shape[1:]), lambda i: (i, 0, 0, 0)),
        out_shape=jax.ShapeDtypeStruct(shape, jnp.bfloat16),
        compiler_params=pltpu.CompilerParams(vmem_limit_bytes=VMEM_BYTES),
        name="table",
    )()


def peak_kernel(freq_total, folded, sources, blocks, *refs):
    def first_step():
        return blocks == 1 or pl.program_id(0) == 0

    def last_step():
        return blocks == 1 or pl.program_id(0) == blocks - 1

    count = len(refs) - 5
    table_ref, noise_ref, peak_ref, found_ref, best_ref = refs[count:]
    columns = peak_ref.shape[1]
    time_block = table_ref.shape[2] // 2

    @pl.when(first_step())
    def _():
        best_ref[...] = jnp.zeros_like(best_ref)

    width = min(2, columns)
    for first in range(0, columns, width):
        parts = []
        for parity in range(2):
            planes = slice(parity * W_DEV, (parity + 1) * W_DEV)
            spectra = jnp.concatenate(
                [
                    jnp.concatenate(
                        [
                            refs[i][row + first + k, planes, :]
                            for i, row in sources
                        ]
                        * 2,
                        axis=0,
                    )
                    for k in range(width)
                ],
                axis=1,
            )
            parts.append(dot(table_ref[0, parity], spectra, ((1,), (0,))))
        powers = []
        for signal in [parts[0] + parts[1]] + [parts[0] - parts[1]] * folded:
            real_part = signal[:time_block]
            imag_part = signal[time_block:]
            powers.append(real_part * real_part + imag_part * imag_part)
        power = jnp.maximum(powers[0], powers[-1]) if folded else powers[0]
        power = jnp.max(power, axis=0, keepdims=True)
        for k in range(width):
            row = pl.ds(first + k, 1)
            best_ref[row, :] = jnp.maximum(
                best_ref[row, :], power[:, k * ROWS : (k + 1) * ROWS]
            )

    @pl.when(last_step())
    def _():
        largest = jnp.max(best_ref[...], axis=1, keepdims=True)
        shape = best_ref.shape
        diagonal = lax.broadcasted_iota(jnp.int32, shape, 0) == lax.broadcasted_iota(
            jnp.int32, shape, 1
        )
        largest = jnp.max(jnp.where(diagonal, largest, 0.0), axis=0, keepdims=True)
        peak = jnp.sqrt(largest[:, :columns]) * (1.0 / math.sqrt(freq_total))
        score = STEEP * (jnp.log(peak + EPS) - jnp.log(noise_ref[...]))
        peak_ref[...] = peak
        found_ref[...] = 1.0 / (1.0 + jnp.exp(-score))


def peaks(spectra, sources, twiddles, noise_level, freq_total, folded):
    columns = noise_level.shape[1]
    blocks = twiddles.shape[0]
    if blocks == 1:
        vmem = pl.BlockSpec(memory_space=pltpu.VMEM)
        grid, in_specs, out_spec = (), [vmem] * (len(spectra) + 2), vmem
    else:
        grid = (blocks,)
        out_spec = pl.BlockSpec((1, columns), lambda i: (0, 0))
        in_specs = [pl.BlockSpec(a.shape, lambda i: (0, 0, 0)) for a in spectra]
        in_specs += [
            pl.BlockSpec((1, *twiddles.shape[1:]), lambda i: (i, 0, 0, 0)),
            out_spec,
        ]
    return pl.pallas_call(
        functools.partial(peak_kernel, freq_total, folded, sources, blocks),
        grid=grid,
        in_specs=in_specs,
        out_specs=[out_spec, out_spec],
        out_shape=[jax.ShapeDtypeStruct((1, columns), jnp.float32)] * 2,
        scratch_shapes=[pltpu.VMEM((max(8, columns), ROWS), jnp.float32)],
        compiler_params=pltpu.CompilerParams(vmem_limit_bytes=VMEM_BYTES),
        name="peaks",
    )(*spectra, twiddles, noise_level)


def body(
    flaw_cells,
    flaw_blocks,
    element_channel,
    focal_delay,
    beam_field,
    flaw_size,
    flaw_slope,
    noise_level,
):
    freq_count = lax.axis_size("freq")
    freq_total = W_DEV * freq_count
    sample_count = min(T_CAP, 2 * freq_total)
    swap = [(0, 1), (1, 0)]
    direct = freq_count == 8
    slots = freq_count if direct else 1
    small = (
        focal_delay,
        element_channel.reshape(1, -1),
        flaw_blocks,
        flaw_cells.reshape(1, -1),
        flaw_size,
        flaw_slope,
    )
    folded = sample_count == 2 * freq_total
    times = sample_count // 2 if folded else sample_count
    twiddles = table(freq_total, slots, times, min(128, times))
    field = beam_field.reshape(W_HALF, 2, *beam_field.shape[1:])
    parts = add(*partials(field, small, swap, freq_total, slots), slots)
    if direct:
        half = slots // 2
        spectra = []
        for slot, masks in enumerate(zip(*slot_masks(slots))):
            pairs = [(a, a ^ masks[((2 * a) ^ a) & half != 0]) for a in range(slots)]
            own = slot == slots - 1
            spectra.append(parts[slot] if own else lax.ppermute(parts[slot], "freq", pairs))
        order = (*range(half, slots - 1), *range(half), slots - 1)
        spectra = [spectra[slot] for slot in order]
        sources = [(order.index(slot), 0) for slot in range(slots)]
    else:
        whole = jnp.concatenate(parts, axis=0)
        spectra = [
            lax.all_to_all(whole, "freq", split_axis=0, concat_axis=0, tiled=True)
        ]
        sources = [(0, s * (FG // freq_count)) for s in range(freq_count)]
    return tuple(peaks(spectra, sources, twiddles, noise_level, freq_total, folded))


def solution(mesh):
    in_specs = (
        P("batch"),
        P("batch"),
        P("elem"),
        P(),
        P("freq", None, "elem", None),
        P("batch", None),
        P("batch", None),
        P(("batch", "elem"), "freq"),
    )
    out_specs = (P(("batch", "elem"), "freq"), P(("batch", "elem"), "freq"))
    return jax.shard_map(body, mesh=mesh, in_specs=in_specs, out_specs=out_specs, check_vma=False)
```

```python
import functools
import math

import jax
import jax.numpy as jnp
from jax import lax
from jax.experimental import pallas as pl
from jax.experimental.pallas import tpu as pltpu
from jax.sharding import PartitionSpec as P

W_DEV = 16
W_HALF = W_DEV // 2
FG = 128
NB = 4
SB = 32
T_CAP = 1024

EDGE = 0.6
STEEP = 3.0
EPS = 1e-05

ROWS = NB * SB
VMEM_BYTES = 48 * 1024 * 1024


def sin_half_turn(turns):
    angle = turns * math.pi
    square = angle * angle
    sine = 1.0 / 6227020800.0
    for factorial in (-39916800.0, 362880.0, -5040.0, 120.0, -6.0, 1.0):
        sine = sine * square + 1.0 / factorial
    cosine = 1.0 / 479001600.0
    for factorial in (-3628800.0, 40320.0, -720.0, 24.0, -2.0, 1.0):
        cosine = cosine * square + 1.0 / factorial
    return sine * angle, cosine


def sincos_turns(turns):
    rest = turns - jnp.floor(turns + 0.5)
    sine, cosine = sin_half_turn(rest)
    return 2.0 * sine * cosine, 1.0 - 2.0 * sine * sine


def dot(left, right, contract):
    return lax.dot_general(
        left, right, (contract, ((), ())), preferred_element_type=jnp.float32
    )


def slot_masks(slots):
    half = slots // 2
    between = (2, half + 1, slots - 1, 3, half)
    return (1, *between, slots - 2, 0), (slots - 2, *between, 1, 0)


def partner(slots, slot):
    index = lax.axis_index("freq")
    inner = ((index * 2) ^ index) & (slots // 2) != 0
    mask = jnp.zeros_like(slot)
    for s, (outer_mask, inner_mask) in enumerate(zip(*slot_masks(slots))):
        mask = jnp.where(slot == s, jnp.where(inner, inner_mask, outer_mask), mask)
    return mask ^ index


def slot_order(slots):
    size = FG // slots
    row = lax.broadcasted_iota(jnp.int32, (FG, 1), 0)
    column = lax.broadcasted_iota(jnp.int32, (FG, FG), 1)
    if slots > 1:
        row = partner(slots, row // size) * size + row % size
    return row == column


def flaw_pick(order, which, cells_ref):
    cells = jnp.where(which == 0, cells_ref[:, :FG], cells_ref[:, FG:])
    cell_sel = lax.broadcasted_iota(jnp.int32, (cells_ref.shape[1], FG), 0) == cells
    return dot(
        order.astype(jnp.bfloat16), cell_sel.astype(jnp.bfloat16), ((1,), (1,))
    ).astype(jnp.bfloat16)


def delays_of(channel_ref, delay_ref, blocks_ref, groups, elements):
    lane = lax.broadcasted_iota(jnp.int32, (1, 2 * ROWS), 1)
    position = lane & (SB - 1)
    for j in range(2 * NB):
        block = blocks_ref[groups[j // NB] * NB + j % NB]
        position = position + jnp.where((lane >> 5) == j, block * SB, 0)
    channels, positions = delay_ref.shape
    scan_sel = (
        lax.broadcasted_iota(jnp.int32, (positions, 2 * ROWS), 0) == position
    ).astype(jnp.bfloat16)
    channel_sel = (
        (lax.broadcasted_iota(jnp.int32, (channels, elements), 0) == channel_ref[...])
        .astype(jnp.float32)
        .T.astype(jnp.bfloat16)
    )
    rest = delay_ref[...]
    pieces = []
    for _ in range(3):
        pieces.append(rest.astype(jnp.bfloat16))
        rest = rest - pieces[-1].astype(jnp.float32)
    moved = jnp.concatenate(
        [dot(channel_sel, piece, ((1,), (0,))).astype(jnp.bfloat16) for piece in pieces], axis=0
    )
    moved = dot(moved, scan_sel, ((1,), (0,)))
    return moved[:elements] + moved[elements : 2 * elements] + moved[2 * elements :]


def turned(law, step):
    return law[0] * step[0] - law[1] * step[1], law[1] * step[0] + law[0] * step[1]


def focal_base(freq_total, delays):
    first_freq = lax.axis_index("freq") * W_DEV
    phase = delays * (0.5 / freq_total)
    unit = sincos_turns(phase)[::-1]
    base = sincos_turns(phase * first_freq.astype(jnp.float32))[::-1]
    return base, turned(unit, unit), turned(base, unit)


def kirchhoff(freq_total, order, which, size_ref, slope_ref):
    first_freq = lax.axis_index("freq") * W_DEV
    size = size_ref[pl.ds(which, 1), :]
    turn = size * slope_ref[pl.ds(which, 1), :] * (1.0 / freq_total)
    size = jnp.sum(jnp.where(order, size, 0.0), axis=1, keepdims=True)
    turn = jnp.sum(jnp.where(order, turn, 0.0), axis=1, keepdims=True)
    freq = first_freq + lax.broadcasted_iota(jnp.int32, (FG, FG), 1)
    sine, cosine = sincos_turns(turn * freq.astype(jnp.float32))
    return size * (1.0 + EDGE) * cosine, size * (EDGE - 1.0) * sine


def store_law(law_ref, law, step):
    elements = law_ref.shape[1] // 2
    double = 2.0 * step[0]
    following = turned(law, step)
    for w in range(W_HALF):
        c = law[0].astype(jnp.bfloat16)
        s = law[1].astype(jnp.bfloat16)
        law_ref[w, :elements, :ROWS] = c
        law_ref[w, :elements, ROWS:] = -s
        law_ref[w, elements:, :ROWS] = s
        law_ref[w, elements:, ROWS:] = c
        law, following = following, [double * x - y for x, y in zip(following, law)]


def pick_fields(parity, picks, field_ref, picked_refs):
    elements, sites = field_ref.shape[3:]
    for w in range(W_HALF):
        picked = dot(
            picks, field_ref[w, parity].reshape(2 * elements, sites), ((1,), (1,))
        ).astype(jnp.bfloat16)
        for i, ref in enumerate(picked_refs):
            ref[parity, w] = picked[i * FG : (i + 1) * FG]


def store_spectra(picked_ref, law_ref, k_real, k_imag, out_refs):
    size = out_refs[0].shape[1]
    for parity in range(2):
        for w in range(W_HALF):
            product = dot(picked_ref[parity, w], law_ref[parity, w], ((1,), (0,)))
            real_part = product[:, :ROWS]
            imag_part = product[:, ROWS:]
            kr = k_real[:, 2 * w + parity : 2 * w + parity + 1]
            ki = k_imag[:, 2 * w + parity : 2 * w + parity + 1]
            parts = (kr * real_part - ki * imag_part, kr * imag_part + ki * real_part)
            for k, part in enumerate(parts):
                part = part.astype(jnp.bfloat16)
                for i, out_ref in enumerate(out_refs):
                    out_ref[parity * W_DEV + 2 * w + k] = part[i * size : (i + 1) * size]


def other_kernel(freq_total, slots, *refs):
    field_hbm, *small_hbm = refs[:7]
    first_ref, second_ref, own_picked_ref, size_ref, slope_ref, delays_ref = refs[7:13]
    delay_ref, channel_ref, blocks_ref, cells_ref = refs[13:17]
    field_ref, field_sem, small_sem, picked_ref, law_ref = refs[17:]
    small = (delay_ref, channel_ref, blocks_ref, cells_ref, size_ref, slope_ref)
    copies = [
        pltpu.make_async_copy(source, target, small_sem.at[i])
        for i, (source, target) in enumerate(zip(small_hbm, small))
    ]
    for copy in copies:
        copy.start()
    field_copies = [
        pltpu.make_async_copy(
            field_hbm.at[:, parity], field_ref.at[:, parity], field_sem.at[parity]
        )
        for parity in range(2)
    ]
    field_copies[0].start()
    order = slot_order(slots)
    for copy in copies:
        copy.wait()
    field_copies[1].start()
    group = lax.axis_index("elem")
    groups = (1 - group, group)
    picks = jnp.concatenate(
        [flaw_pick(order, which, cells_ref) for which in groups], axis=0
    )
    factors = kirchhoff(freq_total, order, groups[0], size_ref, slope_ref)
    delays = delays_of(channel_ref, delay_ref, blocks_ref, groups, field_ref.shape[3])
    delays_ref[...] = delays[:, ROWS:]
    even, step, odd = focal_base(freq_total, delays[:, :ROWS])
    for parity, law in enumerate((even, odd)):
        store_law(law_ref.at[parity], law, step)
        field_copies[parity].wait()
        pick_fields(parity, picks, field_ref, (picked_ref, own_picked_ref))
    store_spectra(picked_ref, law_ref, *factors, (first_ref, second_ref))


def own_kernel(freq_total, slots, *refs):
    picked_ref, delays_ref, size_ref, slope_ref, out_ref, law_ref = refs
    even, step, odd = focal_base(freq_total, delays_ref[...])
    for parity, law in enumerate((even, odd)):
        store_law(law_ref.at[parity], law, step)
    group = lax.axis_index("elem")
    factors = kirchhoff(freq_total, slot_order(slots), group, size_ref, slope_ref)
    store_spectra(picked_ref, law_ref, *factors, (out_ref,))


def call(kernel, name, in_specs, out_shape, scratch):
    vmem = pl.BlockSpec(memory_space=pltpu.VMEM)
    return pl.pallas_call(
        kernel,
        in_specs=in_specs,
        out_specs=[vmem] * len(out_shape),
        out_shape=out_shape,
        scratch_shapes=scratch,
        compiler_params=pltpu.CompilerParams(vmem_limit_bytes=VMEM_BYTES),
        cost_estimate=pl.CostEstimate(flops=1000, bytes_accessed=1000, transcendentals=0),
        name=name,
    )


def partials(field, small, swap, freq_total, slots):
    elements, sites = field.shape[3:]
    vmem = pl.BlockSpec(memory_space=pltpu.VMEM)
    hbm = pl.BlockSpec(memory_space=pltpu.HBM)
    pinned = [pltpu.with_memory_space_constraint(a, pltpu.HBM) for a in (field, *small)]
    out = jax.ShapeDtypeStruct((2 * W_DEV, FG, ROWS), jnp.bfloat16)
    half = jax.ShapeDtypeStruct((2 * W_DEV, FG // 2, ROWS), jnp.bfloat16)
    picked = jax.ShapeDtypeStruct((2, W_HALF, FG, 2 * elements), jnp.bfloat16)
    law = pltpu.VMEM((2, W_HALF, 2 * elements, 2 * ROWS), jnp.bfloat16)
    copied = [jax.ShapeDtypeStruct(a.shape, a.dtype) for a in small[4:]]
    delays = jax.ShapeDtypeStruct((elements, ROWS), jnp.float32)
    first, second, own_picked, size, slope, delays = call(
        functools.partial(other_kernel, freq_total, slots),
        "other",
        [hbm] * len(pinned),
        [half, half, picked, *copied, delays],
        [
            pltpu.SMEM(a.shape, a.dtype) if a.ndim == 1 else pltpu.VMEM(a.shape, a.dtype)
            for a in small[:4]
        ]
        + [
            pltpu.VMEM(field.shape, field.dtype),
            pltpu.SemaphoreType.DMA((2,)),
            pltpu.SemaphoreType.DMA((len(small),)),
            pltpu.VMEM(picked.shape, picked.dtype),
            law,
        ],
    )(*pinned)
    first = lax.ppermute(first, "elem", swap)
    second = lax.ppermute(second, "elem", swap)
    (own,) = call(
        functools.partial(own_kernel, freq_total, slots), "own", [vmem] * 4, [out], [law]
    )(own_picked, delays, size, slope)
    return own, first, second


def add_kernel(first, own_ref, moved_ref, *refs):
    size = refs[0].shape[0]
    for slot, ref in enumerate(refs):
        own = own_ref[:, pl.ds(first + slot * size, size)].astype(jnp.float32)
        both = own + moved_ref[:, pl.ds(slot * size, size)].astype(jnp.float32)
        ref[...] = jnp.swapaxes(both, 0, 1).astype(jnp.bfloat16)


def add(own, first, second, slots):
    vmem = pl.BlockSpec(memory_space=pltpu.VMEM)
    planes, flaws, rows = own.shape
    count = max(1, slots // 2)
    shape = jax.ShapeDtypeStruct((flaws // 2 // count, planes, rows), own.dtype)
    parts = []
    for name, start, moved in (("add_first", 0, first), ("add_second", flaws // 2, second)):
        kernel = functools.partial(add_kernel, start)
        parts += call(kernel, name, [vmem] * 2, [shape] * count, [])(own, moved)
    return parts


def table_kernel(freq_total, slots, table_ref):
    height, depth = table_ref.shape[2:]
    time_block = height // 2
    row = lax.broadcasted_iota(jnp.int32, (height, depth // 2), 0)
    column = lax.broadcasted_iota(jnp.int32, (height, depth // 2), 1)
    out_imag = (row >= time_block).astype(jnp.int32)
    time = pl.program_id(0) * time_block + row - out_imag * time_block
    for parity in range(2):
        freq = (column >> 1) * 2 + parity
        if slots > 1:
            lane = lax.broadcasted_iota(jnp.int32, (1, depth // 2), 1)
            lane = (lane >> 1) * 2 + parity
            freq = partner(slots, lane // W_DEV) * W_DEV + lane % W_DEV
        steps = freq * time + ((column & 1) - out_imag) * (freq_total // 2)
        steps = (steps + 2 * freq_total) & (2 * freq_total - 1)
        _, value = sincos_turns(steps.astype(jnp.float32) * (0.5 / freq_total))
        high = value.astype(jnp.bfloat16)
        table_ref[0, parity, :, : depth // 2] = high
        table_ref[0, parity, :, depth // 2 :] = (
            value - high.astype(jnp.float32)
        ).astype(jnp.bfloat16)


def table(freq_total, slots, times, time_block):
    blocks = times // time_block
    shape = (blocks, 2, 2 * time_block, 2 * freq_total)
    return pl.pallas_call(
        functools.partial(table_kernel, freq_total, slots),
        grid=(blocks,),
        out_specs=pl.BlockSpec((1, *shape[1:]), lambda i: (i, 0, 0, 0)),
        out_shape=jax.ShapeDtypeStruct(shape, jnp.bfloat16),
        compiler_params=pltpu.CompilerParams(vmem_limit_bytes=VMEM_BYTES),
        name="table",
    )()


def peak_kernel(freq_total, folded, sources, blocks, *refs):
    def first_step():
        return blocks == 1 or pl.program_id(0) == 0

    def last_step():
        return blocks == 1 or pl.program_id(0) == blocks - 1

    count = len(refs) - 5
    table_ref, noise_ref, peak_ref, found_ref, best_ref = refs[count:]
    columns = peak_ref.shape[1]
    time_block = table_ref.shape[2] // 2

    @pl.when(first_step())
    def _():
        best_ref[...] = jnp.zeros_like(best_ref)

    width = min(2, columns)
    for first in range(0, columns, width):
        parts = []
        for parity in range(2):
            planes = slice(parity * W_DEV, (parity + 1) * W_DEV)
            spectra = jnp.concatenate(
                [
                    jnp.concatenate(
                        [
                            refs[i][row + first + k, planes, :]
                            for i, row in sources
                        ]
                        * 2,
                        axis=0,
                    )
                    for k in range(width)
                ],
                axis=1,
            )
            parts.append(dot(table_ref[0, parity], spectra, ((1,), (0,))))
        powers = []
        for signal in [parts[0] + parts[1]] + [parts[0] - parts[1]] * folded:
            real_part = signal[:time_block]
            imag_part = signal[time_block:]
            powers.append(real_part * real_part + imag_part * imag_part)
        power = jnp.maximum(powers[0], powers[-1]) if folded else powers[0]
        power = jnp.max(power, axis=0, keepdims=True)
        for k in range(width):
            row = pl.ds(first + k, 1)
            best_ref[row, :] = jnp.maximum(
                best_ref[row, :], power[:, k * ROWS : (k + 1) * ROWS]
            )

    @pl.when(last_step())
    def _():
        largest = jnp.max(best_ref[...], axis=1, keepdims=True)
        shape = best_ref.shape
        diagonal = lax.broadcasted_iota(jnp.int32, shape, 0) == lax.broadcasted_iota(
            jnp.int32, shape, 1
        )
        largest = jnp.max(jnp.where(diagonal, largest, 0.0), axis=0, keepdims=True)
        peak = jnp.sqrt(largest[:, :columns]) * (1.0 / math.sqrt(freq_total))
        score = STEEP * (jnp.log(peak + EPS) - jnp.log(noise_ref[...]))
        peak_ref[...] = peak
        found_ref[...] = 1.0 / (1.0 + jnp.exp(-score))


def peaks(spectra, sources, twiddles, noise_level, freq_total, folded):
    columns = noise_level.shape[1]
    blocks = twiddles.shape[0]
    if blocks == 1:
        vmem = pl.BlockSpec(memory_space=pltpu.VMEM)
        grid, in_specs, out_spec = (), [vmem] * (len(spectra) + 2), vmem
    else:
        grid = (blocks,)
        out_spec = pl.BlockSpec((1, columns), lambda i: (0, 0))
        in_specs = [pl.BlockSpec(a.shape, lambda i: (0, 0, 0)) for a in spectra]
        in_specs += [
            pl.BlockSpec((1, *twiddles.shape[1:]), lambda i: (i, 0, 0, 0)),
            out_spec,
        ]
    return pl.pallas_call(
        functools.partial(peak_kernel, freq_total, folded, sources, blocks),
        grid=grid,
        in_specs=in_specs,
        out_specs=[out_spec, out_spec],
        out_shape=[jax.ShapeDtypeStruct((1, columns), jnp.float32)] * 2,
        scratch_shapes=[pltpu.VMEM((max(8, columns), ROWS), jnp.float32)],
        compiler_params=pltpu.CompilerParams(vmem_limit_bytes=VMEM_BYTES),
        name="peaks",
    )(*spectra, twiddles, noise_level)


def body(
    flaw_cells,
    flaw_blocks,
    element_channel,
    focal_delay,
    beam_field,
    flaw_size,
    flaw_slope,
    noise_level,
):
    freq_count = lax.axis_size("freq")
    freq_total = W_DEV * freq_count
    sample_count = min(T_CAP, 2 * freq_total)
    swap = [(0, 1), (1, 0)]
    direct = freq_count == 8
    slots = freq_count if direct else 1
    small = (
        focal_delay,
        element_channel.reshape(1, -1),
        flaw_blocks,
        flaw_cells.reshape(1, -1),
        flaw_size,
        flaw_slope,
    )
    folded = sample_count == 2 * freq_total
    times = sample_count // 2 if folded else sample_count
    twiddles = table(freq_total, slots, times, min(128, times))
    field = beam_field.reshape(W_HALF, 2, *beam_field.shape[1:])
    parts = add(*partials(field, small, swap, freq_total, slots), slots)
    if direct:
        half = slots // 2
        spectra = []
        for slot, masks in enumerate(zip(*slot_masks(slots))):
            pairs = [(a, a ^ masks[((2 * a) ^ a) & half != 0]) for a in range(slots)]
            own = slot == slots - 1
            spectra.append(parts[slot] if own else lax.ppermute(parts[slot], "freq", pairs))
        order = (*range(half, slots - 1), *range(half), slots - 1)
        spectra = [spectra[slot] for slot in order]
        sources = [(order.index(slot), 0) for slot in range(slots)]
    else:
        whole = jnp.concatenate(parts, axis=0)
        spectra = [
            lax.all_to_all(whole, "freq", split_axis=0, concat_axis=0, tiled=True)
        ]
        sources = [(0, s * (FG // freq_count)) for s in range(freq_count)]
    return tuple(peaks(spectra, sources, twiddles, noise_level, freq_total, folded))


def solution(mesh):
    in_specs = (
        P("batch"),
        P("batch"),
        P("elem"),
        P(),
        P("freq", None, "elem", None),
        P("batch", None),
        P("batch", None),
        P(("batch", "elem"), "freq"),
    )
    out_specs = (P(("batch", "elem"), "freq"), P(("batch", "elem"), "freq"))
    return jax.shard_map(body, mesh=mesh, in_specs=in_specs, out_specs=out_specs, check_vma=False)
```

```python
import functools
import math

import jax
import jax.numpy as jnp
from jax import lax
from jax.experimental import pallas as pl
from jax.experimental.pallas import tpu as pltpu
from jax.sharding import PartitionSpec as P

W_DEV = 16
W_HALF = W_DEV // 2
FG = 128
NB = 4
SB = 32
T_CAP = 1024

EDGE = 0.6
STEEP = 3.0
EPS = 1e-05

ROWS = NB * SB
VMEM_BYTES = 48 * 1024 * 1024


def sin_half_turn(turns):
    angle = turns * math.pi
    square = angle * angle
    sine = 1.0 / 6227020800.0
    for factorial in (-39916800.0, 362880.0, -5040.0, 120.0, -6.0, 1.0):
        sine = sine * square + 1.0 / factorial
    cosine = 1.0 / 479001600.0
    for factorial in (-3628800.0, 40320.0, -720.0, 24.0, -2.0, 1.0):
        cosine = cosine * square + 1.0 / factorial
    return sine * angle, cosine


def sincos_turns(turns):
    rest = turns - jnp.floor(turns + 0.5)
    sine, cosine = sin_half_turn(rest)
    return 2.0 * sine * cosine, 1.0 - 2.0 * sine * sine


def dot(left, right, contract):
    return lax.dot_general(
        left, right, (contract, ((), ())), preferred_element_type=jnp.float32
    )


def slot_masks(slots):
    half = slots // 2
    between = (2, half + 1, slots - 1, 3, half)
    return (slots - 2, *between, 1, 0), (1, *between, slots - 2, 0)


def partner(slots, slot):
    index = lax.axis_index("freq")
    inner = ((index * 2) ^ index) & (slots // 2) != 0
    mask = jnp.zeros_like(slot)
    for s, (outer_mask, inner_mask) in enumerate(zip(*slot_masks(slots))):
        mask = jnp.where(slot == s, jnp.where(inner, inner_mask, outer_mask), mask)
    return mask ^ index


def slot_order(slots):
    size = FG // slots
    row = lax.broadcasted_iota(jnp.int32, (FG, 1), 0)
    column = lax.broadcasted_iota(jnp.int32, (FG, FG), 1)
    if slots > 1:
        row = partner(slots, row // size) * size + row % size
    return row == column


def flaw_pick(order, which, cells_ref):
    cells = jnp.where(which == 0, cells_ref[:, :FG], cells_ref[:, FG:])
    cell_sel = lax.broadcasted_iota(jnp.int32, (cells_ref.shape[1], FG), 0) == cells
    return dot(
        order.astype(jnp.bfloat16), cell_sel.astype(jnp.bfloat16), ((1,), (1,))
    ).astype(jnp.bfloat16)


def delays_of(channel_ref, delay_ref, blocks_ref, groups, elements):
    lane = lax.broadcasted_iota(jnp.int32, (1, 2 * ROWS), 1)
    position = lane & (SB - 1)
    for j in range(2 * NB):
        block = blocks_ref[groups[j // NB] * NB + j % NB]
        position = position + jnp.where((lane >> 5) == j, block * SB, 0)
    channels, positions = delay_ref.shape
    scan_sel = (
        lax.broadcasted_iota(jnp.int32, (positions, 2 * ROWS), 0) == position
    ).astype(jnp.bfloat16)
    channel_sel = (
        (lax.broadcasted_iota(jnp.int32, (channels, elements), 0) == channel_ref[...])
        .astype(jnp.float32)
        .T.astype(jnp.bfloat16)
    )
    rest = delay_ref[...]
    pieces = []
    for _ in range(3):
        pieces.append(rest.astype(jnp.bfloat16))
        rest = rest - pieces[-1].astype(jnp.float32)
    moved = jnp.concatenate(
        [dot(channel_sel, piece, ((1,), (0,))).astype(jnp.bfloat16) for piece in pieces], axis=0
    )
    moved = dot(moved, scan_sel, ((1,), (0,)))
    return moved[:elements] + moved[elements : 2 * elements] + moved[2 * elements :]


def turned(law, step):
    return law[0] * step[0] - law[1] * step[1], law[1] * step[0] + law[0] * step[1]


def focal_base(freq_total, delays):
    first_freq = lax.axis_index("freq") * W_DEV
    phase = delays * (0.5 / freq_total)
    unit = sincos_turns(phase)[::-1]
    base = sincos_turns(phase * first_freq.astype(jnp.float32))[::-1]
    return base, turned(unit, unit), turned(base, unit)


def kirchhoff(freq_total, order, which, size_ref, slope_ref):
    first_freq = lax.axis_index("freq") * W_DEV
    size = size_ref[pl.ds(which, 1), :]
    turn = size * slope_ref[pl.ds(which, 1), :] * (1.0 / freq_total)
    size = jnp.sum(jnp.where(order, size, 0.0), axis=1, keepdims=True)
    turn = jnp.sum(jnp.where(order, turn, 0.0), axis=1, keepdims=True)
    freq = first_freq + lax.broadcasted_iota(jnp.int32, (FG, FG), 1)
    sine, cosine = sincos_turns(turn * freq.astype(jnp.float32))
    return size * (1.0 + EDGE) * cosine, size * (EDGE - 1.0) * sine


def store_law(law_ref, law, step):
    elements = law_ref.shape[1] // 2
    double = 2.0 * step[0]
    following = turned(law, step)
    for w in range(W_HALF):
        c = law[0].astype(jnp.bfloat16)
        s = law[1].astype(jnp.bfloat16)
        law_ref[w, :elements, :ROWS] = c
        law_ref[w, :elements, ROWS:] = -s
        law_ref[w, elements:, :ROWS] = s
        law_ref[w, elements:, ROWS:] = c
        law, following = following, [double * x - y for x, y in zip(following, law)]


def pick_fields(parity, picks, field_ref, picked_refs):
    elements, sites = field_ref.shape[3:]
    for w in range(W_HALF):
        picked = dot(
            picks, field_ref[w, parity].reshape(2 * elements, sites), ((1,), (1,))
        ).astype(jnp.bfloat16)
        for i, ref in enumerate(picked_refs):
            ref[parity, w] = picked[i * FG : (i + 1) * FG]


def store_spectra(picked_ref, law_ref, k_real, k_imag, out_refs):
    size = out_refs[0].shape[1]
    for parity in range(2):
        for w in range(W_HALF):
            product = dot(picked_ref[parity, w], law_ref[parity, w], ((1,), (0,)))
            real_part = product[:, :ROWS]
            imag_part = product[:, ROWS:]
            kr = k_real[:, 2 * w + parity : 2 * w + parity + 1]
            ki = k_imag[:, 2 * w + parity : 2 * w + parity + 1]
            parts = (kr * real_part - ki * imag_part, kr * imag_part + ki * real_part)
            for k, part in enumerate(parts):
                part = part.astype(jnp.bfloat16)
                for i, out_ref in enumerate(out_refs):
                    out_ref[parity * W_DEV + 2 * w + k] = part[i * size : (i + 1) * size]


def other_kernel(freq_total, slots, *refs):
    field_hbm, *small_hbm = refs[:7]
    first_ref, second_ref, own_picked_ref, size_ref, slope_ref, delays_ref = refs[7:13]
    delay_ref, channel_ref, blocks_ref, cells_ref = refs[13:17]
    field_ref, field_sem, small_sem, picked_ref, law_ref = refs[17:]
    small = (delay_ref, channel_ref, blocks_ref, cells_ref, size_ref, slope_ref)
    copies = [
        pltpu.make_async_copy(source, target, small_sem.at[i])
        for i, (source, target) in enumerate(zip(small_hbm, small))
    ]
    for copy in copies:
        copy.start()
    field_copies = [
        pltpu.make_async_copy(
            field_hbm.at[:, parity], field_ref.at[:, parity], field_sem.at[parity]
        )
        for parity in range(2)
    ]
    field_copies[0].start()
    order = slot_order(slots)
    for copy in copies:
        copy.wait()
    field_copies[1].start()
    group = lax.axis_index("elem")
    groups = (1 - group, group)
    picks = jnp.concatenate(
        [flaw_pick(order, which, cells_ref) for which in groups], axis=0
    )
    factors = kirchhoff(freq_total, order, groups[0], size_ref, slope_ref)
    delays = delays_of(channel_ref, delay_ref, blocks_ref, groups, field_ref.shape[3])
    delays_ref[...] = delays[:, ROWS:]
    even, step, odd = focal_base(freq_total, delays[:, :ROWS])
    for parity, law in enumerate((even, odd)):
        store_law(law_ref.at[parity], law, step)
        field_copies[parity].wait()
        pick_fields(parity, picks, field_ref, (picked_ref, own_picked_ref))
    store_spectra(picked_ref, law_ref, *factors, (first_ref, second_ref))


def own_kernel(freq_total, slots, *refs):
    picked_ref, delays_ref, size_ref, slope_ref, out_ref, law_ref = refs
    even, step, odd = focal_base(freq_total, delays_ref[...])
    for parity, law in enumerate((even, odd)):
        store_law(law_ref.at[parity], law, step)
    group = lax.axis_index("elem")
    factors = kirchhoff(freq_total, slot_order(slots), group, size_ref, slope_ref)
    store_spectra(picked_ref, law_ref, *factors, (out_ref,))


def call(kernel, name, in_specs, out_shape, scratch):
    vmem = pl.BlockSpec(memory_space=pltpu.VMEM)
    return pl.pallas_call(
        kernel,
        in_specs=in_specs,
        out_specs=[vmem] * len(out_shape),
        out_shape=out_shape,
        scratch_shapes=scratch,
        compiler_params=pltpu.CompilerParams(vmem_limit_bytes=VMEM_BYTES),
        cost_estimate=pl.CostEstimate(flops=1000, bytes_accessed=1000, transcendentals=0),
        name=name,
    )


def partials(field, small, swap, freq_total, slots):
    elements, sites = field.shape[3:]
    vmem = pl.BlockSpec(memory_space=pltpu.VMEM)
    hbm = pl.BlockSpec(memory_space=pltpu.HBM)
    pinned = [pltpu.with_memory_space_constraint(a, pltpu.HBM) for a in (field, *small)]
    out = jax.ShapeDtypeStruct((2 * W_DEV, FG, ROWS), jnp.bfloat16)
    half = jax.ShapeDtypeStruct((2 * W_DEV, FG // 2, ROWS), jnp.bfloat16)
    picked = jax.ShapeDtypeStruct((2, W_HALF, FG, 2 * elements), jnp.bfloat16)
    law = pltpu.VMEM((2, W_HALF, 2 * elements, 2 * ROWS), jnp.bfloat16)
    copied = [jax.ShapeDtypeStruct(a.shape, a.dtype) for a in small[4:]]
    delays = jax.ShapeDtypeStruct((elements, ROWS), jnp.float32)
    first, second, own_picked, size, slope, delays = call(
        functools.partial(other_kernel, freq_total, slots),
        "other",
        [hbm] * len(pinned),
        [half, half, picked, *copied, delays],
        [
            pltpu.SMEM(a.shape, a.dtype) if a.ndim == 1 else pltpu.VMEM(a.shape, a.dtype)
            for a in small[:4]
        ]
        + [
            pltpu.VMEM(field.shape, field.dtype),
            pltpu.SemaphoreType.DMA((2,)),
            pltpu.SemaphoreType.DMA((len(small),)),
            pltpu.VMEM(picked.shape, picked.dtype),
            law,
        ],
    )(*pinned)
    first = lax.ppermute(first, "elem", swap)
    second = lax.ppermute(second, "elem", swap)
    (own,) = call(
        functools.partial(own_kernel, freq_total, slots), "own", [vmem] * 4, [out], [law]
    )(own_picked, delays, size, slope)
    return own, first, second


def add_kernel(first, own_ref, moved_ref, *refs):
    size = refs[0].shape[0]
    for slot, ref in enumerate(refs):
        own = own_ref[:, pl.ds(first + slot * size, size)].astype(jnp.float32)
        both = own + moved_ref[:, pl.ds(slot * size, size)].astype(jnp.float32)
        ref[...] = jnp.swapaxes(both, 0, 1).astype(jnp.bfloat16)


def add(own, first, second, slots):
    vmem = pl.BlockSpec(memory_space=pltpu.VMEM)
    planes, flaws, rows = own.shape
    count = max(1, slots // 2)
    shape = jax.ShapeDtypeStruct((flaws // 2 // count, planes, rows), own.dtype)
    parts = []
    for name, start, moved in (("add_first", 0, first), ("add_second", flaws // 2, second)):
        kernel = functools.partial(add_kernel, start)
        parts += call(kernel, name, [vmem] * 2, [shape] * count, [])(own, moved)
    return parts


def table_kernel(freq_total, slots, table_ref):
    height, depth = table_ref.shape[2:]
    time_block = height // 2
    row = lax.broadcasted_iota(jnp.int32, (height, depth // 2), 0)
    column = lax.broadcasted_iota(jnp.int32, (height, depth // 2), 1)
    out_imag = (row >= time_block).astype(jnp.int32)
    time = pl.program_id(0) * time_block + row - out_imag * time_block
    for parity in range(2):
        freq = (column >> 1) * 2 + parity
        if slots > 1:
            lane = lax.broadcasted_iota(jnp.int32, (1, depth // 2), 1)
            lane = (lane >> 1) * 2 + parity
            freq = partner(slots, lane // W_DEV) * W_DEV + lane % W_DEV
        steps = freq * time + ((column & 1) - out_imag) * (freq_total // 2)
        steps = (steps + 2 * freq_total) & (2 * freq_total - 1)
        _, value = sincos_turns(steps.astype(jnp.float32) * (0.5 / freq_total))
        high = value.astype(jnp.bfloat16)
        table_ref[0, parity, :, : depth // 2] = high
        table_ref[0, parity, :, depth // 2 :] = (
            value - high.astype(jnp.float32)
        ).astype(jnp.bfloat16)


def table(freq_total, slots, times, time_block):
    blocks = times // time_block
    shape = (blocks, 2, 2 * time_block, 2 * freq_total)
    return pl.pallas_call(
        functools.partial(table_kernel, freq_total, slots),
        grid=(blocks,),
        out_specs=pl.BlockSpec((1, *shape[1:]), lambda i: (i, 0, 0, 0)),
        out_shape=jax.ShapeDtypeStruct(shape, jnp.bfloat16),
        compiler_params=pltpu.CompilerParams(vmem_limit_bytes=VMEM_BYTES),
        name="table",
    )()


def peak_kernel(freq_total, folded, sources, blocks, *refs):
    def first_step():
        return blocks == 1 or pl.program_id(0) == 0

    def last_step():
        return blocks == 1 or pl.program_id(0) == blocks - 1

    count = len(refs) - 5
    table_ref, noise_ref, peak_ref, found_ref, best_ref = refs[count:]
    columns = peak_ref.shape[1]
    time_block = table_ref.shape[2] // 2

    @pl.when(first_step())
    def _():
        best_ref[...] = jnp.zeros_like(best_ref)

    width = min(2, columns)
    for first in range(0, columns, width):
        parts = []
        for parity in range(2):
            planes = slice(parity * W_DEV, (parity + 1) * W_DEV)
            spectra = jnp.concatenate(
                [
                    jnp.concatenate(
                        [
                            refs[i][row + first + k, planes, :]
                            for i, row in sources
                        ]
                        * 2,
                        axis=0,
                    )
                    for k in range(width)
                ],
                axis=1,
            )
            parts.append(dot(table_ref[0, parity], spectra, ((1,), (0,))))
        powers = []
        for signal in [parts[0] + parts[1]] + [parts[0] - parts[1]] * folded:
            real_part = signal[:time_block]
            imag_part = signal[time_block:]
            powers.append(real_part * real_part + imag_part * imag_part)
        power = jnp.maximum(powers[0], powers[-1]) if folded else powers[0]
        power = jnp.max(power, axis=0, keepdims=True)
        for k in range(width):
            row = pl.ds(first + k, 1)
            best_ref[row, :] = jnp.maximum(
                best_ref[row, :], power[:, k * ROWS : (k + 1) * ROWS]
            )

    @pl.when(last_step())
    def _():
        largest = jnp.max(best_ref[...], axis=1, keepdims=True)
        shape = best_ref.shape
        diagonal = lax.broadcasted_iota(jnp.int32, shape, 0) == lax.broadcasted_iota(
            jnp.int32, shape, 1
        )
        largest = jnp.max(jnp.where(diagonal, largest, 0.0), axis=0, keepdims=True)
        peak = jnp.sqrt(largest[:, :columns]) * (1.0 / math.sqrt(freq_total))
        score = STEEP * (jnp.log(peak + EPS) - jnp.log(noise_ref[...]))
        peak_ref[...] = peak
        found_ref[...] = 1.0 / (1.0 + jnp.exp(-score))


def peaks(spectra, sources, twiddles, noise_level, freq_total, folded):
    columns = noise_level.shape[1]
    blocks = twiddles.shape[0]
    if blocks == 1:
        vmem = pl.BlockSpec(memory_space=pltpu.VMEM)
        grid, in_specs, out_spec = (), [vmem] * (len(spectra) + 2), vmem
    else:
        grid = (blocks,)
        out_spec = pl.BlockSpec((1, columns), lambda i: (0, 0))
        in_specs = [pl.BlockSpec(a.shape, lambda i: (0, 0, 0)) for a in spectra]
        in_specs += [
            pl.BlockSpec((1, *twiddles.shape[1:]), lambda i: (i, 0, 0, 0)),
            out_spec,
        ]
    return pl.pallas_call(
        functools.partial(peak_kernel, freq_total, folded, sources, blocks),
        grid=grid,
        in_specs=in_specs,
        out_specs=[out_spec, out_spec],
        out_shape=[jax.ShapeDtypeStruct((1, columns), jnp.float32)] * 2,
        scratch_shapes=[pltpu.VMEM((max(8, columns), ROWS), jnp.float32)],
        compiler_params=pltpu.CompilerParams(vmem_limit_bytes=VMEM_BYTES),
        name="peaks",
    )(*spectra, twiddles, noise_level)


def body(
    flaw_cells,
    flaw_blocks,
    element_channel,
    focal_delay,
    beam_field,
    flaw_size,
    flaw_slope,
    noise_level,
):
    freq_count = lax.axis_size("freq")
    freq_total = W_DEV * freq_count
    sample_count = min(T_CAP, 2 * freq_total)
    swap = [(0, 1), (1, 0)]
    direct = freq_count == 8
    slots = freq_count if direct else 1
    small = (
        focal_delay,
        element_channel.reshape(1, -1),
        flaw_blocks,
        flaw_cells.reshape(1, -1),
        flaw_size,
        flaw_slope,
    )
    folded = sample_count == 2 * freq_total
    times = sample_count // 2 if folded else sample_count
    twiddles = table(freq_total, slots, times, min(128, times))
    field = beam_field.reshape(W_HALF, 2, *beam_field.shape[1:])
    parts = add(*partials(field, small, swap, freq_total, slots), slots)
    if direct:
        half = slots // 2
        spectra = []
        for slot, masks in enumerate(zip(*slot_masks(slots))):
            pairs = [(a, a ^ masks[((2 * a) ^ a) & half != 0]) for a in range(slots)]
            own = slot == slots - 1
            spectra.append(parts[slot] if own else lax.ppermute(parts[slot], "freq", pairs))
        order = (*range(half, slots - 1), *range(half), slots - 1)
        spectra = [spectra[slot] for slot in order]
        sources = [(order.index(slot), 0) for slot in range(slots)]
    else:
        whole = jnp.concatenate(parts, axis=0)
        spectra = [
            lax.all_to_all(whole, "freq", split_axis=0, concat_axis=0, tiled=True)
        ]
        sources = [(0, s * (FG // freq_count)) for s in range(freq_count)]
    return tuple(peaks(spectra, sources, twiddles, noise_level, freq_total, folded))


def solution(mesh):
    in_specs = (
        P("batch"),
        P("batch"),
        P("elem"),
        P(),
        P("freq", None, "elem", None),
        P("batch", None),
        P("batch", None),
        P(("batch", "elem"), "freq"),
    )
    out_specs = (P(("batch", "elem"), "freq"), P(("batch", "elem"), "freq"))
    return jax.shard_map(body, mesh=mesh, in_specs=in_specs, out_specs=out_specs, check_vma=False)
```

```python
import functools
import math

import jax
import jax.numpy as jnp
from jax import lax
from jax.experimental import pallas as pl
from jax.experimental.pallas import tpu as pltpu
from jax.sharding import PartitionSpec as P

W_DEV = 16
W_HALF = W_DEV // 2
FG = 128
NB = 4
SB = 32
T_CAP = 1024

EDGE = 0.6
STEEP = 3.0
EPS = 1e-05

ROWS = NB * SB
VMEM_BYTES = 48 * 1024 * 1024


def sin_half_turn(turns):
    angle = turns * math.pi
    square = angle * angle
    sine = 1.0 / 6227020800.0
    for factorial in (-39916800.0, 362880.0, -5040.0, 120.0, -6.0, 1.0):
        sine = sine * square + 1.0 / factorial
    cosine = 1.0 / 479001600.0
    for factorial in (-3628800.0, 40320.0, -720.0, 24.0, -2.0, 1.0):
        cosine = cosine * square + 1.0 / factorial
    return sine * angle, cosine


def sincos_turns(turns):
    rest = turns - jnp.floor(turns + 0.5)
    sine, cosine = sin_half_turn(rest)
    return 2.0 * sine * cosine, 1.0 - 2.0 * sine * sine


def dot(left, right, contract):
    return lax.dot_general(
        left, right, (contract, ((), ())), preferred_element_type=jnp.float32
    )


def slot_masks(slots):
    half = slots // 2
    between = (2, half + 1, half, slots - 1, 3)
    return (1, *between, slots - 2, 0), (slots - 2, *between, 1, 0)


def partner(slots, slot):
    index = lax.axis_index("freq")
    inner = ((index * 2) ^ index) & (slots // 2) != 0
    mask = jnp.zeros_like(slot)
    for s, (outer_mask, inner_mask) in enumerate(zip(*slot_masks(slots))):
        mask = jnp.where(slot == s, jnp.where(inner, inner_mask, outer_mask), mask)
    return mask ^ index


def slot_order(slots):
    size = FG // slots
    row = lax.broadcasted_iota(jnp.int32, (FG, 1), 0)
    column = lax.broadcasted_iota(jnp.int32, (FG, FG), 1)
    if slots > 1:
        row = partner(slots, row // size) * size + row % size
    return row == column


def flaw_pick(order, which, cells_ref):
    cells = jnp.where(which == 0, cells_ref[:, :FG], cells_ref[:, FG:])
    cell_sel = lax.broadcasted_iota(jnp.int32, (cells_ref.shape[1], FG), 0) == cells
    return dot(
        order.astype(jnp.bfloat16), cell_sel.astype(jnp.bfloat16), ((1,), (1,))
    ).astype(jnp.bfloat16)


def delays_of(channel_ref, delay_ref, blocks_ref, groups, elements):
    lane = lax.broadcasted_iota(jnp.int32, (1, 2 * ROWS), 1)
    position = lane & (SB - 1)
    for j in range(2 * NB):
        block = blocks_ref[groups[j // NB] * NB + j % NB]
        position = position + jnp.where((lane >> 5) == j, block * SB, 0)
    channels, positions = delay_ref.shape
    scan_sel = (
        lax.broadcasted_iota(jnp.int32, (positions, 2 * ROWS), 0) == position
    ).astype(jnp.bfloat16)
    channel_sel = (
        (lax.broadcasted_iota(jnp.int32, (channels, elements), 0) == channel_ref[...])
        .astype(jnp.float32)
        .T.astype(jnp.bfloat16)
    )
    rest = delay_ref[...]
    pieces = []
    for _ in range(3):
        pieces.append(rest.astype(jnp.bfloat16))
        rest = rest - pieces[-1].astype(jnp.float32)
    moved = jnp.concatenate(
        [dot(channel_sel, piece, ((1,), (0,))).astype(jnp.bfloat16) for piece in pieces], axis=0
    )
    moved = dot(moved, scan_sel, ((1,), (0,)))
    return moved[:elements] + moved[elements : 2 * elements] + moved[2 * elements :]


def turned(law, step):
    return law[0] * step[0] - law[1] * step[1], law[1] * step[0] + law[0] * step[1]


def focal_base(freq_total, delays):
    first_freq = lax.axis_index("freq") * W_DEV
    phase = delays * (0.5 / freq_total)
    unit = sincos_turns(phase)[::-1]
    base = sincos_turns(phase * first_freq.astype(jnp.float32))[::-1]
    return base, turned(unit, unit), turned(base, unit)


def kirchhoff(freq_total, order, which, size_ref, slope_ref):
    first_freq = lax.axis_index("freq") * W_DEV
    size = size_ref[pl.ds(which, 1), :]
    turn = size * slope_ref[pl.ds(which, 1), :] * (1.0 / freq_total)
    size = jnp.sum(jnp.where(order, size, 0.0), axis=1, keepdims=True)
    turn = jnp.sum(jnp.where(order, turn, 0.0), axis=1, keepdims=True)
    freq = first_freq + lax.broadcasted_iota(jnp.int32, (FG, FG), 1)
    sine, cosine = sincos_turns(turn * freq.astype(jnp.float32))
    return size * (1.0 + EDGE) * cosine, size * (EDGE - 1.0) * sine


def store_law(law_ref, law, step):
    elements = law_ref.shape[1] // 2
    double = 2.0 * step[0]
    following = turned(law, step)
    for w in range(W_HALF):
        c = law[0].astype(jnp.bfloat16)
        s = law[1].astype(jnp.bfloat16)
        law_ref[w, :elements, :ROWS] = c
        law_ref[w, :elements, ROWS:] = -s
        law_ref[w, elements:, :ROWS] = s
        law_ref[w, elements:, ROWS:] = c
        law, following = following, [double * x - y for x, y in zip(following, law)]


def pick_fields(parity, picks, field_ref, picked_refs):
    elements, sites = field_ref.shape[3:]
    for w in range(W_HALF):
        picked = dot(
            picks, field_ref[w, parity].reshape(2 * elements, sites), ((1,), (1,))
        ).astype(jnp.bfloat16)
        for i, ref in enumerate(picked_refs):
            ref[parity, w] = picked[i * FG : (i + 1) * FG]


def store_spectra(picked_ref, law_ref, k_real, k_imag, out_refs):
    size = out_refs[0].shape[1]
    for parity in range(2):
        for w in range(W_HALF):
            product = dot(picked_ref[parity, w], law_ref[parity, w], ((1,), (0,)))
            real_part = product[:, :ROWS]
            imag_part = product[:, ROWS:]
            kr = k_real[:, 2 * w + parity : 2 * w + parity + 1]
            ki = k_imag[:, 2 * w + parity : 2 * w + parity + 1]
            parts = (kr * real_part - ki * imag_part, kr * imag_part + ki * real_part)
            for k, part in enumerate(parts):
                part = part.astype(jnp.bfloat16)
                for i, out_ref in enumerate(out_refs):
                    out_ref[parity * W_DEV + 2 * w + k] = part[i * size : (i + 1) * size]


def other_kernel(freq_total, slots, *refs):
    field_hbm, *small_hbm = refs[:7]
    first_ref, second_ref, own_picked_ref, size_ref, slope_ref, delays_ref = refs[7:13]
    delay_ref, channel_ref, blocks_ref, cells_ref = refs[13:17]
    field_ref, field_sem, small_sem, picked_ref, law_ref = refs[17:]
    small = (delay_ref, channel_ref, blocks_ref, cells_ref, size_ref, slope_ref)
    copies = [
        pltpu.make_async_copy(source, target, small_sem.at[i])
        for i, (source, target) in enumerate(zip(small_hbm, small))
    ]
    for copy in copies:
        copy.start()
    field_copies = [
        pltpu.make_async_copy(
            field_hbm.at[:, parity], field_ref.at[:, parity], field_sem.at[parity]
        )
        for parity in range(2)
    ]
    field_copies[0].start()
    order = slot_order(slots)
    for copy in copies:
        copy.wait()
    field_copies[1].start()
    group = lax.axis_index("elem")
    groups = (1 - group, group)
    picks = jnp.concatenate(
        [flaw_pick(order, which, cells_ref) for which in groups], axis=0
    )
    factors = kirchhoff(freq_total, order, groups[0], size_ref, slope_ref)
    delays = delays_of(channel_ref, delay_ref, blocks_ref, groups, field_ref.shape[3])
    delays_ref[...] = delays[:, ROWS:]
    even, step, odd = focal_base(freq_total, delays[:, :ROWS])
    for parity, law in enumerate((even, odd)):
        store_law(law_ref.at[parity], law, step)
        field_copies[parity].wait()
        pick_fields(parity, picks, field_ref, (picked_ref, own_picked_ref))
    store_spectra(picked_ref, law_ref, *factors, (first_ref, second_ref))


def own_kernel(freq_total, slots, *refs):
    picked_ref, delays_ref, size_ref, slope_ref, out_ref, law_ref = refs
    even, step, odd = focal_base(freq_total, delays_ref[...])
    for parity, law in enumerate((even, odd)):
        store_law(law_ref.at[parity], law, step)
    group = lax.axis_index("elem")
    factors = kirchhoff(freq_total, slot_order(slots), group, size_ref, slope_ref)
    store_spectra(picked_ref, law_ref, *factors, (out_ref,))


def call(kernel, name, in_specs, out_shape, scratch):
    vmem = pl.BlockSpec(memory_space=pltpu.VMEM)
    return pl.pallas_call(
        kernel,
        in_specs=in_specs,
        out_specs=[vmem] * len(out_shape),
        out_shape=out_shape,
        scratch_shapes=scratch,
        compiler_params=pltpu.CompilerParams(vmem_limit_bytes=VMEM_BYTES),
        cost_estimate=pl.CostEstimate(flops=1000, bytes_accessed=1000, transcendentals=0),
        name=name,
    )


def partials(field, small, swap, freq_total, slots):
    elements, sites = field.shape[3:]
    vmem = pl.BlockSpec(memory_space=pltpu.VMEM)
    hbm = pl.BlockSpec(memory_space=pltpu.HBM)
    pinned = [pltpu.with_memory_space_constraint(a, pltpu.HBM) for a in (field, *small)]
    out = jax.ShapeDtypeStruct((2 * W_DEV, FG, ROWS), jnp.bfloat16)
    half = jax.ShapeDtypeStruct((2 * W_DEV, FG // 2, ROWS), jnp.bfloat16)
    picked = jax.ShapeDtypeStruct((2, W_HALF, FG, 2 * elements), jnp.bfloat16)
    law = pltpu.VMEM((2, W_HALF, 2 * elements, 2 * ROWS), jnp.bfloat16)
    copied = [jax.ShapeDtypeStruct(a.shape, a.dtype) for a in small[4:]]
    delays = jax.ShapeDtypeStruct((elements, ROWS), jnp.float32)
    first, second, own_picked, size, slope, delays = call(
        functools.partial(other_kernel, freq_total, slots),
        "other",
        [hbm] * len(pinned),
        [half, half, picked, *copied, delays],
        [
            pltpu.SMEM(a.shape, a.dtype) if a.ndim == 1 else pltpu.VMEM(a.shape, a.dtype)
            for a in small[:4]
        ]
        + [
            pltpu.VMEM(field.shape, field.dtype),
            pltpu.SemaphoreType.DMA((2,)),
            pltpu.SemaphoreType.DMA((len(small),)),
            pltpu.VMEM(picked.shape, picked.dtype),
            law,
        ],
    )(*pinned)
    first = lax.ppermute(first, "elem", swap)
    second = lax.ppermute(second, "elem", swap)
    (own,) = call(
        functools.partial(own_kernel, freq_total, slots), "own", [vmem] * 4, [out], [law]
    )(own_picked, delays, size, slope)
    return own, first, second


def add_kernel(first, own_ref, moved_ref, *refs):
    size = refs[0].shape[0]
    for slot, ref in enumerate(refs):
        own = own_ref[:, pl.ds(first + slot * size, size)].astype(jnp.float32)
        both = own + moved_ref[:, pl.ds(slot * size, size)].astype(jnp.float32)
        ref[...] = jnp.swapaxes(both, 0, 1).astype(jnp.bfloat16)


def add(own, first, second, slots):
    vmem = pl.BlockSpec(memory_space=pltpu.VMEM)
    planes, flaws, rows = own.shape
    count = max(1, slots // 2)
    shape = jax.ShapeDtypeStruct((flaws // 2 // count, planes, rows), own.dtype)
    parts = []
    for name, start, moved in (("add_first", 0, first), ("add_second", flaws // 2, second)):
        kernel = functools.partial(add_kernel, start)
        parts += call(kernel, name, [vmem] * 2, [shape] * count, [])(own, moved)
    return parts


def table_kernel(freq_total, slots, table_ref):
    height, depth = table_ref.shape[2:]
    time_block = height // 2
    row = lax.broadcasted_iota(jnp.int32, (height, depth // 2), 0)
    column = lax.broadcasted_iota(jnp.int32, (height, depth // 2), 1)
    out_imag = (row >= time_block).astype(jnp.int32)
    time = pl.program_id(0) * time_block + row - out_imag * time_block
    for parity in range(2):
        freq = (column >> 1) * 2 + parity
        if slots > 1:
            lane = lax.broadcasted_iota(jnp.int32, (1, depth // 2), 1)
            lane = (lane >> 1) * 2 + parity
            freq = partner(slots, lane // W_DEV) * W_DEV + lane % W_DEV
        steps = freq * time + ((column & 1) - out_imag) * (freq_total // 2)
        steps = (steps + 2 * freq_total) & (2 * freq_total - 1)
        _, value = sincos_turns(steps.astype(jnp.float32) * (0.5 / freq_total))
        high = value.astype(jnp.bfloat16)
        table_ref[0, parity, :, : depth // 2] = high
        table_ref[0, parity, :, depth // 2 :] = (
            value - high.astype(jnp.float32)
        ).astype(jnp.bfloat16)


def table(freq_total, slots, times, time_block):
    blocks = times // time_block
    shape = (blocks, 2, 2 * time_block, 2 * freq_total)
    return pl.pallas_call(
        functools.partial(table_kernel, freq_total, slots),
        grid=(blocks,),
        out_specs=pl.BlockSpec((1, *shape[1:]), lambda i: (i, 0, 0, 0)),
        out_shape=jax.ShapeDtypeStruct(shape, jnp.bfloat16),
        compiler_params=pltpu.CompilerParams(vmem_limit_bytes=VMEM_BYTES),
        name="table",
    )()


def peak_kernel(freq_total, folded, sources, blocks, *refs):
    def first_step():
        return blocks == 1 or pl.program_id(0) == 0

    def last_step():
        return blocks == 1 or pl.program_id(0) == blocks - 1

    count = len(refs) - 5
    table_ref, noise_ref, peak_ref, found_ref, best_ref = refs[count:]
    columns = peak_ref.shape[1]
    time_block = table_ref.shape[2] // 2

    @pl.when(first_step())
    def _():
        best_ref[...] = jnp.zeros_like(best_ref)

    width = min(2, columns)
    for first in range(0, columns, width):
        parts = []
        for parity in range(2):
            planes = slice(parity * W_DEV, (parity + 1) * W_DEV)
            spectra = jnp.concatenate(
                [
                    jnp.concatenate(
                        [
                            refs[i][row + first + k, planes, :]
                            for i, row in sources
                        ]
                        * 2,
                        axis=0,
                    )
                    for k in range(width)
                ],
                axis=1,
            )
            parts.append(dot(table_ref[0, parity], spectra, ((1,), (0,))))
        powers = []
        for signal in [parts[0] + parts[1]] + [parts[0] - parts[1]] * folded:
            real_part = signal[:time_block]
            imag_part = signal[time_block:]
            powers.append(real_part * real_part + imag_part * imag_part)
        power = jnp.maximum(powers[0], powers[-1]) if folded else powers[0]
        power = jnp.max(power, axis=0, keepdims=True)
        for k in range(width):
            row = pl.ds(first + k, 1)
            best_ref[row, :] = jnp.maximum(
                best_ref[row, :], power[:, k * ROWS : (k + 1) * ROWS]
            )

    @pl.when(last_step())
    def _():
        largest = jnp.max(best_ref[...], axis=1, keepdims=True)
        shape = best_ref.shape
        diagonal = lax.broadcasted_iota(jnp.int32, shape, 0) == lax.broadcasted_iota(
            jnp.int32, shape, 1
        )
        largest = jnp.max(jnp.where(diagonal, largest, 0.0), axis=0, keepdims=True)
        peak = jnp.sqrt(largest[:, :columns]) * (1.0 / math.sqrt(freq_total))
        score = STEEP * (jnp.log(peak + EPS) - jnp.log(noise_ref[...]))
        peak_ref[...] = peak
        found_ref[...] = 1.0 / (1.0 + jnp.exp(-score))


def peaks(spectra, sources, twiddles, noise_level, freq_total, folded):
    columns = noise_level.shape[1]
    blocks = twiddles.shape[0]
    if blocks == 1:
        vmem = pl.BlockSpec(memory_space=pltpu.VMEM)
        grid, in_specs, out_spec = (), [vmem] * (len(spectra) + 2), vmem
    else:
        grid = (blocks,)
        out_spec = pl.BlockSpec((1, columns), lambda i: (0, 0))
        in_specs = [pl.BlockSpec(a.shape, lambda i: (0, 0, 0)) for a in spectra]
        in_specs += [
            pl.BlockSpec((1, *twiddles.shape[1:]), lambda i: (i, 0, 0, 0)),
            out_spec,
        ]
    return pl.pallas_call(
        functools.partial(peak_kernel, freq_total, folded, sources, blocks),
        grid=grid,
        in_specs=in_specs,
        out_specs=[out_spec, out_spec],
        out_shape=[jax.ShapeDtypeStruct((1, columns), jnp.float32)] * 2,
        scratch_shapes=[pltpu.VMEM((max(8, columns), ROWS), jnp.float32)],
        compiler_params=pltpu.CompilerParams(vmem_limit_bytes=VMEM_BYTES),
        name="peaks",
    )(*spectra, twiddles, noise_level)


def body(
    flaw_cells,
    flaw_blocks,
    element_channel,
    focal_delay,
    beam_field,
    flaw_size,
    flaw_slope,
    noise_level,
):
    freq_count = lax.axis_size("freq")
    freq_total = W_DEV * freq_count
    sample_count = min(T_CAP, 2 * freq_total)
    swap = [(0, 1), (1, 0)]
    direct = freq_count == 8
    slots = freq_count if direct else 1
    small = (
        focal_delay,
        element_channel.reshape(1, -1),
        flaw_blocks,
        flaw_cells.reshape(1, -1),
        flaw_size,
        flaw_slope,
    )
    folded = sample_count == 2 * freq_total
    times = sample_count // 2 if folded else sample_count
    twiddles = table(freq_total, slots, times, min(128, times))
    field = beam_field.reshape(W_HALF, 2, *beam_field.shape[1:])
    parts = add(*partials(field, small, swap, freq_total, slots), slots)
    if direct:
        half = slots // 2
        spectra = []
        for slot, masks in enumerate(zip(*slot_masks(slots))):
            pairs = [(a, a ^ masks[((2 * a) ^ a) & half != 0]) for a in range(slots)]
            own = slot == slots - 1
            spectra.append(parts[slot] if own else lax.ppermute(parts[slot], "freq", pairs))
        order = (*range(half, slots - 1), *range(half), slots - 1)
        spectra = [spectra[slot] for slot in order]
        sources = [(order.index(slot), 0) for slot in range(slots)]
    else:
        whole = jnp.concatenate(parts, axis=0)
        spectra = [
            lax.all_to_all(whole, "freq", split_axis=0, concat_axis=0, tiled=True)
        ]
        sources = [(0, s * (FG // freq_count)) for s in range(freq_count)]
    return tuple(peaks(spectra, sources, twiddles, noise_level, freq_total, folded))


def solution(mesh):
    in_specs = (
        P("batch"),
        P("batch"),
        P("elem"),
        P(),
        P("freq", None, "elem", None),
        P("batch", None),
        P("batch", None),
        P(("batch", "elem"), "freq"),
    )
    out_specs = (P(("batch", "elem"), "freq"), P(("batch", "elem"), "freq"))
    return jax.shard_map(body, mesh=mesh, in_specs=in_specs, out_specs=out_specs, check_vma=False)
```

```python
import functools
import math

import jax
import jax.numpy as jnp
from jax import lax
from jax.experimental import pallas as pl
from jax.experimental.pallas import tpu as pltpu
from jax.sharding import PartitionSpec as P

W_DEV = 16
W_HALF = W_DEV // 2
FG = 128
NB = 4
SB = 32
T_CAP = 1024

EDGE = 0.6
STEEP = 3.0
EPS = 1e-05

ROWS = NB * SB
VMEM_BYTES = 48 * 1024 * 1024


def sin_half_turn(turns):
    angle = turns * math.pi
    square = angle * angle
    sine = 1.0 / 6227020800.0
    for factorial in (-39916800.0, 362880.0, -5040.0, 120.0, -6.0, 1.0):
        sine = sine * square + 1.0 / factorial
    cosine = 1.0 / 479001600.0
    for factorial in (-3628800.0, 40320.0, -720.0, 24.0, -2.0, 1.0):
        cosine = cosine * square + 1.0 / factorial
    return sine * angle, cosine


def sincos_turns(turns):
    rest = turns - jnp.floor(turns + 0.5)
    sine, cosine = sin_half_turn(rest)
    return 2.0 * sine * cosine, 1.0 - 2.0 * sine * sine


def dot(left, right, contract):
    return lax.dot_general(
        left, right, (contract, ((), ())), preferred_element_type=jnp.float32
    )


def slot_masks(slots):
    half = slots // 2
    between = (2, half + 1, half, 3, slots - 1)
    return (1, *between, slots - 2, 0), (slots - 2, *between, 1, 0)


def partner(slots, slot):
    index = lax.axis_index("freq")
    inner = ((index * 2) ^ index) & (slots // 2) != 0
    mask = jnp.zeros_like(slot)
    for s, (outer_mask, inner_mask) in enumerate(zip(*slot_masks(slots))):
        mask = jnp.where(slot == s, jnp.where(inner, inner_mask, outer_mask), mask)
    return mask ^ index


def slot_order(slots):
    size = FG // slots
    row = lax.broadcasted_iota(jnp.int32, (FG, 1), 0)
    column = lax.broadcasted_iota(jnp.int32, (FG, FG), 1)
    if slots > 1:
        row = partner(slots, row // size) * size + row % size
    return row == column


def flaw_pick(order, which, cells_ref):
    cells = jnp.where(which == 0, cells_ref[:, :FG], cells_ref[:, FG:])
    cell_sel = lax.broadcasted_iota(jnp.int32, (cells_ref.shape[1], FG), 0) == cells
    return dot(
        order.astype(jnp.bfloat16), cell_sel.astype(jnp.bfloat16), ((1,), (1,))
    ).astype(jnp.bfloat16)


def delays_of(channel_ref, delay_ref, blocks_ref, groups, elements):
    lane = lax.broadcasted_iota(jnp.int32, (1, 2 * ROWS), 1)
    position = lane & (SB - 1)
    for j in range(2 * NB):
        block = blocks_ref[groups[j // NB] * NB + j % NB]
        position = position + jnp.where((lane >> 5) == j, block * SB, 0)
    channels, positions = delay_ref.shape
    scan_sel = (
        lax.broadcasted_iota(jnp.int32, (positions, 2 * ROWS), 0) == position
    ).astype(jnp.bfloat16)
    channel_sel = (
        (lax.broadcasted_iota(jnp.int32, (channels, elements), 0) == channel_ref[...])
        .astype(jnp.float32)
        .T.astype(jnp.bfloat16)
    )
    rest = delay_ref[...]
    pieces = []
    for _ in range(3):
        pieces.append(rest.astype(jnp.bfloat16))
        rest = rest - pieces[-1].astype(jnp.float32)
    moved = jnp.concatenate(
        [dot(channel_sel, piece, ((1,), (0,))).astype(jnp.bfloat16) for piece in pieces], axis=0
    )
    moved = dot(moved, scan_sel, ((1,), (0,)))
    return moved[:elements] + moved[elements : 2 * elements] + moved[2 * elements :]


def turned(law, step):
    return law[0] * step[0] - law[1] * step[1], law[1] * step[0] + law[0] * step[1]


def focal_base(freq_total, delays):
    first_freq = lax.axis_index("freq") * W_DEV
    phase = delays * (0.5 / freq_total)
    unit = sincos_turns(phase)[::-1]
    base = sincos_turns(phase * first_freq.astype(jnp.float32))[::-1]
    return base, turned(unit, unit), turned(base, unit)


def kirchhoff(freq_total, order, which, size_ref, slope_ref):
    first_freq = lax.axis_index("freq") * W_DEV
    size = size_ref[pl.ds(which, 1), :]
    turn = size * slope_ref[pl.ds(which, 1), :] * (1.0 / freq_total)
    size = jnp.sum(jnp.where(order, size, 0.0), axis=1, keepdims=True)
    turn = jnp.sum(jnp.where(order, turn, 0.0), axis=1, keepdims=True)
    freq = first_freq + lax.broadcasted_iota(jnp.int32, (FG, FG), 1)
    sine, cosine = sincos_turns(turn * freq.astype(jnp.float32))
    return size * (1.0 + EDGE) * cosine, size * (EDGE - 1.0) * sine


def store_law(law_ref, law, step):
    elements = law_ref.shape[1] // 2
    double = 2.0 * step[0]
    following = turned(law, step)
    for w in range(W_HALF):
        c = law[0].astype(jnp.bfloat16)
        s = law[1].astype(jnp.bfloat16)
        law_ref[w, :elements, :ROWS] = c
        law_ref[w, :elements, ROWS:] = -s
        law_ref[w, elements:, :ROWS] = s
        law_ref[w, elements:, ROWS:] = c
        law, following = following, [double * x - y for x, y in zip(following, law)]


def pick_fields(parity, picks, field_ref, picked_refs):
    elements, sites = field_ref.shape[3:]
    for w in range(W_HALF):
        picked = dot(
            picks, field_ref[w, parity].reshape(2 * elements, sites), ((1,), (1,))
        ).astype(jnp.bfloat16)
        for i, ref in enumerate(picked_refs):
            ref[parity, w] = picked[i * FG : (i + 1) * FG]


def store_spectra(picked_ref, law_ref, k_real, k_imag, out_refs):
    size = out_refs[0].shape[1]
    for parity in range(2):
        for w in range(W_HALF):
            product = dot(picked_ref[parity, w], law_ref[parity, w], ((1,), (0,)))
            real_part = product[:, :ROWS]
            imag_part = product[:, ROWS:]
            kr = k_real[:, 2 * w + parity : 2 * w + parity + 1]
            ki = k_imag[:, 2 * w + parity : 2 * w + parity + 1]
            parts = (kr * real_part - ki * imag_part, kr * imag_part + ki * real_part)
            for k, part in enumerate(parts):
                part = part.astype(jnp.bfloat16)
                for i, out_ref in enumerate(out_refs):
                    out_ref[parity * W_DEV + 2 * w + k] = part[i * size : (i + 1) * size]


def other_kernel(freq_total, slots, *refs):
    field_hbm, *small_hbm = refs[:7]
    first_ref, second_ref, own_picked_ref, size_ref, slope_ref, delays_ref = refs[7:13]
    delay_ref, channel_ref, blocks_ref, cells_ref = refs[13:17]
    field_ref, field_sem, small_sem, picked_ref, law_ref = refs[17:]
    small = (delay_ref, channel_ref, blocks_ref, cells_ref, size_ref, slope_ref)
    copies = [
        pltpu.make_async_copy(source, target, small_sem.at[i])
        for i, (source, target) in enumerate(zip(small_hbm, small))
    ]
    for copy in copies:
        copy.start()
    field_copies = [
        pltpu.make_async_copy(
            field_hbm.at[:, parity], field_ref.at[:, parity], field_sem.at[parity]
        )
        for parity in range(2)
    ]
    field_copies[0].start()
    order = slot_order(slots)
    for copy in copies:
        copy.wait()
    field_copies[1].start()
    group = lax.axis_index("elem")
    groups = (1 - group, group)
    picks = jnp.concatenate(
        [flaw_pick(order, which, cells_ref) for which in groups], axis=0
    )
    factors = kirchhoff(freq_total, order, groups[0], size_ref, slope_ref)
    delays = delays_of(channel_ref, delay_ref, blocks_ref, groups, field_ref.shape[3])
    delays_ref[...] = delays[:, ROWS:]
    even, step, odd = focal_base(freq_total, delays[:, :ROWS])
    for parity, law in enumerate((even, odd)):
        store_law(law_ref.at[parity], law, step)
        field_copies[parity].wait()
        pick_fields(parity, picks, field_ref, (picked_ref, own_picked_ref))
    store_spectra(picked_ref, law_ref, *factors, (first_ref, second_ref))


def own_kernel(freq_total, slots, *refs):
    picked_ref, delays_ref, size_ref, slope_ref, out_ref, law_ref = refs
    even, step, odd = focal_base(freq_total, delays_ref[...])
    for parity, law in enumerate((even, odd)):
        store_law(law_ref.at[parity], law, step)
    group = lax.axis_index("elem")
    factors = kirchhoff(freq_total, slot_order(slots), group, size_ref, slope_ref)
    store_spectra(picked_ref, law_ref, *factors, (out_ref,))


def call(kernel, name, in_specs, out_shape, scratch):
    vmem = pl.BlockSpec(memory_space=pltpu.VMEM)
    return pl.pallas_call(
        kernel,
        in_specs=in_specs,
        out_specs=[vmem] * len(out_shape),
        out_shape=out_shape,
        scratch_shapes=scratch,
        compiler_params=pltpu.CompilerParams(vmem_limit_bytes=VMEM_BYTES),
        cost_estimate=pl.CostEstimate(flops=1000, bytes_accessed=1000, transcendentals=0),
        name=name,
    )


def partials(field, small, swap, freq_total, slots):
    elements, sites = field.shape[3:]
    vmem = pl.BlockSpec(memory_space=pltpu.VMEM)
    hbm = pl.BlockSpec(memory_space=pltpu.HBM)
    pinned = [pltpu.with_memory_space_constraint(a, pltpu.HBM) for a in (field, *small)]
    out = jax.ShapeDtypeStruct((2 * W_DEV, FG, ROWS), jnp.bfloat16)
    half = jax.ShapeDtypeStruct((2 * W_DEV, FG // 2, ROWS), jnp.bfloat16)
    picked = jax.ShapeDtypeStruct((2, W_HALF, FG, 2 * elements), jnp.bfloat16)
    law = pltpu.VMEM((2, W_HALF, 2 * elements, 2 * ROWS), jnp.bfloat16)
    copied = [jax.ShapeDtypeStruct(a.shape, a.dtype) for a in small[4:]]
    delays = jax.ShapeDtypeStruct((elements, ROWS), jnp.float32)
    first, second, own_picked, size, slope, delays = call(
        functools.partial(other_kernel, freq_total, slots),
        "other",
        [hbm] * len(pinned),
        [half, half, picked, *copied, delays],
        [
            pltpu.SMEM(a.shape, a.dtype) if a.ndim == 1 else pltpu.VMEM(a.shape, a.dtype)
            for a in small[:4]
        ]
        + [
            pltpu.VMEM(field.shape, field.dtype),
            pltpu.SemaphoreType.DMA((2,)),
            pltpu.SemaphoreType.DMA((len(small),)),
            pltpu.VMEM(picked.shape, picked.dtype),
            law,
        ],
    )(*pinned)
    first = lax.ppermute(first, "elem", swap)
    second = lax.ppermute(second, "elem", swap)
    (own,) = call(
        functools.partial(own_kernel, freq_total, slots), "own", [vmem] * 4, [out], [law]
    )(own_picked, delays, size, slope)
    return own, first, second


def add_kernel(first, own_ref, moved_ref, *refs):
    size = refs[0].shape[0]
    for slot, ref in enumerate(refs):
        own = own_ref[:, pl.ds(first + slot * size, size)].astype(jnp.float32)
        both = own + moved_ref[:, pl.ds(slot * size, size)].astype(jnp.float32)
        ref[...] = jnp.swapaxes(both, 0, 1).astype(jnp.bfloat16)


def add(own, first, second, slots):
    vmem = pl.BlockSpec(memory_space=pltpu.VMEM)
    planes, flaws, rows = own.shape
    count = max(1, slots // 2)
    shape = jax.ShapeDtypeStruct((flaws // 2 // count, planes, rows), own.dtype)
    parts = []
    for name, start, moved in (("add_first", 0, first), ("add_second", flaws // 2, second)):
        kernel = functools.partial(add_kernel, start)
        parts += call(kernel, name, [vmem] * 2, [shape] * count, [])(own, moved)
    return parts


def table_kernel(freq_total, slots, table_ref):
    height, depth = table_ref.shape[2:]
    time_block = height // 2
    row = lax.broadcasted_iota(jnp.int32, (height, depth // 2), 0)
    column = lax.broadcasted_iota(jnp.int32, (height, depth // 2), 1)
    out_imag = (row >= time_block).astype(jnp.int32)
    time = pl.program_id(0) * time_block + row - out_imag * time_block
    for parity in range(2):
        freq = (column >> 1) * 2 + parity
        if slots > 1:
            lane = lax.broadcasted_iota(jnp.int32, (1, depth // 2), 1)
            lane = (lane >> 1) * 2 + parity
            freq = partner(slots, lane // W_DEV) * W_DEV + lane % W_DEV
        steps = freq * time + ((column & 1) - out_imag) * (freq_total // 2)
        steps = (steps + 2 * freq_total) & (2 * freq_total - 1)
        _, value = sincos_turns(steps.astype(jnp.float32) * (0.5 / freq_total))
        high = value.astype(jnp.bfloat16)
        table_ref[0, parity, :, : depth // 2] = high
        table_ref[0, parity, :, depth // 2 :] = (
            value - high.astype(jnp.float32)
        ).astype(jnp.bfloat16)


def table(freq_total, slots, times, time_block):
    blocks = times // time_block
    shape = (blocks, 2, 2 * time_block, 2 * freq_total)
    return pl.pallas_call(
        functools.partial(table_kernel, freq_total, slots),
        grid=(blocks,),
        out_specs=pl.BlockSpec((1, *shape[1:]), lambda i: (i, 0, 0, 0)),
        out_shape=jax.ShapeDtypeStruct(shape, jnp.bfloat16),
        compiler_params=pltpu.CompilerParams(vmem_limit_bytes=VMEM_BYTES),
        name="table",
    )()


def peak_kernel(freq_total, folded, sources, blocks, *refs):
    def first_step():
        return blocks == 1 or pl.program_id(0) == 0

    def last_step():
        return blocks == 1 or pl.program_id(0) == blocks - 1

    count = len(refs) - 5
    table_ref, noise_ref, peak_ref, found_ref, best_ref = refs[count:]
    columns = peak_ref.shape[1]
    time_block = table_ref.shape[2] // 2

    @pl.when(first_step() and (blocks > 1 or columns < best_ref.shape[0]) if blocks == 1 else first_step())
    def _():
        best_ref[...] = jnp.zeros_like(best_ref)

    width = min(2, columns)
    for first in range(0, columns, width):
        parts = []
        for parity in range(2):
            planes = slice(parity * W_DEV, (parity + 1) * W_DEV)
            spectra = jnp.concatenate(
                [
                    jnp.concatenate(
                        [
                            refs[i][row + first + k, planes, :]
                            for i, row in sources
                        ]
                        * 2,
                        axis=0,
                    )
                    for k in range(width)
                ],
                axis=1,
            )
            parts.append(dot(table_ref[0, parity], spectra, ((1,), (0,))))
        powers = []
        for signal in [parts[0] + parts[1]] + [parts[0] - parts[1]] * folded:
            real_part = signal[:time_block]
            imag_part = signal[time_block:]
            powers.append(real_part * real_part + imag_part * imag_part)
        power = jnp.maximum(powers[0], powers[-1]) if folded else powers[0]
        power = jnp.max(power, axis=0, keepdims=True)
        for k in range(width):
            row = pl.ds(first + k, 1)
            value = power[:, k * ROWS : (k + 1) * ROWS]
            best_ref[row, :] = value if blocks == 1 else jnp.maximum(best_ref[row, :], value)

    @pl.when(last_step())
    def _():
        largest = jnp.max(best_ref[...], axis=1, keepdims=True)
        shape = best_ref.shape
        diagonal = lax.broadcasted_iota(jnp.int32, shape, 0) == lax.broadcasted_iota(
            jnp.int32, shape, 1
        )
        largest = jnp.max(jnp.where(diagonal, largest, 0.0), axis=0, keepdims=True)
        peak = jnp.sqrt(largest[:, :columns]) * (1.0 / math.sqrt(freq_total))
        score = STEEP * (jnp.log(peak + EPS) - jnp.log(noise_ref[...]))
        peak_ref[...] = peak
        found_ref[...] = 1.0 / (1.0 + jnp.exp(-score))


def peaks(spectra, sources, twiddles, noise_level, freq_total, folded):
    columns = noise_level.shape[1]
    blocks = twiddles.shape[0]
    if blocks == 1:
        vmem = pl.BlockSpec(memory_space=pltpu.VMEM)
        grid, in_specs, out_spec = (), [vmem] * (len(spectra) + 2), vmem
    else:
        grid = (blocks,)
        out_spec = pl.BlockSpec((1, columns), lambda i: (0, 0))
        in_specs = [pl.BlockSpec(a.shape, lambda i: (0, 0, 0)) for a in spectra]
        in_specs += [
            pl.BlockSpec((1, *twiddles.shape[1:]), lambda i: (i, 0, 0, 0)),
            out_spec,
        ]
    return pl.pallas_call(
        functools.partial(peak_kernel, freq_total, folded, sources, blocks),
        grid=grid,
        in_specs=in_specs,
        out_specs=[out_spec, out_spec],
        out_shape=[jax.ShapeDtypeStruct((1, columns), jnp.float32)] * 2,
        scratch_shapes=[pltpu.VMEM((max(8, columns), ROWS), jnp.float32)],
        compiler_params=pltpu.CompilerParams(vmem_limit_bytes=VMEM_BYTES),
        name="peaks",
    )(*spectra, twiddles, noise_level)


def body(
    flaw_cells,
    flaw_blocks,
    element_channel,
    focal_delay,
    beam_field,
    flaw_size,
    flaw_slope,
    noise_level,
):
    freq_count = lax.axis_size("freq")
    freq_total = W_DEV * freq_count
    sample_count = min(T_CAP, 2 * freq_total)
    swap = [(0, 1), (1, 0)]
    direct = freq_count == 8
    slots = freq_count if direct else 1
    small = (
        focal_delay,
        element_channel.reshape(1, -1),
        flaw_blocks,
        flaw_cells.reshape(1, -1),
        flaw_size,
        flaw_slope,
    )
    folded = sample_count == 2 * freq_total
    times = sample_count // 2 if folded else sample_count
    twiddles = table(freq_total, slots, times, min(128, times))
    field = beam_field.reshape(W_HALF, 2, *beam_field.shape[1:])
    parts = add(*partials(field, small, swap, freq_total, slots), slots)
    if direct:
        half = slots // 2
        spectra = []
        for slot, masks in enumerate(zip(*slot_masks(slots))):
            pairs = [(a, a ^ masks[((2 * a) ^ a) & half != 0]) for a in range(slots)]
            own = slot == slots - 1
            spectra.append(parts[slot] if own else lax.ppermute(parts[slot], "freq", pairs))
        order = (*range(half, slots - 1), *range(half), slots - 1)
        spectra = [spectra[slot] for slot in order]
        sources = [(order.index(slot), 0) for slot in range(slots)]
    else:
        whole = jnp.concatenate(parts, axis=0)
        spectra = [
            lax.all_to_all(whole, "freq", split_axis=0, concat_axis=0, tiled=True)
        ]
        sources = [(0, s * (FG // freq_count)) for s in range(freq_count)]
    return tuple(peaks(spectra, sources, twiddles, noise_level, freq_total, folded))


def solution(mesh):
    in_specs = (
        P("batch"),
        P("batch"),
        P("elem"),
        P(),
        P("freq", None, "elem", None),
        P("batch", None),
        P("batch", None),
        P(("batch", "elem"), "freq"),
    )
    out_specs = (P(("batch", "elem"), "freq"), P(("batch", "elem"), "freq"))
    return jax.shard_map(body, mesh=mesh, in_specs=in_specs, out_specs=out_specs, check_vma=False)
```

```python
import functools
import math

import jax
import jax.numpy as jnp
from jax import lax
from jax.experimental import pallas as pl
from jax.experimental.pallas import tpu as pltpu
from jax.sharding import PartitionSpec as P

W_DEV = 16
W_HALF = W_DEV // 2
FG = 128
NB = 4
SB = 32
T_CAP = 1024

EDGE = 0.6
STEEP = 3.0
EPS = 1e-05

ROWS = NB * SB
VMEM_BYTES = 48 * 1024 * 1024


def sin_half_turn(turns):
    angle = turns * math.pi
    square = angle * angle
    sine = 1.0 / 6227020800.0
    for factorial in (-39916800.0, 362880.0, -5040.0, 120.0, -6.0, 1.0):
        sine = sine * square + 1.0 / factorial
    cosine = 1.0 / 479001600.0
    for factorial in (-3628800.0, 40320.0, -720.0, 24.0, -2.0, 1.0):
        cosine = cosine * square + 1.0 / factorial
    return sine * angle, cosine


def sincos_turns(turns):
    rest = turns - jnp.floor(turns + 0.5)
    sine, cosine = sin_half_turn(rest)
    return 2.0 * sine * cosine, 1.0 - 2.0 * sine * sine


def dot(left, right, contract):
    return lax.dot_general(
        left, right, (contract, ((), ())), preferred_element_type=jnp.float32
    )


def slot_masks(slots):
    half = slots // 2
    between = (2, half + 1, half, 3, slots - 1)
    return (1, *between, slots - 2, 0), (slots - 2, *between, 1, 0)


def partner(slots, slot):
    index = lax.axis_index("freq")
    inner = ((index * 2) ^ index) & (slots // 2) != 0
    mask = jnp.zeros_like(slot)
    for s, (outer_mask, inner_mask) in enumerate(zip(*slot_masks(slots))):
        mask = jnp.where(slot == s, jnp.where(inner, inner_mask, outer_mask), mask)
    return mask ^ index


def slot_order(slots):
    size = FG // slots
    row = lax.broadcasted_iota(jnp.int32, (FG, 1), 0)
    column = lax.broadcasted_iota(jnp.int32, (FG, FG), 1)
    if slots > 1:
        row = partner(slots, row // size) * size + row % size
    return row == column


def flaw_pick(order, which, cells_ref):
    cells = jnp.where(which == 0, cells_ref[:, :FG], cells_ref[:, FG:])
    cell_sel = lax.broadcasted_iota(jnp.int32, (cells_ref.shape[1], FG), 0) == cells
    return dot(
        order.astype(jnp.bfloat16), cell_sel.astype(jnp.bfloat16), ((1,), (1,))
    ).astype(jnp.bfloat16)


def delays_of(channel_ref, delay_ref, blocks_ref, groups, elements):
    lane = lax.broadcasted_iota(jnp.int32, (1, 2 * ROWS), 1)
    position = lane & (SB - 1)
    for j in range(2 * NB):
        block = blocks_ref[groups[j // NB] * NB + j % NB]
        position = position + jnp.where((lane >> 5) == j, block * SB, 0)
    channels, positions = delay_ref.shape
    scan_sel = (
        lax.broadcasted_iota(jnp.int32, (positions, 2 * ROWS), 0) == position
    ).astype(jnp.bfloat16)
    channel_sel = (
        (lax.broadcasted_iota(jnp.int32, (channels, elements), 0) == channel_ref[...])
        .astype(jnp.float32)
        .T.astype(jnp.bfloat16)
    )
    rest = delay_ref[...]
    pieces = []
    for _ in range(3):
        pieces.append(rest.astype(jnp.bfloat16))
        rest = rest - pieces[-1].astype(jnp.float32)
    moved = jnp.concatenate(
        [dot(channel_sel, piece, ((1,), (0,))).astype(jnp.bfloat16) for piece in pieces], axis=0
    )
    moved = dot(moved, scan_sel, ((1,), (0,)))
    return moved[:elements] + moved[elements : 2 * elements] + moved[2 * elements :]


def turned(law, step):
    return law[0] * step[0] - law[1] * step[1], law[1] * step[0] + law[0] * step[1]


def focal_base(freq_total, delays):
    first_freq = lax.axis_index("freq") * W_DEV
    phase = delays * (0.5 / freq_total)
    unit = sincos_turns(phase)[::-1]
    base = sincos_turns(phase * first_freq.astype(jnp.float32))[::-1]
    return base, turned(unit, unit), turned(base, unit)


def kirchhoff(freq_total, order, which, size_ref, slope_ref):
    first_freq = lax.axis_index("freq") * W_DEV
    size = size_ref[pl.ds(which, 1), :]
    turn = size * slope_ref[pl.ds(which, 1), :] * (1.0 / freq_total)
    size = jnp.sum(jnp.where(order, size, 0.0), axis=1, keepdims=True)
    turn = jnp.sum(jnp.where(order, turn, 0.0), axis=1, keepdims=True)
    freq = first_freq + lax.broadcasted_iota(jnp.int32, (FG, FG), 1)
    sine, cosine = sincos_turns(turn * freq.astype(jnp.float32))
    return size * (1.0 + EDGE) * cosine, size * (EDGE - 1.0) * sine


def store_law(law_ref, law, step):
    elements = law_ref.shape[1] // 2
    double = 2.0 * step[0]
    following = turned(law, step)
    for w in range(W_HALF):
        c = law[0].astype(jnp.bfloat16)
        s = law[1].astype(jnp.bfloat16)
        law_ref[w, :elements, :ROWS] = c
        law_ref[w, :elements, ROWS:] = -s
        law_ref[w, elements:, :ROWS] = s
        law_ref[w, elements:, ROWS:] = c
        law, following = following, [double * x - y for x, y in zip(following, law)]


def pick_fields(parity, picks, field_ref, picked_refs):
    elements, sites = field_ref.shape[3:]
    for w in range(W_HALF):
        picked = dot(
            picks, field_ref[w, parity].reshape(2 * elements, sites), ((1,), (1,))
        ).astype(jnp.bfloat16)
        for i, ref in enumerate(picked_refs):
            ref[parity, w] = picked[i * FG : (i + 1) * FG]


def store_spectra(picked_ref, law_ref, k_real, k_imag, out_refs):
    size = out_refs[0].shape[1]
    for parity in range(2):
        for w in range(W_HALF):
            product = dot(picked_ref[parity, w], law_ref[parity, w], ((1,), (0,)))
            real_part = product[:, :ROWS]
            imag_part = product[:, ROWS:]
            kr = k_real[:, 2 * w + parity : 2 * w + parity + 1]
            ki = k_imag[:, 2 * w + parity : 2 * w + parity + 1]
            parts = (kr * real_part - ki * imag_part, kr * imag_part + ki * real_part)
            for k, part in enumerate(parts):
                part = part.astype(jnp.bfloat16)
                for i, out_ref in enumerate(out_refs):
                    out_ref[parity * W_DEV + 2 * w + k] = part[i * size : (i + 1) * size]


def other_kernel(freq_total, slots, *refs):
    field_hbm, *small_hbm = refs[:7]
    first_ref, second_ref, own_picked_ref, size_ref, slope_ref, delays_ref = refs[7:13]
    delay_ref, channel_ref, blocks_ref, cells_ref = refs[13:17]
    field_ref, field_sem, small_sem, picked_ref, law_ref = refs[17:]
    small = (delay_ref, channel_ref, blocks_ref, cells_ref, size_ref, slope_ref)
    copies = [
        pltpu.make_async_copy(source, target, small_sem.at[i])
        for i, (source, target) in enumerate(zip(small_hbm, small))
    ]
    for copy in copies:
        copy.start()
    field_copies = [
        pltpu.make_async_copy(
            field_hbm.at[:, parity], field_ref.at[:, parity], field_sem.at[parity]
        )
        for parity in range(2)
    ]
    order = slot_order(slots)
    for copy in copies[1:]:
        copy.wait()
    field_copies[0].start()
    copies[0].wait()
    field_copies[1].start()
    group = lax.axis_index("elem")
    groups = (1 - group, group)
    picks = jnp.concatenate(
        [flaw_pick(order, which, cells_ref) for which in groups], axis=0
    )
    factors = kirchhoff(freq_total, order, groups[0], size_ref, slope_ref)
    delays = delays_of(channel_ref, delay_ref, blocks_ref, groups, field_ref.shape[3])
    delays_ref[...] = delays[:, ROWS:]
    even, step, odd = focal_base(freq_total, delays[:, :ROWS])
    for parity, law in enumerate((even, odd)):
        store_law(law_ref.at[parity], law, step)
        field_copies[parity].wait()
        pick_fields(parity, picks, field_ref, (picked_ref, own_picked_ref))
    store_spectra(picked_ref, law_ref, *factors, (first_ref, second_ref))


def own_kernel(freq_total, slots, *refs):
    picked_ref, delays_ref, size_ref, slope_ref, out_ref, law_ref = refs
    even, step, odd = focal_base(freq_total, delays_ref[...])
    for parity, law in enumerate((even, odd)):
        store_law(law_ref.at[parity], law, step)
    group = lax.axis_index("elem")
    factors = kirchhoff(freq_total, slot_order(slots), group, size_ref, slope_ref)
    store_spectra(picked_ref, law_ref, *factors, (out_ref,))


def call(kernel, name, in_specs, out_shape, scratch):
    vmem = pl.BlockSpec(memory_space=pltpu.VMEM)
    return pl.pallas_call(
        kernel,
        in_specs=in_specs,
        out_specs=[vmem] * len(out_shape),
        out_shape=out_shape,
        scratch_shapes=scratch,
        compiler_params=pltpu.CompilerParams(vmem_limit_bytes=VMEM_BYTES),
        cost_estimate=pl.CostEstimate(flops=1000, bytes_accessed=1000, transcendentals=0),
        name=name,
    )


def partials(field, small, swap, freq_total, slots):
    elements, sites = field.shape[3:]
    vmem = pl.BlockSpec(memory_space=pltpu.VMEM)
    hbm = pl.BlockSpec(memory_space=pltpu.HBM)
    pinned = [pltpu.with_memory_space_constraint(a, pltpu.HBM) for a in (field, *small)]
    out = jax.ShapeDtypeStruct((2 * W_DEV, FG, ROWS), jnp.bfloat16)
    half = jax.ShapeDtypeStruct((2 * W_DEV, FG // 2, ROWS), jnp.bfloat16)
    picked = jax.ShapeDtypeStruct((2, W_HALF, FG, 2 * elements), jnp.bfloat16)
    law = pltpu.VMEM((2, W_HALF, 2 * elements, 2 * ROWS), jnp.bfloat16)
    copied = [jax.ShapeDtypeStruct(a.shape, a.dtype) for a in small[4:]]
    delays = jax.ShapeDtypeStruct((elements, ROWS), jnp.float32)
    first, second, own_picked, size, slope, delays = call(
        functools.partial(other_kernel, freq_total, slots),
        "other",
        [hbm] * len(pinned),
        [half, half, picked, *copied, delays],
        [
            pltpu.SMEM(a.shape, a.dtype) if a.ndim == 1 else pltpu.VMEM(a.shape, a.dtype)
            for a in small[:4]
        ]
        + [
            pltpu.VMEM(field.shape, field.dtype),
            pltpu.SemaphoreType.DMA((2,)),
            pltpu.SemaphoreType.DMA((len(small),)),
            pltpu.VMEM(picked.shape, picked.dtype),
            law,
        ],
    )(*pinned)
    first = lax.ppermute(first, "elem", swap)
    second = lax.ppermute(second, "elem", swap)
    (own,) = call(
        functools.partial(own_kernel, freq_total, slots), "own", [vmem] * 4, [out], [law]
    )(own_picked, delays, size, slope)
    return own, first, second


def add_kernel(first, own_ref, moved_ref, *refs):
    size = refs[0].shape[0]
    for slot, ref in enumerate(refs):
        own = own_ref[:, pl.ds(first + slot * size, size)].astype(jnp.float32)
        both = own + moved_ref[:, pl.ds(slot * size, size)].astype(jnp.float32)
        ref[...] = jnp.swapaxes(both, 0, 1).astype(jnp.bfloat16)


def add(own, first, second, slots):
    vmem = pl.BlockSpec(memory_space=pltpu.VMEM)
    planes, flaws, rows = own.shape
    count = max(1, slots // 2)
    shape = jax.ShapeDtypeStruct((flaws // 2 // count, planes, rows), own.dtype)
    parts = []
    for name, start, moved in (("add_first", 0, first), ("add_second", flaws // 2, second)):
        kernel = functools.partial(add_kernel, start)
        parts += call(kernel, name, [vmem] * 2, [shape] * count, [])(own, moved)
    return parts


def table_kernel(freq_total, slots, table_ref):
    height, depth = table_ref.shape[2:]
    time_block = height // 2
    row = lax.broadcasted_iota(jnp.int32, (height, depth // 2), 0)
    column = lax.broadcasted_iota(jnp.int32, (height, depth // 2), 1)
    out_imag = (row >= time_block).astype(jnp.int32)
    time = pl.program_id(0) * time_block + row - out_imag * time_block
    for parity in range(2):
        freq = (column >> 1) * 2 + parity
        if slots > 1:
            lane = lax.broadcasted_iota(jnp.int32, (1, depth // 2), 1)
            lane = (lane >> 1) * 2 + parity
            freq = partner(slots, lane // W_DEV) * W_DEV + lane % W_DEV
        steps = freq * time + ((column & 1) - out_imag) * (freq_total // 2)
        steps = (steps + 2 * freq_total) & (2 * freq_total - 1)
        _, value = sincos_turns(steps.astype(jnp.float32) * (0.5 / freq_total))
        high = value.astype(jnp.bfloat16)
        table_ref[0, parity, :, : depth // 2] = high
        table_ref[0, parity, :, depth // 2 :] = (
            value - high.astype(jnp.float32)
        ).astype(jnp.bfloat16)


def table(freq_total, slots, times, time_block):
    blocks = times // time_block
    shape = (blocks, 2, 2 * time_block, 2 * freq_total)
    return pl.pallas_call(
        functools.partial(table_kernel, freq_total, slots),
        grid=(blocks,),
        out_specs=pl.BlockSpec((1, *shape[1:]), lambda i: (i, 0, 0, 0)),
        out_shape=jax.ShapeDtypeStruct(shape, jnp.bfloat16),
        compiler_params=pltpu.CompilerParams(vmem_limit_bytes=VMEM_BYTES),
        name="table",
    )()


def peak_kernel(freq_total, folded, sources, blocks, *refs):
    def first_step():
        return blocks == 1 or pl.program_id(0) == 0

    def last_step():
        return blocks == 1 or pl.program_id(0) == blocks - 1

    count = len(refs) - 5
    table_ref, noise_ref, peak_ref, found_ref, best_ref = refs[count:]
    columns = peak_ref.shape[1]
    time_block = table_ref.shape[2] // 2

    @pl.when(first_step())
    def _():
        best_ref[...] = jnp.zeros_like(best_ref)

    width = min(2, columns)
    for first in range(0, columns, width):
        parts = []
        for parity in range(2):
            planes = slice(parity * W_DEV, (parity + 1) * W_DEV)
            spectra = jnp.concatenate(
                [
                    jnp.concatenate(
                        [
                            refs[i][row + first + k, planes, :]
                            for i, row in sources
                        ]
                        * 2,
                        axis=0,
                    )
                    for k in range(width)
                ],
                axis=1,
            )
            parts.append(dot(table_ref[0, parity], spectra, ((1,), (0,))))
        powers = []
        for signal in [parts[0] + parts[1]] + [parts[0] - parts[1]] * folded:
            real_part = signal[:time_block]
            imag_part = signal[time_block:]
            powers.append(real_part * real_part + imag_part * imag_part)
        power = jnp.maximum(powers[0], powers[-1]) if folded else powers[0]
        power = jnp.max(power, axis=0, keepdims=True)
        for k in range(width):
            row = pl.ds(first + k, 1)
            best_ref[row, :] = jnp.maximum(
                best_ref[row, :], power[:, k * ROWS : (k + 1) * ROWS]
            )

    @pl.when(last_step())
    def _():
        largest = jnp.max(best_ref[...], axis=1, keepdims=True)
        shape = best_ref.shape
        diagonal = lax.broadcasted_iota(jnp.int32, shape, 0) == lax.broadcasted_iota(
            jnp.int32, shape, 1
        )
        largest = jnp.max(jnp.where(diagonal, largest, 0.0), axis=0, keepdims=True)
        peak = jnp.sqrt(largest[:, :columns]) * (1.0 / math.sqrt(freq_total))
        score = STEEP * (jnp.log(peak + EPS) - jnp.log(noise_ref[...]))
        peak_ref[...] = peak
        found_ref[...] = 1.0 / (1.0 + jnp.exp(-score))


def peaks(spectra, sources, twiddles, noise_level, freq_total, folded):
    columns = noise_level.shape[1]
    blocks = twiddles.shape[0]
    if blocks == 1:
        vmem = pl.BlockSpec(memory_space=pltpu.VMEM)
        grid, in_specs, out_spec = (), [vmem] * (len(spectra) + 2), vmem
    else:
        grid = (blocks,)
        out_spec = pl.BlockSpec((1, columns), lambda i: (0, 0))
        in_specs = [pl.BlockSpec(a.shape, lambda i: (0, 0, 0)) for a in spectra]
        in_specs += [
            pl.BlockSpec((1, *twiddles.shape[1:]), lambda i: (i, 0, 0, 0)),
            out_spec,
        ]
    return pl.pallas_call(
        functools.partial(peak_kernel, freq_total, folded, sources, blocks),
        grid=grid,
        in_specs=in_specs,
        out_specs=[out_spec, out_spec],
        out_shape=[jax.ShapeDtypeStruct((1, columns), jnp.float32)] * 2,
        scratch_shapes=[pltpu.VMEM((max(8, columns), ROWS), jnp.float32)],
        compiler_params=pltpu.CompilerParams(vmem_limit_bytes=VMEM_BYTES),
        name="peaks",
    )(*spectra, twiddles, noise_level)


def body(
    flaw_cells,
    flaw_blocks,
    element_channel,
    focal_delay,
    beam_field,
    flaw_size,
    flaw_slope,
    noise_level,
):
    freq_count = lax.axis_size("freq")
    freq_total = W_DEV * freq_count
    sample_count = min(T_CAP, 2 * freq_total)
    swap = [(0, 1), (1, 0)]
    direct = freq_count == 8
    slots = freq_count if direct else 1
    small = (
        focal_delay,
        element_channel.reshape(1, -1),
        flaw_blocks,
        flaw_cells.reshape(1, -1),
        flaw_size,
        flaw_slope,
    )
    folded = sample_count == 2 * freq_total
    times = sample_count // 2 if folded else sample_count
    twiddles = table(freq_total, slots, times, min(128, times))
    field = beam_field.reshape(W_HALF, 2, *beam_field.shape[1:])
    parts = add(*partials(field, small, swap, freq_total, slots), slots)
    if direct:
        half = slots // 2
        spectra = []
        for slot, masks in enumerate(zip(*slot_masks(slots))):
            pairs = [(a, a ^ masks[((2 * a) ^ a) & half != 0]) for a in range(slots)]
            own = slot == slots - 1
            spectra.append(parts[slot] if own else lax.ppermute(parts[slot], "freq", pairs))
        order = (*range(half, slots - 1), *range(half), slots - 1)
        spectra = [spectra[slot] for slot in order]
        sources = [(order.index(slot), 0) for slot in range(slots)]
    else:
        whole = jnp.concatenate(parts, axis=0)
        spectra = [
            lax.all_to_all(whole, "freq", split_axis=0, concat_axis=0, tiled=True)
        ]
        sources = [(0, s * (FG // freq_count)) for s in range(freq_count)]
    return tuple(peaks(spectra, sources, twiddles, noise_level, freq_total, folded))


def solution(mesh):
    in_specs = (
        P("batch"),
        P("batch"),
        P("elem"),
        P(),
        P("freq", None, "elem", None),
        P("batch", None),
        P("batch", None),
        P(("batch", "elem"), "freq"),
    )
    out_specs = (P(("batch", "elem"), "freq"), P(("batch", "elem"), "freq"))
    return jax.shard_map(body, mesh=mesh, in_specs=in_specs, out_specs=out_specs, check_vma=False)
```
